32 devices in a mesh: dp: 4 (over x, core), row: 4 (over z), col: 2 (over y).
Axes of the slice: x: 2, y: 2, z: 4, core: 2. Of those that a mesh axis runs over, the one named last changes fastest.
Arguments:
- tokens: bfloat16 [16, 16, 32, 1152], P('dp', 'row', 'col'), may hold values from -6 to 6
- conditioning: bfloat16 [16, 1152], P('dp'), may hold values from -6 to 6
- heights: int32 [16], P('dp'), may hold values from 8 to 16, as said below
- widths: int32 [16], P('dp'), may hold values from 16 to 32, as said below
- cotangent: bfloat16 [16, 16, 32, 1152], P('dp', 'row', 'col'), may hold values from -6 to 6
- w_mod: bfloat16 [1152, 6912], P(None, ('dp', 'row', 'col')), may hold values from -0.1875 to 0.1875
- b_mod: bfloat16 [6912], P(('dp', 'row', 'col')), may hold values from -2 to 2
- w_qkv: bfloat16 [1152, 3456], P(('dp', 'row', 'col')), may hold values from -0.1875 to 0.1875
- b_qkv: bfloat16 [3456], P(('dp', 'row', 'col')), may hold values from -2 to 2
- query_gain: float32 [72], replicated, may hold values from 0.5 to 1.5
- key_gain: float32 [72], replicated, may hold values from 0.5 to 1.5
- w_proj: bfloat16 [1152, 1152], P(('dp', 'row', 'col')), may hold values from -3 to 3
- b_proj: bfloat16 [1152], P(('dp', 'row', 'col')), may hold values from -2 to 2
- w_gu: bfloat16 [1152, 6144], P(('dp', 'row', 'col')), may hold values from -0.1875 to 0.1875
- b_gu: bfloat16 [6144], P(('dp', 'row', 'col')), may hold values from -2 to 2
- w_down: bfloat16 [3072, 1152], P(('dp', 'row', 'col')), may hold values from -0.109375 to 0.109375
- b_down: bfloat16 [1152], P(('dp', 'row', 'col')), may hold values from -2 to 2
Outputs:
- block_out: bfloat16 [16, 16, 32, 1152], P('dp', 'row', 'col')
- d_tokens: float32 [16, 16, 32, 1152], P('dp', 'row', 'col')
- d_conditioning: float32 [16, 1152], P('dp', ('row', 'col'))
- d_w_mod: float32 [1152, 6912], P(None, ('dp', 'row', 'col'))
- d_b_mod: float32 [6912], P(('dp', 'row', 'col'))
- d_w_qkv: float32 [1152, 3456], P(('dp', 'row', 'col'))
- d_b_query_key: float32 [2304], P(('dp', 'row', 'col'))
- d_b_value: float32 [1152], P(('dp', 'row', 'col'))
- d_query_gain: float32 [72], replicated
- d_key_gain: float32 [72], replicated
- d_w_proj: float32 [1152, 1152], P(('dp', 'row', 'col'))
- d_b_proj: float32 [1152], P(('dp', 'row', 'col'))
- d_w_gu: float32 [1152, 6144], P(('dp', 'row', 'col'))
- d_b_gu: float32 [6144], P(('dp', 'row', 'col'))
- d_w_down: float32 [3072, 1152], P(('dp', 'row', 'col'))
- d_b_down: float32 [1152], P(('dp', 'row', 'col'))
The draws below stay inside these ranges and needn't reach their ends.
Inputs may be any that keep to these rules, and one draw needn't show every extreme that they name: `heights`: each item's grid height; in every draw some item has exactly 16. `widths`: each item's grid width; in every draw some item has exactly 32.
All inputs are finite; a program needn't handle non-finite values.
Results may differ from the reference program's by a relative error of at most 0.014.
Values may be sent and summed in bfloat16 or wider, within the bound.
A program may use at most 320 MiB of HBM per device.

```python
import math
import jax
import jax.numpy as jnp
from jax import lax

D = 1152
HEADS = 16
HEAD = 72
FF = 3072
GRID_ROWS = 16
GRID_COLS = 32
ITEMS = 16


def grid_extent(key, salt_value, largest):
    draw_key, spot_key = jax.random.split(jax.random.fold_in(key, salt_value))
    extents = jax.random.randint(draw_key, (ITEMS,), largest // 2, largest + 1)
    chosen = jax.random.randint(spot_key, (), 0, ITEMS)
    return jnp.where(jnp.arange(ITEMS) == chosen, largest, extents).astype(jnp.int32)


def draw_heights(key, part):
    return grid_extent(key, 101, GRID_ROWS)


def draw_widths(key, part):
    return grid_extent(key, 202, GRID_COLS)


def level_of(stream_key, extent, pieces, smallest, high):
    gain = 1.0
    for position, shards_of in pieces:
        steps = jax.random.uniform(jax.random.fold_in(jax.random.fold_in(stream_key, 6), position), (shards_of,), jnp.float32, smallest / len(pieces), high / len(pieces))
        gain = gain * jnp.repeat(jnp.exp(steps), extent[position] // shards_of).reshape((-1,) + (1,) * (len(extent) - 1 - position))
    return gain


def bell_draw(stream_key, dims, spread, bound, shards=(), dtype=jnp.bfloat16):
    entries = jax.random.normal(stream_key, dims, jnp.float32) * spread
    if len(shards) > 0:
        entries = level_of(stream_key, dims, shards, -0.22, 0.18) * entries
    return jnp.clip(entries, min=-bound, max=bound).astype(dtype)


def setup_inputs(seed: int = 0) -> dict:
    key_list = jax.random.split(jax.random.key(seed), 18)
    tokens = bell_draw(key_list[0], (ITEMS, GRID_ROWS, GRID_COLS, D), 1.0, 6.0, ((0, 4), (1, 4), (2, 2)))
    conditioning = bell_draw(key_list[1], (ITEMS, D), 1.0, 6.0, ((0, 4),))
    heights = draw_heights(jax.random.fold_in(key_list[17], 71), 0)
    widths = draw_widths(jax.random.fold_in(key_list[17], 71), 0)
    cotangent = bell_draw(key_list[4], (ITEMS, GRID_ROWS, GRID_COLS, D), 1.0, 6.0, ((0, 4), (1, 4), (2, 2)))
    w_mod = bell_draw(key_list[5], (D, 6 * D), D ** -0.5, 0.1875, ((1, 32),))
    b_mod = bell_draw(key_list[6], (6 * D,), 0.3, 2.0, ((0, 32),))
    w_qkv = bell_draw(key_list[7], (D, 3 * D), D ** -0.5, 0.1875, ((0, 32),))
    b_qkv = bell_draw(key_list[8], (3 * D,), 0.3, 2.0, ((0, 32),))
    query_gain = jnp.clip(1.0 + 0.1 * jax.random.normal(key_list[9], (HEAD,), jnp.float32), 0.5, 1.5)
    key_gain = jnp.clip(1.0 + 0.1 * jax.random.normal(key_list[10], (HEAD,), jnp.float32), 0.5, 1.5)
    w_proj = bell_draw(key_list[11], (D, D), (max(1, 2 * D // (GRID_ROWS * GRID_COLS))) ** -0.5, 3.0, ((0, 32),))
    b_proj = bell_draw(key_list[12], (D,), 0.3, 2.0, ((0, 32),))
    w_gu = bell_draw(key_list[13], (D, 2 * FF), D ** -0.5, 0.1875, ((0, 32),))
    b_gu = bell_draw(key_list[14], (2 * FF,), 0.3, 2.0, ((0, 32),))
    w_down = bell_draw(key_list[15], (FF, D), FF ** -0.5, 0.109375, ((0, 32),))
    b_down = bell_draw(key_list[16], (D,), 0.3, 2.0, ((0, 32),))
    return {"tokens": tokens, "conditioning": conditioning, "heights": heights, "widths": widths, "cotangent": cotangent, "w_mod": w_mod, "b_mod": b_mod, "w_qkv": w_qkv, "b_qkv": b_qkv, "query_gain": query_gain, "key_gain": key_gain, "w_proj": w_proj, "b_proj": b_proj, "w_gu": w_gu, "b_gu": b_gu, "w_down": w_down, "b_down": b_down}


@jax.custom_vjp
def low(v):
    return lax.optimization_barrier(v.astype(jnp.bfloat16)).astype(jnp.float32)

@jax.custom_vjp
def low_back(v):
    return v

def low_keep(v):
    return (low(v), None)

def low_pass(kept, grad):
    return (grad,)

def back_keep(v):
    return (v, None)

def back_low(kept, grad):
    return (low(grad),)
low.defvjp(low_keep, low_pass)
low_back.defvjp(back_keep, back_low)
EPSILON = 1e-06
MASKED = -1000000000.0
PRECISE = lax.Precision.HIGHEST

def matmul(left_side, right_side):
    return jnp.dot(left_side, right_side, precision=PRECISE)

def silu_of(values):
    return values * jax.nn.sigmoid(values)

def rope_tables(row_pos, col_pos, head_size):
    half_size = head_size // 2
    lane_index = jnp.arange(head_size)
    pair_index = (lane_index % half_size // 2).astype(jnp.float32)
    frequency = jnp.exp(-math.log(10000.0) * 2.0 * pair_index / half_size)
    places = jnp.where(lane_index[None, :] >= half_size, col_pos[:, None], row_pos[:, None]).astype(jnp.float32)
    angles = places * frequency[None, :]
    return (jnp.cos(angles), jnp.sin(angles))

def rotate(values):
    pair_view = values.reshape(values.shape[:-1] + (values.shape[-1] // 2, 2))
    turned = jnp.stack((-pair_view[..., 1], pair_view[..., 0]), axis=-1)
    return turned.reshape(values.shape)

def layer_norm(values):
    centered = values - lax.optimization_barrier(jnp.mean(values, -1, keepdims=True))
    return centered * lax.rsqrt(lax.optimization_barrier(jnp.mean(centered * centered, -1, keepdims=True)) + EPSILON)

def head_norm(values, gain_vec):
    return values * lax.rsqrt(lax.optimization_barrier(jnp.mean(values * values, -1, keepdims=True)) + EPSILON) * gain_vec

def turn_heads(values, cos_tab, sin_tab):
    return values * cos_tab[:, None, :] + rotate(values) * sin_tab[:, None, :]

def forward(tokens_f, cond_f, w_mod, b_mod, w_qkv, b_qkv, query_gain, key_gain, w_proj, b_proj, w_gu, b_gu, w_down, b_down, valid, cos_tab, sin_tab):
    inv_root = 1.0 / math.sqrt(HEAD)
    act_low = low(silu_of(cond_f))
    modul = matmul(act_low[None, :], w_mod)[0] + b_mod
    shift_a, scale_a, gate_a, shift_m, scale_m, gate_m = jnp.split(modul, 6)
    h_attn = low(layer_norm(tokens_f) * (1.0 + scale_a) + shift_a)
    qkv_all = low_back(matmul(h_attn, w_qkv) + b_qkv)
    query_raw, key_raw, value_raw = jnp.split(qkv_all, 3, axis=1)
    query_rot = low(turn_heads(head_norm(query_raw.reshape(-1, HEADS, HEAD), query_gain), cos_tab, sin_tab))
    key_rot = low(turn_heads(head_norm(key_raw.reshape(-1, HEADS, HEAD), key_gain), cos_tab, sin_tab))
    value_low = low(value_raw.reshape(-1, HEADS, HEAD))
    scores = low_back(jnp.einsum('thd,khd->htk', query_rot, key_rot, precision=PRECISE) * inv_root)
    scores = jnp.where(valid[None, None, :], scores, MASKED)
    row_max = lax.optimization_barrier(jnp.max(scores, -1, keepdims=True))
    exponent = jnp.exp(scores - row_max)
    probs = low(exponent / lax.optimization_barrier(jnp.sum(exponent, -1, keepdims=True)))
    attended = jnp.einsum('htk,khd->thd', probs, value_low, precision=PRECISE).reshape(-1, D)
    attended = low_back(low(attended))
    attn_out = low_back(matmul(attended, w_proj) + b_proj)
    resid_mid = tokens_f + gate_a * attn_out
    h_mlp = low(layer_norm(resid_mid) * (1.0 + scale_m) + shift_m)
    gate_up = low_back(matmul(h_mlp, w_gu) + b_gu)
    gate_part, up_part = jnp.split(gate_up, 2, axis=1)
    hidden = low(silu_of(gate_part) * up_part)
    mlp_out = low_back(matmul(hidden, w_down) + b_down)
    return (resid_mid + gate_m * mlp_out) * valid[:, None].astype(jnp.float32)

def reference(tokens, conditioning, heights, widths, cotangent, w_mod, b_mod, w_qkv, b_qkv, query_gain, key_gain, w_proj, b_proj, w_gu, b_gu, w_down, b_down):
    grid_size = GRID_ROWS * GRID_COLS
    cell_index = jnp.arange(grid_size)
    row_pos = cell_index // GRID_COLS
    col_pos = cell_index % GRID_COLS
    cos_tab, sin_tab = rope_tables(row_pos, col_pos, HEAD)
    weight_list = tuple((weight.astype(jnp.float32) for weight in (w_mod, b_mod, w_qkv, b_qkv, query_gain, key_gain, w_proj, b_proj, w_gu, b_gu, w_down, b_down)))
    tokens_all = tokens.reshape(ITEMS, grid_size, D).astype(jnp.float32)
    cot_all = cotangent.reshape(ITEMS, grid_size, D).astype(jnp.float32)
    cond_all = conditioning.astype(jnp.float32)

    def one_item(running, item_data):
        tokens_f, cond_f, height_now, width_now, out_grad = item_data
        valid = (row_pos < height_now) & (col_pos < width_now)

        def apply_block(tokens_in, cond_in, *weights):
            return forward(tokens_in, cond_in, *weights, valid, cos_tab, sin_tab)
        result, pullback = jax.vjp(apply_block, tokens_f, cond_f, *weight_list)
        grads = pullback(out_grad)
        running = tuple((summed + fresh for summed, fresh in zip(running, grads[2:])))
        return (running, (result.astype(jnp.bfloat16), grads[0], grads[1]))
    start_sums = tuple((jnp.zeros(weight.shape, jnp.float32) for weight in weight_list))
    totals, (outputs, token_grads, cond_grads) = lax.scan(one_item, start_sums, (tokens_all, cond_all, heights, widths, cot_all))
    return (outputs.reshape(ITEMS, GRID_ROWS, GRID_COLS, D), token_grads.reshape(ITEMS, GRID_ROWS, GRID_COLS, D), cond_grads, totals[0], totals[1], totals[2], totals[3][:2 * D], totals[3][2 * D:], totals[4], totals[5], totals[6], totals[7], totals[8], totals[9], totals[10], totals[11])
```

```python
import math

import jax
import jax.numpy as jnp
import numpy as np
from jax import lax
from jax.experimental import pallas as pl
from jax.experimental.pallas import tpu as pltpu
from jax.sharding import PartitionSpec as P

HEADS = 16
HEAD = 72
FF = 3072


EPSILON = 1e-06
MASKED = -1000000000.0
PRECISE = lax.Precision.HIGHEST


def rope_tables(row_pos, col_pos, head_size):
    half_size = head_size // 2
    lane_index = jnp.arange(head_size)
    pair_index = (lane_index % half_size // 2).astype(jnp.float32)
    frequency = jnp.exp(-math.log(10000.0) * 2.0 * pair_index / half_size)
    places = jnp.where(lane_index[None, :] >= half_size, col_pos[:, None], row_pos[:, None]).astype(
        jnp.float32
    )
    angles = places * frequency[None, :]
    return (jnp.cos(angles), jnp.sin(angles))


def rotate(values):
    pair_view = values.reshape(values.shape[:-1] + (values.shape[-1] // 2, 2))
    turned = jnp.stack((-pair_view[..., 1], pair_view[..., 0]), axis=-1)
    return turned.reshape(values.shape)


def norm_parts(values):
    centered = values - jnp.mean(values, -1, keepdims=True)
    recip = lax.rsqrt(jnp.mean(centered * centered, -1, keepdims=True) + EPSILON)
    return (centered * recip, recip)


def norm_back(gradient, normed, recip):
    return recip * (
        gradient
        - jnp.mean(gradient, -1, keepdims=True)
        - normed * jnp.mean(gradient * normed, -1, keepdims=True)
    )


def head_back(gradient, raw_value, recip, gain_vec):
    scaled = gradient * gain_vec
    gain_grad = jnp.sum(gradient * raw_value * recip, axis=(0, 1, 2))
    raw_grad = recip * scaled - raw_value * (recip * recip * recip) * jnp.mean(
        scaled * raw_value, -1, keepdims=True
    )
    return (raw_grad, gain_grad)


def general(
    tokens,
    conditioning,
    heights,
    widths,
    cotangent,
    w_mod,
    b_mod,
    w_qkv,
    b_qkv,
    query_gain,
    key_gain,
    w_proj,
    b_proj,
    w_gu,
    b_gu,
    w_down,
    b_down,
):
    item_count, tile_rows, tile_cols, model_width = tokens.shape
    tile_span = tile_rows * tile_cols
    n_row = lax.axis_size("row")
    n_col = lax.axis_size("col")
    groups = n_row * n_col
    key_count = tile_span * groups
    inv_root = 1.0 / math.sqrt(HEAD)
    row_at = lax.axis_index("row")
    col_at = lax.axis_index("col")
    local_index = jnp.arange(tile_span)
    query_rows = row_at * tile_rows + local_index // tile_cols
    query_cols = col_at * tile_cols + local_index % tile_cols
    valid_query = (query_rows[None, :] < heights[:, None]) & (query_cols[None, :] < widths[:, None])
    key_index = jnp.arange(key_count)
    key_owner = key_index // tile_span
    key_spot = key_index % tile_span
    key_rows = key_owner // n_col * tile_rows + key_spot // tile_cols
    key_cols = key_owner % n_col * tile_cols + key_spot % tile_cols
    valid_key = (key_rows[None, :] < heights[:, None]) & (key_cols[None, :] < widths[:, None])
    cos_tab, sin_tab = rope_tables(query_rows, query_cols, HEAD)
    cos_four = cos_tab[None, :, None, :]
    sin_four = sin_tab[None, :, None, :]
    cond_f = conditioning.astype(jnp.float32)
    cond_sig = jax.nn.sigmoid(cond_f)
    act_low = (cond_f * cond_sig).astype(jnp.bfloat16)
    gathered = (
        lax.all_gather(w_mod, ("dp", "row", "col"), axis=1, tiled=True),
        lax.all_gather(b_mod, ("dp", "row", "col"), axis=0, tiled=True),
        lax.all_gather(w_qkv, ("dp", "row", "col"), axis=0, tiled=True),
        lax.all_gather(b_qkv, ("dp", "row", "col"), axis=0, tiled=True),
        lax.all_gather(w_proj, ("dp", "row", "col"), axis=0, tiled=True),
        lax.all_gather(b_proj, ("dp", "row", "col"), axis=0, tiled=True),
        lax.all_gather(w_gu, ("dp", "row", "col"), axis=0, tiled=True),
        lax.all_gather(b_gu, ("dp", "row", "col"), axis=0, tiled=True),
        lax.all_gather(w_down, ("dp", "row", "col"), axis=0, tiled=True),
        lax.all_gather(b_down, ("dp", "row", "col"), axis=0, tiled=True),
    )
    (
        w_mod_all,
        b_mod_all,
        w_qkv_all,
        b_qkv_all,
        w_proj_all,
        b_proj_all,
        w_gu_all,
        b_gu_all,
        w_down_all,
        b_down_all,
    ) = gathered
    modul = jnp.dot(act_low, w_mod_all, preferred_element_type=jnp.float32) + b_mod_all.astype(
        jnp.float32
    )
    shift_a, scale_a, gate_a, shift_m, scale_m, gate_m = [
        modul[:, piece * model_width : (piece + 1) * model_width][:, None, :] for piece in range(6)
    ]
    resid_in = tokens.reshape(item_count, tile_span, model_width).astype(jnp.float32)
    normed_a, recip_a = norm_parts(resid_in)
    h_attn = (normed_a * (1.0 + scale_a) + shift_a).astype(jnp.bfloat16)
    qkv_all = jnp.dot(h_attn, w_qkv_all, preferred_element_type=jnp.float32) + b_qkv_all.astype(
        jnp.float32
    )
    query_raw = qkv_all[..., :model_width].reshape(item_count, tile_span, HEADS, HEAD)
    key_raw = qkv_all[..., model_width : 2 * model_width].reshape(
        item_count, tile_span, HEADS, HEAD
    )
    value_raw = qkv_all[..., 2 * model_width :]
    query_recip = lax.rsqrt(jnp.mean(query_raw * query_raw, -1, keepdims=True) + EPSILON)
    key_recip = lax.rsqrt(jnp.mean(key_raw * key_raw, -1, keepdims=True) + EPSILON)
    query_normed = query_raw * query_recip * query_gain
    key_normed = key_raw * key_recip * key_gain
    query_rot = (query_normed * cos_four + rotate(query_normed) * sin_four).astype(jnp.bfloat16)
    key_rot = (key_normed * cos_four + rotate(key_normed) * sin_four).astype(jnp.bfloat16)
    value_low = value_raw.astype(jnp.bfloat16)
    kv_local = jnp.concatenate([key_rot.reshape(item_count, tile_span, model_width), value_low], -1)
    kv_every = lax.all_gather(kv_local, ("row", "col"), axis=1, tiled=True)
    query_heads = query_rot.transpose(2, 0, 1, 3)
    key_part = (
        kv_every[..., :model_width]
        .reshape(item_count, key_count, HEADS, HEAD)
        .transpose(2, 0, 1, 3)
    )
    value_part = (
        kv_every[..., model_width:]
        .reshape(item_count, key_count, HEADS, HEAD)
        .transpose(2, 0, 1, 3)
    )
    key_mask = valid_key[:, None, :]

    def attend(head_block):
        query_h, key_h, value_h = head_block
        scores = (
            jnp.einsum("itd,ikd->itk", query_h, key_h, preferred_element_type=jnp.float32)
            * inv_root
        )
        scores = jnp.where(key_mask, scores, MASKED)
        row_max = jnp.max(scores, -1, keepdims=True)
        exponent = jnp.exp(scores - row_max)
        row_sum = jnp.sum(exponent, -1, keepdims=True)
        probs = (exponent / row_sum).astype(jnp.bfloat16)
        result = jnp.einsum("itk,ikd->itd", probs, value_h, preferred_element_type=jnp.float32)
        return (result, row_max, row_sum)

    attended_heads, max_kept, sum_kept = lax.map(attend, (query_heads, key_part, value_part))
    attended = (
        attended_heads.transpose(1, 2, 0, 3)
        .reshape(item_count, tile_span, model_width)
        .astype(jnp.bfloat16)
    )
    attn_out = jnp.dot(
        attended, w_proj_all, preferred_element_type=jnp.float32
    ) + b_proj_all.astype(jnp.float32)
    resid_mid = resid_in + gate_a * attn_out
    normed_m, recip_m = norm_parts(resid_mid)
    h_mlp = (normed_m * (1.0 + scale_m) + shift_m).astype(jnp.bfloat16)
    gate_up = jnp.dot(h_mlp, w_gu_all, preferred_element_type=jnp.float32) + b_gu_all.astype(
        jnp.float32
    )
    gate_part = gate_up[..., :FF]
    up_part = gate_up[..., FF:]
    gate_sig = jax.nn.sigmoid(gate_part)
    gate_act = gate_part * gate_sig
    hidden = (gate_act * up_part).astype(jnp.bfloat16)
    mlp_out = jnp.dot(hidden, w_down_all, preferred_element_type=jnp.float32) + b_down_all.astype(
        jnp.float32
    )
    mask_f = valid_query[..., None].astype(jnp.float32)
    block_out = ((resid_mid + gate_m * mlp_out) * mask_f).astype(jnp.bfloat16)
    out_grad = cotangent.reshape(item_count, tile_span, model_width).astype(jnp.float32) * mask_f
    d_mlp = (gate_m * out_grad).astype(jnp.bfloat16)
    d_gate_m = jnp.sum(out_grad * mlp_out, 1)
    dw_down = jnp.einsum("itf,itd->fd", hidden, d_mlp, preferred_element_type=jnp.float32)
    db_down = jnp.sum(d_mlp.astype(jnp.float32), (0, 1))
    d_hidden = jnp.einsum("itd,fd->itf", d_mlp, w_down_all, preferred_element_type=jnp.float32)
    d_gate = d_hidden * up_part * gate_sig * (1.0 + gate_part * (1.0 - gate_sig))
    d_up = d_hidden * gate_act
    d_gate_up = jnp.concatenate([d_gate, d_up], -1).astype(jnp.bfloat16)
    dw_gu = jnp.einsum("itd,ite->de", h_mlp, d_gate_up, preferred_element_type=jnp.float32)
    db_gu = jnp.sum(d_gate_up.astype(jnp.float32), (0, 1))
    d_hmlp = jnp.einsum("ite,de->itd", d_gate_up, w_gu_all, preferred_element_type=jnp.float32)
    d_shift_m = jnp.sum(d_hmlp, 1)
    d_scale_m = jnp.sum(d_hmlp * normed_m, 1)
    d_mid = out_grad + norm_back(d_hmlp * (1.0 + scale_m), normed_m, recip_m)
    d_attn = (gate_a * d_mid).astype(jnp.bfloat16)
    d_gate_a = jnp.sum(d_mid * attn_out, 1)
    dw_proj = jnp.einsum("itd,ite->de", attended, d_attn, preferred_element_type=jnp.float32)
    db_proj = jnp.sum(d_attn.astype(jnp.float32), (0, 1))
    d_attended = jnp.einsum(
        "ite,de->itd", d_attn, w_proj_all, preferred_element_type=jnp.float32
    ).astype(jnp.bfloat16)
    d_att_heads = d_attended.reshape(item_count, tile_span, HEADS, HEAD).transpose(2, 0, 1, 3)
    key_back, value_back = (key_part, value_part)

    def attend_back(head_block):
        query_h, key_h, value_h, grad_h, max_h, sum_h = head_block
        scores = (
            jnp.einsum("itd,ikd->itk", query_h, key_h, preferred_element_type=jnp.float32)
            * inv_root
        )
        scores = jnp.where(key_mask, scores, MASKED)
        probs = jnp.exp(scores - max_h) / sum_h
        d_probs = jnp.einsum("itd,ikd->itk", grad_h, value_h, preferred_element_type=jnp.float32)
        delta = jnp.sum(probs * d_probs, -1, keepdims=True)
        d_scores = (probs * (d_probs - delta)).astype(jnp.bfloat16)
        d_query = (
            jnp.einsum("itk,ikd->itd", d_scores, key_h, preferred_element_type=jnp.float32)
            * inv_root
        )
        d_key = (
            jnp.einsum("itk,itd->ikd", d_scores, query_h, preferred_element_type=jnp.float32)
            * inv_root
        )
        d_value = jnp.einsum(
            "itk,itd->ikd", probs.astype(jnp.bfloat16), grad_h, preferred_element_type=jnp.float32
        )
        return (d_query, d_key, d_value)

    dq_heads, dk_heads, dv_heads = lax.map(
        attend_back, (query_heads, key_back, value_back, d_att_heads, max_kept, sum_kept)
    )
    dkv_term = jnp.concatenate(
        [
            dk_heads.transpose(1, 2, 0, 3).reshape(item_count, key_count, model_width),
            dv_heads.transpose(1, 2, 0, 3).reshape(item_count, key_count, model_width),
        ],
        -1,
    )
    dkv_own = lax.psum_scatter(dkv_term, ("row", "col"), scatter_dimension=1, tiled=True)
    d_key_rot = dkv_own[..., :model_width].reshape(item_count, tile_span, HEADS, HEAD)
    d_value = dkv_own[..., model_width:]
    d_query_rot = dq_heads.transpose(1, 2, 0, 3)
    d_query_n = d_query_rot * cos_four - rotate(d_query_rot * sin_four)
    d_key_n = d_key_rot * cos_four - rotate(d_key_rot * sin_four)
    d_query_raw, dq_gain = head_back(d_query_n, query_raw, query_recip, query_gain)
    d_key_raw, dk_gain = head_back(d_key_n, key_raw, key_recip, key_gain)
    gain_total = lax.psum((dq_gain, dk_gain), ("dp", "row", "col"))
    d_qkv = jnp.concatenate(
        [
            d_query_raw.reshape(item_count, tile_span, model_width),
            d_key_raw.reshape(item_count, tile_span, model_width),
            d_value,
        ],
        -1,
    ).astype(jnp.bfloat16)
    dw_qkv = jnp.einsum("itd,ite->de", h_attn, d_qkv, preferred_element_type=jnp.float32)
    db_qkv = jnp.sum(d_qkv.astype(jnp.float32), (0, 1))
    db_query_key = db_qkv[: 2 * model_width]
    db_value = db_qkv[2 * model_width :]
    d_hattn = jnp.einsum("ite,de->itd", d_qkv, w_qkv_all, preferred_element_type=jnp.float32)
    d_shift_a = jnp.sum(d_hattn, 1)
    d_scale_a = jnp.sum(d_hattn * normed_a, 1)
    d_tokens = d_mid + norm_back(d_hattn * (1.0 + scale_a), normed_a, recip_a)
    d_modul = jnp.concatenate([d_shift_a, d_scale_a, d_gate_a, d_shift_m, d_scale_m, d_gate_m], -1)
    act_f = act_low.astype(jnp.float32)
    dw_mod = jnp.einsum("id,ie->de", act_f, d_modul, precision=PRECISE)
    db_mod = jnp.sum(d_modul, 0)
    d_act = jnp.einsum("ie,de->id", d_modul, w_mod_all.astype(jnp.float32), precision=PRECISE)
    d_cond_part = d_act * cond_sig * (1.0 + cond_f * (1.0 - cond_sig))
    d_cond = lax.psum_scatter(d_cond_part, ("row", "col"), scatter_dimension=1, tiled=True)
    summed = (
        lax.psum_scatter(dw_mod, ("dp", "row", "col"), scatter_dimension=1, tiled=True),
        lax.psum_scatter(db_mod, ("dp", "row", "col"), scatter_dimension=0, tiled=True),
        lax.psum_scatter(dw_qkv, ("dp", "row", "col"), scatter_dimension=0, tiled=True),
        lax.psum_scatter(db_query_key, ("dp", "row", "col"), scatter_dimension=0, tiled=True),
        lax.psum_scatter(db_value, ("dp", "row", "col"), scatter_dimension=0, tiled=True),
        lax.psum_scatter(dw_proj, ("dp", "row", "col"), scatter_dimension=0, tiled=True),
        lax.psum_scatter(db_proj, ("dp", "row", "col"), scatter_dimension=0, tiled=True),
        lax.psum_scatter(dw_gu, ("dp", "row", "col"), scatter_dimension=0, tiled=True),
        lax.psum_scatter(db_gu, ("dp", "row", "col"), scatter_dimension=0, tiled=True),
        lax.psum_scatter(dw_down, ("dp", "row", "col"), scatter_dimension=0, tiled=True),
        lax.psum_scatter(db_down, ("dp", "row", "col"), scatter_dimension=0, tiled=True),
    )
    (
        g_w_mod,
        g_b_mod,
        g_w_qkv,
        g_b_query_key,
        g_b_value,
        g_w_proj,
        g_b_proj,
        g_w_gu,
        g_b_gu,
        g_w_down,
        g_b_down,
    ) = summed
    return (
        block_out.reshape(item_count, tile_rows, tile_cols, model_width),
        d_tokens.reshape(item_count, tile_rows, tile_cols, model_width),
        d_cond,
        g_w_mod,
        g_b_mod,
        g_w_qkv,
        g_b_query_key,
        g_b_value,
        gain_total[0],
        gain_total[1],
        g_w_proj,
        g_b_proj,
        g_w_gu,
        g_b_gu,
        g_w_down,
        g_b_down,
    )


MESH = pl.DeviceIdType.MESH
BF = jnp.bfloat16
F32 = jnp.float32
LIMIT = 60 * 1024 * 1024
D = 1152
UNIT = 36
PAD = 48
TOK = 256
GROUP = 1024
SPLIT_Q, SPLIT_P, SPLIT_G, SPLIT_D = 384, 640, 768, 640
ROOT = 1.0 / math.sqrt(HEAD)


def nn(a, b):
    return lax.dot_general(a, b, (((1,), (0,)), ((), ())), preferred_element_type=F32)


def nt(a, b):
    return lax.dot_general(a, b, (((1,), (1,)), ((), ())), preferred_element_type=F32)


def tn(a, b):
    return lax.dot_general(a, b, (((0,), (0,)), ((), ())), preferred_element_type=F32)


def width_order():
    xx, zh, yy, zl, cc, jj = np.indices((2, 2, 2, 2, 2, UNIT)).reshape(6, -1)
    return ((((xx * 2 + cc) * 2 + zh) * 2 + zl) * 2 + yy) * UNIT + jj


def constants():
    perm = np.zeros((D, D), np.float32)
    perm[width_order(), np.arange(D)] = 1.0
    spread = np.zeros((864, 1536), np.float32)
    tt, hh, yy, jj = np.indices((3, 4, 2, UNIT)).reshape(4, -1)
    spread[tt * 288 + hh * 72 + yy * 36 + jj, tt * 512 + hh * 128 + yy * 64 + jj] = 1.0
    pick = np.zeros((144, 192), np.float32)
    kk, jj = np.indices((4, UNIT)).reshape(2, -1)
    pick[kk * 36 + jj, kk * 48 + jj] = 1.0
    spot = np.arange(512)
    row = spot // 128 * 4 + spot // 16 % 4
    col = spot // 64 % 2 * 16 + spot % 16
    lane = np.arange(128)
    part = lane % 64
    freq = np.exp(-math.log(10000.0) * 2.0 * (part // 2) / 36.0)
    place = np.where(lane[None, :] >= 64, col[:, None], row[:, None]).astype(np.float64)
    angle = place * freq[None, :]
    live = part < UNIT
    cos = np.where(live, np.cos(angle), 0.0)
    sin = np.where(live, np.sin(angle), 0.0)
    even = lane % 2 == 0
    tabs = np.stack([cos, np.where(even, -sin, 0.0), np.where(even, 0.0, sin)]).astype(np.float32)
    return (
        jnp.asarray(perm, BF),
        jnp.asarray(spread, BF),
        jnp.asarray(pick, BF),
        jnp.asarray(tabs, F32),
        row,
        col,
    )


class Place:
    def __init__(self):
        dp = lax.axis_index("dp")
        self.z = lax.axis_index("row")
        self.y = lax.axis_index("col")
        self.x = dp // 2
        self.c = dp % 2
        self.zh = self.z // 2
        self.zl = self.z % 2
        self.m = self.zl * 2 + self.c
        self.dp = dp

    def mate(self, r):
        c = 1 - self.c if r % 2 else self.c
        zl = 1 - self.zl if r // 2 else self.zl
        return zl * 2 + c, (self.x * 2 + c, self.zh * 2 + zl, self.y)

    def xpeer(self):
        return ((1 - self.x) * 2 + self.c, self.z, self.y)

    def ypeer(self):
        return (self.dp, self.z, 1 - self.y)

    def zpeer(self):
        return (self.dp, (1 - self.zh) * 2 + self.zl, self.y)

    def item_home(self, j):
        return (self.x * 2 + self.zh, j, self.c)

    def item_source(self, blk):
        return (self.x * 2 + self.y, self.c * 2 + blk // 2, blk % 2)

    def is_me(self, dev):
        return (dev[0] == self.dp) & (dev[1] == self.z) & (dev[2] == self.y)


class Link:
    def __init__(self, here, ssem, rsem):
        self.here, self.ssem, self.rsem, self.n, self.open = here, ssem, rsem, 0, []

    def greet(self, items):
        here = self.here
        bar = pltpu.get_barrier_semaphore()
        devs = [here.mate(r)[1] for r in (1, 2, 3)]
        devs += [here.xpeer(), here.ypeer(), here.zpeer()]
        for d in devs:
            pl.semaphore_signal(bar, inc=1, device_id=d, device_id_type=MESH)
        total = len(devs)
        if items:
            for d in [here.item_home(j) for j in range(4)] + [here.item_source(j) for j in range(4)]:


                @pl.when(jnp.logical_not(here.is_me(d)))
                def _():
                    pl.semaphore_signal(bar, inc=1, device_id=d, device_id_type=MESH)

            far = (here.zh - here.c) * (here.zh - here.c)
            off = (here.y - here.c) * (here.y - here.c)
            total += 8 - 2 * (1 - far) * (1 - off)
        pl.semaphore_wait(bar, total)

    def send(self, src, dst, dev):
        k = self.n
        self.n += 1
        copy = pltpu.make_async_remote_copy(
            src_ref=src,
            dst_ref=dst,
            send_sem=self.ssem.at[k],
            recv_sem=self.rsem.at[k],
            device_id=dev,
            device_id_type=MESH,
        )
        copy.start()
        self.open.append(copy)
        return copy

    def scatter(self, src_of, dst, dev_of, slot):
        base = self.n
        self.n += 4
        here = self.here
        copies = []
        for j in range(4):
            dev = dev_of(j)
            mine = here.is_me(dev)
            remote = pltpu.make_async_remote_copy(
                src_ref=src_of(j),
                dst_ref=dst,
                send_sem=self.ssem.at[base + j],
                recv_sem=self.rsem.at[base + slot],
                device_id=dev,
                device_id_type=MESH,
            )
            local_copy = pltpu.make_async_copy(src_of(j), dst, self.rsem.at[base + slot])

            @pl.when(mine)
            def _():
                local_copy.start()

            @pl.when(jnp.logical_not(mine))
            def _():
                remote.start()

            copies.append((mine, remote))

        def wait_send():
            for mine, remote in copies:

                @pl.when(jnp.logical_not(mine))
                def _():
                    remote.wait_send()

        def wait_recv(src, dst_of):
            for j in range(4):
                pltpu.make_async_copy(src, dst_of(j), self.rsem.at[base + j]).wait()

        return wait_send, wait_recv

    def finish(self):
        for copy in self.open:
            copy.wait_send()
        self.open = []


def norm_rows(x):
    mean = jnp.sum(x, -1, keepdims=True) * (1.0 / D)
    cent = x - mean
    var = jnp.sum(cent * cent, -1, keepdims=True) * (1.0 / D)
    recip = lax.rsqrt(var + EPSILON)
    return cent * recip, recip


def norm_rows_back(g, y, recip):
    mg = jnp.sum(g, -1, keepdims=True) * (1.0 / D)
    mgy = jnp.sum(g * y, -1, keepdims=True) * (1.0 / D)
    return recip * (g - mg - y * mgy)


def at(i, n):
    return pl.ds(pl.multiple_of(i * n, n), n)


class Gather:
    def __init__(self, link, ref, rows, split):
        self.link, self.ref, self.rows, self.split = link, ref, rows, split

    def cut(self, i, j, k, cols):
        return self.ref.at[i, j, k, pl.ds(0, self.rows), cols]

    def hop1(self):
        h = self.link.here
        part = self.cut(h.x, h.zh, h.y, slice(None))
        self.a = self.link.send(part, part, h.zpeer())

    def hop2(self):
        h = self.link.here
        self.a.wait_recv()
        pa = self.cut(h.x, slice(None), h.y, pl.ds(0, self.split))
        pb = self.cut(h.x, slice(None), h.y, pl.ds(self.split, self.ref.shape[-1] - self.split))
        self.a = self.link.send(pa, pa, h.xpeer())
        self.b = self.link.send(pb, pb, h.ypeer())

    def hop3(self):
        h = self.link.here
        self.a.wait_recv()
        self.b.wait_recv()
        pa = self.cut(slice(None), slice(None), h.y, pl.ds(0, self.split))
        pb = self.cut(
            h.x, slice(None), slice(None), pl.ds(self.split, self.ref.shape[-1] - self.split)
        )
        self.a = self.link.send(pa, pa, h.ypeer())
        self.b = self.link.send(pb, pb, h.xpeer())

    def done(self):
        self.a.wait_recv()
        self.b.wait_recv()


class Reduce:
    def __init__(self, link, ref, bufs, split):
        self.link, self.ref, self.split = link, ref, split
        self.cols = ref.shape[-1]
        self.r1a, self.r1b, self.r2a, self.r2b, self.r3a, self.r3b = bufs

    @staticmethod
    def buffers(rows, cols, split):
        rest = cols - split
        return [
            pltpu.VMEM((2, 2, rows, split), BF),
            pltpu.VMEM((2, 2, rows, rest), BF),
            pltpu.VMEM((2, rows, split), BF),
            pltpu.VMEM((2, rows, rest), BF),
            pltpu.VMEM((rows, split), BF),
            pltpu.VMEM((rows, rest), BF),
        ]

    def hop1(self):
        h = self.link.here
        ca, cb = pl.ds(0, self.split), pl.ds(self.split, self.cols - self.split)
        self.a = self.link.send(self.ref.at[1 - h.x, :, :, :, ca], self.r1a, h.xpeer())
        self.b = self.link.send(self.ref.at[:, :, 1 - h.y, :, cb], self.r1b, h.ypeer())

    def hop2(self):
        h = self.link.here
        ca, cb = pl.ds(0, self.split), pl.ds(self.split, self.cols - self.split)
        self.a.wait_recv()
        self.b.wait_recv()

        def add(i, carry):
            u, v = i // 2, i % 2
            own = self.ref[h.x, u, v, :, ca].astype(F32)
            self.r1a[u, v] = (self.r1a[u, v].astype(F32) + own).astype(BF)
            own = self.ref[u, v, h.y, :, cb].astype(F32)
            self.r1b[u, v] = (self.r1b[u, v].astype(F32) + own).astype(BF)
            return carry

        lax.fori_loop(0, 4, add, 0)
        self.a = self.link.send(self.r1a.at[:, 1 - h.y], self.r2a, h.ypeer())
        self.b = self.link.send(self.r1b.at[1 - h.x], self.r2b, h.xpeer())

    def hop3(self):
        h = self.link.here
        self.a.wait_recv()
        self.b.wait_recv()

        def add(u, carry):
            own = self.r1a[u, h.y].astype(F32)
            self.r2a[u] = (self.r2a[u].astype(F32) + own).astype(BF)
            own = self.r1b[h.x, u].astype(F32)
            self.r2b[u] = (self.r2b[u].astype(F32) + own).astype(BF)
            return carry

        lax.fori_loop(0, 2, add, 0)
        self.a = self.link.send(self.r2a.at[1 - h.zh], self.r3a, h.zpeer())
        self.b = self.link.send(self.r2b.at[1 - h.zh], self.r3b, h.zpeer())

    def done(self):
        h = self.link.here
        self.a.wait_recv()
        self.b.wait_recv()
        left = self.r2a[h.zh].astype(F32) + self.r3a[...].astype(F32)
        right = self.r2b[h.zh].astype(F32) + self.r3b[...].astype(F32)
        return left.astype(BF), right.astype(BF)


def all_rows(link, ref):
    here = link.here
    own = ref.at[at(here.m, TOK)]
    return {r: link.send(own, own, here.mate(r)[1]) for r in (2, 3, 1)}


def turn(v, cos, sina, sinb):
    return v * cos + pltpu.roll(v, 127, 1) * sina + pltpu.roll(v, 1, 1) * sinb


def turn_back(d, cos, sina, sinb):
    return d * cos - pltpu.roll(d, 127, 1) * sina - pltpu.roll(d, 1, 1) * sinb


def kernel_a(
    tok_in, cot_in, wq_in, wg_in, wp_in, wd_in, perm, spread, pick, tabs, gains, modv, bq, bp, maskb, valid,
    wq, wp, wg, wd, ha, rawq, rawk, qr, kr, vv, att, hm, dmlp, tokp, og, attn_out,
    s0q, s0g, tokr, cotr, wqe, psend, precv, pown, ssem, rsem, lsem,
):
    here = Place()
    link = Link(here, ssem, rsem)
    link.greet(True)
    m = here.m
    slot = here.zl * 2 + here.y
    rows_in = at(slot, 64)
    tok_sent, tok_got = link.scatter(lambda j: tok_in.at[j], tokr.at[rows_in], here.item_home, slot)
    sq, sg = {}, {}
    for r in (2, 3, 1):
        k, dev = here.mate(r)
        sq[r] = link.send(wq_in.at[k], s0q.at[m], dev)
    own_q = pltpu.make_async_copy(wq_in.at[m], s0q.at[m], lsem.at[0])
    own_q.start()
    for r in (2, 3, 1):
        k, dev = here.mate(r)
        sg[r] = link.send(wg_in.at[k], s0g.at[m], dev)
    own_g = pltpu.make_async_copy(wg_in.at[m], s0g.at[m], lsem.at[1])
    own_g.start()

    gq = Gather(link, wq, 144, SPLIT_Q)
    gp = Gather(link, wp, PAD, SPLIT_P)
    gg = Gather(link, wg, 144, SPLIT_G)
    gd = Gather(link, wd, 96, SPLIT_D)

    own_q.wait()
    for r in (1, 2, 3):
        sq[r].wait_recv()
    wq[here.x, here.zh, here.y] = nn(pick[...], s0q[...].reshape(192, 864)).astype(BF)
    gq.hop1()
    wp[:, :, :, PAD:64, :] = jnp.zeros((2, 2, 2, 64 - PAD, D), BF)
    wp[here.x, here.zh, here.y, 0:PAD, :] = nn(wp_in[...], perm[...]).astype(BF)
    gp.hop1()
    own_g.wait()
    for r in (1, 2, 3):
        sg[r].wait_recv()
    wg[here.x, here.zh, here.y] = nn(pick[...], s0g[...].reshape(192, 1536)).astype(BF)
    tok_got(tok_in.at[0], lambda j: tokr.at[pl.ds(j * 64, 64)])
    gg.hop1()
    wd[here.x, here.zh, here.y] = nn(wd_in[...], perm[...]).astype(BF)
    gd.hop1()

    tokp[...] = nn(tokr[...], perm[...]).astype(BF)

    def first_norm(i, carry):
        n, _ = norm_rows(tokp[at(i, 32), :].astype(F32))
        h = n * (1.0 + modv[1:2, :]) + modv[0:1, :]
        ha[pl.ds(pl.multiple_of(m * TOK + i * 32, 32), 32), :] = h.astype(BF)
        return carry

    lax.fori_loop(0, 8, first_norm, 0)
    ha_sent = all_rows(link, ha)
    cot_sent, cot_got = link.scatter(lambda j: cot_in.at[j], cotr.at[rows_in], here.item_home, slot)
    gq.hop2()
    gp.hop2()
    gq.hop3()
    gp.hop3()
    for r in (1, 2, 3):
        ha_sent[r].wait_recv()
    gq.done()

    def widen(i, carry):
        part = wq[i // 2, i % 2].reshape(288, 864)
        wqe[at(i, 288), :] = nn(part, spread[...]).astype(BF)
        return carry

    lax.fori_loop(0, 4, widen, 0)

    def project(b, carry):
        acc = nn(ha[at(b, TOK), :], wqe[...]) + bq[...]
        item, half = b // 2, at(b % 2, TOK)
        cos, sina, sinb = tabs[0, half, :], tabs[1, half, :], tabs[2, half, :]
        for h in range(4):
            p = item * 4 + h
            for t, raw, rot in ((0, rawq, qr), (1, rawk, kr)):
                v = acc[:, t * 512 + h * 128 : t * 512 + h * 128 + 128]
                recip = lax.rsqrt(jnp.sum(v * v, -1, keepdims=True) * (1.0 / HEAD) + EPSILON)
                raw[p, half, :] = v
                n = v * recip * gains[t : t + 1, :]
                rot[p, half, :] = turn(n, cos, sina, sinb).astype(BF)
            vv[p, half, :] = acc[:, 1024 + h * 128 : 1152 + h * 128].astype(BF)
        return carry

    lax.fori_loop(0, 4, project, 0)
    gg.hop2()
    gd.hop2()

    def attend(p, carry):
        item = p // 4
        lanes = at(p % 4, 128)
        for half in range(2):
            rows = pl.ds(half * TOK, TOK)
            s = nt(qr[p, rows, :], kr[p]) * ROOT + maskb[item]
            top = jnp.max(s, -1, keepdims=True)
            e = jnp.exp(s - top)
            pr = (e / jnp.sum(e, -1, keepdims=True)).astype(BF)
            out_rows = pl.ds(pl.multiple_of(item * 512 + half * TOK, TOK), TOK)
            att[out_rows, lanes] = nn(pr, vv[p]).astype(BF)
        return carry

    lax.fori_loop(0, 4, attend, 0)
    gg.hop3()
    gd.hop3()
    lax.fori_loop(4, 8, attend, 0)
    gp.done()
    wpf = wp[...].reshape(512, D)
    sent = {}
    for r in (2, 3, 1):
        k, dev = here.mate(r)
        psend[r - 1] = nn(att[at(k, TOK), :], wpf).astype(BF)
        sent[r] = link.send(psend.at[r - 1], precv.at[r - 1], dev)
    pown[...] = nn(att[at(m, TOK), :], wpf)
    cot_got(cot_in.at[0], lambda j: cotr.at[pl.ds(j * 64, 64)])
    og[...] = (nn(cotr[...], perm[...]) * valid[...]).astype(BF)

    def scale_grad(i, carry):
        g = og[at(i, 32), :].astype(F32) * modv[5:6, :]
        dmlp[pl.ds(pl.multiple_of(m * TOK + i * 32, 32), 32), :] = g.astype(BF)
        return carry

    lax.fori_loop(0, 8, scale_grad, 0)
    for r in (1, 2, 3):
        sent[r].wait_recv()

    def second_norm(i, carry):
        rows = at(i, 32)
        a = pown[rows, :] + bp[...]
        for r in range(3):
            a += precv[r, rows, :].astype(F32)
        attn_out[rows, :] = a
        n, _ = norm_rows(tokp[rows, :].astype(F32) + modv[2:3, :] * a)
        h = n * (1.0 + modv[4:5, :]) + modv[3:4, :]
        hm[pl.ds(pl.multiple_of(m * TOK + i * 32, 32), 32), :] = h.astype(BF)
        return carry

    lax.fori_loop(0, 8, second_norm, 0)
    hm_sent = all_rows(link, hm)
    dm_sent = all_rows(link, dmlp)
    for r in (1, 2, 3):
        hm_sent[r].wait_recv()
        dm_sent[r].wait_recv()
    gg.done()
    gd.done()
    link.finish()
    tok_sent()
    cot_sent()


def store_tiles(val, ref, base, piece, keep):
    block = ref.shape[3] if keep is None else piece
    for q in range(val.shape[0] // piece):
        row = base + q * piece
        f, off = row // block, row % block
        n = piece if keep is None else keep
        ref[f // 4, f // 2 % 2, f % 2, off : off + n, :] = val[q * piece : q * piece + n, :].astype(BF)


def kernel_b(
    wg, wd, hm, dmlp, tokp, og, attn_out, modv, bg, bd, perm, valid,
    dwg, dwd, dattn, dmid, bout, small, dbg,
    gu, coef, hid, hsend, hrecv, hown, msend, mrecv, mown, bo, ssem, rsem,
):
    here = Place()
    link = Link(here, ssem, rsem)
    link.greet(True)
    m = here.m
    wgf = wg[...].reshape(D, 1536)
    wdf = wd[...].reshape(768, D)
    small[...] = jnp.zeros_like(small)
    dbg[...] = jnp.zeros_like(dbg)

    def mlp(k):
        gu[...] = nn(hm[at(k, TOK), :], wgf) + bg[...]

        def acts(i, carry):
            rows = at(i, 32)
            out = pl.ds(pl.multiple_of(k * TOK + i * 32, 32), 32)
            g, u = gu[rows, 0:768], gu[rows, 768:1536]
            sig = jax.nn.sigmoid(g)
            act = g * sig
            hid[out, :] = (act * u).astype(BF)
            gu[rows, 0:768] = u * sig * (1.0 + g * (1.0 - sig))
            gu[rows, 768:1536] = act
            return carry

        lax.fori_loop(0, 8, acts, 0)
        dh = nt(dmlp[at(k, TOK), :], wdf)
        out = at(k, TOK)
        coef[out, 0:768] = (gu[:, 0:768] * dh).astype(BF)
        coef[out, 768:1536] = (gu[:, 768:1536] * dh).astype(BF)
        dbg[0:1, :] += jnp.sum(coef[out, :].astype(F32), 0, keepdims=True)

    hs, ms = {}, {}
    for r in (2, 3, 1):
        k, dev = here.mate(r)
        mlp(k)
        hsend[r - 1] = nt(coef[at(k, TOK), :], wgf).astype(BF)
        hs[r] = link.send(hsend.at[r - 1], hrecv.at[r - 1], dev)
    mlp(m)
    hown[...] = nt(coef[at(m, TOK), :], wgf)
    for r in (2, 3, 1):
        k, dev = here.mate(r)
        msend[r - 1] = nn(hid[at(k, TOK), :], wdf).astype(BF)
        ms[r] = link.send(msend.at[r - 1], mrecv.at[r - 1], dev)
    mown[...] = nn(hid[at(m, TOK), :], wdf)
    for r in (1, 2, 3):
        hs[r].wait_recv()

    def mid_back(i, carry):
        rows = at(i, 32)
        d = hown[rows, :]
        for r in range(3):
            d += hrecv[r, rows, :].astype(F32)
        a = attn_out[rows, :]
        n, recip = norm_rows(tokp[rows, :].astype(F32) + modv[2:3, :] * a)
        small[1:2, :] += jnp.sum(d, 0, keepdims=True)
        small[2:3, :] += jnp.sum(d * n, 0, keepdims=True)
        g = og[rows, :].astype(F32) + norm_rows_back(d * (1.0 + modv[4:5, :]), n, recip)
        dmid[rows, :] = g
        small[3:4, :] += jnp.sum(g * a, 0, keepdims=True)
        low = (modv[2:3, :] * g).astype(BF)
        dattn[pl.ds(pl.multiple_of(m * TOK + i * 32, 32), 32), :] = low
        small[5:6, :] += jnp.sum(low.astype(F32), 0, keepdims=True)
        return carry

    lax.fori_loop(0, 8, mid_back, 0)
    da = all_rows(link, dattn)
    for i in range(3):
        store_tiles(tn(hm[:, i * 384 : i * 384 + 384], coef[...]), dwg, i * 384, 48, None)
    for i in range(2):
        store_tiles(tn(hid[:, i * 384 : i * 384 + 384], dmlp[...]), dwd, i * 384, 96, None)
    for r in (1, 2, 3):
        ms[r].wait_recv()

    def finish_out(i, carry):
        rows = at(i, 32)
        o = mown[rows, :] + bd[...]
        for r in range(3):
            o += mrecv[r, rows, :].astype(F32)
        g = og[rows, :].astype(F32)
        small[0:1, :] += jnp.sum(g * o, 0, keepdims=True)
        mine = dmlp[pl.ds(pl.multiple_of(m * TOK + i * 32, 32), 32), :]
        small[4:5, :] += jnp.sum(mine.astype(F32), 0, keepdims=True)
        mid = tokp[rows, :].astype(F32) + modv[2:3, :] * attn_out[rows, :]
        bo[rows, :] = ((mid + modv[5:6, :] * o) * valid[rows, :]).astype(BF)
        return carry

    lax.fori_loop(0, 8, finish_out, 0)
    bo[...] = nt(bo[...], perm[...]).astype(BF)
    sent, got = link.scatter(
        lambda j: bo.at[pl.ds(j * 64, 64)], bout.at[here.z], here.item_source, here.z
    )
    for r in (1, 2, 3):
        da[r].wait_recv()
    got(bo.at[pl.ds(0, 64)], lambda j: bout.at[j])
    link.finish()
    sent()


def kernel_c(
    dwg, dwd, dattn, att, wp, wq, ha, rawq, rawk, qr, kr, vv, maskb, dmid, tokp, modv, gains, tabs, perm, spread, pick,
    dtok, fq, fg, fp, fd, small, dbq, dgain,
    dwq, dwp, datt, de, dc, tsend, trecv, town, to, eq, eg,
    g1a, g1b, g2a, g2b, g3a, g3b, d1a, d1b, d2a, d2b, d3a, d3b,
    q1a, q1b, q2a, q2b, q3a, q3b, p1a, p1b, p2a, p2b, p3a, p3b, ssem, rsem,
):
    here = Place()
    link = Link(here, ssem, rsem)
    link.greet(True)
    m = here.m
    rg = Reduce(link, dwg, (g1a, g1b, g2a, g2b, g3a, g3b), SPLIT_G)
    rd = Reduce(link, dwd, (d1a, d1b, d2a, d2b, d3a, d3b), SPLIT_D)
    rq = Reduce(link, dwq, (q1a, q1b, q2a, q2b, q3a, q3b), SPLIT_Q)
    rp = Reduce(link, dwp, (p1a, p1b, p2a, p2b, p3a, p3b), SPLIT_P)
    rg.hop1()
    rd.hop1()
    small[...] = jnp.zeros_like(small)
    dgain[...] = jnp.zeros_like(dgain)
    dbq[...] = jnp.zeros_like(dbq)
    wpf = wp[...].reshape(512, D)

    def back_proj(b, carry):
        datt[at(b, TOK), :] = nt(dattn[at(b, TOK), :], wpf).astype(BF)
        return carry

    lax.fori_loop(0, 4, back_proj, 0)
    store_tiles(tn(att[...], dattn[...]), dwp, 0, 64, PAD)
    rp.hop1()

    def attend_back(p, carry):
        item = p // 4
        lanes = at(p % 4, 128)
        rows_all = at(item, 512)
        dk = jnp.zeros((512, 128), F32)
        dv = jnp.zeros((512, 128), F32)

        def head_back_store(d, raw_ref, row, t, rows, out_rows):
            cos, sina, sinb = tabs[0, rows, :], tabs[1, rows, :], tabs[2, rows, :]
            raw = raw_ref[p, rows, :]
            recip = lax.rsqrt(jnp.sum(raw * raw, -1, keepdims=True) * (1.0 / HEAD) + EPSILON)
            dn = turn_back(d, cos, sina, sinb)
            dgain[t : t + 1, :] += jnp.sum(dn * raw * recip, 0, keepdims=True)
            u = dn * gains[t : t + 1, :]
            mean = jnp.sum(u * raw, -1, keepdims=True) * (1.0 / HEAD)
            res = recip * u - raw * (recip * recip * recip * mean)
            de[out_rows, at(t * 4 + p % 4, 128)] = res.astype(BF)

        for half in range(2):
            rows = pl.ds(half * TOK, TOK)
            out_rows = pl.ds(pl.multiple_of(item * 512 + half * TOK, TOK), TOK)
            do = datt[out_rows, lanes]
            s = nt(qr[p, rows, :], kr[p]) * ROOT + maskb[item]
            e = jnp.exp(s - jnp.max(s, -1, keepdims=True))
            pf = e / jnp.sum(e, -1, keepdims=True)
            pr = pf.astype(BF)
            dp = nt(do, vv[p])
            delta = jnp.sum(pf * dp, -1, keepdims=True)
            ds = (pf * (dp - delta)).astype(BF)
            dq = nn(ds, kr[p]) * ROOT
            dk += tn(ds, qr[p, rows, :])
            dv += tn(pr, do)
            head_back_store(dq, rawq, None, 0, rows, out_rows)
        dk = dk * ROOT
        for half in range(2):
            rows = pl.ds(half * TOK, TOK)
            out_rows = pl.ds(pl.multiple_of(item * 512 + half * TOK, TOK), TOK)
            head_back_store(dk[half * TOK : half * TOK + TOK], rawk, None, 1, rows, out_rows)
        de[rows_all, at(8 + p % 4, 128)] = dv.astype(BF)
        return carry

    lax.fori_loop(0, 4, attend_back, 0)
    rg.hop2()
    rd.hop2()
    rp.hop2()
    lax.fori_loop(4, 8, attend_back, 0)
    rg.hop3()
    rd.hop3()
    rp.hop3()

    def squeeze(b, carry):
        v = de[at(b, TOK), :]
        dbq[0:1, :] += jnp.sum(v.astype(F32), 0, keepdims=True)
        dc[at(b, TOK), :] = nt(v, spread[...]).astype(BF)
        return carry

    lax.fori_loop(0, 4, squeeze, 0)
    wqf = wq[...].reshape(D, 864)
    ts = {}
    for r in (2, 3, 1):
        k, dev = here.mate(r)
        tsend[r - 1] = nt(dc[at(k, TOK), :], wqf).astype(BF)
        ts[r] = link.send(tsend.at[r - 1], trecv.at[r - 1], dev)
    town[...] = nt(dc[at(m, TOK), :], wqf)
    for i in range(3):
        store_tiles(tn(ha[:, i * 384 : i * 384 + 384], dc[...]), dwq, i * 384, 48, None)
    rq.hop1()
    for r in (1, 2, 3):
        ts[r].wait_recv()

    def first_back(i, carry):
        rows = at(i, 32)
        d = town[rows, :]
        for r in range(3):
            d += trecv[r, rows, :].astype(F32)
        n, recip = norm_rows(tokp[rows, :].astype(F32))
        small[0:1, :] += jnp.sum(d, 0, keepdims=True)
        small[1:2, :] += jnp.sum(d * n, 0, keepdims=True)
        g = dmid[rows, :] + norm_rows_back(d * (1.0 + modv[1:2, :]), n, recip)
        to[rows, :] = g.astype(BF)
        return carry

    lax.fori_loop(0, 8, first_back, 0)
    to[...] = nt(to[...], perm[...]).astype(BF)
    sent, got = link.scatter(
        lambda j: to.at[pl.ds(j * 64, 64)], dtok.at[here.z], here.item_source, here.z
    )
    rq.hop2()

    def hand_out(red, exp, out, cols):
        left, right = red.done()
        exp[:, :, 0 : red.split] = tn(pick[...], left).astype(BF).reshape(4, PAD, red.split)
        exp[:, :, red.split : cols] = tn(pick[...], right).astype(BF).reshape(4, PAD, cols - red.split)
        got_it = {}
        for r in (2, 3, 1):
            k, dev = here.mate(r)
            got_it[r] = link.send(exp.at[k], out.at[m], dev)
        out[m] = exp[m]
        return got_it

    def plain(red, out):
        left, right = red.done()
        out[...] = nt(left, perm[:, 0 : red.split]) + nt(right, perm[:, red.split : D])

    og_ = hand_out(rg, eg, fg, 1536)
    plain(rd, fd)
    plain(rp, fp)
    rq.hop3()
    oq_ = hand_out(rq, eq, fq, 864)
    for r in (1, 2, 3):
        og_[r].wait_recv()
        oq_[r].wait_recv()
    got(to.at[pl.ds(0, 64)], lambda j: dtok.at[j])
    link.finish()
    sent()


def call(kernel, ident, outs, scratch, args, hbm=(), sems=64):
    vm = pl.BlockSpec(memory_space=pltpu.VMEM)
    hb = pl.BlockSpec(memory_space=pltpu.HBM)
    return pl.pallas_call(
        kernel,
        out_shape=[jax.ShapeDtypeStruct(s, t) for s, t in outs],
        in_specs=[hb if i in hbm else vm for i in range(len(args))],
        out_specs=[vm] * len(outs),
        scratch_shapes=scratch + [pltpu.SemaphoreType.DMA((sems,)), pltpu.SemaphoreType.DMA((sems,))]
        + ([pltpu.SemaphoreType.DMA((2,))] if hbm else []),
        compiler_params=pltpu.CompilerParams(
            collective_id=ident, has_side_effects=True, vmem_limit_bytes=LIMIT
        ),
    )(*args)


def to_order(v):
    lead = v.shape[:-1]
    n = len(lead)
    v = v.reshape(lead + (2, 2, 2, 2, 2, UNIT))
    return v.transpose(tuple(range(n)) + tuple(n + i for i in (0, 2, 4, 3, 1, 5))).reshape(lead + (D,))


def from_order(v):
    lead = v.shape[:-1]
    n = len(lead)
    v = v.reshape(lead + (2, 2, 2, 2, 2, UNIT))
    return v.transpose(tuple(range(n)) + tuple(n + i for i in (0, 4, 1, 3, 2, 5))).reshape(lead + (D,))


def local(
    tokens, conditioning, heights, widths, cotangent, w_mod, b_mod, w_qkv, b_qkv, query_gain, key_gain,
    w_proj, b_proj, w_gu, b_gu, w_down, b_down,
):
    args = (
        tokens, conditioning, heights, widths, cotangent, w_mod, b_mod, w_qkv, b_qkv, query_gain, key_gain,
        w_proj, b_proj, w_gu, b_gu, w_down, b_down,
    )
    sizes = tuple(lax.axis_size(a) for a in ("dp", "row", "col"))
    if sizes != (4, 4, 2) or tokens.shape != (4, 4, 16, D):
        return general(*args)
    every = ("dp", "row", "col")
    perm, spread, pick, tabs, row_of, col_of = constants()
    dp, z, y = (lax.axis_index(a) for a in every)
    x, c, zh, zl = dp // 2, dp % 2, z // 2, z % 2
    pack = jnp.concatenate(
        [conditioning.reshape(-1), heights.astype(BF), widths.astype(BF)]
    )
    pack = lax.all_gather(pack, "dp", axis=0)
    cond = pack[:, : 4 * D].reshape(16, D).astype(F32)
    tall = pack[:, 4 * D : 4 * D + 4].reshape(16).astype(jnp.int32)
    wide = pack[:, 4 * D + 4 :].reshape(16).astype(jnp.int32)
    act = (cond * jax.nn.sigmoid(cond)).astype(BF)
    part = jnp.dot(act, w_mod, preferred_element_type=F32) + b_mod.astype(F32)
    pack = jnp.concatenate([part.reshape(-1)] + [b.astype(F32) for b in (b_qkv, b_proj, b_gu, b_down)])
    pack = lax.all_gather(pack, every, axis=0)
    item = (2 * x + y) * 4 + z
    modv = lax.dynamic_index_in_dim(pack[:, :3456].reshape(32, 16, 216), item, 1, False)
    modv = to_order(modv.reshape(6, D))
    modv = jnp.concatenate([modv, jnp.zeros((2, D), F32)])
    own = lambda v: lax.dynamic_index_in_dim(
        lax.dynamic_index_in_dim(v, c, 2, False), zl, 3, False
    )
    bq = own(pack[:, 3456:3564].reshape(3, 2, 2, 2, 2, 2, UNIT))
    bq = jnp.pad(bq, ((0, 0),) * 4 + ((0, 64 - UNIT),)).reshape(1, 1536)
    bp = to_order(pack[:, 3564:3600].reshape(1, D))
    bg = own(pack[:, 3600:3792].reshape(2, 2, 2, 2, 2, 2, 96)).reshape(1, 1536)
    bd = to_order(pack[:, 3792:3828].reshape(1, D))
    pair = (2 * x + y) * 4 + 2 * zh + jnp.arange(2)
    row_of, col_of = jnp.asarray(row_of), jnp.asarray(col_of)
    live = (row_of[None] < tall[pair][:, None]) & (col_of[None] < wide[pair][:, None])
    maskb = jnp.where(live, 0.0, MASKED).astype(F32).reshape(2, 1, 512)
    valid = lax.dynamic_slice(live[zl].astype(F32), (c * TOK,), (TOK,)).reshape(TOK, 1)
    gains = jnp.pad(
        jnp.stack([query_gain, key_gain]).reshape(2, 2, UNIT), ((0, 6), (0, 0), (0, 64 - UNIT))
    ).reshape(8, 128)
    wq = w_qkv.reshape(UNIT, 3, 2, 2, 2, 2, 72).transpose(5, 3, 0, 1, 2, 4, 6).reshape(4, UNIT, 864)
    wq = jnp.pad(wq, ((0, 0), (0, PAD - UNIT), (0, 0)))
    wg = w_gu.reshape(UNIT, 2, 2, 2, 2, 2, 192).transpose(5, 3, 0, 1, 2, 4, 6).reshape(4, UNIT, 1536)
    wg = jnp.pad(wg, ((0, 0), (0, PAD - UNIT), (0, 0)))
    wp = jnp.pad(w_proj, ((0, PAD - UNIT), (0, 0)))

    full = (GROUP, D)
    (
        wq_all, wp_all, wg_all, wd_all, ha, rawq, rawk, qr, kr, vv, att, hm, dmlp, tokp, og, attn_out,
    ) = call(
        kernel_a, 0,
        [
            ((2, 2, 2, 144, 864), BF), ((2, 2, 2, 64, D), BF), ((2, 2, 2, 144, 1536), BF), ((2, 2, 2, 96, D), BF),
            (full, BF), ((8, 512, 128), F32), ((8, 512, 128), F32), ((8, 512, 128), BF), ((8, 512, 128), BF),
            ((8, 512, 128), BF), ((GROUP, 512), BF), (full, BF), (full, BF),
            ((TOK, D), BF), ((TOK, D), BF), ((TOK, D), F32),
        ],
        [
            pltpu.VMEM((4, PAD, 864), BF), pltpu.VMEM((4, PAD, 1536), BF), pltpu.VMEM((TOK, D), BF),
            pltpu.VMEM((TOK, D), BF), pltpu.VMEM((D, 1536), BF), pltpu.VMEM((3, TOK, D), BF),
            pltpu.VMEM((3, TOK, D), BF), pltpu.VMEM((TOK, D), F32),
        ],
        (
            tokens.reshape(4, 64, D), cotangent.reshape(4, 64, D), wq, wg, wp, w_down, perm, spread, pick, tabs,
            gains, modv, bq, bp, maskb, valid,
        ),
        hbm=(0, 1, 2, 3),
    )
    dwg, dwd, dattn, dmid, bout, small_b, dbg = call(
        kernel_b, 1,
        [
            ((2, 2, 2, 144, 1536), BF), ((2, 2, 2, 96, D), BF), (full, BF), ((TOK, D), F32), ((4, 64, D), BF),
            ((8, D), F32), ((8, 1536), F32),
        ],
        [
            pltpu.VMEM((TOK, 1536), F32), pltpu.VMEM((GROUP, 1536), BF), pltpu.VMEM((GROUP, 768), BF),
            pltpu.VMEM((3, TOK, D), BF), pltpu.VMEM((3, TOK, D), BF), pltpu.VMEM((TOK, D), F32),
            pltpu.VMEM((3, TOK, D), BF), pltpu.VMEM((3, TOK, D), BF), pltpu.VMEM((TOK, D), F32),
            pltpu.VMEM((TOK, D), BF),
        ],
        (wg_all, wd_all, hm, dmlp, tokp, og, attn_out, modv, bg, bd, perm, valid),
    )
    dtok, fq, fg, fp, fd, small_c, dbq, dgain = call(
        kernel_c, 2,
        [
            ((4, 64, D), BF), ((4, PAD, 864), BF), ((4, PAD, 1536), BF), ((PAD, D), F32), ((96, D), F32),
            ((8, D), F32), ((8, 1536), F32), ((8, 128), F32),
        ],
        [
            pltpu.VMEM((2, 2, 2, 144, 864), BF), pltpu.VMEM((2, 2, 2, PAD, D), BF), pltpu.VMEM((GROUP, 512), BF),
            pltpu.VMEM((GROUP, 1536), BF), pltpu.VMEM((GROUP, 864), BF), pltpu.VMEM((3, TOK, D), BF),
            pltpu.VMEM((3, TOK, D), BF), pltpu.VMEM((TOK, D), F32), pltpu.VMEM((TOK, D), BF),
            pltpu.VMEM((4, PAD, 864), BF), pltpu.VMEM((4, PAD, 1536), BF),
        ]
        + Reduce.buffers(144, 1536, SPLIT_G) + Reduce.buffers(96, D, SPLIT_D)
        + Reduce.buffers(144, 864, SPLIT_Q) + Reduce.buffers(PAD, D, SPLIT_P),
        (
            dwg, dwd, dattn, att, wp_all, wq_all, ha, rawq, rawk, qr, kr, vv, maskb, dmid, tokp, modv, gains, tabs,
            perm, spread, pick,
        ),
    )

    g_w_qkv = fq[:, :UNIT].reshape(2, 2, UNIT, 3, 2, 2, 72).transpose(2, 3, 4, 1, 5, 0, 6)
    g_w_qkv = g_w_qkv.reshape(UNIT, 3456).astype(F32)
    g_w_gu = fg[:, :UNIT].reshape(2, 2, UNIT, 2, 2, 2, 192).transpose(2, 3, 4, 1, 5, 0, 6)
    g_w_gu = g_w_gu.reshape(UNIT, 6144).astype(F32)
    spread_own = lambda v: lax.dynamic_update_index_in_dim(
        jnp.zeros(v.shape[:2] + (2,) + v.shape[2:3] + (2,) + v.shape[3:], F32),
        lax.dynamic_update_index_in_dim(
            jnp.zeros(v.shape[:3] + (2,) + v.shape[3:], F32), v[:, :, :, None], zl, 3
        )[:, :, None],
        c,
        2,
    )
    db_qkv = spread_own(dbq[0].reshape(3, 2, 2, 2, 64)[..., :UNIT]).reshape(3456)
    db_gu = spread_own(dbg[0].reshape(2, 2, 2, 2, 96)).reshape(32, 192)
    vecs = from_order(jnp.stack([small_c[0], small_c[1], small_b[3], small_b[1], small_b[2], small_b[0],
                                 small_b[5], small_b[4]]))
    d_mod = vecs[:6].reshape(32, 1, 216)
    d_mod = lax.dynamic_update_slice(jnp.zeros((32, 16, 216), F32), d_mod, (0, item, 0)).reshape(32, 3456)
    dg = dgain[:2].reshape(2, 2, 64)[..., :UNIT].reshape(144)
    pack = jnp.concatenate(
        [
            d_mod,
            db_qkv[: 2 * D].reshape(32, 72),
            db_qkv[2 * D :].reshape(32, 36),
            db_gu,
            vecs[6].reshape(32, UNIT),
            vecs[7].reshape(32, UNIT),
            jnp.broadcast_to(dg, (32, 144)),
        ],
        1,
    )
    pack = lax.psum_scatter(pack, every, scatter_dimension=0, tiled=True)[0]
    d_mod = pack[:3456].reshape(16, 216)
    g_b_mod = jnp.sum(d_mod, 0)
    g_w_mod = jnp.einsum("id,ie->de", act.astype(F32), d_mod, precision=PRECISE)
    d_act = jnp.einsum("ie,de->id", d_mod, w_mod.astype(F32), precision=PRECISE)
    sig = jax.nn.sigmoid(cond)
    d_cond = d_act * sig * (1.0 + cond * (1.0 - sig))
    d_cond = d_cond.reshape(4, 4, 8, 144).transpose(0, 2, 1, 3).reshape(32, 4, 144)
    d_cond = lax.psum_scatter(d_cond, every, scatter_dimension=0, tiled=True)[0]
    return (
        bout.reshape(tokens.shape),
        dtok.reshape(tokens.shape).astype(F32),
        d_cond,
        g_w_mod,
        g_b_mod,
        g_w_qkv,
        pack[3456:3528],
        pack[3528:3564],
        pack[3828:3900],
        pack[3900:3972],
        fp[:UNIT],
        pack[3756:3792],
        g_w_gu,
        pack[3564:3756],
        fd,
        pack[3792:3828],
    )


def solution(mesh):
    in_specs = (
        P("dp", "row", "col", None),
        P("dp", None),
        P("dp"),
        P("dp"),
        P("dp", "row", "col", None),
        P(None, ("dp", "row", "col")),
        P(("dp", "row", "col")),
        P(("dp", "row", "col"), None),
        P(("dp", "row", "col")),
        P(),
        P(),
        P(("dp", "row", "col"), None),
        P(("dp", "row", "col")),
        P(("dp", "row", "col"), None),
        P(("dp", "row", "col")),
        P(("dp", "row", "col"), None),
        P(("dp", "row", "col")),
    )
    out_specs = (
        P("dp", "row", "col", None),
        P("dp", "row", "col", None),
        P("dp", ("row", "col")),
        P(None, ("dp", "row", "col")),
        P(("dp", "row", "col")),
        P(("dp", "row", "col"), None),
        P(("dp", "row", "col")),
        P(("dp", "row", "col")),
        P(),
        P(),
        P(("dp", "row", "col"), None),
        P(("dp", "row", "col")),
        P(("dp", "row", "col"), None),
        P(("dp", "row", "col")),
        P(("dp", "row", "col"), None),
        P(("dp", "row", "col")),
    )
    return jax.shard_map(local, mesh=mesh, in_specs=in_specs, out_specs=out_specs, check_vma=False)
```

```python
import math

import jax
import jax.numpy as jnp
import numpy as np
from jax import lax
from jax.experimental import pallas as pl
from jax.experimental.pallas import tpu as pltpu
from jax.sharding import PartitionSpec as P

HEADS = 16
HEAD = 72
FF = 3072


EPSILON = 1e-06
MASKED = -1000000000.0
PRECISE = lax.Precision.HIGHEST


def rope_tables(row_pos, col_pos, head_size):
    half_size = head_size // 2
    lane_index = jnp.arange(head_size)
    pair_index = (lane_index % half_size // 2).astype(jnp.float32)
    frequency = jnp.exp(-math.log(10000.0) * 2.0 * pair_index / half_size)
    places = jnp.where(lane_index[None, :] >= half_size, col_pos[:, None], row_pos[:, None]).astype(
        jnp.float32
    )
    angles = places * frequency[None, :]
    return (jnp.cos(angles), jnp.sin(angles))


def rotate(values):
    pair_view = values.reshape(values.shape[:-1] + (values.shape[-1] // 2, 2))
    turned = jnp.stack((-pair_view[..., 1], pair_view[..., 0]), axis=-1)
    return turned.reshape(values.shape)


def norm_parts(values):
    centered = values - jnp.mean(values, -1, keepdims=True)
    recip = lax.rsqrt(jnp.mean(centered * centered, -1, keepdims=True) + EPSILON)
    return (centered * recip, recip)


def norm_back(gradient, normed, recip):
    return recip * (
        gradient
        - jnp.mean(gradient, -1, keepdims=True)
        - normed * jnp.mean(gradient * normed, -1, keepdims=True)
    )


def head_back(gradient, raw_value, recip, gain_vec):
    scaled = gradient * gain_vec
    gain_grad = jnp.sum(gradient * raw_value * recip, axis=(0, 1, 2))
    raw_grad = recip * scaled - raw_value * (recip * recip * recip) * jnp.mean(
        scaled * raw_value, -1, keepdims=True
    )
    return (raw_grad, gain_grad)


def general(
    tokens,
    conditioning,
    heights,
    widths,
    cotangent,
    w_mod,
    b_mod,
    w_qkv,
    b_qkv,
    query_gain,
    key_gain,
    w_proj,
    b_proj,
    w_gu,
    b_gu,
    w_down,
    b_down,
):
    item_count, tile_rows, tile_cols, model_width = tokens.shape
    tile_span = tile_rows * tile_cols
    n_row = lax.axis_size("row")
    n_col = lax.axis_size("col")
    groups = n_row * n_col
    key_count = tile_span * groups
    inv_root = 1.0 / math.sqrt(HEAD)
    row_at = lax.axis_index("row")
    col_at = lax.axis_index("col")
    local_index = jnp.arange(tile_span)
    query_rows = row_at * tile_rows + local_index // tile_cols
    query_cols = col_at * tile_cols + local_index % tile_cols
    valid_query = (query_rows[None, :] < heights[:, None]) & (query_cols[None, :] < widths[:, None])
    key_index = jnp.arange(key_count)
    key_owner = key_index // tile_span
    key_spot = key_index % tile_span
    key_rows = key_owner // n_col * tile_rows + key_spot // tile_cols
    key_cols = key_owner % n_col * tile_cols + key_spot % tile_cols
    valid_key = (key_rows[None, :] < heights[:, None]) & (key_cols[None, :] < widths[:, None])
    cos_tab, sin_tab = rope_tables(query_rows, query_cols, HEAD)
    cos_four = cos_tab[None, :, None, :]
    sin_four = sin_tab[None, :, None, :]
    cond_f = conditioning.astype(jnp.float32)
    cond_sig = jax.nn.sigmoid(cond_f)
    act_low = (cond_f * cond_sig).astype(jnp.bfloat16)
    gathered = (
        lax.all_gather(w_mod, ("dp", "row", "col"), axis=1, tiled=True),
        lax.all_gather(b_mod, ("dp", "row", "col"), axis=0, tiled=True),
        lax.all_gather(w_qkv, ("dp", "row", "col"), axis=0, tiled=True),
        lax.all_gather(b_qkv, ("dp", "row", "col"), axis=0, tiled=True),
        lax.all_gather(w_proj, ("dp", "row", "col"), axis=0, tiled=True),
        lax.all_gather(b_proj, ("dp", "row", "col"), axis=0, tiled=True),
        lax.all_gather(w_gu, ("dp", "row", "col"), axis=0, tiled=True),
        lax.all_gather(b_gu, ("dp", "row", "col"), axis=0, tiled=True),
        lax.all_gather(w_down, ("dp", "row", "col"), axis=0, tiled=True),
        lax.all_gather(b_down, ("dp", "row", "col"), axis=0, tiled=True),
    )
    (
        w_mod_all,
        b_mod_all,
        w_qkv_all,
        b_qkv_all,
        w_proj_all,
        b_proj_all,
        w_gu_all,
        b_gu_all,
        w_down_all,
        b_down_all,
    ) = gathered
    modul = jnp.dot(act_low, w_mod_all, preferred_element_type=jnp.float32) + b_mod_all.astype(
        jnp.float32
    )
    shift_a, scale_a, gate_a, shift_m, scale_m, gate_m = [
        modul[:, piece * model_width : (piece + 1) * model_width][:, None, :] for piece in range(6)
    ]
    resid_in = tokens.reshape(item_count, tile_span, model_width).astype(jnp.float32)
    normed_a, recip_a = norm_parts(resid_in)
    h_attn = (normed_a * (1.0 + scale_a) + shift_a).astype(jnp.bfloat16)
    qkv_all = jnp.dot(h_attn, w_qkv_all, preferred_element_type=jnp.float32) + b_qkv_all.astype(
        jnp.float32
    )
    query_raw = qkv_all[..., :model_width].reshape(item_count, tile_span, HEADS, HEAD)
    key_raw = qkv_all[..., model_width : 2 * model_width].reshape(
        item_count, tile_span, HEADS, HEAD
    )
    value_raw = qkv_all[..., 2 * model_width :]
    query_recip = lax.rsqrt(jnp.mean(query_raw * query_raw, -1, keepdims=True) + EPSILON)
    key_recip = lax.rsqrt(jnp.mean(key_raw * key_raw, -1, keepdims=True) + EPSILON)
    query_normed = query_raw * query_recip * query_gain
    key_normed = key_raw * key_recip * key_gain
    query_rot = (query_normed * cos_four + rotate(query_normed) * sin_four).astype(jnp.bfloat16)
    key_rot = (key_normed * cos_four + rotate(key_normed) * sin_four).astype(jnp.bfloat16)
    value_low = value_raw.astype(jnp.bfloat16)
    kv_local = jnp.concatenate([key_rot.reshape(item_count, tile_span, model_width), value_low], -1)
    kv_every = lax.all_gather(kv_local, ("row", "col"), axis=1, tiled=True)
    query_heads = query_rot.transpose(2, 0, 1, 3)
    key_part = (
        kv_every[..., :model_width]
        .reshape(item_count, key_count, HEADS, HEAD)
        .transpose(2, 0, 1, 3)
    )
    value_part = (
        kv_every[..., model_width:]
        .reshape(item_count, key_count, HEADS, HEAD)
        .transpose(2, 0, 1, 3)
    )
    key_mask = valid_key[:, None, :]

    def attend(head_block):
        query_h, key_h, value_h = head_block
        scores = (
            jnp.einsum("itd,ikd->itk", query_h, key_h, preferred_element_type=jnp.float32)
            * inv_root
        )
        scores = jnp.where(key_mask, scores, MASKED)
        row_max = jnp.max(scores, -1, keepdims=True)
        exponent = jnp.exp(scores - row_max)
        row_sum = jnp.sum(exponent, -1, keepdims=True)
        probs = (exponent / row_sum).astype(jnp.bfloat16)
        result = jnp.einsum("itk,ikd->itd", probs, value_h, preferred_element_type=jnp.float32)
        return (result, row_max, row_sum)

    attended_heads, max_kept, sum_kept = lax.map(attend, (query_heads, key_part, value_part))
    attended = (
        attended_heads.transpose(1, 2, 0, 3)
        .reshape(item_count, tile_span, model_width)
        .astype(jnp.bfloat16)
    )
    attn_out = jnp.dot(
        attended, w_proj_all, preferred_element_type=jnp.float32
    ) + b_proj_all.astype(jnp.float32)
    resid_mid = resid_in + gate_a * attn_out
    normed_m, recip_m = norm_parts(resid_mid)
    h_mlp = (normed_m * (1.0 + scale_m) + shift_m).astype(jnp.bfloat16)
    gate_up = jnp.dot(h_mlp, w_gu_all, preferred_element_type=jnp.float32) + b_gu_all.astype(
        jnp.float32
    )
    gate_part = gate_up[..., :FF]
    up_part = gate_up[..., FF:]
    gate_sig = jax.nn.sigmoid(gate_part)
    gate_act = gate_part * gate_sig
    hidden = (gate_act * up_part).astype(jnp.bfloat16)
    mlp_out = jnp.dot(hidden, w_down_all, preferred_element_type=jnp.float32) + b_down_all.astype(
        jnp.float32
    )
    mask_f = valid_query[..., None].astype(jnp.float32)
    block_out = ((resid_mid + gate_m * mlp_out) * mask_f).astype(jnp.bfloat16)
    out_grad = cotangent.reshape(item_count, tile_span, model_width).astype(jnp.float32) * mask_f
    d_mlp = (gate_m * out_grad).astype(jnp.bfloat16)
    d_gate_m = jnp.sum(out_grad * mlp_out, 1)
    dw_down = jnp.einsum("itf,itd->fd", hidden, d_mlp, preferred_element_type=jnp.float32)
    db_down = jnp.sum(d_mlp.astype(jnp.float32), (0, 1))
    d_hidden = jnp.einsum("itd,fd->itf", d_mlp, w_down_all, preferred_element_type=jnp.float32)
    d_gate = d_hidden * up_part * gate_sig * (1.0 + gate_part * (1.0 - gate_sig))
    d_up = d_hidden * gate_act
    d_gate_up = jnp.concatenate([d_gate, d_up], -1).astype(jnp.bfloat16)
    dw_gu = jnp.einsum("itd,ite->de", h_mlp, d_gate_up, preferred_element_type=jnp.float32)
    db_gu = jnp.sum(d_gate_up.astype(jnp.float32), (0, 1))
    d_hmlp = jnp.einsum("ite,de->itd", d_gate_up, w_gu_all, preferred_element_type=jnp.float32)
    d_shift_m = jnp.sum(d_hmlp, 1)
    d_scale_m = jnp.sum(d_hmlp * normed_m, 1)
    d_mid = out_grad + norm_back(d_hmlp * (1.0 + scale_m), normed_m, recip_m)
    d_attn = (gate_a * d_mid).astype(jnp.bfloat16)
    d_gate_a = jnp.sum(d_mid * attn_out, 1)
    dw_proj = jnp.einsum("itd,ite->de", attended, d_attn, preferred_element_type=jnp.float32)
    db_proj = jnp.sum(d_attn.astype(jnp.float32), (0, 1))
    d_attended = jnp.einsum(
        "ite,de->itd", d_attn, w_proj_all, preferred_element_type=jnp.float32
    ).astype(jnp.bfloat16)
    d_att_heads = d_attended.reshape(item_count, tile_span, HEADS, HEAD).transpose(2, 0, 1, 3)
    key_back, value_back = (key_part, value_part)

    def attend_back(head_block):
        query_h, key_h, value_h, grad_h, max_h, sum_h = head_block
        scores = (
            jnp.einsum("itd,ikd->itk", query_h, key_h, preferred_element_type=jnp.float32)
            * inv_root
        )
        scores = jnp.where(key_mask, scores, MASKED)
        probs = jnp.exp(scores - max_h) / sum_h
        d_probs = jnp.einsum("itd,ikd->itk", grad_h, value_h, preferred_element_type=jnp.float32)
        delta = jnp.sum(probs * d_probs, -1, keepdims=True)
        d_scores = (probs * (d_probs - delta)).astype(jnp.bfloat16)
        d_query = (
            jnp.einsum("itk,ikd->itd", d_scores, key_h, preferred_element_type=jnp.float32)
            * inv_root
        )
        d_key = (
            jnp.einsum("itk,itd->ikd", d_scores, query_h, preferred_element_type=jnp.float32)
            * inv_root
        )
        d_value = jnp.einsum(
            "itk,itd->ikd", probs.astype(jnp.bfloat16), grad_h, preferred_element_type=jnp.float32
        )
        return (d_query, d_key, d_value)

    dq_heads, dk_heads, dv_heads = lax.map(
        attend_back, (query_heads, key_back, value_back, d_att_heads, max_kept, sum_kept)
    )
    dkv_term = jnp.concatenate(
        [
            dk_heads.transpose(1, 2, 0, 3).reshape(item_count, key_count, model_width),
            dv_heads.transpose(1, 2, 0, 3).reshape(item_count, key_count, model_width),
        ],
        -1,
    )
    dkv_own = lax.psum_scatter(dkv_term, ("row", "col"), scatter_dimension=1, tiled=True)
    d_key_rot = dkv_own[..., :model_width].reshape(item_count, tile_span, HEADS, HEAD)
    d_value = dkv_own[..., model_width:]
    d_query_rot = dq_heads.transpose(1, 2, 0, 3)
    d_query_n = d_query_rot * cos_four - rotate(d_query_rot * sin_four)
    d_key_n = d_key_rot * cos_four - rotate(d_key_rot * sin_four)
    d_query_raw, dq_gain = head_back(d_query_n, query_raw, query_recip, query_gain)
    d_key_raw, dk_gain = head_back(d_key_n, key_raw, key_recip, key_gain)
    gain_total = lax.psum((dq_gain, dk_gain), ("dp", "row", "col"))
    d_qkv = jnp.concatenate(
        [
            d_query_raw.reshape(item_count, tile_span, model_width),
            d_key_raw.reshape(item_count, tile_span, model_width),
            d_value,
        ],
        -1,
    ).astype(jnp.bfloat16)
    dw_qkv = jnp.einsum("itd,ite->de", h_attn, d_qkv, preferred_element_type=jnp.float32)
    db_qkv = jnp.sum(d_qkv.astype(jnp.float32), (0, 1))
    db_query_key = db_qkv[: 2 * model_width]
    db_value = db_qkv[2 * model_width :]
    d_hattn = jnp.einsum("ite,de->itd", d_qkv, w_qkv_all, preferred_element_type=jnp.float32)
    d_shift_a = jnp.sum(d_hattn, 1)
    d_scale_a = jnp.sum(d_hattn * normed_a, 1)
    d_tokens = d_mid + norm_back(d_hattn * (1.0 + scale_a), normed_a, recip_a)
    d_modul = jnp.concatenate([d_shift_a, d_scale_a, d_gate_a, d_shift_m, d_scale_m, d_gate_m], -1)
    act_f = act_low.astype(jnp.float32)
    dw_mod = jnp.einsum("id,ie->de", act_f, d_modul, precision=PRECISE)
    db_mod = jnp.sum(d_modul, 0)
    d_act = jnp.einsum("ie,de->id", d_modul, w_mod_all.astype(jnp.float32), precision=PRECISE)
    d_cond_part = d_act * cond_sig * (1.0 + cond_f * (1.0 - cond_sig))
    d_cond = lax.psum_scatter(d_cond_part, ("row", "col"), scatter_dimension=1, tiled=True)
    summed = (
        lax.psum_scatter(dw_mod, ("dp", "row", "col"), scatter_dimension=1, tiled=True),
        lax.psum_scatter(db_mod, ("dp", "row", "col"), scatter_dimension=0, tiled=True),
        lax.psum_scatter(dw_qkv, ("dp", "row", "col"), scatter_dimension=0, tiled=True),
        lax.psum_scatter(db_query_key, ("dp", "row", "col"), scatter_dimension=0, tiled=True),
        lax.psum_scatter(db_value, ("dp", "row", "col"), scatter_dimension=0, tiled=True),
        lax.psum_scatter(dw_proj, ("dp", "row", "col"), scatter_dimension=0, tiled=True),
        lax.psum_scatter(db_proj, ("dp", "row", "col"), scatter_dimension=0, tiled=True),
        lax.psum_scatter(dw_gu, ("dp", "row", "col"), scatter_dimension=0, tiled=True),
        lax.psum_scatter(db_gu, ("dp", "row", "col"), scatter_dimension=0, tiled=True),
        lax.psum_scatter(dw_down, ("dp", "row", "col"), scatter_dimension=0, tiled=True),
        lax.psum_scatter(db_down, ("dp", "row", "col"), scatter_dimension=0, tiled=True),
    )
    (
        g_w_mod,
        g_b_mod,
        g_w_qkv,
        g_b_query_key,
        g_b_value,
        g_w_proj,
        g_b_proj,
        g_w_gu,
        g_b_gu,
        g_w_down,
        g_b_down,
    ) = summed
    return (
        block_out.reshape(item_count, tile_rows, tile_cols, model_width),
        d_tokens.reshape(item_count, tile_rows, tile_cols, model_width),
        d_cond,
        g_w_mod,
        g_b_mod,
        g_w_qkv,
        g_b_query_key,
        g_b_value,
        gain_total[0],
        gain_total[1],
        g_w_proj,
        g_b_proj,
        g_w_gu,
        g_b_gu,
        g_w_down,
        g_b_down,
    )


MESH = pl.DeviceIdType.MESH
BF = jnp.bfloat16
F32 = jnp.float32
LIMIT = 60 * 1024 * 1024
D = 1152
UNIT = 36
PAD = 48
TOK = 256
GROUP = 1024
SPLIT_Q, SPLIT_P, SPLIT_G, SPLIT_D = 384, 640, 768, 640
ROOT = 1.0 / math.sqrt(HEAD)


def nn(a, b):
    return lax.dot_general(a, b, (((1,), (0,)), ((), ())), preferred_element_type=F32)


def nt(a, b):
    return lax.dot_general(a, b, (((1,), (1,)), ((), ())), preferred_element_type=F32)


def tn(a, b):
    return lax.dot_general(a, b, (((0,), (0,)), ((), ())), preferred_element_type=F32)


def width_order():
    xx, zh, yy, zl, cc, jj = np.indices((2, 2, 2, 2, 2, UNIT)).reshape(6, -1)
    return ((((xx * 2 + cc) * 2 + zh) * 2 + zl) * 2 + yy) * UNIT + jj


def constants():
    perm = np.zeros((D, D), np.float32)
    perm[width_order(), np.arange(D)] = 1.0
    spread = np.zeros((864, 1536), np.float32)
    tt, hh, yy, jj = np.indices((3, 4, 2, UNIT)).reshape(4, -1)
    spread[tt * 288 + hh * 72 + yy * 36 + jj, tt * 512 + hh * 128 + yy * 64 + jj] = 1.0
    pick = np.zeros((144, 192), np.float32)
    kk, jj = np.indices((4, UNIT)).reshape(2, -1)
    pick[kk * 36 + jj, kk * 48 + jj] = 1.0
    spot = np.arange(512)
    row = spot // 128 * 4 + spot // 16 % 4
    col = spot // 64 % 2 * 16 + spot % 16
    lane = np.arange(128)
    part = lane % 64
    freq = np.exp(-math.log(10000.0) * 2.0 * (part // 2) / 36.0)
    place = np.where(lane[None, :] >= 64, col[:, None], row[:, None]).astype(np.float64)
    angle = place * freq[None, :]
    live = part < UNIT
    cos = np.where(live, np.cos(angle), 0.0)
    sin = np.where(live, np.sin(angle), 0.0)
    even = lane % 2 == 0
    tabs = np.stack([cos, np.where(even, -sin, 0.0), np.where(even, 0.0, sin)]).astype(np.float32)
    return (
        jnp.asarray(perm, BF),
        jnp.asarray(spread, BF),
        jnp.asarray(pick, BF),
        jnp.asarray(tabs, F32),
        row,
        col,
    )


class Place:
    def __init__(self):
        dp = lax.axis_index("dp")
        self.z = lax.axis_index("row")
        self.y = lax.axis_index("col")
        self.x = dp // 2
        self.c = dp % 2
        self.zh = self.z // 2
        self.zl = self.z % 2
        self.m = self.zl * 2 + self.c
        self.dp = dp

    def mate(self, r):
        c = 1 - self.c if r % 2 else self.c
        zl = 1 - self.zl if r // 2 else self.zl
        return zl * 2 + c, (self.x * 2 + c, self.zh * 2 + zl, self.y)

    def xpeer(self):
        return ((1 - self.x) * 2 + self.c, self.z, self.y)

    def ypeer(self):
        return (self.dp, self.z, 1 - self.y)

    def zpeer(self):
        return (self.dp, (1 - self.zh) * 2 + self.zl, self.y)

    def item_home(self, j):
        return (self.x * 2 + self.zh, j, self.c)

    def item_source(self, blk):
        return (self.x * 2 + self.y, self.c * 2 + blk // 2, blk % 2)

    def is_me(self, dev):
        return (dev[0] == self.dp) & (dev[1] == self.z) & (dev[2] == self.y)


class Link:
    def __init__(self, here, ssem, rsem):
        self.here, self.ssem, self.rsem, self.n, self.open = here, ssem, rsem, 0, []

    def greet(self, items):
        here = self.here
        bar = pltpu.get_barrier_semaphore()
        devs = [here.mate(r)[1] for r in (1, 2, 3)]
        devs += [here.xpeer(), here.ypeer(), here.zpeer()]
        for d in devs:
            pl.semaphore_signal(bar, inc=1, device_id=d, device_id_type=MESH)
        total = len(devs)
        if items:
            for d in [here.item_home(j) for j in range(4)] + [here.item_source(j) for j in range(4)]:


                @pl.when(jnp.logical_not(here.is_me(d)))
                def _():
                    pl.semaphore_signal(bar, inc=1, device_id=d, device_id_type=MESH)

            far = (here.zh - here.c) * (here.zh - here.c)
            off = (here.y - here.c) * (here.y - here.c)
            total += 8 - 2 * (1 - far) * (1 - off)
        pl.semaphore_wait(bar, total)

    def send(self, src, dst, dev):
        k = self.n
        self.n += 1
        copy = pltpu.make_async_remote_copy(
            src_ref=src,
            dst_ref=dst,
            send_sem=self.ssem.at[k],
            recv_sem=self.rsem.at[k],
            device_id=dev,
            device_id_type=MESH,
        )
        copy.start()
        self.open.append(copy)
        return copy

    def scatter(self, src_of, dst, dev_of, slot):
        base = self.n
        self.n += 4
        here = self.here
        copies = []
        for j in range(4):
            dev = dev_of(j)
            mine = here.is_me(dev)
            remote = pltpu.make_async_remote_copy(
                src_ref=src_of(j),
                dst_ref=dst,
                send_sem=self.ssem.at[base + j],
                recv_sem=self.rsem.at[base + slot],
                device_id=dev,
                device_id_type=MESH,
            )
            local_copy = pltpu.make_async_copy(src_of(j), dst, self.rsem.at[base + slot])

            @pl.when(mine)
            def _():
                local_copy.start()

            @pl.when(jnp.logical_not(mine))
            def _():
                remote.start()

            copies.append((mine, remote))

        def wait_send():
            for mine, remote in copies:

                @pl.when(jnp.logical_not(mine))
                def _():
                    remote.wait_send()

        def wait_recv(src, dst_of):
            for j in range(4):
                pltpu.make_async_copy(src, dst_of(j), self.rsem.at[base + j]).wait()

        return wait_send, wait_recv

    def finish(self):
        for copy in self.open:
            copy.wait_send()
        self.open = []


def norm_rows(x):
    mean = jnp.sum(x, -1, keepdims=True) * (1.0 / D)
    cent = x - mean
    var = jnp.sum(cent * cent, -1, keepdims=True) * (1.0 / D)
    recip = lax.rsqrt(var + EPSILON)
    return cent * recip, recip


def norm_rows_back(g, y, recip):
    mg = jnp.sum(g, -1, keepdims=True) * (1.0 / D)
    mgy = jnp.sum(g * y, -1, keepdims=True) * (1.0 / D)
    return recip * (g - mg - y * mgy)


def at(i, n):
    return pl.ds(pl.multiple_of(i * n, n), n)


class Gather:
    def __init__(self, link, ref, rows, split):
        self.link, self.ref, self.rows, self.split = link, ref, rows, split

    def cut(self, i, j, k, cols):
        return self.ref.at[i, j, k, pl.ds(0, self.rows), cols]

    def hop1(self):
        h = self.link.here
        part = self.cut(h.x, h.zh, h.y, slice(None))
        self.a = self.link.send(part, part, h.zpeer())

    def hop2(self):
        h = self.link.here
        self.a.wait_recv()
        pa = self.cut(h.x, slice(None), h.y, pl.ds(0, self.split))
        pb = self.cut(h.x, slice(None), h.y, pl.ds(self.split, self.ref.shape[-1] - self.split))
        self.a = self.link.send(pa, pa, h.xpeer())
        self.b = self.link.send(pb, pb, h.ypeer())

    def hop3(self):
        h = self.link.here
        self.a.wait_recv()
        self.b.wait_recv()
        pa = self.cut(slice(None), slice(None), h.y, pl.ds(0, self.split))
        pb = self.cut(
            h.x, slice(None), slice(None), pl.ds(self.split, self.ref.shape[-1] - self.split)
        )
        self.a = self.link.send(pa, pa, h.ypeer())
        self.b = self.link.send(pb, pb, h.xpeer())

    def done(self):
        self.a.wait_recv()
        self.b.wait_recv()


class Reduce:
    def __init__(self, link, ref, bufs, split):
        self.link, self.ref, self.split = link, ref, split
        self.cols = ref.shape[-1]
        self.r1a, self.r1b, self.r2a, self.r2b, self.r3a, self.r3b = bufs

    @staticmethod
    def buffers(rows, cols, split):
        rest = cols - split
        return [
            pltpu.VMEM((2, 2, rows, split), BF),
            pltpu.VMEM((2, 2, rows, rest), BF),
            pltpu.VMEM((2, rows, split), BF),
            pltpu.VMEM((2, rows, rest), BF),
            pltpu.VMEM((rows, split), BF),
            pltpu.VMEM((rows, rest), BF),
        ]

    def hop1(self):
        h = self.link.here
        ca, cb = pl.ds(0, self.split), pl.ds(self.split, self.cols - self.split)
        self.a = self.link.send(self.ref.at[1 - h.x, :, :, :, ca], self.r1a, h.xpeer())
        self.b = self.link.send(self.ref.at[:, :, 1 - h.y, :, cb], self.r1b, h.ypeer())

    def hop2(self):
        h = self.link.here
        ca, cb = pl.ds(0, self.split), pl.ds(self.split, self.cols - self.split)
        self.a.wait_recv()
        self.b.wait_recv()

        def add(i, carry):
            u, v = i // 2, i % 2
            own = self.ref[h.x, u, v, :, ca].astype(F32)
            self.r1a[u, v] = (self.r1a[u, v].astype(F32) + own).astype(BF)
            own = self.ref[u, v, h.y, :, cb].astype(F32)
            self.r1b[u, v] = (self.r1b[u, v].astype(F32) + own).astype(BF)
            return carry

        lax.fori_loop(0, 4, add, 0)
        self.a = self.link.send(self.r1a.at[:, 1 - h.y], self.r2a, h.ypeer())
        self.b = self.link.send(self.r1b.at[1 - h.x], self.r2b, h.xpeer())

    def hop3(self):
        h = self.link.here
        self.a.wait_recv()
        self.b.wait_recv()

        def add(u, carry):
            own = self.r1a[u, h.y].astype(F32)
            self.r2a[u] = (self.r2a[u].astype(F32) + own).astype(BF)
            own = self.r1b[h.x, u].astype(F32)
            self.r2b[u] = (self.r2b[u].astype(F32) + own).astype(BF)
            return carry

        lax.fori_loop(0, 2, add, 0)
        self.a = self.link.send(self.r2a.at[1 - h.zh], self.r3a, h.zpeer())
        self.b = self.link.send(self.r2b.at[1 - h.zh], self.r3b, h.zpeer())

    def done(self):
        h = self.link.here
        self.a.wait_recv()
        self.b.wait_recv()
        left = self.r2a[h.zh].astype(F32) + self.r3a[...].astype(F32)
        right = self.r2b[h.zh].astype(F32) + self.r3b[...].astype(F32)
        return left.astype(BF), right.astype(BF)


def all_rows(link, ref):
    here = link.here
    own = ref.at[at(here.m, TOK)]
    return {r: link.send(own, own, here.mate(r)[1]) for r in (2, 3, 1)}


def turn(v, cos, sina, sinb):
    return v * cos + pltpu.roll(v, 127, 1) * sina + pltpu.roll(v, 1, 1) * sinb


def turn_back(d, cos, sina, sinb):
    return d * cos - pltpu.roll(d, 127, 1) * sina - pltpu.roll(d, 1, 1) * sinb


def kernel_a(
    tok_in, cot_in, wq_in, wg_in, wp_in, wd_in, perm, spread, pick, tabs, gains, modv, bq, bp, maskb, valid,
    wq, wp, wg, wd, ha, rawq, rawk, qr, kr, vv, att, hm, dmlp, tokp, og, attn_out,
    s0q, s0g, tokr, cotr, wqe, psend, precv, pown, ssem, rsem, lsem,
):
    here = Place()
    link = Link(here, ssem, rsem)
    link.greet(True)
    m = here.m
    slot = here.zl * 2 + here.y
    rows_in = at(slot, 64)
    tok_sent, tok_got = link.scatter(lambda j: tok_in.at[j], tokr.at[rows_in], here.item_home, slot)
    sq, sg = {}, {}
    for r in (2, 3, 1):
        k, dev = here.mate(r)
        sq[r] = link.send(wq_in.at[k], s0q.at[m], dev)
    own_q = pltpu.make_async_copy(wq_in.at[m], s0q.at[m], lsem.at[0])
    own_q.start()
    for r in (2, 3, 1):
        k, dev = here.mate(r)
        sg[r] = link.send(wg_in.at[k], s0g.at[m], dev)
    own_g = pltpu.make_async_copy(wg_in.at[m], s0g.at[m], lsem.at[1])
    own_g.start()

    gq = Gather(link, wq, 144, SPLIT_Q)
    gp = Gather(link, wp, PAD, SPLIT_P)
    gg = Gather(link, wg, 144, SPLIT_G)
    gd = Gather(link, wd, 96, SPLIT_D)

    own_q.wait()
    for r in (1, 2, 3):
        sq[r].wait_recv()
    wq[here.x, here.zh, here.y] = nn(pick[...], s0q[...].reshape(192, 864)).astype(BF)
    gq.hop1()
    wp[:, :, :, PAD:64, :] = jnp.zeros((2, 2, 2, 64 - PAD, D), BF)
    wp[here.x, here.zh, here.y, 0:PAD, :] = nn(wp_in[...], perm[...]).astype(BF)
    gp.hop1()
    own_g.wait()
    for r in (1, 2, 3):
        sg[r].wait_recv()
    wg[here.x, here.zh, here.y] = nn(pick[...], s0g[...].reshape(192, 1536)).astype(BF)
    tok_got(tok_in.at[0], lambda j: tokr.at[pl.ds(j * 64, 64)])
    gg.hop1()
    wd[here.x, here.zh, here.y] = nn(wd_in[...], perm[...]).astype(BF)
    gd.hop1()

    tokp[...] = nn(tokr[...], perm[...]).astype(BF)

    def first_norm(i, carry):
        n, _ = norm_rows(tokp[at(i, 32), :].astype(F32))
        h = n * (1.0 + modv[1:2, :]) + modv[0:1, :]
        ha[pl.ds(pl.multiple_of(m * TOK + i * 32, 32), 32), :] = h.astype(BF)
        return carry

    lax.fori_loop(0, 8, first_norm, 0)
    ha_sent = all_rows(link, ha)
    cot_sent, cot_got = link.scatter(lambda j: cot_in.at[j], cotr.at[rows_in], here.item_home, slot)
    gq.hop2()
    gp.hop2()
    gq.hop3()
    gp.hop3()
    for r in (1, 2, 3):
        ha_sent[r].wait_recv()
    gq.done()

    def widen(i, carry):
        part = wq[i // 2, i % 2].reshape(288, 864)
        wqe[at(i, 288), :] = nn(part, spread[...]).astype(BF)
        return carry

    lax.fori_loop(0, 4, widen, 0)

    def project(b, carry):
        acc = nn(ha[at(b, TOK), :], wqe[...]) + bq[...]
        item, half = b // 2, at(b % 2, TOK)
        cos, sina, sinb = tabs[0, half, :], tabs[1, half, :], tabs[2, half, :]
        for h in range(4):
            p = item * 4 + h
            for t, raw, rot in ((0, rawq, qr), (1, rawk, kr)):
                v = acc[:, t * 512 + h * 128 : t * 512 + h * 128 + 128]
                recip = lax.rsqrt(jnp.sum(v * v, -1, keepdims=True) * (1.0 / HEAD) + EPSILON)
                raw[p, half, :] = v
                n = v * recip * gains[t : t + 1, :]
                rot[p, half, :] = turn(n, cos, sina, sinb).astype(BF)
            vv[p, half, :] = acc[:, 1024 + h * 128 : 1152 + h * 128].astype(BF)
        return carry

    lax.fori_loop(0, 4, project, 0)
    gg.hop2()
    gd.hop2()

    def attend(p, carry):
        item = p // 4
        lanes = at(p % 4, 128)
        for half in range(2):
            rows = pl.ds(half * TOK, TOK)
            s = nt(qr[p, rows, :], kr[p]) * ROOT + maskb[item]
            top = jnp.max(s, -1, keepdims=True)
            e = jnp.exp(s - top)
            pr = (e / jnp.sum(e, -1, keepdims=True)).astype(BF)
            out_rows = pl.ds(pl.multiple_of(item * 512 + half * TOK, TOK), TOK)
            att[out_rows, lanes] = nn(pr, vv[p]).astype(BF)
        return carry

    lax.fori_loop(0, 4, attend, 0)
    gg.hop3()
    gd.hop3()
    lax.fori_loop(4, 8, attend, 0)
    gp.done()
    wpf = wp[...].reshape(512, D)
    sent = {}
    for r in (2, 3, 1):
        k, dev = here.mate(r)
        psend[r - 1] = nn(att[at(k, TOK), :], wpf).astype(BF)
        sent[r] = link.send(psend.at[r - 1], precv.at[r - 1], dev)
    pown[...] = nn(att[at(m, TOK), :], wpf)
    cot_got(cot_in.at[0], lambda j: cotr.at[pl.ds(j * 64, 64)])
    og[...] = (nn(cotr[...], perm[...]) * valid[...]).astype(BF)

    def scale_grad(i, carry):
        g = og[at(i, 32), :].astype(F32) * modv[5:6, :]
        dmlp[pl.ds(pl.multiple_of(m * TOK + i * 32, 32), 32), :] = g.astype(BF)
        return carry

    lax.fori_loop(0, 8, scale_grad, 0)
    for r in (1, 2, 3):
        sent[r].wait_recv()

    def second_norm(i, carry):
        rows = at(i, 32)
        a = pown[rows, :] + bp[...]
        for r in range(3):
            a += precv[r, rows, :].astype(F32)
        attn_out[rows, :] = a
        n, _ = norm_rows(tokp[rows, :].astype(F32) + modv[2:3, :] * a)
        h = n * (1.0 + modv[4:5, :]) + modv[3:4, :]
        hm[pl.ds(pl.multiple_of(m * TOK + i * 32, 32), 32), :] = h.astype(BF)
        return carry

    lax.fori_loop(0, 8, second_norm, 0)
    hm_sent = all_rows(link, hm)
    dm_sent = all_rows(link, dmlp)
    for r in (1, 2, 3):
        hm_sent[r].wait_recv()
        dm_sent[r].wait_recv()
    gg.done()
    gd.done()
    link.finish()
    tok_sent()
    cot_sent()


def store_tiles(val, ref, base, piece, keep):
    block = ref.shape[3] if keep is None else piece
    for q in range(val.shape[0] // piece):
        row = base + q * piece
        f, off = row // block, row % block
        n = piece if keep is None else keep
        ref[f // 4, f // 2 % 2, f % 2, off : off + n, :] = val[q * piece : q * piece + n, :].astype(BF)


def kernel_b(
    wg, wd, hm, dmlp, tokp, og, attn_out, modv, bg, bd, perm, valid,
    dwg, dwd, dattn, dmid, bout, small, dbg,
    gu, coef, hid, hsend, hrecv, hown, msend, mrecv, mown, bo, ssem, rsem,
):
    here = Place()
    link = Link(here, ssem, rsem)
    link.greet(True)
    m = here.m
    wgf = wg[...].reshape(D, 1536)
    wdf = wd[...].reshape(768, D)
    small[...] = jnp.zeros_like(small)
    dbg[...] = jnp.zeros_like(dbg)

    def mlp(k):
        gu[...] = nn(hm[at(k, TOK), :], wgf) + bg[...]

        def acts(i, carry):
            rows = at(i, 32)
            out = pl.ds(pl.multiple_of(k * TOK + i * 32, 32), 32)
            g, u = gu[rows, 0:768], gu[rows, 768:1536]
            sig = jax.nn.sigmoid(g)
            act = g * sig
            hid[out, :] = (act * u).astype(BF)
            gu[rows, 0:768] = u * sig * (1.0 + g * (1.0 - sig))
            gu[rows, 768:1536] = act
            return carry

        lax.fori_loop(0, 8, acts, 0)
        dh = nt(dmlp[at(k, TOK), :], wdf)
        out = at(k, TOK)
        coef[out, 0:768] = (gu[:, 0:768] * dh).astype(BF)
        coef[out, 768:1536] = (gu[:, 768:1536] * dh).astype(BF)
        dbg[0:1, :] += jnp.sum(coef[out, :].astype(F32), 0, keepdims=True)

    hs, ms = {}, {}
    for r in (2, 3, 1):
        k, dev = here.mate(r)
        mlp(k)
        hsend[r - 1] = nt(coef[at(k, TOK), :], wgf).astype(BF)
        hs[r] = link.send(hsend.at[r - 1], hrecv.at[r - 1], dev)
    mlp(m)
    hown[...] = nt(coef[at(m, TOK), :], wgf)
    for r in (2, 3, 1):
        k, dev = here.mate(r)
        msend[r - 1] = nn(hid[at(k, TOK), :], wdf).astype(BF)
        ms[r] = link.send(msend.at[r - 1], mrecv.at[r - 1], dev)
    mown[...] = nn(hid[at(m, TOK), :], wdf)
    for r in (1, 2, 3):
        hs[r].wait_recv()

    def mid_back(i, carry):
        rows = at(i, 32)
        d = hown[rows, :]
        for r in range(3):
            d += hrecv[r, rows, :].astype(F32)
        a = attn_out[rows, :]
        n, recip = norm_rows(tokp[rows, :].astype(F32) + modv[2:3, :] * a)
        small[1:2, :] += jnp.sum(d, 0, keepdims=True)
        small[2:3, :] += jnp.sum(d * n, 0, keepdims=True)
        g = og[rows, :].astype(F32) + norm_rows_back(d * (1.0 + modv[4:5, :]), n, recip)
        dmid[rows, :] = g
        small[3:4, :] += jnp.sum(g * a, 0, keepdims=True)
        low = (modv[2:3, :] * g).astype(BF)
        dattn[pl.ds(pl.multiple_of(m * TOK + i * 32, 32), 32), :] = low
        small[5:6, :] += jnp.sum(low.astype(F32), 0, keepdims=True)
        return carry

    lax.fori_loop(0, 8, mid_back, 0)
    da = all_rows(link, dattn)
    for i in range(3):
        store_tiles(tn(hm[:, i * 384 : i * 384 + 384], coef[...]), dwg, i * 384, 48, None)
    for i in range(2):
        store_tiles(tn(hid[:, i * 384 : i * 384 + 384], dmlp[...]), dwd, i * 384, 96, None)
    for r in (1, 2, 3):
        ms[r].wait_recv()

    def finish_out(i, carry):
        rows = at(i, 32)
        o = mown[rows, :] + bd[...]
        for r in range(3):
            o += mrecv[r, rows, :].astype(F32)
        g = og[rows, :].astype(F32)
        small[0:1, :] += jnp.sum(g * o, 0, keepdims=True)
        mine = dmlp[pl.ds(pl.multiple_of(m * TOK + i * 32, 32), 32), :]
        small[4:5, :] += jnp.sum(mine.astype(F32), 0, keepdims=True)
        mid = tokp[rows, :].astype(F32) + modv[2:3, :] * attn_out[rows, :]
        bo[rows, :] = ((mid + modv[5:6, :] * o) * valid[rows, :]).astype(BF)
        return carry

    lax.fori_loop(0, 8, finish_out, 0)
    bo[...] = nt(bo[...], perm[...]).astype(BF)
    sent, got = link.scatter(
        lambda j: bo.at[pl.ds(j * 64, 64)], bout.at[here.z], here.item_source, here.z
    )
    for r in (1, 2, 3):
        da[r].wait_recv()
    got(bo.at[pl.ds(0, 64)], lambda j: bout.at[j])
    link.finish()
    sent()


def kernel_c(
    dwg, dwd, dattn, att, wp, wq, ha, rawq, rawk, qr, kr, vv, maskb, dmid, tokp, modv, gains, tabs, perm, spread, pick,
    dtok, fq, fg, fp, fd, small, dbq, dgain,
    dwq, dwp, datt, de, dc, tsend, trecv, town, to, eq, eg,
    g1a, g1b, g2a, g2b, g3a, g3b, d1a, d1b, d2a, d2b, d3a, d3b,
    q1a, q1b, q2a, q2b, q3a, q3b, p1a, p1b, p2a, p2b, p3a, p3b, ssem, rsem,
):
    here = Place()
    link = Link(here, ssem, rsem)
    link.greet(True)
    m = here.m
    rg = Reduce(link, dwg, (g1a, g1b, g2a, g2b, g3a, g3b), SPLIT_G)
    rd = Reduce(link, dwd, (d1a, d1b, d2a, d2b, d3a, d3b), SPLIT_D)
    rq = Reduce(link, dwq, (q1a, q1b, q2a, q2b, q3a, q3b), SPLIT_Q)
    rp = Reduce(link, dwp, (p1a, p1b, p2a, p2b, p3a, p3b), SPLIT_P)
    rg.hop1()
    rd.hop1()
    small[...] = jnp.zeros_like(small)
    dgain[...] = jnp.zeros_like(dgain)
    dbq[...] = jnp.zeros_like(dbq)
    wpf = wp[...].reshape(512, D)

    def back_proj(b, carry):
        datt[at(b, TOK), :] = nt(dattn[at(b, TOK), :], wpf).astype(BF)
        return carry

    lax.fori_loop(0, 4, back_proj, 0)
    store_tiles(tn(att[...], dattn[...]), dwp, 0, 64, PAD)
    rp.hop1()

    def attend_back(p, carry):
        item = p // 4
        lanes = at(p % 4, 128)
        rows_all = at(item, 512)
        dk = jnp.zeros((512, 128), F32)
        dv = jnp.zeros((512, 128), F32)

        def head_back_store(d, raw_ref, row, t, rows, out_rows):
            cos, sina, sinb = tabs[0, rows, :], tabs[1, rows, :], tabs[2, rows, :]
            raw = raw_ref[p, rows, :]
            recip = lax.rsqrt(jnp.sum(raw * raw, -1, keepdims=True) * (1.0 / HEAD) + EPSILON)
            dn = turn_back(d, cos, sina, sinb)
            dgain[t : t + 1, :] += jnp.sum(dn * raw * recip, 0, keepdims=True)
            u = dn * gains[t : t + 1, :]
            mean = jnp.sum(u * raw, -1, keepdims=True) * (1.0 / HEAD)
            res = recip * u - raw * (recip * recip * recip * mean)
            de[out_rows, at(t * 4 + p % 4, 128)] = res.astype(BF)

        for half in range(2):
            rows = pl.ds(half * TOK, TOK)
            out_rows = pl.ds(pl.multiple_of(item * 512 + half * TOK, TOK), TOK)
            do = datt[out_rows, lanes]
            s = nt(qr[p, rows, :], kr[p]) * ROOT + maskb[item]
            e = jnp.exp(s - jnp.max(s, -1, keepdims=True))
            pf = e / jnp.sum(e, -1, keepdims=True)
            pr = pf.astype(BF)
            dp = nt(do, vv[p])
            delta = jnp.sum(pf * dp, -1, keepdims=True)
            ds = (pf * (dp - delta)).astype(BF)
            dq = nn(ds, kr[p]) * ROOT
            dk += tn(ds, qr[p, rows, :])
            dv += tn(pr, do)
            head_back_store(dq, rawq, None, 0, rows, out_rows)
        dk = dk * ROOT
        for half in range(2):
            rows = pl.ds(half * TOK, TOK)
            out_rows = pl.ds(pl.multiple_of(item * 512 + half * TOK, TOK), TOK)
            head_back_store(dk[half * TOK : half * TOK + TOK], rawk, None, 1, rows, out_rows)
        de[rows_all, at(8 + p % 4, 128)] = dv.astype(BF)
        return carry

    lax.fori_loop(0, 4, attend_back, 0)
    rg.hop2()
    rd.hop2()
    rp.hop2()
    lax.fori_loop(4, 8, attend_back, 0)
    rg.hop3()
    rd.hop3()
    rp.hop3()

    def squeeze(b, carry):
        v = de[at(b, TOK), :]
        dbq[0:1, :] += jnp.sum(v.astype(F32), 0, keepdims=True)
        dc[at(b, TOK), :] = nt(v, spread[...]).astype(BF)
        return carry

    lax.fori_loop(0, 4, squeeze, 0)
    wqf = wq[...].reshape(D, 864)
    ts = {}
    for r in (2, 3, 1):
        k, dev = here.mate(r)
        tsend[r - 1] = nt(dc[at(k, TOK), :], wqf).astype(BF)
        ts[r] = link.send(tsend.at[r - 1], trecv.at[r - 1], dev)
    town[...] = nt(dc[at(m, TOK), :], wqf)
    for i in range(3):
        store_tiles(tn(ha[:, i * 384 : i * 384 + 384], dc[...]), dwq, i * 384, 48, None)
    rq.hop1()
    for r in (1, 2, 3):
        ts[r].wait_recv()

    def first_back(i, carry):
        rows = at(i, 32)
        d = town[rows, :]
        for r in range(3):
            d += trecv[r, rows, :].astype(F32)
        n, recip = norm_rows(tokp[rows, :].astype(F32))
        small[0:1, :] += jnp.sum(d, 0, keepdims=True)
        small[1:2, :] += jnp.sum(d * n, 0, keepdims=True)
        g = dmid[rows, :] + norm_rows_back(d * (1.0 + modv[1:2, :]), n, recip)
        to[rows, :] = g.astype(BF)
        return carry

    lax.fori_loop(0, 8, first_back, 0)
    to[...] = nt(to[...], perm[...]).astype(BF)
    sent, got = link.scatter(
        lambda j: to.at[pl.ds(j * 64, 64)], dtok.at[here.z], here.item_source, here.z
    )
    rq.hop2()

    def hand_out(red, exp, out, cols):
        left, right = red.done()
        exp[:, :, 0 : red.split] = tn(pick[...], left).astype(BF).reshape(4, PAD, red.split)
        exp[:, :, red.split : cols] = tn(pick[...], right).astype(BF).reshape(4, PAD, cols - red.split)
        got_it = {}
        for r in (2, 3, 1):
            k, dev = here.mate(r)
            got_it[r] = link.send(exp.at[k], out.at[m], dev)
        out[m] = exp[m]
        return got_it

    def plain(red, out):
        left, right = red.done()
        out[...] = nt(left, perm[:, 0 : red.split]) + nt(right, perm[:, red.split : D])

    og_ = hand_out(rg, eg, fg, 1536)
    plain(rd, fd)
    plain(rp, fp)
    rq.hop3()
    oq_ = hand_out(rq, eq, fq, 864)
    for r in (1, 2, 3):
        og_[r].wait_recv()
        oq_[r].wait_recv()
    got(to.at[pl.ds(0, 64)], lambda j: dtok.at[j])
    link.finish()
    sent()


def near(here, r):
    x = 1 - here.x if r // 4 else here.x
    c = 1 - here.c if r // 2 % 2 else here.c
    y = 1 - here.y if r % 2 else here.y
    return x, c, y, (x * 2 + c, here.z, y)


def along_z(here, r):
    z = (here.z + r) % 4
    return z, (here.dp, z, here.y)


def greet_small(here):
    bar = pltpu.get_barrier_semaphore()
    for d in [near(here, r)[3] for r in range(1, 8)] + [along_z(here, r)[1] for r in (1, 2, 3)]:
        pl.semaphore_signal(bar, inc=1, device_id=d, device_id_type=MESH)
    pl.semaphore_wait(bar, 10)


def kernel_front(cond, w_mod, b_mod, bias, got, condg, msg, p1, m2, ssem, rsem):
    here = Place()
    greet_small(here)
    link = Link(here, ssem, rsem)
    condg[here.dp] = cond[...]
    cs = [link.send(cond, condg.at[here.dp], near(here, r)[3]) for r in (2, 4, 6)]
    for r in range(4):
        msg[r, 4:6, :] = bias[...]
    for c in cs:
        c.wait_recv()
    v = condg[...].reshape(32, D)
    act = (v * jax.nn.sigmoid(v)).astype(BF)
    part = nn(act, w_mod[...]) + b_mod[...]
    for z in range(4):
        for d in range(4):
            msg[z, d : d + 1, 0:216] = part[d * 8 + z : d * 8 + z + 1, :]
    zs = []
    for r in (1, 2, 3):
        z, dev = along_z(here, r)
        zs.append(link.send(msg.at[z], p1.at[here.z], dev))
    p1[here.z] = msg[here.z]
    for c in zs:
        c.wait_recv()
    for z in range(4):
        for d in range(4):
            m2[d, z, 0:1, :] = p1[z, d : d + 1, :]
            m2[d, z, 1:3, :] = p1[z, 4:6, :]
    ns = []
    for r in range(1, 8):
        x, _, y, dev = near(here, r)
        ns.append(link.send(m2.at[x * 2 + y], got.at[here.x, here.c, here.y], dev))
    got[here.x, here.c, here.y] = m2[here.x * 2 + here.y]
    for c in ns:
        c.wait_recv()
    link.finish()


def three(v):
    hi = v.astype(BF)
    rest = v - hi.astype(F32)
    mid = rest.astype(BF)
    return jnp.concatenate([hi, mid, (rest - mid.astype(F32)).astype(BF)], 0)


def kernel_back(pk, condg, w_mod, slope, dwm, sums, dbm, dcond, q1, m2, q2, dm, e0, e1, e2, e3, ssem, rsem):
    here = Place()
    greet_small(here)
    link = Link(here, ssem, rsem)
    ns = []
    for r in range(1, 8):
        x, c, y, dev = near(here, r)
        ns.append(link.send(pk.at[x, c, y], q1.at[here.x, here.c, here.y], dev))
    q1[here.x, here.c, here.y] = pk[here.x, here.c, here.y]
    for n in ns:
        n.wait_recv()
    for z in range(4):
        for x in range(2):
            for y in range(2):
                d = x * 2 + y
                m2[z, d : d + 1, :] = q1[x, 0, y, z, 0:1, :] + q1[x, 1, y, z, 0:1, :]
        total = q1[0, 0, 0, z, 1:4, :]
        for i in range(1, 8):
            total += q1[i // 4, i // 2 % 2, i % 2, z, 1:4, :]
        m2[z, 4:7, :] = total
    zs = []
    for r in (1, 2, 3):
        z, dev = along_z(here, r)
        zs.append(link.send(m2.at[z], q2.at[here.z], dev))
    q2[here.z] = m2[here.z]
    dm[...] = jnp.zeros_like(dm)
    v = condg[...].reshape(32, D)
    act = (v * jax.nn.sigmoid(v)).astype(BF)
    for c in zs:
        c.wait_recv()
    for z in range(4):
        for d in range(4):
            dm[d * 8 + z : d * 8 + z + 1, :] = q2[z, d : d + 1, 0:216]
    sums[...] = q2[0] + q2[1] + q2[2] + q2[3]
    dbm[...] = jnp.broadcast_to(jnp.sum(dm[...], 0, keepdims=True), (8, 216))
    d3 = three(dm[...])
    for b in range(8):
        t = nt(d3, w_mod[b * 144 : b * 144 + 144, :])
        t = t[0:32] + t[32:64] + t[64:96]
        for d in range(4):
            e0[d, b % 2, b // 2] = t[d * 8 : d * 8 + 8, :]
    ns = []
    for r in range(1, 8):
        x, c, y, dev = near(here, r)
        ns.append(link.send(e0.at[x * 2 + c, y], e1.at[here.x, here.c, here.y], dev))
    e1[here.x, here.c, here.y] = e0[here.dp, here.y]
    dwm[...] = tn(jnp.concatenate([act, act, act], 0), d3)
    for n in ns:
        n.wait_recv()
    total = e1[0, 0, 0]
    for i in range(1, 8):
        total += e1[i // 4, i // 2 % 2, i % 2]
    e2[...] = total
    zs = []
    for r in (1, 2, 3):
        z, dev = along_z(here, r)
        zs.append(link.send(e2.at[z], e3.at[here.z], dev))
    e3[here.z] = e2[here.z]
    for c in zs:
        c.wait_recv()
    dcond[...] = (e3[0] + e3[1] + e3[2] + e3[3]) * slope[...]
    link.finish()


def call(kernel, ident, outs, scratch, args, hbm=(), sems=64):
    vm = pl.BlockSpec(memory_space=pltpu.VMEM)
    hb = pl.BlockSpec(memory_space=pltpu.HBM)
    return pl.pallas_call(
        kernel,
        out_shape=[jax.ShapeDtypeStruct(s, t) for s, t in outs],
        in_specs=[hb if i in hbm else vm for i in range(len(args))],
        out_specs=[vm] * len(outs),
        scratch_shapes=scratch + [pltpu.SemaphoreType.DMA((sems,)), pltpu.SemaphoreType.DMA((sems,))]
        + ([pltpu.SemaphoreType.DMA((2,))] if hbm else []),
        compiler_params=pltpu.CompilerParams(
            collective_id=ident, has_side_effects=True, vmem_limit_bytes=LIMIT
        ),
    )(*args)


def to_order(v):
    lead = v.shape[:-1]
    n = len(lead)
    v = v.reshape(lead + (2, 2, 2, 2, 2, UNIT))
    return v.transpose(tuple(range(n)) + tuple(n + i for i in (0, 2, 4, 3, 1, 5))).reshape(lead + (D,))


def from_order(v):
    lead = v.shape[:-1]
    n = len(lead)
    v = v.reshape(lead + (2, 2, 2, 2, 2, UNIT))
    return v.transpose(tuple(range(n)) + tuple(n + i for i in (0, 4, 1, 3, 2, 5))).reshape(lead + (D,))


def local(
    tokens, conditioning, heights, widths, cotangent, w_mod, b_mod, w_qkv, b_qkv, query_gain, key_gain,
    w_proj, b_proj, w_gu, b_gu, w_down, b_down,
):
    args = (
        tokens, conditioning, heights, widths, cotangent, w_mod, b_mod, w_qkv, b_qkv, query_gain, key_gain,
        w_proj, b_proj, w_gu, b_gu, w_down, b_down,
    )
    sizes = tuple(lax.axis_size(a) for a in ("dp", "row", "col"))
    if sizes != (4, 4, 2) or tokens.shape != (4, 4, 16, D):
        return general(*args)
    every = ("dp", "row", "col")
    perm, spread, pick, tabs, row_of, col_of = constants()
    dp, z, y = (lax.axis_index(a) for a in every)
    x, c, zh, zl = dp // 2, dp % 2, z // 2, z % 2
    block = jnp.concatenate(
        [
            conditioning.astype(F32),
            jnp.pad(jnp.stack([heights, widths]).astype(F32), ((0, 0), (0, D - 4))),
            jnp.zeros((2, D), F32),
        ]
    )
    bias = jnp.concatenate([b_qkv, b_proj, b_gu, b_down]).astype(F32)
    bias = jnp.pad(bias, (0, 140)).reshape(2, 256)
    got, condg = call(
        kernel_front, 3,
        [((2, 2, 2, 4, 8, 256), F32), ((4, 8, D), F32)],
        [pltpu.VMEM((4, 8, 256), F32), pltpu.VMEM((4, 8, 256), F32), pltpu.VMEM((4, 4, 8, 256), F32)],
        (block, w_mod, b_mod.astype(F32).reshape(1, 216), bias),
        sems=16,
    )
    tall = condg[:, 4, :4].reshape(16)
    wide = condg[:, 5, :4].reshape(16)
    item = (2 * x + y) * 4 + z
    got = got.transpose(0, 1, 3, 2, 4, 5).reshape(32, 8, 256)
    modv = got[:, 0, :216]
    pack = got[:, 1:3].reshape(32, 512)
    modv = to_order(modv.reshape(6, D))
    modv = jnp.concatenate([modv, jnp.zeros((2, D), F32)])
    own = lambda v: lax.dynamic_index_in_dim(
        lax.dynamic_index_in_dim(v, c, 2, False), zl, 3, False
    )
    bq = own(pack[:, 0:108].reshape(3, 2, 2, 2, 2, 2, UNIT))
    bq = jnp.pad(bq, ((0, 0),) * 4 + ((0, 64 - UNIT),)).reshape(1, 1536)
    bp = to_order(pack[:, 108:144].reshape(1, D))
    bg = own(pack[:, 144:336].reshape(2, 2, 2, 2, 2, 2, 96)).reshape(1, 1536)
    bd = to_order(pack[:, 336:372].reshape(1, D))
    pair = (2 * x + y) * 4 + 2 * zh + jnp.arange(2)
    row_of, col_of = jnp.asarray(row_of), jnp.asarray(col_of)
    live = (row_of[None].astype(F32) < tall[pair][:, None]) & (col_of[None].astype(F32) < wide[pair][:, None])
    maskb = jnp.where(live, 0.0, MASKED).astype(F32).reshape(2, 1, 512)
    valid = lax.dynamic_slice(live[zl].astype(F32), (c * TOK,), (TOK,)).reshape(TOK, 1)
    gains = jnp.pad(
        jnp.stack([query_gain, key_gain]).reshape(2, 2, UNIT), ((0, 6), (0, 0), (0, 64 - UNIT))
    ).reshape(8, 128)
    wq = w_qkv.reshape(UNIT, 3, 2, 2, 2, 2, 72).transpose(5, 3, 0, 1, 2, 4, 6).reshape(4, UNIT, 864)
    wq = jnp.pad(wq, ((0, 0), (0, PAD - UNIT), (0, 0)))
    wg = w_gu.reshape(UNIT, 2, 2, 2, 2, 2, 192).transpose(5, 3, 0, 1, 2, 4, 6).reshape(4, UNIT, 1536)
    wg = jnp.pad(wg, ((0, 0), (0, PAD - UNIT), (0, 0)))
    wp = jnp.pad(w_proj, ((0, PAD - UNIT), (0, 0)))

    full = (GROUP, D)
    (
        wq_all, wp_all, wg_all, wd_all, ha, rawq, rawk, qr, kr, vv, att, hm, dmlp, tokp, og, attn_out,
    ) = call(
        kernel_a, 0,
        [
            ((2, 2, 2, 144, 864), BF), ((2, 2, 2, 64, D), BF), ((2, 2, 2, 144, 1536), BF), ((2, 2, 2, 96, D), BF),
            (full, BF), ((8, 512, 128), F32), ((8, 512, 128), F32), ((8, 512, 128), BF), ((8, 512, 128), BF),
            ((8, 512, 128), BF), ((GROUP, 512), BF), (full, BF), (full, BF),
            ((TOK, D), BF), ((TOK, D), BF), ((TOK, D), F32),
        ],
        [
            pltpu.VMEM((4, PAD, 864), BF), pltpu.VMEM((4, PAD, 1536), BF), pltpu.VMEM((TOK, D), BF),
            pltpu.VMEM((TOK, D), BF), pltpu.VMEM((D, 1536), BF), pltpu.VMEM((3, TOK, D), BF),
            pltpu.VMEM((3, TOK, D), BF), pltpu.VMEM((TOK, D), F32),
        ],
        (
            tokens.reshape(4, 64, D), cotangent.reshape(4, 64, D), wq, wg, wp, w_down, perm, spread, pick, tabs,
            gains, modv, bq, bp, maskb, valid,
        ),
        hbm=(0, 1, 2, 3),
    )
    dwg, dwd, dattn, dmid, bout, small_b, dbg = call(
        kernel_b, 1,
        [
            ((2, 2, 2, 144, 1536), BF), ((2, 2, 2, 96, D), BF), (full, BF), ((TOK, D), F32), ((4, 64, D), BF),
            ((8, D), F32), ((8, 1536), F32),
        ],
        [
            pltpu.VMEM((TOK, 1536), F32), pltpu.VMEM((GROUP, 1536), BF), pltpu.VMEM((GROUP, 768), BF),
            pltpu.VMEM((3, TOK, D), BF), pltpu.VMEM((3, TOK, D), BF), pltpu.VMEM((TOK, D), F32),
            pltpu.VMEM((3, TOK, D), BF), pltpu.VMEM((3, TOK, D), BF), pltpu.VMEM((TOK, D), F32),
            pltpu.VMEM((TOK, D), BF),
        ],
        (wg_all, wd_all, hm, dmlp, tokp, og, attn_out, modv, bg, bd, perm, valid),
    )
    dtok, fq, fg, fp, fd, small_c, dbq, dgain = call(
        kernel_c, 2,
        [
            ((4, 64, D), BF), ((4, PAD, 864), BF), ((4, PAD, 1536), BF), ((PAD, D), F32), ((96, D), F32),
            ((8, D), F32), ((8, 1536), F32), ((8, 128), F32),
        ],
        [
            pltpu.VMEM((2, 2, 2, 144, 864), BF), pltpu.VMEM((2, 2, 2, PAD, D), BF), pltpu.VMEM((GROUP, 512), BF),
            pltpu.VMEM((GROUP, 1536), BF), pltpu.VMEM((GROUP, 864), BF), pltpu.VMEM((3, TOK, D), BF),
            pltpu.VMEM((3, TOK, D), BF), pltpu.VMEM((TOK, D), F32), pltpu.VMEM((TOK, D), BF),
            pltpu.VMEM((4, PAD, 864), BF), pltpu.VMEM((4, PAD, 1536), BF),
        ]
        + Reduce.buffers(144, 1536, SPLIT_G) + Reduce.buffers(96, D, SPLIT_D)
        + Reduce.buffers(144, 864, SPLIT_Q) + Reduce.buffers(PAD, D, SPLIT_P),
        (
            dwg, dwd, dattn, att, wp_all, wq_all, ha, rawq, rawk, qr, kr, vv, maskb, dmid, tokp, modv, gains, tabs,
            perm, spread, pick,
        ),
    )

    g_w_qkv = fq[:, :UNIT].reshape(2, 2, UNIT, 3, 2, 2, 72).transpose(2, 3, 4, 1, 5, 0, 6)
    g_w_qkv = g_w_qkv.reshape(UNIT, 3456).astype(F32)
    g_w_gu = fg[:, :UNIT].reshape(2, 2, UNIT, 2, 2, 2, 192).transpose(2, 3, 4, 1, 5, 0, 6)
    g_w_gu = g_w_gu.reshape(UNIT, 6144).astype(F32)
    spread_own = lambda v: lax.dynamic_update_index_in_dim(
        jnp.zeros(v.shape[:2] + (2,) + v.shape[2:3] + (2,) + v.shape[3:], F32),
        lax.dynamic_update_index_in_dim(
            jnp.zeros(v.shape[:3] + (2,) + v.shape[3:], F32), v[:, :, :, None], zl, 3
        )[:, :, None],
        c,
        2,
    )
    db_qkv = spread_own(dbq[0].reshape(3, 2, 2, 2, 64)[..., :UNIT]).reshape(3456)
    db_gu = spread_own(dbg[0].reshape(2, 2, 2, 2, 96)).reshape(32, 192)
    vecs = from_order(jnp.stack([small_c[0], small_c[1], small_b[3], small_b[1], small_b[2], small_b[0],
                                 small_b[5], small_b[4]]))
    dg = dgain[:2].reshape(2, 2, 64)[..., :UNIT].reshape(144)
    biases = jnp.concatenate(
        [
            db_qkv[: 2 * D].reshape(32, 72),
            db_qkv[2 * D :].reshape(32, 36),
            db_gu,
            vecs[6].reshape(32, UNIT),
            vecs[7].reshape(32, UNIT),
            jnp.zeros((32, 140), F32),
        ],
        1,
    ).reshape(32, 2, 256)
    pack = jnp.concatenate(
        [
            jnp.pad(vecs[:6].reshape(32, 1, 216), ((0, 0), (0, 0), (0, 40))),
            biases,
            jnp.broadcast_to(jnp.pad(dg, (0, 112)), (32, 1, 256)),
            jnp.zeros((32, 4, 256), F32),
        ],
        1,
    )
    pack = pack.reshape(2, 2, 4, 2, 8, 256).transpose(0, 1, 3, 2, 4, 5)
    cond_f = conditioning.astype(F32)
    sig = jax.nn.sigmoid(cond_f)
    slope = lax.dynamic_slice(sig * (1.0 + cond_f * (1.0 - sig)), (0, (z * 2 + y) * 144), (4, 144))
    slope = jnp.concatenate([slope, jnp.zeros((4, 144), F32)])
    g_w_mod, sums, g_b_mod, d_cond = call(
        kernel_back, 4,
        [((D, 216), F32), ((8, 256), F32), ((8, 216), F32), ((8, 144), F32)],
        [
            pltpu.VMEM((2, 2, 2, 4, 8, 256), F32), pltpu.VMEM((4, 8, 256), F32), pltpu.VMEM((4, 8, 256), F32),
            pltpu.VMEM((32, 216), F32), pltpu.VMEM((4, 2, 4, 8, 144), F32), pltpu.VMEM((2, 2, 2, 4, 8, 144), F32),
            pltpu.VMEM((4, 8, 144), F32), pltpu.VMEM((4, 8, 144), F32),
        ],
        (pack, condg, w_mod, slope),
        sems=24,
    )
    biases = sums[4:6].reshape(512)
    gains_out = sums[6, :144]
    return (
        bout.reshape(tokens.shape),
        dtok.reshape(tokens.shape).astype(F32),
        d_cond[:4],
        g_w_mod,
        g_b_mod[0],
        g_w_qkv,
        biases[:72],
        biases[72:108],
        gains_out[:72],
        gains_out[72:],
        fp[:UNIT],
        biases[300:336],
        g_w_gu,
        biases[108:300],
        fd,
        biases[336:372],
    )


def solution(mesh):
    in_specs = (
        P("dp", "row", "col", None),
        P("dp", None),
        P("dp"),
        P("dp"),
        P("dp", "row", "col", None),
        P(None, ("dp", "row", "col")),
        P(("dp", "row", "col")),
        P(("dp", "row", "col"), None),
        P(("dp", "row", "col")),
        P(),
        P(),
        P(("dp", "row", "col"), None),
        P(("dp", "row", "col")),
        P(("dp", "row", "col"), None),
        P(("dp", "row", "col")),
        P(("dp", "row", "col"), None),
        P(("dp", "row", "col")),
    )
    out_specs = (
        P("dp", "row", "col", None),
        P("dp", "row", "col", None),
        P("dp", ("row", "col")),
        P(None, ("dp", "row", "col")),
        P(("dp", "row", "col")),
        P(("dp", "row", "col"), None),
        P(("dp", "row", "col")),
        P(("dp", "row", "col")),
        P(),
        P(),
        P(("dp", "row", "col"), None),
        P(("dp", "row", "col")),
        P(("dp", "row", "col"), None),
        P(("dp", "row", "col")),
        P(("dp", "row", "col"), None),
        P(("dp", "row", "col")),
    )
    return jax.shard_map(local, mesh=mesh, in_specs=in_specs, out_specs=out_specs, check_vma=False)
```

```python
import math

import jax
import jax.numpy as jnp
import numpy as np
from jax import lax
from jax.experimental import pallas as pl
from jax.experimental.pallas import tpu as pltpu
from jax.sharding import PartitionSpec as P

HEADS = 16
HEAD = 72
FF = 3072


EPSILON = 1e-06
MASKED = -1000000000.0
PRECISE = lax.Precision.HIGHEST


def rope_tables(row_pos, col_pos, head_size):
    half_size = head_size // 2
    lane_index = jnp.arange(head_size)
    pair_index = (lane_index % half_size // 2).astype(jnp.float32)
    frequency = jnp.exp(-math.log(10000.0) * 2.0 * pair_index / half_size)
    places = jnp.where(lane_index[None, :] >= half_size, col_pos[:, None], row_pos[:, None]).astype(
        jnp.float32
    )
    angles = places * frequency[None, :]
    return (jnp.cos(angles), jnp.sin(angles))


def rotate(values):
    pair_view = values.reshape(values.shape[:-1] + (values.shape[-1] // 2, 2))
    turned = jnp.stack((-pair_view[..., 1], pair_view[..., 0]), axis=-1)
    return turned.reshape(values.shape)


def norm_parts(values):
    centered = values - jnp.mean(values, -1, keepdims=True)
    recip = lax.rsqrt(jnp.mean(centered * centered, -1, keepdims=True) + EPSILON)
    return (centered * recip, recip)


def norm_back(gradient, normed, recip):
    return recip * (
        gradient
        - jnp.mean(gradient, -1, keepdims=True)
        - normed * jnp.mean(gradient * normed, -1, keepdims=True)
    )


def head_back(gradient, raw_value, recip, gain_vec):
    scaled = gradient * gain_vec
    gain_grad = jnp.sum(gradient * raw_value * recip, axis=(0, 1, 2))
    raw_grad = recip * scaled - raw_value * (recip * recip * recip) * jnp.mean(
        scaled * raw_value, -1, keepdims=True
    )
    return (raw_grad, gain_grad)


def general(
    tokens,
    conditioning,
    heights,
    widths,
    cotangent,
    w_mod,
    b_mod,
    w_qkv,
    b_qkv,
    query_gain,
    key_gain,
    w_proj,
    b_proj,
    w_gu,
    b_gu,
    w_down,
    b_down,
):
    item_count, tile_rows, tile_cols, model_width = tokens.shape
    tile_span = tile_rows * tile_cols
    n_row = lax.axis_size("row")
    n_col = lax.axis_size("col")
    groups = n_row * n_col
    key_count = tile_span * groups
    inv_root = 1.0 / math.sqrt(HEAD)
    row_at = lax.axis_index("row")
    col_at = lax.axis_index("col")
    local_index = jnp.arange(tile_span)
    query_rows = row_at * tile_rows + local_index // tile_cols
    query_cols = col_at * tile_cols + local_index % tile_cols
    valid_query = (query_rows[None, :] < heights[:, None]) & (query_cols[None, :] < widths[:, None])
    key_index = jnp.arange(key_count)
    key_owner = key_index // tile_span
    key_spot = key_index % tile_span
    key_rows = key_owner // n_col * tile_rows + key_spot // tile_cols
    key_cols = key_owner % n_col * tile_cols + key_spot % tile_cols
    valid_key = (key_rows[None, :] < heights[:, None]) & (key_cols[None, :] < widths[:, None])
    cos_tab, sin_tab = rope_tables(query_rows, query_cols, HEAD)
    cos_four = cos_tab[None, :, None, :]
    sin_four = sin_tab[None, :, None, :]
    cond_f = conditioning.astype(jnp.float32)
    cond_sig = jax.nn.sigmoid(cond_f)
    act_low = (cond_f * cond_sig).astype(jnp.bfloat16)
    gathered = (
        lax.all_gather(w_mod, ("dp", "row", "col"), axis=1, tiled=True),
        lax.all_gather(b_mod, ("dp", "row", "col"), axis=0, tiled=True),
        lax.all_gather(w_qkv, ("dp", "row", "col"), axis=0, tiled=True),
        lax.all_gather(b_qkv, ("dp", "row", "col"), axis=0, tiled=True),
        lax.all_gather(w_proj, ("dp", "row", "col"), axis=0, tiled=True),
        lax.all_gather(b_proj, ("dp", "row", "col"), axis=0, tiled=True),
        lax.all_gather(w_gu, ("dp", "row", "col"), axis=0, tiled=True),
        lax.all_gather(b_gu, ("dp", "row", "col"), axis=0, tiled=True),
        lax.all_gather(w_down, ("dp", "row", "col"), axis=0, tiled=True),
        lax.all_gather(b_down, ("dp", "row", "col"), axis=0, tiled=True),
    )
    (
        w_mod_all,
        b_mod_all,
        w_qkv_all,
        b_qkv_all,
        w_proj_all,
        b_proj_all,
        w_gu_all,
        b_gu_all,
        w_down_all,
        b_down_all,
    ) = gathered
    modul = jnp.dot(act_low, w_mod_all, preferred_element_type=jnp.float32) + b_mod_all.astype(
        jnp.float32
    )
    shift_a, scale_a, gate_a, shift_m, scale_m, gate_m = [
        modul[:, piece * model_width : (piece + 1) * model_width][:, None, :] for piece in range(6)
    ]
    resid_in = tokens.reshape(item_count, tile_span, model_width).astype(jnp.float32)
    normed_a, recip_a = norm_parts(resid_in)
    h_attn = (normed_a * (1.0 + scale_a) + shift_a).astype(jnp.bfloat16)
    qkv_all = jnp.dot(h_attn, w_qkv_all, preferred_element_type=jnp.float32) + b_qkv_all.astype(
        jnp.float32
    )
    query_raw = qkv_all[..., :model_width].reshape(item_count, tile_span, HEADS, HEAD)
    key_raw = qkv_all[..., model_width : 2 * model_width].reshape(
        item_count, tile_span, HEADS, HEAD
    )
    value_raw = qkv_all[..., 2 * model_width :]
    query_recip = lax.rsqrt(jnp.mean(query_raw * query_raw, -1, keepdims=True) + EPSILON)
    key_recip = lax.rsqrt(jnp.mean(key_raw * key_raw, -1, keepdims=True) + EPSILON)
    query_normed = query_raw * query_recip * query_gain
    key_normed = key_raw * key_recip * key_gain
    query_rot = (query_normed * cos_four + rotate(query_normed) * sin_four).astype(jnp.bfloat16)
    key_rot = (key_normed * cos_four + rotate(key_normed) * sin_four).astype(jnp.bfloat16)
    value_low = value_raw.astype(jnp.bfloat16)
    kv_local = jnp.concatenate([key_rot.reshape(item_count, tile_span, model_width), value_low], -1)
    kv_every = lax.all_gather(kv_local, ("row", "col"), axis=1, tiled=True)
    query_heads = query_rot.transpose(2, 0, 1, 3)
    key_part = (
        kv_every[..., :model_width]
        .reshape(item_count, key_count, HEADS, HEAD)
        .transpose(2, 0, 1, 3)
    )
    value_part = (
        kv_every[..., model_width:]
        .reshape(item_count, key_count, HEADS, HEAD)
        .transpose(2, 0, 1, 3)
    )
    key_mask = valid_key[:, None, :]

    def attend(head_block):
        query_h, key_h, value_h = head_block
        scores = (
            jnp.einsum("itd,ikd->itk", query_h, key_h, preferred_element_type=jnp.float32)
            * inv_root
        )
        scores = jnp.where(key_mask, scores, MASKED)
        row_max = jnp.max(scores, -1, keepdims=True)
        exponent = jnp.exp(scores - row_max)
        row_sum = jnp.sum(exponent, -1, keepdims=True)
        probs = (exponent / row_sum).astype(jnp.bfloat16)
        result = jnp.einsum("itk,ikd->itd", probs, value_h, preferred_element_type=jnp.float32)
        return (result, row_max, row_sum)

    attended_heads, max_kept, sum_kept = lax.map(attend, (query_heads, key_part, value_part))
    attended = (
        attended_heads.transpose(1, 2, 0, 3)
        .reshape(item_count, tile_span, model_width)
        .astype(jnp.bfloat16)
    )
    attn_out = jnp.dot(
        attended, w_proj_all, preferred_element_type=jnp.float32
    ) + b_proj_all.astype(jnp.float32)
    resid_mid = resid_in + gate_a * attn_out
    normed_m, recip_m = norm_parts(resid_mid)
    h_mlp = (normed_m * (1.0 + scale_m) + shift_m).astype(jnp.bfloat16)
    gate_up = jnp.dot(h_mlp, w_gu_all, preferred_element_type=jnp.float32) + b_gu_all.astype(
        jnp.float32
    )
    gate_part = gate_up[..., :FF]
    up_part = gate_up[..., FF:]
    gate_sig = jax.nn.sigmoid(gate_part)
    gate_act = gate_part * gate_sig
    hidden = (gate_act * up_part).astype(jnp.bfloat16)
    mlp_out = jnp.dot(hidden, w_down_all, preferred_element_type=jnp.float32) + b_down_all.astype(
        jnp.float32
    )
    mask_f = valid_query[..., None].astype(jnp.float32)
    block_out = ((resid_mid + gate_m * mlp_out) * mask_f).astype(jnp.bfloat16)
    out_grad = cotangent.reshape(item_count, tile_span, model_width).astype(jnp.float32) * mask_f
    d_mlp = (gate_m * out_grad).astype(jnp.bfloat16)
    d_gate_m = jnp.sum(out_grad * mlp_out, 1)
    dw_down = jnp.einsum("itf,itd->fd", hidden, d_mlp, preferred_element_type=jnp.float32)
    db_down = jnp.sum(d_mlp.astype(jnp.float32), (0, 1))
    d_hidden = jnp.einsum("itd,fd->itf", d_mlp, w_down_all, preferred_element_type=jnp.float32)
    d_gate = d_hidden * up_part * gate_sig * (1.0 + gate_part * (1.0 - gate_sig))
    d_up = d_hidden * gate_act
    d_gate_up = jnp.concatenate([d_gate, d_up], -1).astype(jnp.bfloat16)
    dw_gu = jnp.einsum("itd,ite->de", h_mlp, d_gate_up, preferred_element_type=jnp.float32)
    db_gu = jnp.sum(d_gate_up.astype(jnp.float32), (0, 1))
    d_hmlp = jnp.einsum("ite,de->itd", d_gate_up, w_gu_all, preferred_element_type=jnp.float32)
    d_shift_m = jnp.sum(d_hmlp, 1)
    d_scale_m = jnp.sum(d_hmlp * normed_m, 1)
    d_mid = out_grad + norm_back(d_hmlp * (1.0 + scale_m), normed_m, recip_m)
    d_attn = (gate_a * d_mid).astype(jnp.bfloat16)
    d_gate_a = jnp.sum(d_mid * attn_out, 1)
    dw_proj = jnp.einsum("itd,ite->de", attended, d_attn, preferred_element_type=jnp.float32)
    db_proj = jnp.sum(d_attn.astype(jnp.float32), (0, 1))
    d_attended = jnp.einsum(
        "ite,de->itd", d_attn, w_proj_all, preferred_element_type=jnp.float32
    ).astype(jnp.bfloat16)
    d_att_heads = d_attended.reshape(item_count, tile_span, HEADS, HEAD).transpose(2, 0, 1, 3)
    key_back, value_back = (key_part, value_part)

    def attend_back(head_block):
        query_h, key_h, value_h, grad_h, max_h, sum_h = head_block
        scores = (
            jnp.einsum("itd,ikd->itk", query_h, key_h, preferred_element_type=jnp.float32)
            * inv_root
        )
        scores = jnp.where(key_mask, scores, MASKED)
        probs = jnp.exp(scores - max_h) / sum_h
        d_probs = jnp.einsum("itd,ikd->itk", grad_h, value_h, preferred_element_type=jnp.float32)
        delta = jnp.sum(probs * d_probs, -1, keepdims=True)
        d_scores = (probs * (d_probs - delta)).astype(jnp.bfloat16)
        d_query = (
            jnp.einsum("itk,ikd->itd", d_scores, key_h, preferred_element_type=jnp.float32)
            * inv_root
        )
        d_key = (
            jnp.einsum("itk,itd->ikd", d_scores, query_h, preferred_element_type=jnp.float32)
            * inv_root
        )
        d_value = jnp.einsum(
            "itk,itd->ikd", probs.astype(jnp.bfloat16), grad_h, preferred_element_type=jnp.float32
        )
        return (d_query, d_key, d_value)

    dq_heads, dk_heads, dv_heads = lax.map(
        attend_back, (query_heads, key_back, value_back, d_att_heads, max_kept, sum_kept)
    )
    dkv_term = jnp.concatenate(
        [
            dk_heads.transpose(1, 2, 0, 3).reshape(item_count, key_count, model_width),
            dv_heads.transpose(1, 2, 0, 3).reshape(item_count, key_count, model_width),
        ],
        -1,
    )
    dkv_own = lax.psum_scatter(dkv_term, ("row", "col"), scatter_dimension=1, tiled=True)
    d_key_rot = dkv_own[..., :model_width].reshape(item_count, tile_span, HEADS, HEAD)
    d_value = dkv_own[..., model_width:]
    d_query_rot = dq_heads.transpose(1, 2, 0, 3)
    d_query_n = d_query_rot * cos_four - rotate(d_query_rot * sin_four)
    d_key_n = d_key_rot * cos_four - rotate(d_key_rot * sin_four)
    d_query_raw, dq_gain = head_back(d_query_n, query_raw, query_recip, query_gain)
    d_key_raw, dk_gain = head_back(d_key_n, key_raw, key_recip, key_gain)
    gain_total = lax.psum((dq_gain, dk_gain), ("dp", "row", "col"))
    d_qkv = jnp.concatenate(
        [
            d_query_raw.reshape(item_count, tile_span, model_width),
            d_key_raw.reshape(item_count, tile_span, model_width),
            d_value,
        ],
        -1,
    ).astype(jnp.bfloat16)
    dw_qkv = jnp.einsum("itd,ite->de", h_attn, d_qkv, preferred_element_type=jnp.float32)
    db_qkv = jnp.sum(d_qkv.astype(jnp.float32), (0, 1))
    db_query_key = db_qkv[: 2 * model_width]
    db_value = db_qkv[2 * model_width :]
    d_hattn = jnp.einsum("ite,de->itd", d_qkv, w_qkv_all, preferred_element_type=jnp.float32)
    d_shift_a = jnp.sum(d_hattn, 1)
    d_scale_a = jnp.sum(d_hattn * normed_a, 1)
    d_tokens = d_mid + norm_back(d_hattn * (1.0 + scale_a), normed_a, recip_a)
    d_modul = jnp.concatenate([d_shift_a, d_scale_a, d_gate_a, d_shift_m, d_scale_m, d_gate_m], -1)
    act_f = act_low.astype(jnp.float32)
    dw_mod = jnp.einsum("id,ie->de", act_f, d_modul, precision=PRECISE)
    db_mod = jnp.sum(d_modul, 0)
    d_act = jnp.einsum("ie,de->id", d_modul, w_mod_all.astype(jnp.float32), precision=PRECISE)
    d_cond_part = d_act * cond_sig * (1.0 + cond_f * (1.0 - cond_sig))
    d_cond = lax.psum_scatter(d_cond_part, ("row", "col"), scatter_dimension=1, tiled=True)
    summed = (
        lax.psum_scatter(dw_mod, ("dp", "row", "col"), scatter_dimension=1, tiled=True),
        lax.psum_scatter(db_mod, ("dp", "row", "col"), scatter_dimension=0, tiled=True),
        lax.psum_scatter(dw_qkv, ("dp", "row", "col"), scatter_dimension=0, tiled=True),
        lax.psum_scatter(db_query_key, ("dp", "row", "col"), scatter_dimension=0, tiled=True),
        lax.psum_scatter(db_value, ("dp", "row", "col"), scatter_dimension=0, tiled=True),
        lax.psum_scatter(dw_proj, ("dp", "row", "col"), scatter_dimension=0, tiled=True),
        lax.psum_scatter(db_proj, ("dp", "row", "col"), scatter_dimension=0, tiled=True),
        lax.psum_scatter(dw_gu, ("dp", "row", "col"), scatter_dimension=0, tiled=True),
        lax.psum_scatter(db_gu, ("dp", "row", "col"), scatter_dimension=0, tiled=True),
        lax.psum_scatter(dw_down, ("dp", "row", "col"), scatter_dimension=0, tiled=True),
        lax.psum_scatter(db_down, ("dp", "row", "col"), scatter_dimension=0, tiled=True),
    )
    (
        g_w_mod,
        g_b_mod,
        g_w_qkv,
        g_b_query_key,
        g_b_value,
        g_w_proj,
        g_b_proj,
        g_w_gu,
        g_b_gu,
        g_w_down,
        g_b_down,
    ) = summed
    return (
        block_out.reshape(item_count, tile_rows, tile_cols, model_width),
        d_tokens.reshape(item_count, tile_rows, tile_cols, model_width),
        d_cond,
        g_w_mod,
        g_b_mod,
        g_w_qkv,
        g_b_query_key,
        g_b_value,
        gain_total[0],
        gain_total[1],
        g_w_proj,
        g_b_proj,
        g_w_gu,
        g_b_gu,
        g_w_down,
        g_b_down,
    )


MESH = pl.DeviceIdType.MESH
BF = jnp.bfloat16
F32 = jnp.float32
LIMIT = 60 * 1024 * 1024
D = 1152
UNIT = 36
PAD = 48
TOK = 256
GROUP = 1024
SPLIT_Q, SPLIT_P, SPLIT_G, SPLIT_D = 384, 640, 768, 640
ROOT = 1.0 / math.sqrt(HEAD)


def nn(a, b):
    return lax.dot_general(a, b, (((1,), (0,)), ((), ())), preferred_element_type=F32)


def nt(a, b):
    return lax.dot_general(a, b, (((1,), (1,)), ((), ())), preferred_element_type=F32)


def tn(a, b):
    return lax.dot_general(a, b, (((0,), (0,)), ((), ())), preferred_element_type=F32)


def width_order():
    xx, zh, yy, zl, cc, jj = np.indices((2, 2, 2, 2, 2, UNIT)).reshape(6, -1)
    return ((((xx * 2 + cc) * 2 + zh) * 2 + zl) * 2 + yy) * UNIT + jj


def constants():
    perm = np.zeros((D, D), np.float32)
    perm[width_order(), np.arange(D)] = 1.0
    spread = np.zeros((864, 1536), np.float32)
    tt, hh, yy, jj = np.indices((3, 4, 2, UNIT)).reshape(4, -1)
    spread[tt * 288 + hh * 72 + yy * 36 + jj, tt * 512 + hh * 128 + yy * 64 + jj] = 1.0
    pick = np.zeros((144, 192), np.float32)
    kk, jj = np.indices((4, UNIT)).reshape(2, -1)
    pick[kk * 36 + jj, kk * 48 + jj] = 1.0
    spot = np.arange(512)
    row = spot // 128 * 4 + spot // 16 % 4
    col = spot // 64 % 2 * 16 + spot % 16
    lane = np.arange(128)
    part = lane % 64
    freq = np.exp(-math.log(10000.0) * 2.0 * (part // 2) / 36.0)
    place = np.where(lane[None, :] >= 64, col[:, None], row[:, None]).astype(np.float64)
    angle = place * freq[None, :]
    live = part < UNIT
    cos = np.where(live, np.cos(angle), 0.0)
    sin = np.where(live, np.sin(angle), 0.0)
    even = lane % 2 == 0
    tabs = np.stack([cos, np.where(even, -sin, 0.0), np.where(even, 0.0, sin)]).astype(np.float32)
    return (
        jnp.asarray(perm, BF),
        jnp.asarray(spread, BF),
        jnp.asarray(pick, BF),
        jnp.asarray(tabs, F32),
        row,
        col,
    )


class Place:
    def __init__(self):
        dp = lax.axis_index("dp")
        self.z = lax.axis_index("row")
        self.y = lax.axis_index("col")
        self.x = dp // 2
        self.c = dp % 2
        self.zh = self.z // 2
        self.zl = self.z % 2
        self.m = self.zl * 2 + self.c
        self.dp = dp

    def mate(self, r):
        c = 1 - self.c if r % 2 else self.c
        zl = 1 - self.zl if r // 2 else self.zl
        return zl * 2 + c, (self.x * 2 + c, self.zh * 2 + zl, self.y)

    def xpeer(self):
        return ((1 - self.x) * 2 + self.c, self.z, self.y)

    def ypeer(self):
        return (self.dp, self.z, 1 - self.y)

    def zpeer(self):
        return (self.dp, (1 - self.zh) * 2 + self.zl, self.y)

    def item_home(self, j):
        return (self.x * 2 + self.zh, j, self.c)

    def item_source(self, blk):
        return (self.x * 2 + self.y, self.c * 2 + blk // 2, blk % 2)

    def is_me(self, dev):
        return (dev[0] == self.dp) & (dev[1] == self.z) & (dev[2] == self.y)


class Link:
    def __init__(self, here, ssem, rsem):
        self.here, self.ssem, self.rsem, self.n, self.open = here, ssem, rsem, 0, []

    def greet(self, items):
        here = self.here
        bar = pltpu.get_barrier_semaphore()
        devs = [here.mate(r)[1] for r in (1, 2, 3)]
        devs += [here.xpeer(), here.ypeer(), here.zpeer()]
        for d in devs:
            pl.semaphore_signal(bar, inc=1, device_id=d, device_id_type=MESH)
        total = len(devs)
        if items:
            for d in [here.item_home(j) for j in range(4)] + [here.item_source(j) for j in range(4)]:


                @pl.when(jnp.logical_not(here.is_me(d)))
                def _():
                    pl.semaphore_signal(bar, inc=1, device_id=d, device_id_type=MESH)

            far = (here.zh - here.c) * (here.zh - here.c)
            off = (here.y - here.c) * (here.y - here.c)
            total += 8 - 2 * (1 - far) * (1 - off)
        pl.semaphore_wait(bar, total)

    def send(self, src, dst, dev):
        k = self.n
        self.n += 1
        copy = pltpu.make_async_remote_copy(
            src_ref=src,
            dst_ref=dst,
            send_sem=self.ssem.at[k],
            recv_sem=self.rsem.at[k],
            device_id=dev,
            device_id_type=MESH,
        )
        copy.start()
        self.open.append(copy)
        return copy

    def scatter(self, src_of, dst, dev_of, slot):
        base = self.n
        self.n += 4
        here = self.here
        copies = []
        for j in range(4):
            dev = dev_of(j)
            mine = here.is_me(dev)
            remote = pltpu.make_async_remote_copy(
                src_ref=src_of(j),
                dst_ref=dst,
                send_sem=self.ssem.at[base + j],
                recv_sem=self.rsem.at[base + slot],
                device_id=dev,
                device_id_type=MESH,
            )
            local_copy = pltpu.make_async_copy(src_of(j), dst, self.rsem.at[base + slot])

            @pl.when(mine)
            def _():
                local_copy.start()

            @pl.when(jnp.logical_not(mine))
            def _():
                remote.start()

            copies.append((mine, remote))

        def wait_send():
            for mine, remote in copies:

                @pl.when(jnp.logical_not(mine))
                def _():
                    remote.wait_send()

        def wait_recv(src, dst_of):
            for j in range(4):
                pltpu.make_async_copy(src, dst_of(j), self.rsem.at[base + j]).wait()

        return wait_send, wait_recv

    def settle(self, *copies):
        for copy in copies:
            copy.wait_send()
            self.open = [c for c in self.open if c is not copy]

    def finish(self):
        for copy in self.open:
            copy.wait_send()
        self.open = []


def norm_rows(x):
    mean = jnp.sum(x, -1, keepdims=True) * (1.0 / D)
    cent = x - mean
    var = jnp.sum(cent * cent, -1, keepdims=True) * (1.0 / D)
    recip = lax.rsqrt(var + EPSILON)
    return cent * recip, recip


def norm_rows_back(g, y, recip):
    mg = jnp.sum(g, -1, keepdims=True) * (1.0 / D)
    mgy = jnp.sum(g * y, -1, keepdims=True) * (1.0 / D)
    return recip * (g - mg - y * mgy)


def at(i, n):
    return pl.ds(pl.multiple_of(i * n, n), n)


class Gather:
    def __init__(self, link, ref, rows, split):
        self.link, self.ref, self.rows, self.split = link, ref, rows, split

    def cut(self, i, j, k, cols):
        return self.ref.at[i, j, k, pl.ds(0, self.rows), cols]

    def hop1(self):
        h = self.link.here
        part = self.cut(h.x, h.zh, h.y, slice(None))
        self.a = self.link.send(part, part, h.zpeer())

    def hop2(self):
        h = self.link.here
        self.a.wait_recv()
        pa = self.cut(h.x, slice(None), h.y, pl.ds(0, self.split))
        pb = self.cut(h.x, slice(None), h.y, pl.ds(self.split, self.ref.shape[-1] - self.split))
        self.a = self.link.send(pa, pa, h.xpeer())
        self.b = self.link.send(pb, pb, h.ypeer())

    def hop3(self):
        h = self.link.here
        self.a.wait_recv()
        self.b.wait_recv()
        pa = self.cut(slice(None), slice(None), h.y, pl.ds(0, self.split))
        pb = self.cut(
            h.x, slice(None), slice(None), pl.ds(self.split, self.ref.shape[-1] - self.split)
        )
        self.a = self.link.send(pa, pa, h.ypeer())
        self.b = self.link.send(pb, pb, h.xpeer())

    def done(self):
        self.a.wait_recv()
        self.b.wait_recv()


class Reduce:
    def __init__(self, link, ref, bufs, split, cols):
        self.link, self.ref, self.split, self.cols = link, ref, split, cols
        self.r1a, self.r1b, self.r2a, self.r2b, self.r3a, self.r3b = bufs

    @staticmethod
    def buffers(rows, cols, split):
        rest = cols - split
        return [
            pltpu.VMEM((2, 2, rows, split), BF),
            pltpu.VMEM((2, 2, rows, rest), BF),
            pltpu.VMEM((2, rows, split), BF),
            pltpu.VMEM((2, rows, rest), BF),
            pltpu.VMEM((rows, split), BF),
            pltpu.VMEM((rows, rest), BF),
        ]

    def hop1(self):
        h = self.link.here
        ca, cb = pl.ds(0, self.split), pl.ds(self.split, self.cols - self.split)
        self.a = self.link.send(self.ref.at[1 - h.x, :, :, :, ca], self.r1a, h.xpeer())
        self.b = self.link.send(self.ref.at[:, :, 1 - h.y, :, cb], self.r1b, h.ypeer())

    def hop2(self):
        h = self.link.here
        ca, cb = pl.ds(0, self.split), pl.ds(self.split, self.cols - self.split)
        self.a.wait_recv()
        self.b.wait_recv()

        def add(i, carry):
            u, v = i // 2, i % 2
            own = self.ref[h.x, u, v, :, ca].astype(F32)
            self.r1a[u, v] = (self.r1a[u, v].astype(F32) + own).astype(BF)
            own = self.ref[u, v, h.y, :, cb].astype(F32)
            self.r1b[u, v] = (self.r1b[u, v].astype(F32) + own).astype(BF)
            return carry

        lax.fori_loop(0, 4, add, 0)
        self.a = self.link.send(self.r1a.at[:, 1 - h.y], self.r2a, h.ypeer())
        self.b = self.link.send(self.r1b.at[1 - h.x], self.r2b, h.xpeer())

    def hop3(self):
        h = self.link.here
        self.a.wait_recv()
        self.b.wait_recv()

        def add(u, carry):
            own = self.r1a[u, h.y].astype(F32)
            self.r2a[u] = (self.r2a[u].astype(F32) + own).astype(BF)
            own = self.r1b[h.x, u].astype(F32)
            self.r2b[u] = (self.r2b[u].astype(F32) + own).astype(BF)
            return carry

        lax.fori_loop(0, 2, add, 0)
        self.a = self.link.send(self.r2a.at[1 - h.zh], self.r3a, h.zpeer())
        self.b = self.link.send(self.r2b.at[1 - h.zh], self.r3b, h.zpeer())

    def done(self):
        h = self.link.here
        self.a.wait_recv()
        self.b.wait_recv()
        left = self.r2a[h.zh].astype(F32) + self.r3a[...].astype(F32)
        right = self.r2b[h.zh].astype(F32) + self.r3b[...].astype(F32)
        return left.astype(BF), right.astype(BF)


class RowGather:
    def __init__(self, link, ref):
        self.link, self.ref = link, ref
        here = link.here
        own = ref.at[at(here.m, TOK)]
        self.far = link.send(own, own, here.mate(2)[1])
        self.near = link.send(own, own, here.mate(1)[1])

    def near_done(self):
        self.near.wait_recv()

    def pass_on(self):
        here = self.link.here
        self.far.wait_recv()
        rows = self.ref.at[at(here.mate(2)[0], TOK)]
        self.last = self.link.send(rows, rows, here.mate(1)[1])

    def last_done(self):
        self.last.wait_recv()


class RowReduce:
    def __init__(self, link, out, into):
        self.link, self.out, self.into = link, out, into

    def give(self, r, val):
        i = 0 if r == 3 else 1
        if val is not None:
            self.out[i] = val.astype(BF)
        sent = self.link.send(self.out.at[i], self.into.at[i], self.link.here.mate(1)[1])
        if r == 3:
            self.s3 = sent
        else:
            self.s1 = sent

    def keep_far(self, val):
        self.out[2] = val.astype(BF)

    def pass_on(self):
        self.s3.wait_recv()

        def add(i, carry):
            rows = at(i, 32)
            both = self.out[2, rows, :].astype(F32) + self.into[0, rows, :].astype(F32)
            self.out[2, rows, :] = both.astype(BF)
            return carry

        lax.fori_loop(0, 8, add, 0)
        self.s2 = self.link.send(self.out.at[2], self.into.at[2], self.link.here.mate(2)[1])

    def arrive(self):
        self.s1.wait_recv()
        self.s2.wait_recv()

    def total(self, rows):
        return self.into[1, rows, :].astype(F32) + self.into[2, rows, :].astype(F32)


def turn(v, cos, sina, sinb):
    return v * cos + pltpu.roll(v, 127, 1) * sina + pltpu.roll(v, 1, 1) * sinb


def turn_back(d, cos, sina, sinb):
    return d * cos - pltpu.roll(d, 127, 1) * sina - pltpu.roll(d, 1, 1) * sinb


def kernel_a(
    tok_in, cot_in, wq_in, wg_in, wp_in, wd_in, perm, spread, pick, tabs, gains, modv, bq, bp, maskb, valid,
    wq_out, wp_out, wg_out, wd_out, ha_out, raw_out, rot_out, att_out, hm, dmlp, tokp, og, attn_out,
    wq, wp, wg, wd, ha, raw, rot, att, s0q, s0g, tokr, cotr, wqe, psend, precv, pown, ssem, rsem, lsem,
):
    here = Place()
    link = Link(here, ssem, rsem)
    fetch = Fetch(lsem)
    m = here.m
    own_q = fetch.go(wq_in.at[m], s0q.at[m])
    own_g = fetch.go(wg_in.at[m], s0g.at[m])
    link.greet(True)
    slot = here.zl * 2 + here.y
    rows_in = at(slot, 64)
    sq, sg = {}, {}
    for r in (2, 3, 1):
        k, dev = here.mate(r)
        sq[r] = link.send(wq_in.at[k], s0q.at[m], dev)
    tok_sent, tok_got = link.scatter(lambda j: tok_in.at[j], tokr.at[rows_in], here.item_home, slot)

    gq = Gather(link, wq, 144, SPLIT_Q)
    gp = Gather(link, wp, PAD, SPLIT_P)
    gg = Gather(link, wg, 144, SPLIT_G)
    gd = Gather(link, wd, 96, SPLIT_D)

    own_q.wait()
    for r in (1, 2, 3):
        sq[r].wait_recv()
    wq[here.x, here.zh, here.y] = nn(pick[...], s0q[...].reshape(192, 864)).astype(BF)
    gq.hop1()
    for r in (2, 3, 1):
        k, dev = here.mate(r)
        sg[r] = link.send(wg_in.at[k], s0g.at[m], dev)
    wp[:, :, :, PAD:64, :] = jnp.zeros((2, 2, 2, 64 - PAD, D), BF)
    wp[here.x, here.zh, here.y, 0:PAD, :] = nn(wp_in[...], perm[...]).astype(BF)
    gp.hop1()
    wd[here.x, here.zh, here.y] = nn(wd_in[...], perm[...]).astype(BF)
    tok_got(tok_in.at[0], lambda j: tokr.at[pl.ds(j * 64, 64)])
    tokp[...] = nn(tokr[...], perm[...]).astype(BF)

    def first_norm(i, carry):
        n, _ = norm_rows(tokp[at(i, 32), :].astype(F32))
        h = n * (1.0 + modv[1:2, :]) + modv[0:1, :]
        ha[pl.ds(pl.multiple_of(m * TOK + i * 32, 32), 32), :] = h.astype(BF)
        return carry

    lax.fori_loop(0, 8, first_norm, 0)
    ha_all = RowGather(link, ha)
    own_g.wait()
    for r in (1, 2, 3):
        sg[r].wait_recv()
    wg[here.x, here.zh, here.y] = nn(pick[...], s0g[...].reshape(192, 1536)).astype(BF)
    gq.hop2()
    gg.hop1()
    gd.hop1()
    gp.hop2()
    gq.hop3()
    ha_all.pass_on()
    cot_sent, cot_got = link.scatter(lambda j: cot_in.at[j], cotr.at[rows_in], here.item_home, slot)
    ha_all.near_done()
    gp.hop3()
    ha_all.last_done()
    outs = [fetch.go(ha, ha_out)]
    gq.done()
    outs.append(fetch.go(wq, wq_out))

    def widen(i, carry):
        part = wq[i // 2, i % 2].reshape(288, 864)
        wqe[at(i, 288), :] = nn(part, spread[...]).astype(BF)
        return carry

    lax.fori_loop(0, 4, widen, 0)

    def project(b, carry):
        acc = nn(ha[at(b, TOK), :], wqe[...]) + bq[...]
        item, half = b // 2, at(b % 2, TOK)
        cos, sina, sinb = tabs[0, half, :], tabs[1, half, :], tabs[2, half, :]
        for h in range(4):
            p = item * 4 + h
            for t in range(2):
                v = acc[:, t * 512 + h * 128 : t * 512 + h * 128 + 128]
                recip = lax.rsqrt(jnp.sum(v * v, -1, keepdims=True) * (1.0 / HEAD) + EPSILON)
                raw[p, t, half, :] = v
                n = v * recip * gains[t : t + 1, :]
                rot[p, t, half, :] = turn(n, cos, sina, sinb).astype(BF)
            rot[p, 2, half, :] = acc[:, 1024 + h * 128 : 1152 + h * 128].astype(BF)
        return carry

    def attend(p, carry):
        item = p // 4
        lanes = at(p % 4, 128)
        for half in range(2):
            rows = pl.ds(half * TOK, TOK)
            s = nt(rot[p, 0, rows, :], rot[p, 1]) * ROOT + maskb[item]
            top = jnp.max(s, -1, keepdims=True)
            e = jnp.exp(s - top)
            pr = (e / jnp.sum(e, -1, keepdims=True)).astype(BF)
            out_rows = pl.ds(pl.multiple_of(item * 512 + half * TOK, TOK), TOK)
            att[out_rows, lanes] = nn(pr, rot[p, 2]).astype(BF)
        return carry

    other = 1 - here.zl
    lax.fori_loop(other * 2, other * 2 + 2, project, 0)
    gg.hop2()
    lax.fori_loop(other * 4, other * 4 + 4, attend, 0)
    gd.hop2()
    gp.done()
    outs.append(fetch.go(wp, wp_out))
    wpf = wp[...].reshape(512, D)
    red = RowReduce(link, psend, precv)
    red.give(3, nn(att[at(here.mate(3)[0], TOK), :], wpf))
    red.keep_far(nn(att[at(here.mate(2)[0], TOK), :], wpf))
    red.pass_on()
    lax.fori_loop(here.zl * 2, here.zl * 2 + 2, project, 0)
    outs.append(fetch.go(raw, raw_out))
    outs.append(fetch.go(rot, rot_out))
    gg.hop3()
    lax.fori_loop(here.zl * 4, here.zl * 4 + 4, attend, 0)
    gd.hop3()
    outs.append(fetch.go(att, att_out))
    red.give(1, nn(att[at(here.mate(1)[0], TOK), :], wpf))
    pown[...] = nn(att[at(m, TOK), :], wpf)
    red.arrive()

    def second_norm(i, carry):
        rows = at(i, 32)
        a = pown[rows, :] + bp[...] + red.total(rows)
        attn_out[rows, :] = a
        n, _ = norm_rows(tokp[rows, :].astype(F32) + modv[2:3, :] * a)
        h = n * (1.0 + modv[4:5, :]) + modv[3:4, :]
        hm[rows, :] = h.astype(BF)
        return carry

    lax.fori_loop(0, 8, second_norm, 0)
    cot_got(cot_in.at[0], lambda j: cotr.at[pl.ds(j * 64, 64)])
    og[...] = (nn(cotr[...], perm[...]) * valid[...]).astype(BF)

    def scale_grad(i, carry):
        g = og[at(i, 32), :].astype(F32) * modv[5:6, :]
        dmlp[at(i, 32), :] = g.astype(BF)
        return carry

    lax.fori_loop(0, 8, scale_grad, 0)
    gg.done()
    outs.append(fetch.go(wg, wg_out))
    gd.done()
    outs.append(fetch.go(wd, wd_out))
    for c in outs:
        c.wait()
    link.finish()
    tok_sent()
    cot_sent()


def store_tiles(val, ref, base, piece, keep):
    block = ref.shape[3] if keep is None else piece
    for q in range(val.shape[0] // piece):
        row = base + q * piece
        f, off = row // block, row % block
        n = piece if keep is None else keep
        part = val[q * piece : q * piece + n, :].astype(BF)
        ref[f // 4, f // 2 % 2, f % 2, off : off + n, 0 : val.shape[1]] = part


class Fetch:
    def __init__(self, sems):
        self.sems, self.n = sems, 0

    def go(self, src, dst):
        copy = pltpu.make_async_copy(src, dst, self.sems.at[self.n])
        self.n += 1
        copy.start()
        return copy


def kernel_b(
    wg_in, wd_in, hm_in, dm_in, tok_in, og_in, attn_in, att_in, wp_in, wq_in, ha_in, raw_in, rot_in, perm_in,
    spread_in, tabs_in, modv, bg, bd, gains, maskb, valid, pick,
    dtok, bout, fq, fg, fp, fd, small, dbg, dbq, dgain,
    wg, wd, hm, dmlp, tokp, og, attn_out, att, wp, wq, perm, tabs, gu, coef, hid, rsend, rrecv, mrecv, own32, dmid,
    dwg, dwd, dwp, dattn, raw, rot, to, bo, eq, eg,
    g1a, g1b, g2a, g2b, g3a, g3b, d1a, d1b, d2a, d2b, d3a, d3b,
    q1a, q1b, q2a, q2b, q3a, q3b, p1a, p1b, p2a, p2b, p3a, p3b, ssem, rsem, lsem,
):
    here = Place()
    link = Link(here, ssem, rsem)
    fetch = Fetch(lsem)
    m = here.m
    k1, k2, k3 = here.mate(1)[0], here.mate(2)[0], here.mate(3)[0]
    at_m, at_1, at_2, at_3 = at(m, TOK), at(k1, TOK), at(k2, TOK), at(k3, TOK)
    get_hm = fetch.go(hm_in, hm.at[at_m])
    get_dm = fetch.go(dm_in, dmlp.at[at_m])
    get_wg = fetch.go(wg_in, wg)
    get_wd = fetch.go(wd_in, wd)
    gets = [fetch.go(a, b) for a, b in ((tok_in, tokp), (og_in, og), (attn_in, attn_out))]
    get_wp = fetch.go(wp_in, wp)
    gets2 = [fetch.go(a, b) for a, b in ((tabs_in, tabs), (att_in, att), (wq_in, wq), (perm_in, perm))]
    base = fetch.n
    fetch.n += 4
    link.greet(True)
    get_hm.wait()
    hm_all = RowGather(link, hm)
    get_dm.wait()
    dm_all = RowGather(link, dmlp)
    small[...] = jnp.zeros_like(small)
    dbg[...] = jnp.zeros_like(dbg)
    dbq[...] = jnp.zeros_like(dbq)
    dgain[...] = jnp.zeros_like(dgain)
    get_wg.wait()
    get_wd.wait()

    def wgf():
        return wg[...].reshape(D, 1536)

    def wdf():
        return wd[...].reshape(768, D)

    def mlp(k):
        gu[...] = nn(hm[at(k, TOK), :], wgf()) + bg[...]

        def acts(i, carry):
            rows = at(i, 32)
            out = pl.ds(pl.multiple_of(k * TOK + i * 32, 32), 32)
            g, u = gu[rows, 0:768], gu[rows, 768:1536]
            sig = jax.nn.sigmoid(g)
            act = g * sig
            hid[out, :] = (act * u).astype(BF)
            gu[rows, 0:768] = u * sig * (1.0 + g * (1.0 - sig))
            gu[rows, 768:1536] = act
            return carry

        lax.fori_loop(0, 8, acts, 0)
        dh = nt(dmlp[at(k, TOK), :], wdf())
        out = at(k, TOK)
        coef[out, 0:768] = (gu[:, 0:768] * dh).astype(BF)
        coef[out, 768:1536] = (gu[:, 768:1536] * dh).astype(BF)
        dbg[0:1, :] += jnp.sum(coef[out, :].astype(F32), 0, keepdims=True)
        return nt(coef[out, :], wgf())

    hred = RowReduce(link, rsend, rrecv)
    own32[...] = mlp(m)
    hm_all.near_done()
    dm_all.near_done()
    hred.give(1, mlp(k1))
    hm_all.pass_on()
    dm_all.pass_on()
    hred.keep_far(mlp(k2))
    hm_all.last_done()
    dm_all.last_done()
    hred.give(3, mlp(k3))
    hred.pass_on()

    rg = Reduce(link, dwg, (g1a, g1b, g2a, g2b, g3a, g3b), SPLIT_G, 1536)
    rd = Reduce(link, dwd, (d1a, d1b, d2a, d2b, d3a, d3b), SPLIT_D, D)
    rq = Reduce(link, wg, (q1a, q1b, q2a, q2b, q3a, q3b), SPLIT_Q, 896)
    rp = Reduce(link, dwp, (p1a, p1b, p2a, p2b, p3a, p3b), SPLIT_P, D)
    for i in range(3):
        for n in range(2):
            cols = slice(n * 768, n * 768 + 768)
            t = tn(hm[:, i * 384 : i * 384 + 384], coef[:, cols])
            for q in range(8):
                row = i * 384 + q * 48
                f, off = row // 144, row % 144
                dwg[f // 4, f // 2 % 2, f % 2, off : off + 48, cols] = t[q * 48 : q * 48 + 48].astype(BF)
    rg.hop1()
    spread_got = fetch.go(spread_in, wg)
    for c in gets:
        c.wait()
    hred.arrive()

    def mid_back(i, carry):
        rows = at(i, 32)
        mine = pl.ds(pl.multiple_of(m * TOK + i * 32, 32), 32)
        d = own32[rows, :] + hred.total(rows)
        a = attn_out[rows, :]
        n, recip = norm_rows(tokp[rows, :].astype(F32) + modv[2:3, :] * a)
        small[1:2, :] += jnp.sum(d, 0, keepdims=True)
        small[2:3, :] += jnp.sum(d * n, 0, keepdims=True)
        g = og[rows, :].astype(F32) + norm_rows_back(d * (1.0 + modv[4:5, :]), n, recip)
        dmid[rows, :] = g
        small[3:4, :] += jnp.sum(g * a, 0, keepdims=True)
        low = (modv[2:3, :] * g).astype(BF)
        dattn[mine, :] = low
        small[5:6, :] += jnp.sum(low.astype(F32), 0, keepdims=True)
        small[4:5, :] += jnp.sum(dmlp[mine, :].astype(F32), 0, keepdims=True)
        return carry

    lax.fori_loop(0, 8, mid_back, 0)
    da_all = RowGather(link, dattn)
    for i in range(2):
        store_tiles(tn(hid[:, i * 384 : i * 384 + 384], dmlp[...]), dwd, i * 384, 96, None)
    rd.hop1()
    link.settle(hred.s1, hred.s2, hred.s3)
    for g in (hm_all, dm_all):
        link.settle(g.far, g.near, g.last)
    ha_got = fetch.go(ha_in, dmlp)
    da_all.near_done()
    mred = RowReduce(link, rsend, mrecv)
    mred.give(3, nn(hid[at_3, :], wdf()))
    mred.give(1, nn(hid[at_1, :], wdf()))
    mred.keep_far(nn(hid[at_2, :], wdf()))
    bo[...] = nn(hid[at_m, :], wdf()).astype(BF)

    def pair_of(n):
        item = here.zl + (1 - 2 * here.zl) * (n // 4)
        return item, item * 4 + n % 4

    def pair_copies(n):
        p = pair_of(n)[1]
        s = n % 2
        return (
            pltpu.make_async_copy(raw_in.at[p], raw.at[s], lsem.at[base + 2 * s]),
            pltpu.make_async_copy(rot_in.at[p], rot.at[s], lsem.at[base + 2 * s + 1]),
        )

    for c in pair_copies(0):
        c.start()
    get_wp.wait()
    for c in gets2:
        c.wait()

    def back_proj(rows):
        hid[rows, 0:512] = nt(dattn[rows, :], wp[...].reshape(512, D)).astype(BF)

    def attend_back(n, carry):
        item, p = pair_of(n)
        s = n % 2
        lanes = at(n % 4, 128)
        for c in pair_copies(n):
            c.wait()

        @pl.when(n < 7)
        def _():
            for c in pair_copies(n + 1):
                c.start()

        dk = jnp.zeros((512, 128), F32)
        dv = jnp.zeros((512, 128), F32)

        def head_back_store(d, t, rows, out_rows):
            cos, sina, sinb = tabs[0, rows, :], tabs[1, rows, :], tabs[2, rows, :]
            v = raw[s, t, rows, :]
            recip = lax.rsqrt(jnp.sum(v * v, -1, keepdims=True) * (1.0 / HEAD) + EPSILON)
            dn = turn_back(d, cos, sina, sinb)
            dgain[t : t + 1, :] += jnp.sum(dn * v * recip, 0, keepdims=True)
            u = dn * gains[t : t + 1, :]
            mean = jnp.sum(u * v, -1, keepdims=True) * (1.0 / HEAD)
            res = recip * u - v * (recip * recip * recip * mean)
            coef[out_rows, at(t * 4 + n % 4, 128)] = res.astype(BF)

        for half in range(2):
            rows = pl.ds(half * TOK, TOK)
            out_rows = pl.ds(pl.multiple_of(item * 512 + half * TOK, TOK), TOK)
            do = hid[out_rows, lanes]
            x = nt(rot[s, 0, rows, :], rot[s, 1]) * ROOT + maskb[item]
            e = jnp.exp(x - jnp.max(x, -1, keepdims=True))
            pf = e / jnp.sum(e, -1, keepdims=True)
            dp = nt(do, rot[s, 2])
            delta = jnp.sum(pf * dp, -1, keepdims=True)
            ds = (pf * (dp - delta)).astype(BF)
            dq = nn(ds, rot[s, 1]) * ROOT
            dk += tn(ds, rot[s, 0, rows, :])
            dv += tn(pf.astype(BF), do)
            head_back_store(dq, 0, rows, out_rows)
        dk = dk * ROOT
        for half in range(2):
            rows = pl.ds(half * TOK, TOK)
            out_rows = pl.ds(pl.multiple_of(item * 512 + half * TOK, TOK), TOK)
            head_back_store(dk[half * TOK : half * TOK + TOK], 1, rows, out_rows)
        coef[at(item, 512), at(8 + n % 4, 128)] = dv.astype(BF)
        return carry

    back_proj(at_m)
    back_proj(at_1)
    lax.fori_loop(0, 2, attend_back, 0)
    da_all.pass_on()
    mred.pass_on()
    lax.fori_loop(2, 4, attend_back, 0)
    rg.hop2()
    da_all.last_done()
    back_proj(at_2)
    back_proj(at_3)
    store_tiles(tn(att[...], dattn[...]), dwp, 0, 64, PAD)
    rp.hop1()
    lax.fori_loop(4, 6, attend_back, 0)
    rd.hop2()
    mred.arrive()

    def finish_out(i, carry):
        rows = at(i, 32)
        o = bo[rows, :].astype(F32) + bd[...] + mred.total(rows)
        small[0:1, :] += jnp.sum(og[rows, :].astype(F32) * o, 0, keepdims=True)
        mid = tokp[rows, :].astype(F32) + modv[2:3, :] * attn_out[rows, :]
        bo[rows, :] = ((mid + modv[5:6, :] * o) * valid[rows, :]).astype(BF)
        return carry

    lax.fori_loop(0, 8, finish_out, 0)
    bo[...] = nt(bo[...], perm[...]).astype(BF)
    b_sent, b_got = link.scatter(
        lambda j: bo.at[pl.ds(j * 64, 64)], bout.at[here.z], here.item_source, here.z
    )
    lax.fori_loop(6, 8, attend_back, 0)
    rp.hop2()
    spread_got.wait()

    def squeeze(rows):
        v = coef[rows, :]
        dbq[0:1, :] += jnp.sum(v.astype(F32), 0, keepdims=True)
        hm[rows, 0:864] = nt(v, wg[...].reshape(D, 1536)[0:864]).astype(BF)

    def to_input(rows):
        return nt(hm[rows, 0:864], wq[...].reshape(D, 864))

    link.settle(mred.s1, mred.s2, mred.s3)
    tred = RowReduce(link, rsend, rrecv)
    squeeze(at_3)
    tred.give(3, to_input(at_3))
    squeeze(at_2)
    tred.keep_far(to_input(at_2))
    tred.pass_on()
    squeeze(at_1)
    tred.give(1, to_input(at_1))
    squeeze(at_m)
    own32[...] = to_input(at_m)
    ha_got.wait()
    for i in range(3):
        store_tiles(tn(dmlp[:, i * 384 : i * 384 + 384], hm[:, 0:864]), wg, i * 384, 48, None)
    rq.hop1()
    rg.hop3()
    rd.hop3()
    rp.hop3()
    tred.arrive()

    def first_back(i, carry):
        rows = at(i, 32)
        d = own32[rows, :] + tred.total(rows)
        n, recip = norm_rows(tokp[rows, :].astype(F32))
        small[6:7, :] += jnp.sum(d, 0, keepdims=True)
        small[7:8, :] += jnp.sum(d * n, 0, keepdims=True)
        g = dmid[rows, :] + norm_rows_back(d * (1.0 + modv[1:2, :]), n, recip)
        to[rows, :] = g.astype(BF)
        return carry

    lax.fori_loop(0, 8, first_back, 0)
    to[...] = nt(to[...], perm[...]).astype(BF)
    sent, got = link.scatter(
        lambda j: to.at[pl.ds(j * 64, 64)], dtok.at[here.z], here.item_source, here.z
    )
    rq.hop2()

    def hand_out(red, exp, out):
        left, right = red.done()
        exp[:, :, 0 : red.split] = tn(pick[...], left).astype(BF).reshape(4, PAD, red.split)
        rest = red.cols - red.split
        exp[:, :, red.split : red.cols] = tn(pick[...], right).astype(BF).reshape(4, PAD, rest)
        over = [link.send(exp.at[here.mate(r)[0]], out.at[m], here.mate(r)[1]) for r in (2, 3, 1)]
        return over, fetch.go(exp.at[m], out.at[m])

    def plain(red, out):
        left, right = red.done()
        out[...] = nt(left, perm[:, 0 : red.split]) + nt(right, perm[:, red.split : D])

    g_over, g_own = hand_out(rg, eg, fg)
    rq.hop3()
    plain(rd, fd)
    plain(rp, fp)
    q_over, q_own = hand_out(rq, eq, fq)
    for c in g_over + q_over:
        c.wait_recv()
    g_own.wait()
    q_own.wait()
    b_got(bo.at[pl.ds(0, 64)], lambda j: bout.at[j])
    got(to.at[pl.ds(0, 64)], lambda j: dtok.at[j])
    link.finish()
    b_sent()
    sent()


def near(here, r):
    x = 1 - here.x if r // 4 else here.x
    c = 1 - here.c if r // 2 % 2 else here.c
    y = 1 - here.y if r % 2 else here.y
    return x, c, y, (x * 2 + c, here.z, y)


def along_z(here, r):
    z = (here.z + r) % 4
    return z, (here.dp, z, here.y)


def greet_small(here):
    bar = pltpu.get_barrier_semaphore()
    for d in [near(here, r)[3] for r in range(1, 8)] + [along_z(here, r)[1] for r in (1, 2, 3)]:
        pl.semaphore_signal(bar, inc=1, device_id=d, device_id_type=MESH)
    pl.semaphore_wait(bar, 10)


def kernel_front(cond, w_mod, b_mod, bias, got, condg, msg, p1, m2, ssem, rsem):
    here = Place()
    greet_small(here)
    link = Link(here, ssem, rsem)
    condg[here.dp] = cond[...]
    cs = [link.send(cond, condg.at[here.dp], near(here, r)[3]) for r in (2, 4, 6)]
    for r in range(4):
        msg[r, 4:6, :] = bias[...]
    for c in cs:
        c.wait_recv()
    v = condg[...].reshape(32, D)
    act = (v * jax.nn.sigmoid(v)).astype(BF)
    part = nn(act, w_mod[...]) + b_mod[...]
    for z in range(4):
        for d in range(4):
            msg[z, d : d + 1, 0:216] = part[d * 8 + z : d * 8 + z + 1, :]
    zs = []
    for r in (1, 2, 3):
        z, dev = along_z(here, r)
        zs.append(link.send(msg.at[z], p1.at[here.z], dev))
    p1[here.z] = msg[here.z]
    for c in zs:
        c.wait_recv()
    for z in range(4):
        for d in range(4):
            m2[d, z, 0:1, :] = p1[z, d : d + 1, :]
            m2[d, z, 1:3, :] = p1[z, 4:6, :]
    ns = []
    for r in range(1, 8):
        x, _, y, dev = near(here, r)
        ns.append(link.send(m2.at[x * 2 + y], got.at[here.x, here.c, here.y], dev))
    got[here.x, here.c, here.y] = m2[here.x * 2 + here.y]
    for c in ns:
        c.wait_recv()
    link.finish()


def three(v):
    hi = v.astype(BF)
    rest = v - hi.astype(F32)
    mid = rest.astype(BF)
    return jnp.concatenate([hi, mid, (rest - mid.astype(F32)).astype(BF)], 0)


def kernel_back(pk, condg, w_mod, slope, dwm, sums, dbm, dcond, q1, m2, q2, dm, e0, e1, e2, e3, ssem, rsem):
    here = Place()
    greet_small(here)
    link = Link(here, ssem, rsem)
    ns = []
    for r in range(1, 8):
        x, c, y, dev = near(here, r)
        ns.append(link.send(pk.at[x, c, y], q1.at[here.x, here.c, here.y], dev))
    q1[here.x, here.c, here.y] = pk[here.x, here.c, here.y]
    for n in ns:
        n.wait_recv()
    for z in range(4):
        for x in range(2):
            for y in range(2):
                d = x * 2 + y
                m2[z, d : d + 1, :] = q1[x, 0, y, z, 0:1, :] + q1[x, 1, y, z, 0:1, :]
        total = q1[0, 0, 0, z, 1:4, :]
        for i in range(1, 8):
            total += q1[i // 4, i // 2 % 2, i % 2, z, 1:4, :]
        m2[z, 4:7, :] = total
    zs = []
    for r in (1, 2, 3):
        z, dev = along_z(here, r)
        zs.append(link.send(m2.at[z], q2.at[here.z], dev))
    q2[here.z] = m2[here.z]
    dm[...] = jnp.zeros_like(dm)
    v = condg[...].reshape(32, D)
    act = (v * jax.nn.sigmoid(v)).astype(BF)
    for c in zs:
        c.wait_recv()
    for z in range(4):
        for d in range(4):
            dm[d * 8 + z : d * 8 + z + 1, :] = q2[z, d : d + 1, 0:216]
    sums[...] = q2[0] + q2[1] + q2[2] + q2[3]
    dbm[...] = jnp.broadcast_to(jnp.sum(dm[...], 0, keepdims=True), (8, 216))
    d3 = three(dm[...])
    for b in range(8):
        t = nt(d3, w_mod[b * 144 : b * 144 + 144, :])
        t = t[0:32] + t[32:64] + t[64:96]
        for d in range(4):
            e0[d, b % 2, b // 2] = t[d * 8 : d * 8 + 8, :]
    ns = []
    for r in range(1, 8):
        x, c, y, dev = near(here, r)
        ns.append(link.send(e0.at[x * 2 + c, y], e1.at[here.x, here.c, here.y], dev))
    e1[here.x, here.c, here.y] = e0[here.dp, here.y]
    dwm[...] = tn(jnp.concatenate([act, act, act], 0), d3)
    for n in ns:
        n.wait_recv()
    total = e1[0, 0, 0]
    for i in range(1, 8):
        total += e1[i // 4, i // 2 % 2, i % 2]
    e2[...] = total
    zs = []
    for r in (1, 2, 3):
        z, dev = along_z(here, r)
        zs.append(link.send(e2.at[z], e3.at[here.z], dev))
    e3[here.z] = e2[here.z]
    for c in zs:
        c.wait_recv()
    dcond[...] = (e3[0] + e3[1] + e3[2] + e3[3]) * slope[...]
    link.finish()


def call(kernel, ident, outs, scratch, args, hbm=(), hbm_out=(), sems=64, local=32):
    vm = pl.BlockSpec(memory_space=pltpu.VMEM)
    hb = pl.BlockSpec(memory_space=pltpu.HBM)
    return pl.pallas_call(
        kernel,
        out_shape=[jax.ShapeDtypeStruct(s, t) for s, t in outs],
        in_specs=[hb if i in hbm else vm for i in range(len(args))],
        out_specs=[hb if i in hbm_out else vm for i in range(len(outs))],
        scratch_shapes=scratch + [pltpu.SemaphoreType.DMA((sems,)), pltpu.SemaphoreType.DMA((sems,))]
        + ([pltpu.SemaphoreType.DMA((local,))] if hbm else []),
        compiler_params=pltpu.CompilerParams(
            collective_id=ident, has_side_effects=True, vmem_limit_bytes=LIMIT
        ),
    )(*args)


def to_order(v):
    lead = v.shape[:-1]
    n = len(lead)
    v = v.reshape(lead + (2, 2, 2, 2, 2, UNIT))
    return v.transpose(tuple(range(n)) + tuple(n + i for i in (0, 2, 4, 3, 1, 5))).reshape(lead + (D,))


def from_order(v):
    lead = v.shape[:-1]
    n = len(lead)
    v = v.reshape(lead + (2, 2, 2, 2, 2, UNIT))
    return v.transpose(tuple(range(n)) + tuple(n + i for i in (0, 4, 1, 3, 2, 5))).reshape(lead + (D,))


def local(
    tokens, conditioning, heights, widths, cotangent, w_mod, b_mod, w_qkv, b_qkv, query_gain, key_gain,
    w_proj, b_proj, w_gu, b_gu, w_down, b_down,
):
    args = (
        tokens, conditioning, heights, widths, cotangent, w_mod, b_mod, w_qkv, b_qkv, query_gain, key_gain,
        w_proj, b_proj, w_gu, b_gu, w_down, b_down,
    )
    sizes = tuple(lax.axis_size(a) for a in ("dp", "row", "col"))
    if sizes != (4, 4, 2) or tokens.shape != (4, 4, 16, D):
        return general(*args)
    every = ("dp", "row", "col")
    perm, spread, pick, tabs, row_of, col_of = constants()
    dp, z, y = (lax.axis_index(a) for a in every)
    x, c, zh, zl = dp // 2, dp % 2, z // 2, z % 2
    block = jnp.concatenate(
        [
            conditioning.astype(F32),
            jnp.pad(jnp.stack([heights, widths]).astype(F32), ((0, 0), (0, D - 4))),
            jnp.zeros((2, D), F32),
        ]
    )
    bias = jnp.concatenate([b_qkv, b_proj, b_gu, b_down]).astype(F32)
    bias = jnp.pad(bias, (0, 140)).reshape(2, 256)
    got, condg = call(
        kernel_front, 3,
        [((2, 2, 2, 4, 8, 256), F32), ((4, 8, D), F32)],
        [pltpu.VMEM((4, 8, 256), F32), pltpu.VMEM((4, 8, 256), F32), pltpu.VMEM((4, 4, 8, 256), F32)],
        (block, w_mod, b_mod.astype(F32).reshape(1, 216), bias),
        sems=16,
    )
    tall = condg[:, 4, :4].reshape(16)
    wide = condg[:, 5, :4].reshape(16)
    item = (2 * x + y) * 4 + z
    got = got.transpose(0, 1, 3, 2, 4, 5).reshape(32, 8, 256)
    modv = got[:, 0, :216]
    pack = got[:, 1:3].reshape(32, 512)
    modv = to_order(modv.reshape(6, D))
    modv = jnp.concatenate([modv, jnp.zeros((2, D), F32)])
    own = lambda v: lax.dynamic_index_in_dim(
        lax.dynamic_index_in_dim(v, c, 2, False), zl, 3, False
    )
    bq = own(pack[:, 0:108].reshape(3, 2, 2, 2, 2, 2, UNIT))
    bq = jnp.pad(bq, ((0, 0),) * 4 + ((0, 64 - UNIT),)).reshape(1, 1536)
    bp = to_order(pack[:, 108:144].reshape(1, D))
    bg = own(pack[:, 144:336].reshape(2, 2, 2, 2, 2, 2, 96)).reshape(1, 1536)
    bd = to_order(pack[:, 336:372].reshape(1, D))
    pair = (2 * x + y) * 4 + 2 * zh + jnp.arange(2)
    row_of, col_of = jnp.asarray(row_of), jnp.asarray(col_of)
    live = (row_of[None].astype(F32) < tall[pair][:, None]) & (col_of[None].astype(F32) < wide[pair][:, None])
    maskb = jnp.where(live, 0.0, MASKED).astype(F32).reshape(2, 1, 512)
    valid = lax.dynamic_slice(live[zl].astype(F32), (c * TOK,), (TOK,)).reshape(TOK, 1)
    gains = jnp.pad(
        jnp.stack([query_gain, key_gain]).reshape(2, 2, UNIT), ((0, 6), (0, 0), (0, 64 - UNIT))
    ).reshape(8, 128)
    wq = w_qkv.reshape(UNIT, 3, 2, 2, 2, 2, 72).transpose(5, 3, 0, 1, 2, 4, 6).reshape(4, UNIT, 864)
    wq = jnp.pad(wq, ((0, 0), (0, PAD - UNIT), (0, 0)))
    wg = w_gu.reshape(UNIT, 2, 2, 2, 2, 2, 192).transpose(5, 3, 0, 1, 2, 4, 6).reshape(4, UNIT, 1536)
    wg = jnp.pad(wg, ((0, 0), (0, PAD - UNIT), (0, 0)))
    wp = jnp.pad(w_proj, ((0, PAD - UNIT), (0, 0)))

    full = (GROUP, D)
    block = (TOK, D)
    weights = [(2, 2, 2, 144, 864), (2, 2, 2, 64, D), (2, 2, 2, 144, 1536), (2, 2, 2, 96, D)]
    pairs = [((8, 2, 512, 128), F32), ((8, 3, 512, 128), BF)]
    (
        wq_all, wp_all, wg_all, wd_all, ha, raw, rot, att, hm, dmlp, tokp, og, attn_out,
    ) = call(
        kernel_a, 0,
        [(w, BF) for w in weights] + [(full, BF)] + pairs + [((GROUP, 512), BF)]
        + [(block, BF)] * 4 + [(block, F32)],
        [pltpu.VMEM(w, BF) for w in weights] + [pltpu.VMEM(full, BF)] + [pltpu.VMEM(w, t) for w, t in pairs]
        + [
            pltpu.VMEM((GROUP, 512), BF), pltpu.VMEM((4, PAD, 864), BF), pltpu.VMEM((4, PAD, 1536), BF),
            pltpu.VMEM(block, BF), pltpu.VMEM(block, BF), pltpu.VMEM((D, 1536), BF), pltpu.VMEM((3, TOK, D), BF),
            pltpu.VMEM((3, TOK, D), BF), pltpu.VMEM(block, F32),
        ],
        (
            tokens.reshape(4, 64, D), cotangent.reshape(4, 64, D), wq, wg, wp, w_down, perm, spread, pick, tabs,
            gains, modv, bq, bp, maskb, valid,
        ),
        hbm=(0, 1, 2, 3),
        hbm_out=range(8),
    )
    spread = jnp.pad(spread, ((0, D - 864), (0, 0))).reshape(2, 2, 2, 144, 1536)
    dtok, bout, fq, fg, fp, fd, small, dbg, dbq, dgain = call(
        kernel_b, 1,
        [
            ((4, 64, D), BF), ((4, 64, D), BF), ((4, PAD, 896), BF), ((4, PAD, 1536), BF), ((PAD, D), F32),
            ((96, D), F32), ((8, D), F32), ((8, 1536), F32), ((8, 1536), F32), ((8, 128), F32),
        ],
        [
            pltpu.VMEM((2, 2, 2, 144, 1536), BF), pltpu.VMEM((2, 2, 2, 96, D), BF), pltpu.VMEM(full, BF),
            pltpu.VMEM(full, BF), pltpu.VMEM(block, BF), pltpu.VMEM(block, BF), pltpu.VMEM(block, F32),
            pltpu.VMEM((GROUP, 512), BF), pltpu.VMEM((2, 2, 2, 64, D), BF), pltpu.VMEM((2, 2, 2, 144, 864), BF),
            pltpu.VMEM((D, D), BF), pltpu.VMEM((3, 512, 128), F32), pltpu.VMEM((TOK, 1536), F32),
            pltpu.VMEM((GROUP, 1536), BF), pltpu.VMEM((GROUP, 768), BF), pltpu.VMEM((3, TOK, D), BF),
            pltpu.VMEM((3, TOK, D), BF), pltpu.VMEM((3, TOK, D), BF), pltpu.VMEM(block, F32), pltpu.VMEM(block, F32),
            pltpu.VMEM((2, 2, 2, 144, 1536), BF), pltpu.VMEM((2, 2, 2, 96, D), BF), pltpu.VMEM((2, 2, 2, PAD, D), BF),
            pltpu.VMEM(full, BF), pltpu.VMEM((2, 2, 512, 128), F32), pltpu.VMEM((2, 3, 512, 128), BF),
            pltpu.VMEM(block, BF), pltpu.VMEM(block, BF), pltpu.VMEM((4, PAD, 896), BF),
            pltpu.VMEM((4, PAD, 1536), BF),
        ]
        + Reduce.buffers(144, 1536, SPLIT_G) + Reduce.buffers(96, D, SPLIT_D)
        + Reduce.buffers(144, 896, SPLIT_Q) + Reduce.buffers(PAD, D, SPLIT_P),
        (
            wg_all, wd_all, hm, dmlp, tokp, og, attn_out, att, wp_all, wq_all, ha, raw, rot, perm, spread, tabs,
            modv, bg, bd, gains, maskb, valid, pick,
        ),
        hbm=range(16),
        hbm_out=range(4),
    )

    g_w_qkv = fq[:, :UNIT, :864].reshape(2, 2, UNIT, 3, 2, 2, 72).transpose(2, 3, 4, 1, 5, 0, 6)
    g_w_qkv = g_w_qkv.reshape(UNIT, 3456).astype(F32)
    g_w_gu = fg[:, :UNIT].reshape(2, 2, UNIT, 2, 2, 2, 192).transpose(2, 3, 4, 1, 5, 0, 6)
    g_w_gu = g_w_gu.reshape(UNIT, 6144).astype(F32)
    spread_own = lambda v: lax.dynamic_update_index_in_dim(
        jnp.zeros(v.shape[:2] + (2,) + v.shape[2:3] + (2,) + v.shape[3:], F32),
        lax.dynamic_update_index_in_dim(
            jnp.zeros(v.shape[:3] + (2,) + v.shape[3:], F32), v[:, :, :, None], zl, 3
        )[:, :, None],
        c,
        2,
    )
    db_qkv = spread_own(dbq[0].reshape(3, 2, 2, 2, 64)[..., :UNIT]).reshape(3456)
    db_gu = spread_own(dbg[0].reshape(2, 2, 2, 2, 96)).reshape(32, 192)
    vecs = from_order(jnp.stack([small[i] for i in (6, 7, 3, 1, 2, 0, 5, 4)]))
    dg = dgain[:2].reshape(2, 2, 64)[..., :UNIT].reshape(144)
    biases = jnp.concatenate(
        [
            db_qkv[: 2 * D].reshape(32, 72),
            db_qkv[2 * D :].reshape(32, 36),
            db_gu,
            vecs[6].reshape(32, UNIT),
            vecs[7].reshape(32, UNIT),
            jnp.zeros((32, 140), F32),
        ],
        1,
    ).reshape(32, 2, 256)
    pack = jnp.concatenate(
        [
            jnp.pad(vecs[:6].reshape(32, 1, 216), ((0, 0), (0, 0), (0, 40))),
            biases,
            jnp.broadcast_to(jnp.pad(dg, (0, 112)), (32, 1, 256)),
            jnp.zeros((32, 4, 256), F32),
        ],
        1,
    )
    pack = pack.reshape(2, 2, 4, 2, 8, 256).transpose(0, 1, 3, 2, 4, 5)
    cond_f = conditioning.astype(F32)
    sig = jax.nn.sigmoid(cond_f)
    slope = lax.dynamic_slice(sig * (1.0 + cond_f * (1.0 - sig)), (0, (z * 2 + y) * 144), (4, 144))
    slope = jnp.concatenate([slope, jnp.zeros((4, 144), F32)])
    g_w_mod, sums, g_b_mod, d_cond = call(
        kernel_back, 4,
        [((D, 216), F32), ((8, 256), F32), ((8, 216), F32), ((8, 144), F32)],
        [
            pltpu.VMEM((2, 2, 2, 4, 8, 256), F32), pltpu.VMEM((4, 8, 256), F32), pltpu.VMEM((4, 8, 256), F32),
            pltpu.VMEM((32, 216), F32), pltpu.VMEM((4, 2, 4, 8, 144), F32), pltpu.VMEM((2, 2, 2, 4, 8, 144), F32),
            pltpu.VMEM((4, 8, 144), F32), pltpu.VMEM((4, 8, 144), F32),
        ],
        (pack, condg, w_mod, slope),
        sems=24,
    )
    biases = sums[4:6].reshape(512)
    gains_out = sums[6, :144]
    return (
        bout.reshape(tokens.shape),
        dtok.reshape(tokens.shape).astype(F32),
        d_cond[:4],
        g_w_mod,
        g_b_mod[0],
        g_w_qkv,
        biases[:72],
        biases[72:108],
        gains_out[:72],
        gains_out[72:],
        fp[:UNIT],
        biases[300:336],
        g_w_gu,
        biases[108:300],
        fd,
        biases[336:372],
    )


def solution(mesh):
    in_specs = (
        P("dp", "row", "col", None),
        P("dp", None),
        P("dp"),
        P("dp"),
        P("dp", "row", "col", None),
        P(None, ("dp", "row", "col")),
        P(("dp", "row", "col")),
        P(("dp", "row", "col"), None),
        P(("dp", "row", "col")),
        P(),
        P(),
        P(("dp", "row", "col"), None),
        P(("dp", "row", "col")),
        P(("dp", "row", "col"), None),
        P(("dp", "row", "col")),
        P(("dp", "row", "col"), None),
        P(("dp", "row", "col")),
    )
    out_specs = (
        P("dp", "row", "col", None),
        P("dp", "row", "col", None),
        P("dp", ("row", "col")),
        P(None, ("dp", "row", "col")),
        P(("dp", "row", "col")),
        P(("dp", "row", "col"), None),
        P(("dp", "row", "col")),
        P(("dp", "row", "col")),
        P(),
        P(),
        P(("dp", "row", "col"), None),
        P(("dp", "row", "col")),
        P(("dp", "row", "col"), None),
        P(("dp", "row", "col")),
        P(("dp", "row", "col"), None),
        P(("dp", "row", "col")),
    )
    return jax.shard_map(local, mesh=mesh, in_specs=in_specs, out_specs=out_specs, check_vma=False)
```

```python
import math

import jax
import jax.numpy as jnp
import numpy as np
from jax import lax
from jax.experimental import pallas as pl
from jax.experimental.pallas import tpu as pltpu
from jax.sharding import PartitionSpec as P

HEADS = 16
HEAD = 72
FF = 3072


EPSILON = 1e-06
MASKED = -1000000000.0
PRECISE = lax.Precision.HIGHEST


def rope_tables(row_pos, col_pos, head_size):
    half_size = head_size // 2
    lane_index = jnp.arange(head_size)
    pair_index = (lane_index % half_size // 2).astype(jnp.float32)
    frequency = jnp.exp(-math.log(10000.0) * 2.0 * pair_index / half_size)
    places = jnp.where(lane_index[None, :] >= half_size, col_pos[:, None], row_pos[:, None]).astype(
        jnp.float32
    )
    angles = places * frequency[None, :]
    return (jnp.cos(angles), jnp.sin(angles))


def rotate(values):
    pair_view = values.reshape(values.shape[:-1] + (values.shape[-1] // 2, 2))
    turned = jnp.stack((-pair_view[..., 1], pair_view[..., 0]), axis=-1)
    return turned.reshape(values.shape)


def norm_parts(values):
    centered = values - jnp.mean(values, -1, keepdims=True)
    recip = lax.rsqrt(jnp.mean(centered * centered, -1, keepdims=True) + EPSILON)
    return (centered * recip, recip)


def norm_back(gradient, normed, recip):
    return recip * (
        gradient
        - jnp.mean(gradient, -1, keepdims=True)
        - normed * jnp.mean(gradient * normed, -1, keepdims=True)
    )


def head_back(gradient, raw_value, recip, gain_vec):
    scaled = gradient * gain_vec
    gain_grad = jnp.sum(gradient * raw_value * recip, axis=(0, 1, 2))
    raw_grad = recip * scaled - raw_value * (recip * recip * recip) * jnp.mean(
        scaled * raw_value, -1, keepdims=True
    )
    return (raw_grad, gain_grad)


def general(
    tokens,
    conditioning,
    heights,
    widths,
    cotangent,
    w_mod,
    b_mod,
    w_qkv,
    b_qkv,
    query_gain,
    key_gain,
    w_proj,
    b_proj,
    w_gu,
    b_gu,
    w_down,
    b_down,
):
    item_count, tile_rows, tile_cols, model_width = tokens.shape
    tile_span = tile_rows * tile_cols
    n_row = lax.axis_size("row")
    n_col = lax.axis_size("col")
    groups = n_row * n_col
    key_count = tile_span * groups
    inv_root = 1.0 / math.sqrt(HEAD)
    row_at = lax.axis_index("row")
    col_at = lax.axis_index("col")
    local_index = jnp.arange(tile_span)
    query_rows = row_at * tile_rows + local_index // tile_cols
    query_cols = col_at * tile_cols + local_index % tile_cols
    valid_query = (query_rows[None, :] < heights[:, None]) & (query_cols[None, :] < widths[:, None])
    key_index = jnp.arange(key_count)
    key_owner = key_index // tile_span
    key_spot = key_index % tile_span
    key_rows = key_owner // n_col * tile_rows + key_spot // tile_cols
    key_cols = key_owner % n_col * tile_cols + key_spot % tile_cols
    valid_key = (key_rows[None, :] < heights[:, None]) & (key_cols[None, :] < widths[:, None])
    cos_tab, sin_tab = rope_tables(query_rows, query_cols, HEAD)
    cos_four = cos_tab[None, :, None, :]
    sin_four = sin_tab[None, :, None, :]
    cond_f = conditioning.astype(jnp.float32)
    cond_sig = jax.nn.sigmoid(cond_f)
    act_low = (cond_f * cond_sig).astype(jnp.bfloat16)
    gathered = (
        lax.all_gather(w_mod, ("dp", "row", "col"), axis=1, tiled=True),
        lax.all_gather(b_mod, ("dp", "row", "col"), axis=0, tiled=True),
        lax.all_gather(w_qkv, ("dp", "row", "col"), axis=0, tiled=True),
        lax.all_gather(b_qkv, ("dp", "row", "col"), axis=0, tiled=True),
        lax.all_gather(w_proj, ("dp", "row", "col"), axis=0, tiled=True),
        lax.all_gather(b_proj, ("dp", "row", "col"), axis=0, tiled=True),
        lax.all_gather(w_gu, ("dp", "row", "col"), axis=0, tiled=True),
        lax.all_gather(b_gu, ("dp", "row", "col"), axis=0, tiled=True),
        lax.all_gather(w_down, ("dp", "row", "col"), axis=0, tiled=True),
        lax.all_gather(b_down, ("dp", "row", "col"), axis=0, tiled=True),
    )
    (
        w_mod_all,
        b_mod_all,
        w_qkv_all,
        b_qkv_all,
        w_proj_all,
        b_proj_all,
        w_gu_all,
        b_gu_all,
        w_down_all,
        b_down_all,
    ) = gathered
    modul = jnp.dot(act_low, w_mod_all, preferred_element_type=jnp.float32) + b_mod_all.astype(
        jnp.float32
    )
    shift_a, scale_a, gate_a, shift_m, scale_m, gate_m = [
        modul[:, piece * model_width : (piece + 1) * model_width][:, None, :] for piece in range(6)
    ]
    resid_in = tokens.reshape(item_count, tile_span, model_width).astype(jnp.float32)
    normed_a, recip_a = norm_parts(resid_in)
    h_attn = (normed_a * (1.0 + scale_a) + shift_a).astype(jnp.bfloat16)
    qkv_all = jnp.dot(h_attn, w_qkv_all, preferred_element_type=jnp.float32) + b_qkv_all.astype(
        jnp.float32
    )
    query_raw = qkv_all[..., :model_width].reshape(item_count, tile_span, HEADS, HEAD)
    key_raw = qkv_all[..., model_width : 2 * model_width].reshape(
        item_count, tile_span, HEADS, HEAD
    )
    value_raw = qkv_all[..., 2 * model_width :]
    query_recip = lax.rsqrt(jnp.mean(query_raw * query_raw, -1, keepdims=True) + EPSILON)
    key_recip = lax.rsqrt(jnp.mean(key_raw * key_raw, -1, keepdims=True) + EPSILON)
    query_normed = query_raw * query_recip * query_gain
    key_normed = key_raw * key_recip * key_gain
    query_rot = (query_normed * cos_four + rotate(query_normed) * sin_four).astype(jnp.bfloat16)
    key_rot = (key_normed * cos_four + rotate(key_normed) * sin_four).astype(jnp.bfloat16)
    value_low = value_raw.astype(jnp.bfloat16)
    kv_local = jnp.concatenate([key_rot.reshape(item_count, tile_span, model_width), value_low], -1)
    kv_every = lax.all_gather(kv_local, ("row", "col"), axis=1, tiled=True)
    query_heads = query_rot.transpose(2, 0, 1, 3)
    key_part = (
        kv_every[..., :model_width]
        .reshape(item_count, key_count, HEADS, HEAD)
        .transpose(2, 0, 1, 3)
    )
    value_part = (
        kv_every[..., model_width:]
        .reshape(item_count, key_count, HEADS, HEAD)
        .transpose(2, 0, 1, 3)
    )
    key_mask = valid_key[:, None, :]

    def attend(head_block):
        query_h, key_h, value_h = head_block
        scores = (
            jnp.einsum("itd,ikd->itk", query_h, key_h, preferred_element_type=jnp.float32)
            * inv_root
        )
        scores = jnp.where(key_mask, scores, MASKED)
        row_max = jnp.max(scores, -1, keepdims=True)
        exponent = jnp.exp(scores - row_max)
        row_sum = jnp.sum(exponent, -1, keepdims=True)
        probs = (exponent / row_sum).astype(jnp.bfloat16)
        result = jnp.einsum("itk,ikd->itd", probs, value_h, preferred_element_type=jnp.float32)
        return (result, row_max, row_sum)

    attended_heads, max_kept, sum_kept = lax.map(attend, (query_heads, key_part, value_part))
    attended = (
        attended_heads.transpose(1, 2, 0, 3)
        .reshape(item_count, tile_span, model_width)
        .astype(jnp.bfloat16)
    )
    attn_out = jnp.dot(
        attended, w_proj_all, preferred_element_type=jnp.float32
    ) + b_proj_all.astype(jnp.float32)
    resid_mid = resid_in + gate_a * attn_out
    normed_m, recip_m = norm_parts(resid_mid)
    h_mlp = (normed_m * (1.0 + scale_m) + shift_m).astype(jnp.bfloat16)
    gate_up = jnp.dot(h_mlp, w_gu_all, preferred_element_type=jnp.float32) + b_gu_all.astype(
        jnp.float32
    )
    gate_part = gate_up[..., :FF]
    up_part = gate_up[..., FF:]
    gate_sig = jax.nn.sigmoid(gate_part)
    gate_act = gate_part * gate_sig
    hidden = (gate_act * up_part).astype(jnp.bfloat16)
    mlp_out = jnp.dot(hidden, w_down_all, preferred_element_type=jnp.float32) + b_down_all.astype(
        jnp.float32
    )
    mask_f = valid_query[..., None].astype(jnp.float32)
    block_out = ((resid_mid + gate_m * mlp_out) * mask_f).astype(jnp.bfloat16)
    out_grad = cotangent.reshape(item_count, tile_span, model_width).astype(jnp.float32) * mask_f
    d_mlp = (gate_m * out_grad).astype(jnp.bfloat16)
    d_gate_m = jnp.sum(out_grad * mlp_out, 1)
    dw_down = jnp.einsum("itf,itd->fd", hidden, d_mlp, preferred_element_type=jnp.float32)
    db_down = jnp.sum(d_mlp.astype(jnp.float32), (0, 1))
    d_hidden = jnp.einsum("itd,fd->itf", d_mlp, w_down_all, preferred_element_type=jnp.float32)
    d_gate = d_hidden * up_part * gate_sig * (1.0 + gate_part * (1.0 - gate_sig))
    d_up = d_hidden * gate_act
    d_gate_up = jnp.concatenate([d_gate, d_up], -1).astype(jnp.bfloat16)
    dw_gu = jnp.einsum("itd,ite->de", h_mlp, d_gate_up, preferred_element_type=jnp.float32)
    db_gu = jnp.sum(d_gate_up.astype(jnp.float32), (0, 1))
    d_hmlp = jnp.einsum("ite,de->itd", d_gate_up, w_gu_all, preferred_element_type=jnp.float32)
    d_shift_m = jnp.sum(d_hmlp, 1)
    d_scale_m = jnp.sum(d_hmlp * normed_m, 1)
    d_mid = out_grad + norm_back(d_hmlp * (1.0 + scale_m), normed_m, recip_m)
    d_attn = (gate_a * d_mid).astype(jnp.bfloat16)
    d_gate_a = jnp.sum(d_mid * attn_out, 1)
    dw_proj = jnp.einsum("itd,ite->de", attended, d_attn, preferred_element_type=jnp.float32)
    db_proj = jnp.sum(d_attn.astype(jnp.float32), (0, 1))
    d_attended = jnp.einsum(
        "ite,de->itd", d_attn, w_proj_all, preferred_element_type=jnp.float32
    ).astype(jnp.bfloat16)
    d_att_heads = d_attended.reshape(item_count, tile_span, HEADS, HEAD).transpose(2, 0, 1, 3)
    key_back, value_back = (key_part, value_part)

    def attend_back(head_block):
        query_h, key_h, value_h, grad_h, max_h, sum_h = head_block
        scores = (
            jnp.einsum("itd,ikd->itk", query_h, key_h, preferred_element_type=jnp.float32)
            * inv_root
        )
        scores = jnp.where(key_mask, scores, MASKED)
        probs = jnp.exp(scores - max_h) / sum_h
        d_probs = jnp.einsum("itd,ikd->itk", grad_h, value_h, preferred_element_type=jnp.float32)
        delta = jnp.sum(probs * d_probs, -1, keepdims=True)
        d_scores = (probs * (d_probs - delta)).astype(jnp.bfloat16)
        d_query = (
            jnp.einsum("itk,ikd->itd", d_scores, key_h, preferred_element_type=jnp.float32)
            * inv_root
        )
        d_key = (
            jnp.einsum("itk,itd->ikd", d_scores, query_h, preferred_element_type=jnp.float32)
            * inv_root
        )
        d_value = jnp.einsum(
            "itk,itd->ikd", probs.astype(jnp.bfloat16), grad_h, preferred_element_type=jnp.float32
        )
        return (d_query, d_key, d_value)

    dq_heads, dk_heads, dv_heads = lax.map(
        attend_back, (query_heads, key_back, value_back, d_att_heads, max_kept, sum_kept)
    )
    dkv_term = jnp.concatenate(
        [
            dk_heads.transpose(1, 2, 0, 3).reshape(item_count, key_count, model_width),
            dv_heads.transpose(1, 2, 0, 3).reshape(item_count, key_count, model_width),
        ],
        -1,
    )
    dkv_own = lax.psum_scatter(dkv_term, ("row", "col"), scatter_dimension=1, tiled=True)
    d_key_rot = dkv_own[..., :model_width].reshape(item_count, tile_span, HEADS, HEAD)
    d_value = dkv_own[..., model_width:]
    d_query_rot = dq_heads.transpose(1, 2, 0, 3)
    d_query_n = d_query_rot * cos_four - rotate(d_query_rot * sin_four)
    d_key_n = d_key_rot * cos_four - rotate(d_key_rot * sin_four)
    d_query_raw, dq_gain = head_back(d_query_n, query_raw, query_recip, query_gain)
    d_key_raw, dk_gain = head_back(d_key_n, key_raw, key_recip, key_gain)
    gain_total = lax.psum((dq_gain, dk_gain), ("dp", "row", "col"))
    d_qkv = jnp.concatenate(
        [
            d_query_raw.reshape(item_count, tile_span, model_width),
            d_key_raw.reshape(item_count, tile_span, model_width),
            d_value,
        ],
        -1,
    ).astype(jnp.bfloat16)
    dw_qkv = jnp.einsum("itd,ite->de", h_attn, d_qkv, preferred_element_type=jnp.float32)
    db_qkv = jnp.sum(d_qkv.astype(jnp.float32), (0, 1))
    db_query_key = db_qkv[: 2 * model_width]
    db_value = db_qkv[2 * model_width :]
    d_hattn = jnp.einsum("ite,de->itd", d_qkv, w_qkv_all, preferred_element_type=jnp.float32)
    d_shift_a = jnp.sum(d_hattn, 1)
    d_scale_a = jnp.sum(d_hattn * normed_a, 1)
    d_tokens = d_mid + norm_back(d_hattn * (1.0 + scale_a), normed_a, recip_a)
    d_modul = jnp.concatenate([d_shift_a, d_scale_a, d_gate_a, d_shift_m, d_scale_m, d_gate_m], -1)
    act_f = act_low.astype(jnp.float32)
    dw_mod = jnp.einsum("id,ie->de", act_f, d_modul, precision=PRECISE)
    db_mod = jnp.sum(d_modul, 0)
    d_act = jnp.einsum("ie,de->id", d_modul, w_mod_all.astype(jnp.float32), precision=PRECISE)
    d_cond_part = d_act * cond_sig * (1.0 + cond_f * (1.0 - cond_sig))
    d_cond = lax.psum_scatter(d_cond_part, ("row", "col"), scatter_dimension=1, tiled=True)
    summed = (
        lax.psum_scatter(dw_mod, ("dp", "row", "col"), scatter_dimension=1, tiled=True),
        lax.psum_scatter(db_mod, ("dp", "row", "col"), scatter_dimension=0, tiled=True),
        lax.psum_scatter(dw_qkv, ("dp", "row", "col"), scatter_dimension=0, tiled=True),
        lax.psum_scatter(db_query_key, ("dp", "row", "col"), scatter_dimension=0, tiled=True),
        lax.psum_scatter(db_value, ("dp", "row", "col"), scatter_dimension=0, tiled=True),
        lax.psum_scatter(dw_proj, ("dp", "row", "col"), scatter_dimension=0, tiled=True),
        lax.psum_scatter(db_proj, ("dp", "row", "col"), scatter_dimension=0, tiled=True),
        lax.psum_scatter(dw_gu, ("dp", "row", "col"), scatter_dimension=0, tiled=True),
        lax.psum_scatter(db_gu, ("dp", "row", "col"), scatter_dimension=0, tiled=True),
        lax.psum_scatter(dw_down, ("dp", "row", "col"), scatter_dimension=0, tiled=True),
        lax.psum_scatter(db_down, ("dp", "row", "col"), scatter_dimension=0, tiled=True),
    )
    (
        g_w_mod,
        g_b_mod,
        g_w_qkv,
        g_b_query_key,
        g_b_value,
        g_w_proj,
        g_b_proj,
        g_w_gu,
        g_b_gu,
        g_w_down,
        g_b_down,
    ) = summed
    return (
        block_out.reshape(item_count, tile_rows, tile_cols, model_width),
        d_tokens.reshape(item_count, tile_rows, tile_cols, model_width),
        d_cond,
        g_w_mod,
        g_b_mod,
        g_w_qkv,
        g_b_query_key,
        g_b_value,
        gain_total[0],
        gain_total[1],
        g_w_proj,
        g_b_proj,
        g_w_gu,
        g_b_gu,
        g_w_down,
        g_b_down,
    )


MESH = pl.DeviceIdType.MESH
BF = jnp.bfloat16
F32 = jnp.float32
LIMIT = 60 * 1024 * 1024
D = 1152
UNIT = 36
PAD = 48
TOK = 256
GROUP = 1024
SPLIT_Q, SPLIT_P, SPLIT_G, SPLIT_D = 384, 640, 768, 640
ROOT = 1.0 / math.sqrt(HEAD)


def nn(a, b):
    return lax.dot_general(a, b, (((1,), (0,)), ((), ())), preferred_element_type=F32)


def nt(a, b):
    return lax.dot_general(a, b, (((1,), (1,)), ((), ())), preferred_element_type=F32)


def tn(a, b):
    return lax.dot_general(a, b, (((0,), (0,)), ((), ())), preferred_element_type=F32)


def width_order():
    xx, zh, yy, zl, cc, jj = np.indices((2, 2, 2, 2, 2, UNIT)).reshape(6, -1)
    return ((((xx * 2 + cc) * 2 + zh) * 2 + zl) * 2 + yy) * UNIT + jj


def constants():
    perm = np.zeros((D, D), np.float32)
    perm[width_order(), np.arange(D)] = 1.0
    spread = np.zeros((864, 1536), np.float32)
    tt, hh, yy, jj = np.indices((3, 4, 2, UNIT)).reshape(4, -1)
    spread[tt * 288 + hh * 72 + yy * 36 + jj, tt * 512 + hh * 128 + yy * 64 + jj] = 1.0
    pick = np.zeros((144, 192), np.float32)
    kk, jj = np.indices((4, UNIT)).reshape(2, -1)
    pick[kk * 36 + jj, kk * 48 + jj] = 1.0
    spot = np.arange(512)
    row = spot // 128 * 4 + spot // 16 % 4
    col = spot // 64 % 2 * 16 + spot % 16
    lane = np.arange(128)
    part = lane % 64
    freq = np.exp(-math.log(10000.0) * 2.0 * (part // 2) / 36.0)
    place = np.where(lane[None, :] >= 64, col[:, None], row[:, None]).astype(np.float64)
    angle = place * freq[None, :]
    live = part < UNIT
    cos = np.where(live, np.cos(angle), 0.0)
    sin = np.where(live, np.sin(angle), 0.0)
    even = lane % 2 == 0
    tabs = np.stack([cos, np.where(even, -sin, 0.0), np.where(even, 0.0, sin)]).astype(np.float32)
    return (
        jnp.asarray(perm, BF),
        jnp.asarray(spread, BF),
        jnp.asarray(pick, BF),
        jnp.asarray(tabs, F32),
    )


class Place:
    def __init__(self):
        dp = lax.axis_index("dp")
        self.z = lax.axis_index("row")
        self.y = lax.axis_index("col")
        self.x = dp // 2
        self.c = dp % 2
        self.zh = self.z // 2
        self.zl = self.z % 2
        self.m = self.zl * 2 + self.c
        self.dp = dp

    def mate(self, r):
        c = 1 - self.c if r % 2 else self.c
        zl = 1 - self.zl if r // 2 else self.zl
        return zl * 2 + c, (self.x * 2 + c, self.zh * 2 + zl, self.y)

    def xpeer(self):
        return ((1 - self.x) * 2 + self.c, self.z, self.y)

    def ypeer(self):
        return (self.dp, self.z, 1 - self.y)

    def zpeer(self):
        return (self.dp, (1 - self.zh) * 2 + self.zl, self.y)

    def item_home(self, j):
        return (self.x * 2 + self.zh, j, self.c)

    def item_source(self, blk):
        return (self.x * 2 + self.y, self.c * 2 + blk // 2, blk % 2)

    def is_me(self, dev):
        return (dev[0] == self.dp) & (dev[1] == self.z) & (dev[2] == self.y)


class Link:
    def __init__(self, here, ssem, rsem):
        self.here, self.ssem, self.rsem, self.n, self.open = here, ssem, rsem, 0, []

    def greet(self, items):
        here = self.here
        bar = pltpu.get_barrier_semaphore()
        devs = [here.mate(r)[1] for r in (1, 2, 3)]
        devs += [here.xpeer(), here.ypeer(), here.zpeer()]
        devs += [near(here, r)[3] for r in range(1, 8)] + [along_z(here, r)[1] for r in (1, 2, 3)]
        for d in devs:
            pl.semaphore_signal(bar, inc=1, device_id=d, device_id_type=MESH)
        total = len(devs)
        if items:
            for d in [here.item_home(j) for j in range(4)] + [here.item_source(j) for j in range(4)]:


                @pl.when(jnp.logical_not(here.is_me(d)))
                def _():
                    pl.semaphore_signal(bar, inc=1, device_id=d, device_id_type=MESH)

            far = (here.zh - here.c) * (here.zh - here.c)
            off = (here.y - here.c) * (here.y - here.c)
            total += 8 - 2 * (1 - far) * (1 - off)
        pl.semaphore_wait(bar, total)

    def send(self, src, dst, dev):
        k = self.n
        self.n += 1
        copy = pltpu.make_async_remote_copy(
            src_ref=src,
            dst_ref=dst,
            send_sem=self.ssem.at[k],
            recv_sem=self.rsem.at[k],
            device_id=dev,
            device_id_type=MESH,
        )
        copy.start()
        self.open.append(copy)
        return copy

    def scatter(self, src_of, dst, dev_of, slot):
        base = self.n
        self.n += 4
        here = self.here
        copies = []
        for j in range(4):
            dev = dev_of(j)
            mine = here.is_me(dev)
            remote = pltpu.make_async_remote_copy(
                src_ref=src_of(j),
                dst_ref=dst,
                send_sem=self.ssem.at[base + j],
                recv_sem=self.rsem.at[base + slot],
                device_id=dev,
                device_id_type=MESH,
            )
            local_copy = pltpu.make_async_copy(src_of(j), dst, self.rsem.at[base + slot])

            @pl.when(mine)
            def _():
                local_copy.start()

            @pl.when(jnp.logical_not(mine))
            def _():
                remote.start()

            copies.append((mine, remote))

        def wait_send():
            for mine, remote in copies:

                @pl.when(jnp.logical_not(mine))
                def _():
                    remote.wait_send()

        def wait_recv(src, dst_of):
            for j in range(4):
                pltpu.make_async_copy(src, dst_of(j), self.rsem.at[base + j]).wait()

        return wait_send, wait_recv

    def settle(self, *copies):
        for copy in copies:
            copy.wait_send()
            self.open = [c for c in self.open if c is not copy]

    def finish(self):
        for copy in self.open:
            copy.wait_send()
        self.open = []


def norm_rows(x):
    mean = jnp.sum(x, -1, keepdims=True) * (1.0 / D)
    cent = x - mean
    var = jnp.sum(cent * cent, -1, keepdims=True) * (1.0 / D)
    recip = lax.rsqrt(var + EPSILON)
    return cent * recip, recip


def norm_rows_back(g, y, recip):
    mg = jnp.sum(g, -1, keepdims=True) * (1.0 / D)
    mgy = jnp.sum(g * y, -1, keepdims=True) * (1.0 / D)
    return recip * (g - mg - y * mgy)


def at(i, n):
    return pl.ds(pl.multiple_of(i * n, n), n)


class Gather:
    def __init__(self, link, ref, rows, split):
        self.link, self.ref, self.rows, self.split = link, ref, rows, split

    def cut(self, i, j, k, cols):
        return self.ref.at[i, j, k, pl.ds(0, self.rows), cols]

    def hop1(self):
        h = self.link.here
        part = self.cut(h.x, h.zh, h.y, slice(None))
        self.a = self.link.send(part, part, h.zpeer())

    def hop2(self):
        h = self.link.here
        self.a.wait_recv()
        pa = self.cut(h.x, slice(None), h.y, pl.ds(0, self.split))
        pb = self.cut(h.x, slice(None), h.y, pl.ds(self.split, self.ref.shape[-1] - self.split))
        self.a = self.link.send(pa, pa, h.xpeer())
        self.b = self.link.send(pb, pb, h.ypeer())

    def hop3(self):
        h = self.link.here
        self.a.wait_recv()
        self.b.wait_recv()
        pa = self.cut(slice(None), slice(None), h.y, pl.ds(0, self.split))
        pb = self.cut(
            h.x, slice(None), slice(None), pl.ds(self.split, self.ref.shape[-1] - self.split)
        )
        self.a = self.link.send(pa, pa, h.ypeer())
        self.b = self.link.send(pb, pb, h.xpeer())

    def done(self):
        self.a.wait_recv()
        self.b.wait_recv()


class Reduce:
    def __init__(self, link, ref, bufs, split, cols):
        self.link, self.ref, self.split, self.cols = link, ref, split, cols
        self.r1a, self.r1b, self.r2a, self.r2b, self.r3a, self.r3b = bufs

    @staticmethod
    def buffers(rows, cols, split):
        rest = cols - split
        return [
            pltpu.VMEM((2, 2, rows, split), BF),
            pltpu.VMEM((2, 2, rows, rest), BF),
            pltpu.VMEM((2, rows, split), BF),
            pltpu.VMEM((2, rows, rest), BF),
            pltpu.VMEM((rows, split), BF),
            pltpu.VMEM((rows, rest), BF),
        ]

    def hop1(self):
        h = self.link.here
        ca, cb = pl.ds(0, self.split), pl.ds(self.split, self.cols - self.split)
        self.a = self.link.send(self.ref.at[1 - h.x, :, :, :, ca], self.r1a, h.xpeer())
        self.b = self.link.send(self.ref.at[:, :, 1 - h.y, :, cb], self.r1b, h.ypeer())

    def hop2(self):
        h = self.link.here
        ca, cb = pl.ds(0, self.split), pl.ds(self.split, self.cols - self.split)
        self.a.wait_recv()
        self.b.wait_recv()

        def add(i, carry):
            u, v = i // 2, i % 2
            own = self.ref[h.x, u, v, :, ca].astype(F32)
            self.r1a[u, v] = (self.r1a[u, v].astype(F32) + own).astype(BF)
            own = self.ref[u, v, h.y, :, cb].astype(F32)
            self.r1b[u, v] = (self.r1b[u, v].astype(F32) + own).astype(BF)
            return carry

        lax.fori_loop(0, 4, add, 0)
        self.a = self.link.send(self.r1a.at[:, 1 - h.y], self.r2a, h.ypeer())
        self.b = self.link.send(self.r1b.at[1 - h.x], self.r2b, h.xpeer())

    def hop3(self):
        h = self.link.here
        self.a.wait_recv()
        self.b.wait_recv()

        def add(u, carry):
            own = self.r1a[u, h.y].astype(F32)
            self.r2a[u] = (self.r2a[u].astype(F32) + own).astype(BF)
            own = self.r1b[h.x, u].astype(F32)
            self.r2b[u] = (self.r2b[u].astype(F32) + own).astype(BF)
            return carry

        lax.fori_loop(0, 2, add, 0)
        self.a = self.link.send(self.r2a.at[1 - h.zh], self.r3a, h.zpeer())
        self.b = self.link.send(self.r2b.at[1 - h.zh], self.r3b, h.zpeer())

    def done(self):
        h = self.link.here
        self.a.wait_recv()
        self.b.wait_recv()
        left = self.r2a[h.zh].astype(F32) + self.r3a[...].astype(F32)
        right = self.r2b[h.zh].astype(F32) + self.r3b[...].astype(F32)
        return left.astype(BF), right.astype(BF)


class RowGather:
    def __init__(self, link, ref):
        self.link, self.ref = link, ref
        here = link.here
        own = ref.at[at(here.m, TOK)]
        self.far = link.send(own, own, here.mate(2)[1])
        self.near = link.send(own, own, here.mate(1)[1])

    def near_done(self):
        self.near.wait_recv()

    def pass_on(self):
        here = self.link.here
        self.far.wait_recv()
        rows = self.ref.at[at(here.mate(2)[0], TOK)]
        self.last = self.link.send(rows, rows, here.mate(1)[1])

    def last_done(self):
        self.last.wait_recv()


class RowReduce:
    def __init__(self, link, out, into):
        self.link, self.out, self.into = link, out, into

    def give(self, r, val):
        i = 0 if r == 3 else 1
        if val is not None:
            self.out[i] = val.astype(BF)
        sent = self.link.send(self.out.at[i], self.into.at[i], self.link.here.mate(1)[1])
        if r == 3:
            self.s3 = sent
        else:
            self.s1 = sent

    def keep_far(self, val):
        self.out[2] = val.astype(BF)

    def pass_on(self):
        self.s3.wait_recv()

        def add(i, carry):
            rows = at(i, 32)
            both = self.out[2, rows, :].astype(F32) + self.into[0, rows, :].astype(F32)
            self.out[2, rows, :] = both.astype(BF)
            return carry

        lax.fori_loop(0, 8, add, 0)
        self.s2 = self.link.send(self.out.at[2], self.into.at[2], self.link.here.mate(2)[1])

    def arrive(self):
        self.s1.wait_recv()
        self.s2.wait_recv()

    def total(self, rows):
        return self.into[1, rows, :].astype(F32) + self.into[2, rows, :].astype(F32)


def turn(v, cos, sina, sinb):
    return v * cos + pltpu.roll(v, 127, 1) * sina + pltpu.roll(v, 1, 1) * sinb


def turn_back(d, cos, sina, sinb):
    return d * cos - pltpu.roll(d, 127, 1) * sina - pltpu.roll(d, 1, 1) * sinb


def near(here, r):
    x = 1 - here.x if r // 4 else here.x
    c = 1 - here.c if r // 2 % 2 else here.c
    y = 1 - here.y if r % 2 else here.y
    return x, c, y, (x * 2 + c, here.z, y)


def along_z(here, r):
    z = (here.z + r) % 4
    return z, (here.dp, z, here.y)


def shard_parts(s):
    x, c, zh, zl, y = s // 16, s // 8 % 2, s // 4 % 2, s // 2 % 2, s % 2
    member, spot = zl * 2 + c, (x * 2 + zh) * 2 + y
    return spot * 4 + member, member, spot


def three(v):
    hi = v.astype(BF)
    rest = v - hi.astype(F32)
    mid = rest.astype(BF)
    return jnp.concatenate([hi, mid, (rest - mid.astype(F32)).astype(BF)], 0)


def by_member(src, out, tmp, width, pieces):
    cols = pieces * 4 * width
    for t in range(pieces):
        for h in range(16):
            unit = shard_parts(h * 2)
            dst = t * 4 * width + unit[2] // 2 * width
            tmp[unit[1], 0:UNIT, dst : dst + width] = src[
                :, (t * 16 + h) * width : (t * 16 + h + 1) * width
            ].astype(F32)
    for m in range(4):
        out[m] = tmp[m, :, 0:cols].astype(BF)


def by_column(src, out, width, pieces):
    for t in range(pieces):
        for h in range(16):
            unit = shard_parts(h * 2)
            at_ = t * 4 * width + unit[2] // 2 * width
            out[:, (t * 16 + h) * width : (t * 16 + h + 1) * width] = src[
                unit[1], 0:UNIT, at_ : at_ + width
            ].astype(F32)


def silu_slope(v):
    sig = jax.nn.sigmoid(v)
    return sig * (1.0 + v * (1.0 - sig))


def kernel_a(
    tok_in, cot_in, wqkv, wgu, wp_in, wd_in, cond, w_mod_t, vecs, perm, spread, pick, tabs,
    wq_out, wp_out, wg_out, wd_out, ha_out, raw_out, rot_out, att_out, hm, dmlp, tokp, og, attn_out,
    condg, modv, bg, bd, gains, maskb, valid,
    wq, wp, wg, wd, ha, raw, rot, att, s0q, s0g, tokr, cotr, wqe, psend, precv, pown,
    wqs, wgs, tmp, block, msg, p1, m2, got, bq4, bg4, bp, ssem, rsem, lsem,
):
    here = Place()
    link = Link(here, ssem, rsem)
    fetch = Fetch(lsem)
    m = here.m
    block[...] = jnp.zeros_like(block)
    block[0:4, :] = cond[...].astype(F32)
    block[4:5, 0:8] = vecs[5:6, 0:8]
    condg[here.dp] = block[...]
    link.greet(True)
    slot = here.zl * 2 + here.y
    rows_in = at(slot, 64)
    cs = [link.send(block, condg.at[here.dp], near(here, r)[3]) for r in (2, 4, 6)]
    tmp[...] = jnp.zeros_like(tmp)
    by_member(wqkv, wqs, tmp, 72, 3)
    sq, sg = {}, {}
    for r in (2, 3, 1):
        k, dev = here.mate(r)
        sq[r] = link.send(wqs.at[k], s0q.at[m], dev)
    own_q = fetch.go(wqs.at[m], s0q.at[m])
    tok_sent, tok_got = link.scatter(lambda j: tok_in.at[j], tokr.at[rows_in], here.item_home, slot)

    for c in cs:
        c.wait_recv()
    v = condg[...].reshape(32, D)
    part = nt((v * jax.nn.sigmoid(v)).astype(BF), w_mod_t[...]) + vecs[0:1, 0:216]
    for z in range(4):
        msg[z, 4:6, :] = vecs[1:3, :]
        for d in range(4):
            msg[z, d : d + 1, 0:216] = part[d * 8 + z : d * 8 + z + 1, :]
    zs = []
    for r in (1, 2, 3):
        z, dev = along_z(here, r)
        zs.append(link.send(msg.at[z], p1.at[here.z], dev))
    p1[here.z] = msg[here.z]

    gq = Gather(link, wq, 144, SPLIT_Q)
    gp = Gather(link, wp, PAD, SPLIT_P)
    gg = Gather(link, wg, 144, SPLIT_G)
    gd = Gather(link, wd, 96, SPLIT_D)

    own_q.wait()
    for r in (1, 2, 3):
        sq[r].wait_recv()
    wq[here.x, here.zh, here.y] = nn(pick[...], s0q[...].reshape(192, 864)).astype(BF)
    gq.hop1()
    for c in zs:
        c.wait_recv()
    for z in range(4):
        for d in range(4):
            m2[d, z, 0:1, :] = p1[z, d : d + 1, :]
            m2[d, z, 1:3, :] = p1[z, 4:6, :]
    ns = []
    for r in range(1, 8):
        x, _, y, dev = near(here, r)
        ns.append(link.send(m2.at[x * 2 + y], got.at[here.x, here.c, here.y], dev))
    got[here.x, here.c, here.y] = m2[here.x * 2 + here.y]
    wp[:, :, :, PAD:64, :] = jnp.zeros((2, 2, 2, 64 - PAD, D), BF)
    tmp[0, 0:UNIT, 0:D] = nn(wp_in[...], perm[...])
    tmp[0, UNIT:PAD, :] = jnp.zeros((PAD - UNIT, 1536), F32)
    wp[here.x, here.zh, here.y, 0:PAD, :] = tmp[0, :, 0:D].astype(BF)
    gp.hop1()
    by_member(wgu, wgs, tmp, 192, 2)
    for r in (2, 3, 1):
        k, dev = here.mate(r)
        sg[r] = link.send(wgs.at[k], s0g.at[m], dev)
    own_g = fetch.go(wgs.at[m], s0g.at[m])
    ext = condg[here.x * 2 + here.y, 4:5, :]
    lane = lax.broadcasted_iota(jnp.int32, (1, D), 1)
    spot = lax.broadcasted_iota(jnp.int32, (1, 512), 1)
    row_at = spot // 128 * 4 + spot // 16 % 4
    col_at = spot // 64 % 2 * 16 + spot % 16

    def extent(item, first):
        return jnp.sum(jnp.where(lane == item + first, ext, 0.0), -1, keepdims=True)

    for i in range(2):
        tall, wide = extent(here.zh * 2 + i, 0), extent(here.zh * 2 + i, 4)
        live = (row_at.astype(F32) < tall) & (col_at.astype(F32) < wide)
        maskb[i] = jnp.where(live, 0.0, MASKED)
    spot = lax.broadcasted_iota(jnp.int32, (TOK, 1), 0) + here.c * TOK
    row_at = (spot // 128 * 4 + spot // 16 % 4).astype(F32)
    col_at = (spot // 64 % 2 * 16 + spot % 16).astype(F32)
    live = (row_at < extent(here.z, 0)) & (col_at < extent(here.z, 4))
    valid[...] = jnp.where(live, 1.0, 0.0)
    gains[...] = jnp.zeros_like(gains)
    for t in range(2):
        for e in range(2):
            gains[t : t + 1, e * 64 : e * 64 + UNIT] = vecs[3 + t : 4 + t, e * UNIT : e * UNIT + UNIT]
    for c in ns:
        c.wait_recv()
    modv[...] = jnp.zeros_like(modv)
    bq4[...] = jnp.zeros_like(bq4)
    for s in range(32):
        line = got[s // 16, s // 8 % 2, s % 2, s // 2 % 4]
        for q in range(6):
            piece, unit = divmod(6 * s + q, 32)
            to = shard_parts(unit)[0] * UNIT
            modv[piece : piece + 1, to : to + UNIT] = line[0:1, q * UNIT : q * UNIT + UNIT]
        for q in range(3):
            piece, unit = divmod(3 * s + q, 32)
            _, member, spot = shard_parts(unit)
            to = piece * 512 + spot * 64
            bq4[member, :, to : to + UNIT] = line[1:2, q * UNIT : q * UNIT + UNIT]
        to = shard_parts(s)[0] * UNIT
        bp[:, to : to + UNIT] = line[1:2, 108:144]
        bd[:, to : to + UNIT] = line[1:2, 144:180]
        for q in range(2):
            piece, unit = divmod(2 * s + q, 32)
            _, member, spot = shard_parts(unit)
            to = piece * 768 + spot * 96
            bg4[member, :, to : to + 96] = line[2:3, q * 96 : q * 96 + 96]
    bg[...] = bg4[m]
    wd[here.x, here.zh, here.y] = nn(wd_in[...], perm[...]).astype(BF)
    tok_got(tok_in.at[0], lambda j: tokr.at[pl.ds(j * 64, 64)])
    tokp[...] = nn(tokr[...], perm[...]).astype(BF)

    def first_norm(i, carry):
        n, _ = norm_rows(tokp[at(i, 32), :].astype(F32))
        h = n * (1.0 + modv[1:2, :]) + modv[0:1, :]
        ha[pl.ds(pl.multiple_of(m * TOK + i * 32, 32), 32), :] = h.astype(BF)
        return carry

    lax.fori_loop(0, 8, first_norm, 0)
    ha_all = RowGather(link, ha)
    own_g.wait()
    for r in (1, 2, 3):
        sg[r].wait_recv()
    wg[here.x, here.zh, here.y] = nn(pick[...], s0g[...].reshape(192, 1536)).astype(BF)
    gq.hop2()
    gg.hop1()
    gd.hop1()
    gp.hop2()
    gq.hop3()
    ha_all.pass_on()
    cot_sent, cot_got = link.scatter(lambda j: cot_in.at[j], cotr.at[rows_in], here.item_home, slot)
    ha_all.near_done()
    gp.hop3()
    ha_all.last_done()
    outs = [fetch.go(ha, ha_out)]
    gq.done()
    outs.append(fetch.go(wq, wq_out))

    def widen(i, carry):
        part = wq[i // 2, i % 2].reshape(288, 864)
        wqe[at(i, 288), :] = nn(part, spread[...]).astype(BF)
        return carry

    lax.fori_loop(0, 4, widen, 0)

    def project(b, carry):
        acc = nn(ha[at(b, TOK), :], wqe[...]) + bq4[m]
        item, half = b // 2, at(b % 2, TOK)
        cos, sina, sinb = tabs[0, half, :], tabs[1, half, :], tabs[2, half, :]
        for h in range(4):
            p = item * 4 + h
            for t in range(2):
                v = acc[:, t * 512 + h * 128 : t * 512 + h * 128 + 128]
                recip = lax.rsqrt(jnp.sum(v * v, -1, keepdims=True) * (1.0 / HEAD) + EPSILON)
                raw[p, t, half, :] = v
                n = v * recip * gains[t : t + 1, :]
                rot[p, t, half, :] = turn(n, cos, sina, sinb).astype(BF)
            rot[p, 2, half, :] = acc[:, 1024 + h * 128 : 1152 + h * 128].astype(BF)
        return carry

    def attend(p, carry):
        item = p // 4
        lanes = at(p % 4, 128)
        for half in range(2):
            rows = pl.ds(half * TOK, TOK)
            s = nt(rot[p, 0, rows, :], rot[p, 1]) * ROOT + maskb[item]
            top = jnp.max(s, -1, keepdims=True)
            e = jnp.exp(s - top)
            pr = (e / jnp.sum(e, -1, keepdims=True)).astype(BF)
            out_rows = pl.ds(pl.multiple_of(item * 512 + half * TOK, TOK), TOK)
            att[out_rows, lanes] = nn(pr, rot[p, 2]).astype(BF)
        return carry

    other = 1 - here.zl
    lax.fori_loop(other * 2, other * 2 + 2, project, 0)
    gg.hop2()
    lax.fori_loop(other * 4, other * 4 + 4, attend, 0)
    gd.hop2()
    gp.done()
    outs.append(fetch.go(wp, wp_out))
    wpf = wp[...].reshape(512, D)
    red = RowReduce(link, psend, precv)
    red.give(3, nn(att[at(here.mate(3)[0], TOK), :], wpf))
    red.keep_far(nn(att[at(here.mate(2)[0], TOK), :], wpf))
    red.pass_on()
    lax.fori_loop(here.zl * 2, here.zl * 2 + 2, project, 0)
    outs.append(fetch.go(raw, raw_out))
    outs.append(fetch.go(rot, rot_out))
    gg.hop3()
    lax.fori_loop(here.zl * 4, here.zl * 4 + 4, attend, 0)
    gd.hop3()
    outs.append(fetch.go(att, att_out))
    red.give(1, nn(att[at(here.mate(1)[0], TOK), :], wpf))
    pown[...] = nn(att[at(m, TOK), :], wpf)
    red.arrive()

    def second_norm(i, carry):
        rows = at(i, 32)
        a = pown[rows, :] + bp[...] + red.total(rows)
        attn_out[rows, :] = a
        n, _ = norm_rows(tokp[rows, :].astype(F32) + modv[2:3, :] * a)
        h = n * (1.0 + modv[4:5, :]) + modv[3:4, :]
        hm[rows, :] = h.astype(BF)
        return carry

    lax.fori_loop(0, 8, second_norm, 0)
    cot_got(cot_in.at[0], lambda j: cotr.at[pl.ds(j * 64, 64)])
    og[...] = (nn(cotr[...], perm[...]) * valid[...]).astype(BF)

    def scale_grad(i, carry):
        g = og[at(i, 32), :].astype(F32) * modv[5:6, :]
        dmlp[at(i, 32), :] = g.astype(BF)
        return carry

    lax.fori_loop(0, 8, scale_grad, 0)
    gg.done()
    outs.append(fetch.go(wg, wg_out))
    gd.done()
    outs.append(fetch.go(wd, wd_out))
    for c in outs:
        c.wait()
    link.finish()
    tok_sent()
    cot_sent()


def store_tiles(val, ref, base, piece, keep):
    block = ref.shape[3] if keep is None else piece
    for q in range(val.shape[0] // piece):
        row = base + q * piece
        f, off = row // block, row % block
        n = piece if keep is None else keep
        part = val[q * piece : q * piece + n, :].astype(BF)
        ref[f // 4, f // 2 % 2, f % 2, off : off + n, 0 : val.shape[1]] = part


class Fetch:
    def __init__(self, sems):
        self.sems, self.n = sems, 0

    def go(self, src, dst):
        copy = pltpu.make_async_copy(src, dst, self.sems.at[self.n])
        self.n += 1
        copy.start()
        return copy


def kernel_b(
    wg_in, wd_in, hm_in, dm_in, tok_in, og_in, attn_in, att_in, wp_in, wq_in, ha_in, raw_in, rot_in, perm_in,
    spread_in, tabs_in, modv, bg, bd, gains, maskb, valid, pick, condg, w_mod_t,
    dtok, bout, g_qkv, g_gu, fp, fd, dwm, sums, dbm, dcond,
    wg, wd, hm, dmlp, tokp, og, attn_out, att, wp, wq, perm, tabs, gu, coef, hid, rsend, rrecv, mrecv, own32, dmid,
    dwg, dwd, dwp, dattn, raw, rot, to, bo, fq, fg, small, dbg, dbq, dgain,
    pk, q1, m2, q2, dm, e0, e1, e2, e3, line, bq4, bg4, slope,
    g1a, g1b, g2a, g2b, g3a, g3b, d1a, d1b, d2a, d2b, d3a, d3b,
    q1a, q1b, q2a, q2b, q3a, q3b, p1a, p1b, p2a, p2b, p3a, p3b, ssem, rsem, lsem,
):
    here = Place()
    link = Link(here, ssem, rsem)
    fetch = Fetch(lsem)
    m = here.m
    k1, k2, k3 = here.mate(1)[0], here.mate(2)[0], here.mate(3)[0]
    at_m, at_1, at_2, at_3 = at(m, TOK), at(k1, TOK), at(k2, TOK), at(k3, TOK)
    get_hm = fetch.go(hm_in, hm.at[at_m])
    get_dm = fetch.go(dm_in, dmlp.at[at_m])
    get_wg = fetch.go(wg_in, wg)
    get_wd = fetch.go(wd_in, wd)
    gets = [fetch.go(a, b) for a, b in ((tok_in, tokp), (og_in, og), (attn_in, attn_out))]
    get_wp = fetch.go(wp_in, wp)
    gets2 = [fetch.go(a, b) for a, b in ((tabs_in, tabs), (att_in, att), (wq_in, wq), (perm_in, perm))]
    base = fetch.n
    fetch.n += 4
    link.greet(True)
    get_hm.wait()
    hm_all = RowGather(link, hm)
    get_dm.wait()
    dm_all = RowGather(link, dmlp)
    small[...] = jnp.zeros_like(small)
    dbg[...] = jnp.zeros_like(dbg)
    dbq[...] = jnp.zeros_like(dbq)
    dgain[...] = jnp.zeros_like(dgain)
    get_wg.wait()
    get_wd.wait()

    def wgf():
        return wg[...].reshape(D, 1536)

    def wdf():
        return wd[...].reshape(768, D)

    def mlp(k):
        gu[...] = nn(hm[at(k, TOK), :], wgf()) + bg[...]

        def acts(i, carry):
            rows = at(i, 32)
            out = pl.ds(pl.multiple_of(k * TOK + i * 32, 32), 32)
            g, u = gu[rows, 0:768], gu[rows, 768:1536]
            sig = jax.nn.sigmoid(g)
            act = g * sig
            hid[out, :] = (act * u).astype(BF)
            gu[rows, 0:768] = u * sig * (1.0 + g * (1.0 - sig))
            gu[rows, 768:1536] = act
            return carry

        lax.fori_loop(0, 8, acts, 0)
        dh = nt(dmlp[at(k, TOK), :], wdf())
        out = at(k, TOK)
        coef[out, 0:768] = (gu[:, 0:768] * dh).astype(BF)
        coef[out, 768:1536] = (gu[:, 768:1536] * dh).astype(BF)
        dbg[0:1, :] += jnp.sum(coef[out, :].astype(F32), 0, keepdims=True)
        return nt(coef[out, :], wgf())

    hred = RowReduce(link, rsend, rrecv)
    own32[...] = mlp(m)
    hm_all.near_done()
    dm_all.near_done()
    hred.give(1, mlp(k1))
    hm_all.pass_on()
    dm_all.pass_on()
    hred.keep_far(mlp(k2))
    hm_all.last_done()
    dm_all.last_done()
    hred.give(3, mlp(k3))
    hred.pass_on()

    rg = Reduce(link, dwg, (g1a, g1b, g2a, g2b, g3a, g3b), SPLIT_G, 1536)
    rd = Reduce(link, dwd, (d1a, d1b, d2a, d2b, d3a, d3b), SPLIT_D, D)
    rq = Reduce(link, wg, (q1a, q1b, q2a, q2b, q3a, q3b), SPLIT_Q, 896)
    rp = Reduce(link, dwp, (p1a, p1b, p2a, p2b, p3a, p3b), SPLIT_P, D)
    for i in range(3):
        for n in range(2):
            cols = slice(n * 768, n * 768 + 768)
            t = tn(hm[:, i * 384 : i * 384 + 384], coef[:, cols])
            for q in range(8):
                row = i * 384 + q * 48
                f, off = row // 144, row % 144
                dwg[f // 4, f // 2 % 2, f % 2, off : off + 48, cols] = t[q * 48 : q * 48 + 48].astype(BF)
    rg.hop1()
    spread_got = fetch.go(spread_in, wg)
    for c in gets:
        c.wait()
    hred.arrive()

    def mid_back(i, carry):
        rows = at(i, 32)
        mine = pl.ds(pl.multiple_of(m * TOK + i * 32, 32), 32)
        d = own32[rows, :] + hred.total(rows)
        a = attn_out[rows, :]
        n, recip = norm_rows(tokp[rows, :].astype(F32) + modv[2:3, :] * a)
        small[1:2, :] += jnp.sum(d, 0, keepdims=True)
        small[2:3, :] += jnp.sum(d * n, 0, keepdims=True)
        g = og[rows, :].astype(F32) + norm_rows_back(d * (1.0 + modv[4:5, :]), n, recip)
        dmid[rows, :] = g
        small[3:4, :] += jnp.sum(g * a, 0, keepdims=True)
        low = (modv[2:3, :] * g).astype(BF)
        dattn[mine, :] = low
        small[5:6, :] += jnp.sum(low.astype(F32), 0, keepdims=True)
        small[4:5, :] += jnp.sum(dmlp[mine, :].astype(F32), 0, keepdims=True)
        return carry

    lax.fori_loop(0, 8, mid_back, 0)
    da_all = RowGather(link, dattn)
    for i in range(2):
        store_tiles(tn(hid[:, i * 384 : i * 384 + 384], dmlp[...]), dwd, i * 384, 96, None)
    rd.hop1()
    link.settle(hred.s1, hred.s2, hred.s3)
    for g in (hm_all, dm_all):
        link.settle(g.far, g.near, g.last)
    ha_got = fetch.go(ha_in, dmlp)
    da_all.near_done()
    mred = RowReduce(link, rsend, mrecv)
    mred.give(3, nn(hid[at_3, :], wdf()))
    mred.give(1, nn(hid[at_1, :], wdf()))
    mred.keep_far(nn(hid[at_2, :], wdf()))
    bo[...] = nn(hid[at_m, :], wdf()).astype(BF)

    def pair_of(n):
        item = here.zl + (1 - 2 * here.zl) * (n // 4)
        return item, item * 4 + n % 4

    def pair_copies(n):
        p = pair_of(n)[1]
        s = n % 2
        return (
            pltpu.make_async_copy(raw_in.at[p], raw.at[s], lsem.at[base + 2 * s]),
            pltpu.make_async_copy(rot_in.at[p], rot.at[s], lsem.at[base + 2 * s + 1]),
        )

    for c in pair_copies(0):
        c.start()
    get_wp.wait()
    for c in gets2:
        c.wait()

    def back_proj(rows):
        hid[rows, 0:512] = nt(dattn[rows, :], wp[...].reshape(512, D)).astype(BF)

    def attend_back(n, carry):
        item, p = pair_of(n)
        s = n % 2
        lanes = at(n % 4, 128)
        for c in pair_copies(n):
            c.wait()

        @pl.when(n < 7)
        def _():
            for c in pair_copies(n + 1):
                c.start()

        dk = jnp.zeros((512, 128), F32)
        dv = jnp.zeros((512, 128), F32)

        def head_back_store(d, t, rows, out_rows):
            cos, sina, sinb = tabs[0, rows, :], tabs[1, rows, :], tabs[2, rows, :]
            v = raw[s, t, rows, :]
            recip = lax.rsqrt(jnp.sum(v * v, -1, keepdims=True) * (1.0 / HEAD) + EPSILON)
            dn = turn_back(d, cos, sina, sinb)
            dgain[t : t + 1, :] += jnp.sum(dn * v * recip, 0, keepdims=True)
            u = dn * gains[t : t + 1, :]
            mean = jnp.sum(u * v, -1, keepdims=True) * (1.0 / HEAD)
            res = recip * u - v * (recip * recip * recip * mean)
            coef[out_rows, at(t * 4 + n % 4, 128)] = res.astype(BF)

        for half in range(2):
            rows = pl.ds(half * TOK, TOK)
            out_rows = pl.ds(pl.multiple_of(item * 512 + half * TOK, TOK), TOK)
            do = hid[out_rows, lanes]
            x = nt(rot[s, 0, rows, :], rot[s, 1]) * ROOT + maskb[item]
            e = jnp.exp(x - jnp.max(x, -1, keepdims=True))
            pf = e / jnp.sum(e, -1, keepdims=True)
            dp = nt(do, rot[s, 2])
            delta = jnp.sum(pf * dp, -1, keepdims=True)
            ds = (pf * (dp - delta)).astype(BF)
            dq = nn(ds, rot[s, 1]) * ROOT
            dk += tn(ds, rot[s, 0, rows, :])
            dv += tn(pf.astype(BF), do)
            head_back_store(dq, 0, rows, out_rows)
        dk = dk * ROOT
        for half in range(2):
            rows = pl.ds(half * TOK, TOK)
            out_rows = pl.ds(pl.multiple_of(item * 512 + half * TOK, TOK), TOK)
            head_back_store(dk[half * TOK : half * TOK + TOK], 1, rows, out_rows)
        coef[at(item, 512), at(8 + n % 4, 128)] = dv.astype(BF)
        return carry

    back_proj(at_m)
    back_proj(at_1)
    lax.fori_loop(0, 2, attend_back, 0)
    da_all.pass_on()
    mred.pass_on()
    lax.fori_loop(2, 4, attend_back, 0)
    rg.hop2()
    da_all.last_done()
    back_proj(at_2)
    back_proj(at_3)
    store_tiles(tn(att[...], dattn[...]), dwp, 0, 64, PAD)
    rp.hop1()
    lax.fori_loop(4, 6, attend_back, 0)
    rd.hop2()
    mred.arrive()

    def finish_out(i, carry):
        rows = at(i, 32)
        o = bo[rows, :].astype(F32) + bd[...] + mred.total(rows)
        small[0:1, :] += jnp.sum(og[rows, :].astype(F32) * o, 0, keepdims=True)
        mid = tokp[rows, :].astype(F32) + modv[2:3, :] * attn_out[rows, :]
        bo[rows, :] = ((mid + modv[5:6, :] * o) * valid[rows, :]).astype(BF)
        return carry

    lax.fori_loop(0, 8, finish_out, 0)
    bo[...] = nt(bo[...], perm[...]).astype(BF)
    b_sent, b_got = link.scatter(
        lambda j: bo.at[pl.ds(j * 64, 64)], bout.at[here.z], here.item_source, here.z
    )
    lax.fori_loop(6, 8, attend_back, 0)
    rp.hop2()
    spread_got.wait()

    def squeeze(rows):
        v = coef[rows, :]
        dbq[0:1, :] += jnp.sum(v.astype(F32), 0, keepdims=True)
        hm[rows, 0:864] = nt(v, wg[...].reshape(D, 1536)[0:864]).astype(BF)

    def to_input(rows):
        return nt(hm[rows, 0:864], wq[...].reshape(D, 864))

    link.settle(mred.s1, mred.s2, mred.s3)
    tred = RowReduce(link, rsend, rrecv)
    squeeze(at_3)
    tred.give(3, to_input(at_3))
    squeeze(at_2)
    tred.keep_far(to_input(at_2))
    tred.pass_on()
    squeeze(at_1)
    tred.give(1, to_input(at_1))
    squeeze(at_m)
    own32[...] = to_input(at_m)
    pk[...] = jnp.zeros_like(pk)
    bq4[...] = jnp.zeros_like(bq4)
    bg4[...] = jnp.zeros_like(bg4)
    bq4[m] = dbq[0:1, :]
    bg4[m] = dbg[0:1, :]
    for t in range(2):
        for e in range(2):
            to_ = t * 72 + e * UNIT
            line[:, to_ : to_ + UNIT] = dgain[t : t + 1, e * 64 : e * 64 + UNIT]
    for s in range(32):
        x, c, z, y = s // 16, s // 8 % 2, s // 2 % 4, s % 2
        for q in range(3):
            piece, unit = divmod(2 * s + q, 32) if q < 2 else (2, s)
            _, member, spot = shard_parts(unit)
            from_ = piece * 512 + spot * 64
            pk[x, c, y, z, 1:2, q * UNIT : q * UNIT + UNIT] = bq4[member, :, from_ : from_ + UNIT]
        from_ = shard_parts(s)[0] * UNIT
        pk[x, c, y, z, 1:2, 108:144] = small[5:6, from_ : from_ + UNIT]
        pk[x, c, y, z, 1:2, 144:180] = small[4:5, from_ : from_ + UNIT]
        for q in range(2):
            piece, unit = divmod(2 * s + q, 32)
            _, member, spot = shard_parts(unit)
            from_ = piece * 768 + spot * 96
            pk[x, c, y, z, 2:3, q * 96 : q * 96 + 96] = bg4[member, :, from_ : from_ + 96]
        pk[x, c, y, z, 3:4, 0:144] = line[:, 0:144]
    full_slope = silu_slope(condg[here.dp])
    for b in range(8):
        slope[b] = full_slope[:, b * 144 : b * 144 + 144]
    ha_got.wait()
    for i in range(3):
        store_tiles(tn(dmlp[:, i * 384 : i * 384 + 384], hm[:, 0:864]), wg, i * 384, 48, None)
    rq.hop1()
    rg.hop3()
    rd.hop3()
    rp.hop3()
    tred.arrive()

    def first_back(i, carry):
        rows = at(i, 32)
        d = own32[rows, :] + tred.total(rows)
        n, recip = norm_rows(tokp[rows, :].astype(F32))
        small[6:7, :] += jnp.sum(d, 0, keepdims=True)
        small[7:8, :] += jnp.sum(d * n, 0, keepdims=True)
        g = dmid[rows, :] + norm_rows_back(d * (1.0 + modv[1:2, :]), n, recip)
        to[rows, :] = g.astype(BF)
        return carry

    lax.fori_loop(0, 8, first_back, 0)
    to[...] = nt(to[...], perm[...]).astype(BF)
    sent, got = link.scatter(
        lambda j: to.at[pl.ds(j * 64, 64)], dtok.at[here.z], here.item_source, here.z
    )
    rq.hop2()
    rows_of = (6, 7, 3, 1, 2, 0)
    for s in range(32):
        x, c, z, y = s // 16, s // 8 % 2, s // 2 % 4, s % 2
        for q in range(6):
            piece, unit = divmod(6 * s + q, 32)
            from_ = shard_parts(unit)[0] * UNIT
            row = rows_of[piece]
            pk[x, c, y, z, 0:1, q * UNIT : q * UNIT + UNIT] = small[row : row + 1, from_ : from_ + UNIT]
    ns = []
    for r in range(1, 8):
        x, c, y, dev = near(here, r)
        ns.append(link.send(pk.at[x, c, y], q1.at[here.x, here.c, here.y], dev))
    q1[here.x, here.c, here.y] = pk[here.x, here.c, here.y]

    def hand_out(red, base_row, out):
        left, right = red.done()
        rows = slice(base_row, base_row + 4 * PAD)
        coef[rows, 0 : red.split] = tn(pick[...], left).astype(BF)
        coef[rows, red.split : red.cols] = tn(pick[...], right).astype(BF)

        def share(k):
            return coef.at[pl.ds(pl.multiple_of(base_row + k * PAD, 16), PAD), pl.ds(0, red.cols)]

        over = [link.send(share(here.mate(r)[0]), out.at[m], here.mate(r)[1]) for r in (2, 3, 1)]
        return over, fetch.go(share(m), out.at[m])

    def plain(red, out):
        left, right = red.done()
        out[...] = nt(left, perm[:, 0 : red.split]) + nt(right, perm[:, red.split : D])

    rq.hop3()
    g_over, g_own = hand_out(rg, 0, fg)
    for n in ns:
        n.wait_recv()
    for z in range(4):
        for x in range(2):
            for y in range(2):
                d = x * 2 + y
                m2[z, d : d + 1, :] = q1[x, 0, y, z, 0:1, :] + q1[x, 1, y, z, 0:1, :]
        total = q1[0, 0, 0, z, 1:4, :]
        for i in range(1, 8):
            total += q1[i // 4, i // 2 % 2, i % 2, z, 1:4, :]
        m2[z, 4:7, :] = total
    zs = []
    for r in (1, 2, 3):
        z, dev = along_z(here, r)
        zs.append(link.send(m2.at[z], q2.at[here.z], dev))
    q2[here.z] = m2[here.z]
    dm[...] = jnp.zeros_like(dm)
    v = condg[...].reshape(32, D)
    act = (v * jax.nn.sigmoid(v)).astype(BF)
    plain(rd, fd)
    plain(rp, fp)
    for c in zs:
        c.wait_recv()
    for z in range(4):
        for d in range(4):
            dm[d * 8 + z : d * 8 + z + 1, :] = q2[z, d : d + 1, 0:216]
    sums[...] = q2[0] + q2[1] + q2[2] + q2[3]
    dbm[...] = jnp.broadcast_to(jnp.sum(dm[...], 0, keepdims=True), (8, 216))
    d3 = three(dm[...])
    da = nn(d3, w_mod_t[...])
    da = da[0:32] + da[32:64] + da[64:96]
    for b in range(8):
        for d in range(4):
            e0[d, b % 2, b // 2] = da[d * 8 : d * 8 + 8, b * 144 : b * 144 + 144]
    ns = []
    for r in range(1, 8):
        x, c, y, dev = near(here, r)
        ns.append(link.send(e0.at[x * 2 + c, y], e1.at[here.x, here.c, here.y], dev))
    e1[here.x, here.c, here.y] = e0[here.dp, here.y]
    dwm[...] = tn(d3, jnp.concatenate([act, act, act], 0))
    g_own.wait()
    for c in g_over:
        c.wait_recv()
    by_column(fg, g_gu, 192, 2)
    q_over, q_own = hand_out(rq, 4 * PAD, fq)
    for n in ns:
        n.wait_recv()
    total = e1[0, 0, 0]
    for i in range(1, 8):
        total += e1[i // 4, i // 2 % 2, i % 2]
    e2[...] = total
    zs = []
    for r in (1, 2, 3):
        z, dev = along_z(here, r)
        zs.append(link.send(e2.at[z], e3.at[here.z], dev))
    e3[here.z] = e2[here.z]
    q_own.wait()
    for c in q_over:
        c.wait_recv()
    by_column(fq, g_qkv, 72, 3)
    for c in zs:
        c.wait_recv()
    dcond[...] = (e3[0] + e3[1] + e3[2] + e3[3]) * slope[here.z * 2 + here.y]
    b_got(bo.at[pl.ds(0, 64)], lambda j: bout.at[j])
    got(to.at[pl.ds(0, 64)], lambda j: dtok.at[j])
    link.finish()
    b_sent()
    sent()


def call(kernel, ident, outs, scratch, args, hbm=(), hbm_out=(), sems=64, local=32):
    vm = pl.BlockSpec(memory_space=pltpu.VMEM)
    hb = pl.BlockSpec(memory_space=pltpu.HBM)
    return pl.pallas_call(
        kernel,
        out_shape=[jax.ShapeDtypeStruct(s, t) for s, t in outs],
        in_specs=[hb if i in hbm else vm for i in range(len(args))],
        out_specs=[hb if i in hbm_out else vm for i in range(len(outs))],
        scratch_shapes=scratch + [pltpu.SemaphoreType.DMA((sems,)), pltpu.SemaphoreType.DMA((sems,))]
        + ([pltpu.SemaphoreType.DMA((local,))] if hbm else []),
        compiler_params=pltpu.CompilerParams(
            collective_id=ident, has_side_effects=True, vmem_limit_bytes=LIMIT
        ),
    )(*args)


def local(
    tokens, conditioning, heights, widths, cotangent, w_mod, b_mod, w_qkv, b_qkv, query_gain, key_gain,
    w_proj, b_proj, w_gu, b_gu, w_down, b_down,
):
    args = (
        tokens, conditioning, heights, widths, cotangent, w_mod, b_mod, w_qkv, b_qkv, query_gain, key_gain,
        w_proj, b_proj, w_gu, b_gu, w_down, b_down,
    )
    sizes = tuple(lax.axis_size(a) for a in ("dp", "row", "col"))
    if sizes != (4, 4, 2) or tokens.shape != (4, 4, 16, D):
        return general(*args)
    every = ("dp", "row", "col")
    perm, spread, pick, tabs = constants()
    row = lambda *v: jnp.pad(jnp.concatenate([a.astype(F32) for a in v]), (0, 256 - sum(a.shape[0] for a in v)))
    vecs = [row(b_mod), row(b_qkv, b_proj, b_down), row(b_gu), row(query_gain), row(key_gain), row(heights, widths)]
    vecs = jnp.concatenate(vecs + [jnp.zeros((512,), F32)]).reshape(8, 256)
    w_mod_t = w_mod.T
    full = (GROUP, D)
    block = (TOK, D)
    weights = [(2, 2, 2, 144, 864), (2, 2, 2, 64, D), (2, 2, 2, 144, 1536), (2, 2, 2, 96, D)]
    pairs = [((8, 2, 512, 128), F32), ((8, 3, 512, 128), BF)]
    small_rows = pltpu.VMEM((4, 8, 256), F32)
    (
        wq_all, wp_all, wg_all, wd_all, ha, raw, rot, att, hm, dmlp, tokp, og, attn_out,
        condg, modv, bg, bd, gains, maskb, valid,
    ) = call(
        kernel_a, 0,
        [(w, BF) for w in weights] + [(full, BF)] + pairs + [((GROUP, 512), BF)]
        + [(block, BF)] * 4
        + [
            (s, F32)
            for s in (block, (4, 8, D), (8, D), (1, 1536), (1, D), (8, 128), (2, 1, 512), (TOK, 1))
        ],
        [pltpu.VMEM(w, BF) for w in weights] + [pltpu.VMEM(full, BF)] + [pltpu.VMEM(w, t) for w, t in pairs]
        + [
            pltpu.VMEM((GROUP, 512), BF), pltpu.VMEM((4, PAD, 864), BF), pltpu.VMEM((4, PAD, 1536), BF),
            pltpu.VMEM(block, BF), pltpu.VMEM(block, BF), pltpu.VMEM((D, 1536), BF), pltpu.VMEM((3, TOK, D), BF),
            pltpu.VMEM((3, TOK, D), BF), pltpu.VMEM(block, F32),
            pltpu.VMEM((4, PAD, 864), BF), pltpu.VMEM((4, PAD, 1536), BF), pltpu.VMEM((4, PAD, 1536), F32),
            pltpu.VMEM((8, D), F32), small_rows, small_rows, pltpu.VMEM((4, 4, 8, 256), F32),
            pltpu.VMEM((2, 2, 2, 4, 8, 256), F32), pltpu.VMEM((4, 1, 1536), F32), pltpu.VMEM((4, 1, 1536), F32),
            pltpu.VMEM((1, D), F32),
        ],
        (
            tokens.reshape(4, 64, D), cotangent.reshape(4, 64, D), w_qkv, w_gu, w_proj, w_down, conditioning, w_mod_t,
            vecs, perm, spread, pick, tabs,
        ),
        hbm=(0, 1),
        hbm_out=range(8),
        sems=128,
    )
    spread = jnp.pad(spread, ((0, D - 864), (0, 0))).reshape(2, 2, 2, 144, 1536)
    dtok, bout, g_w_qkv, g_w_gu, fp, fd, g_w_mod, sums, g_b_mod, d_cond = call(
        kernel_b, 1,
        [
            ((4, 64, D), BF), ((4, 64, D), BF), ((UNIT, 3456), F32), ((UNIT, 6144), F32), ((PAD, D), F32),
            ((96, D), F32), ((216, D), F32), ((8, 256), F32), ((8, 216), F32), ((8, 144), F32),
        ],
        [
            pltpu.VMEM((2, 2, 2, 144, 1536), BF), pltpu.VMEM((2, 2, 2, 96, D), BF), pltpu.VMEM(full, BF),
            pltpu.VMEM(full, BF), pltpu.VMEM(block, BF), pltpu.VMEM(block, BF), pltpu.VMEM(block, F32),
            pltpu.VMEM((GROUP, 512), BF), pltpu.VMEM((2, 2, 2, 64, D), BF), pltpu.VMEM((2, 2, 2, 144, 864), BF),
            pltpu.VMEM((D, D), BF), pltpu.VMEM((3, 512, 128), F32), pltpu.VMEM((TOK, 1536), F32),
            pltpu.VMEM((GROUP, 1536), BF), pltpu.VMEM((GROUP, 768), BF), pltpu.VMEM((3, TOK, D), BF),
            pltpu.VMEM((3, TOK, D), BF), pltpu.VMEM((3, TOK, D), BF), pltpu.VMEM(block, F32), pltpu.VMEM(block, F32),
            pltpu.VMEM((2, 2, 2, 144, 1536), BF), pltpu.VMEM((2, 2, 2, 96, D), BF), pltpu.VMEM((2, 2, 2, PAD, D), BF),
            pltpu.VMEM(full, BF), pltpu.VMEM((2, 2, 512, 128), F32), pltpu.VMEM((2, 3, 512, 128), BF),
            pltpu.VMEM(block, BF), pltpu.VMEM(block, BF), pltpu.VMEM((4, PAD, 896), BF), pltpu.VMEM((4, PAD, 1536), BF),
            pltpu.VMEM((8, D), F32), pltpu.VMEM((8, 1536), F32), pltpu.VMEM((8, 1536), F32), pltpu.VMEM((8, 128), F32),
            pltpu.VMEM((2, 2, 2, 4, 8, 256), F32), pltpu.VMEM((2, 2, 2, 4, 8, 256), F32), small_rows, small_rows,
            pltpu.VMEM((32, 216), F32), pltpu.VMEM((4, 2, 4, 8, 144), F32), pltpu.VMEM((2, 2, 2, 4, 8, 144), F32),
            pltpu.VMEM((4, 8, 144), F32), pltpu.VMEM((4, 8, 144), F32), pltpu.VMEM((1, 256), F32),
            pltpu.VMEM((4, 1, 1536), F32), pltpu.VMEM((4, 1, 1536), F32), pltpu.VMEM((8, 8, 144), F32),
        ]
        + Reduce.buffers(144, 1536, SPLIT_G) + Reduce.buffers(96, D, SPLIT_D)
        + Reduce.buffers(144, 896, SPLIT_Q) + Reduce.buffers(PAD, D, SPLIT_P),
        (
            wg_all, wd_all, hm, dmlp, tokp, og, attn_out, att, wp_all, wq_all, ha, raw, rot, perm, spread, tabs,
            modv, bg, bd, gains, maskb, valid, pick, condg, w_mod_t,
        ),
        hbm=range(16),
        hbm_out=range(2),
        sems=128,
    )

    one, two = sums[4], sums[5]
    gains_out = sums[6]
    return (
        bout.reshape(tokens.shape),
        dtok.reshape(tokens.shape).astype(F32),
        d_cond[:4],
        g_w_mod.T,
        g_b_mod[0],
        g_w_qkv,
        one[:72],
        one[72:108],
        gains_out[:72],
        gains_out[72:144],
        fp[:UNIT],
        one[108:144],
        g_w_gu,
        two[:192],
        fd,
        one[144:180],
    )


def solution(mesh):
    in_specs = (
        P("dp", "row", "col", None),
        P("dp", None),
        P("dp"),
        P("dp"),
        P("dp", "row", "col", None),
        P(None, ("dp", "row", "col")),
        P(("dp", "row", "col")),
        P(("dp", "row", "col"), None),
        P(("dp", "row", "col")),
        P(),
        P(),
        P(("dp", "row", "col"), None),
        P(("dp", "row", "col")),
        P(("dp", "row", "col"), None),
        P(("dp", "row", "col")),
        P(("dp", "row", "col"), None),
        P(("dp", "row", "col")),
    )
    out_specs = (
        P("dp", "row", "col", None),
        P("dp", "row", "col", None),
        P("dp", ("row", "col")),
        P(None, ("dp", "row", "col")),
        P(("dp", "row", "col")),
        P(("dp", "row", "col"), None),
        P(("dp", "row", "col")),
        P(("dp", "row", "col")),
        P(),
        P(),
        P(("dp", "row", "col"), None),
        P(("dp", "row", "col")),
        P(("dp", "row", "col"), None),
        P(("dp", "row", "col")),
        P(("dp", "row", "col"), None),
        P(("dp", "row", "col")),
    )
    return jax.shard_map(local, mesh=mesh, in_specs=in_specs, out_specs=out_specs, check_vma=False)
```

```python
import math

import jax
import jax.numpy as jnp
import numpy as np
from jax import lax
from jax.experimental import pallas as pl
from jax.experimental.pallas import tpu as pltpu
from jax.sharding import PartitionSpec as P

HEADS = 16
HEAD = 72
FF = 3072


EPSILON = 1e-06
MASKED = -1000000000.0
PRECISE = lax.Precision.HIGHEST


def rope_tables(row_pos, col_pos, head_size):
    half_size = head_size // 2
    lane_index = jnp.arange(head_size)
    pair_index = (lane_index % half_size // 2).astype(jnp.float32)
    frequency = jnp.exp(-math.log(10000.0) * 2.0 * pair_index / half_size)
    places = jnp.where(lane_index[None, :] >= half_size, col_pos[:, None], row_pos[:, None]).astype(
        jnp.float32
    )
    angles = places * frequency[None, :]
    return (jnp.cos(angles), jnp.sin(angles))


def rotate(values):
    pair_view = values.reshape(values.shape[:-1] + (values.shape[-1] // 2, 2))
    turned = jnp.stack((-pair_view[..., 1], pair_view[..., 0]), axis=-1)
    return turned.reshape(values.shape)


def norm_parts(values):
    centered = values - jnp.mean(values, -1, keepdims=True)
    recip = lax.rsqrt(jnp.mean(centered * centered, -1, keepdims=True) + EPSILON)
    return (centered * recip, recip)


def norm_back(gradient, normed, recip):
    return recip * (
        gradient
        - jnp.mean(gradient, -1, keepdims=True)
        - normed * jnp.mean(gradient * normed, -1, keepdims=True)
    )


def head_back(gradient, raw_value, recip, gain_vec):
    scaled = gradient * gain_vec
    gain_grad = jnp.sum(gradient * raw_value * recip, axis=(0, 1, 2))
    raw_grad = recip * scaled - raw_value * (recip * recip * recip) * jnp.mean(
        scaled * raw_value, -1, keepdims=True
    )
    return (raw_grad, gain_grad)


def general(
    tokens,
    conditioning,
    heights,
    widths,
    cotangent,
    w_mod,
    b_mod,
    w_qkv,
    b_qkv,
    query_gain,
    key_gain,
    w_proj,
    b_proj,
    w_gu,
    b_gu,
    w_down,
    b_down,
):
    item_count, tile_rows, tile_cols, model_width = tokens.shape
    tile_span = tile_rows * tile_cols
    n_row = lax.axis_size("row")
    n_col = lax.axis_size("col")
    groups = n_row * n_col
    key_count = tile_span * groups
    inv_root = 1.0 / math.sqrt(HEAD)
    row_at = lax.axis_index("row")
    col_at = lax.axis_index("col")
    local_index = jnp.arange(tile_span)
    query_rows = row_at * tile_rows + local_index // tile_cols
    query_cols = col_at * tile_cols + local_index % tile_cols
    valid_query = (query_rows[None, :] < heights[:, None]) & (query_cols[None, :] < widths[:, None])
    key_index = jnp.arange(key_count)
    key_owner = key_index // tile_span
    key_spot = key_index % tile_span
    key_rows = key_owner // n_col * tile_rows + key_spot // tile_cols
    key_cols = key_owner % n_col * tile_cols + key_spot % tile_cols
    valid_key = (key_rows[None, :] < heights[:, None]) & (key_cols[None, :] < widths[:, None])
    cos_tab, sin_tab = rope_tables(query_rows, query_cols, HEAD)
    cos_four = cos_tab[None, :, None, :]
    sin_four = sin_tab[None, :, None, :]
    cond_f = conditioning.astype(jnp.float32)
    cond_sig = jax.nn.sigmoid(cond_f)
    act_low = (cond_f * cond_sig).astype(jnp.bfloat16)
    gathered = (
        lax.all_gather(w_mod, ("dp", "row", "col"), axis=1, tiled=True),
        lax.all_gather(b_mod, ("dp", "row", "col"), axis=0, tiled=True),
        lax.all_gather(w_qkv, ("dp", "row", "col"), axis=0, tiled=True),
        lax.all_gather(b_qkv, ("dp", "row", "col"), axis=0, tiled=True),
        lax.all_gather(w_proj, ("dp", "row", "col"), axis=0, tiled=True),
        lax.all_gather(b_proj, ("dp", "row", "col"), axis=0, tiled=True),
        lax.all_gather(w_gu, ("dp", "row", "col"), axis=0, tiled=True),
        lax.all_gather(b_gu, ("dp", "row", "col"), axis=0, tiled=True),
        lax.all_gather(w_down, ("dp", "row", "col"), axis=0, tiled=True),
        lax.all_gather(b_down, ("dp", "row", "col"), axis=0, tiled=True),
    )
    (
        w_mod_all,
        b_mod_all,
        w_qkv_all,
        b_qkv_all,
        w_proj_all,
        b_proj_all,
        w_gu_all,
        b_gu_all,
        w_down_all,
        b_down_all,
    ) = gathered
    modul = jnp.dot(act_low, w_mod_all, preferred_element_type=jnp.float32) + b_mod_all.astype(
        jnp.float32
    )
    shift_a, scale_a, gate_a, shift_m, scale_m, gate_m = [
        modul[:, piece * model_width : (piece + 1) * model_width][:, None, :] for piece in range(6)
    ]
    resid_in = tokens.reshape(item_count, tile_span, model_width).astype(jnp.float32)
    normed_a, recip_a = norm_parts(resid_in)
    h_attn = (normed_a * (1.0 + scale_a) + shift_a).astype(jnp.bfloat16)
    qkv_all = jnp.dot(h_attn, w_qkv_all, preferred_element_type=jnp.float32) + b_qkv_all.astype(
        jnp.float32
    )
    query_raw = qkv_all[..., :model_width].reshape(item_count, tile_span, HEADS, HEAD)
    key_raw = qkv_all[..., model_width : 2 * model_width].reshape(
        item_count, tile_span, HEADS, HEAD
    )
    value_raw = qkv_all[..., 2 * model_width :]
    query_recip = lax.rsqrt(jnp.mean(query_raw * query_raw, -1, keepdims=True) + EPSILON)
    key_recip = lax.rsqrt(jnp.mean(key_raw * key_raw, -1, keepdims=True) + EPSILON)
    query_normed = query_raw * query_recip * query_gain
    key_normed = key_raw * key_recip * key_gain
    query_rot = (query_normed * cos_four + rotate(query_normed) * sin_four).astype(jnp.bfloat16)
    key_rot = (key_normed * cos_four + rotate(key_normed) * sin_four).astype(jnp.bfloat16)
    value_low = value_raw.astype(jnp.bfloat16)
    kv_local = jnp.concatenate([key_rot.reshape(item_count, tile_span, model_width), value_low], -1)
    kv_every = lax.all_gather(kv_local, ("row", "col"), axis=1, tiled=True)
    query_heads = query_rot.transpose(2, 0, 1, 3)
    key_part = (
        kv_every[..., :model_width]
        .reshape(item_count, key_count, HEADS, HEAD)
        .transpose(2, 0, 1, 3)
    )
    value_part = (
        kv_every[..., model_width:]
        .reshape(item_count, key_count, HEADS, HEAD)
        .transpose(2, 0, 1, 3)
    )
    key_mask = valid_key[:, None, :]

    def attend(head_block):
        query_h, key_h, value_h = head_block
        scores = (
            jnp.einsum("itd,ikd->itk", query_h, key_h, preferred_element_type=jnp.float32)
            * inv_root
        )
        scores = jnp.where(key_mask, scores, MASKED)
        row_max = jnp.max(scores, -1, keepdims=True)
        exponent = jnp.exp(scores - row_max)
        row_sum = jnp.sum(exponent, -1, keepdims=True)
        probs = (exponent / row_sum).astype(jnp.bfloat16)
        result = jnp.einsum("itk,ikd->itd", probs, value_h, preferred_element_type=jnp.float32)
        return (result, row_max, row_sum)

    attended_heads, max_kept, sum_kept = lax.map(attend, (query_heads, key_part, value_part))
    attended = (
        attended_heads.transpose(1, 2, 0, 3)
        .reshape(item_count, tile_span, model_width)
        .astype(jnp.bfloat16)
    )
    attn_out = jnp.dot(
        attended, w_proj_all, preferred_element_type=jnp.float32
    ) + b_proj_all.astype(jnp.float32)
    resid_mid = resid_in + gate_a * attn_out
    normed_m, recip_m = norm_parts(resid_mid)
    h_mlp = (normed_m * (1.0 + scale_m) + shift_m).astype(jnp.bfloat16)
    gate_up = jnp.dot(h_mlp, w_gu_all, preferred_element_type=jnp.float32) + b_gu_all.astype(
        jnp.float32
    )
    gate_part = gate_up[..., :FF]
    up_part = gate_up[..., FF:]
    gate_sig = jax.nn.sigmoid(gate_part)
    gate_act = gate_part * gate_sig
    hidden = (gate_act * up_part).astype(jnp.bfloat16)
    mlp_out = jnp.dot(hidden, w_down_all, preferred_element_type=jnp.float32) + b_down_all.astype(
        jnp.float32
    )
    mask_f = valid_query[..., None].astype(jnp.float32)
    block_out = ((resid_mid + gate_m * mlp_out) * mask_f).astype(jnp.bfloat16)
    out_grad = cotangent.reshape(item_count, tile_span, model_width).astype(jnp.float32) * mask_f
    d_mlp = (gate_m * out_grad).astype(jnp.bfloat16)
    d_gate_m = jnp.sum(out_grad * mlp_out, 1)
    dw_down = jnp.einsum("itf,itd->fd", hidden, d_mlp, preferred_element_type=jnp.float32)
    db_down = jnp.sum(d_mlp.astype(jnp.float32), (0, 1))
    d_hidden = jnp.einsum("itd,fd->itf", d_mlp, w_down_all, preferred_element_type=jnp.float32)
    d_gate = d_hidden * up_part * gate_sig * (1.0 + gate_part * (1.0 - gate_sig))
    d_up = d_hidden * gate_act
    d_gate_up = jnp.concatenate([d_gate, d_up], -1).astype(jnp.bfloat16)
    dw_gu = jnp.einsum("itd,ite->de", h_mlp, d_gate_up, preferred_element_type=jnp.float32)
    db_gu = jnp.sum(d_gate_up.astype(jnp.float32), (0, 1))
    d_hmlp = jnp.einsum("ite,de->itd", d_gate_up, w_gu_all, preferred_element_type=jnp.float32)
    d_shift_m = jnp.sum(d_hmlp, 1)
    d_scale_m = jnp.sum(d_hmlp * normed_m, 1)
    d_mid = out_grad + norm_back(d_hmlp * (1.0 + scale_m), normed_m, recip_m)
    d_attn = (gate_a * d_mid).astype(jnp.bfloat16)
    d_gate_a = jnp.sum(d_mid * attn_out, 1)
    dw_proj = jnp.einsum("itd,ite->de", attended, d_attn, preferred_element_type=jnp.float32)
    db_proj = jnp.sum(d_attn.astype(jnp.float32), (0, 1))
    d_attended = jnp.einsum(
        "ite,de->itd", d_attn, w_proj_all, preferred_element_type=jnp.float32
    ).astype(jnp.bfloat16)
    d_att_heads = d_attended.reshape(item_count, tile_span, HEADS, HEAD).transpose(2, 0, 1, 3)
    key_back, value_back = (key_part, value_part)

    def attend_back(head_block):
        query_h, key_h, value_h, grad_h, max_h, sum_h = head_block
        scores = (
            jnp.einsum("itd,ikd->itk", query_h, key_h, preferred_element_type=jnp.float32)
            * inv_root
        )
        scores = jnp.where(key_mask, scores, MASKED)
        probs = jnp.exp(scores - max_h) / sum_h
        d_probs = jnp.einsum("itd,ikd->itk", grad_h, value_h, preferred_element_type=jnp.float32)
        delta = jnp.sum(probs * d_probs, -1, keepdims=True)
        d_scores = (probs * (d_probs - delta)).astype(jnp.bfloat16)
        d_query = (
            jnp.einsum("itk,ikd->itd", d_scores, key_h, preferred_element_type=jnp.float32)
            * inv_root
        )
        d_key = (
            jnp.einsum("itk,itd->ikd", d_scores, query_h, preferred_element_type=jnp.float32)
            * inv_root
        )
        d_value = jnp.einsum(
            "itk,itd->ikd", probs.astype(jnp.bfloat16), grad_h, preferred_element_type=jnp.float32
        )
        return (d_query, d_key, d_value)

    dq_heads, dk_heads, dv_heads = lax.map(
        attend_back, (query_heads, key_back, value_back, d_att_heads, max_kept, sum_kept)
    )
    dkv_term = jnp.concatenate(
        [
            dk_heads.transpose(1, 2, 0, 3).reshape(item_count, key_count, model_width),
            dv_heads.transpose(1, 2, 0, 3).reshape(item_count, key_count, model_width),
        ],
        -1,
    )
    dkv_own = lax.psum_scatter(dkv_term, ("row", "col"), scatter_dimension=1, tiled=True)
    d_key_rot = dkv_own[..., :model_width].reshape(item_count, tile_span, HEADS, HEAD)
    d_value = dkv_own[..., model_width:]
    d_query_rot = dq_heads.transpose(1, 2, 0, 3)
    d_query_n = d_query_rot * cos_four - rotate(d_query_rot * sin_four)
    d_key_n = d_key_rot * cos_four - rotate(d_key_rot * sin_four)
    d_query_raw, dq_gain = head_back(d_query_n, query_raw, query_recip, query_gain)
    d_key_raw, dk_gain = head_back(d_key_n, key_raw, key_recip, key_gain)
    gain_total = lax.psum((dq_gain, dk_gain), ("dp", "row", "col"))
    d_qkv = jnp.concatenate(
        [
            d_query_raw.reshape(item_count, tile_span, model_width),
            d_key_raw.reshape(item_count, tile_span, model_width),
            d_value,
        ],
        -1,
    ).astype(jnp.bfloat16)
    dw_qkv = jnp.einsum("itd,ite->de", h_attn, d_qkv, preferred_element_type=jnp.float32)
    db_qkv = jnp.sum(d_qkv.astype(jnp.float32), (0, 1))
    db_query_key = db_qkv[: 2 * model_width]
    db_value = db_qkv[2 * model_width :]
    d_hattn = jnp.einsum("ite,de->itd", d_qkv, w_qkv_all, preferred_element_type=jnp.float32)
    d_shift_a = jnp.sum(d_hattn, 1)
    d_scale_a = jnp.sum(d_hattn * normed_a, 1)
    d_tokens = d_mid + norm_back(d_hattn * (1.0 + scale_a), normed_a, recip_a)
    d_modul = jnp.concatenate([d_shift_a, d_scale_a, d_gate_a, d_shift_m, d_scale_m, d_gate_m], -1)
    act_f = act_low.astype(jnp.float32)
    dw_mod = jnp.einsum("id,ie->de", act_f, d_modul, precision=PRECISE)
    db_mod = jnp.sum(d_modul, 0)
    d_act = jnp.einsum("ie,de->id", d_modul, w_mod_all.astype(jnp.float32), precision=PRECISE)
    d_cond_part = d_act * cond_sig * (1.0 + cond_f * (1.0 - cond_sig))
    d_cond = lax.psum_scatter(d_cond_part, ("row", "col"), scatter_dimension=1, tiled=True)
    summed = (
        lax.psum_scatter(dw_mod, ("dp", "row", "col"), scatter_dimension=1, tiled=True),
        lax.psum_scatter(db_mod, ("dp", "row", "col"), scatter_dimension=0, tiled=True),
        lax.psum_scatter(dw_qkv, ("dp", "row", "col"), scatter_dimension=0, tiled=True),
        lax.psum_scatter(db_query_key, ("dp", "row", "col"), scatter_dimension=0, tiled=True),
        lax.psum_scatter(db_value, ("dp", "row", "col"), scatter_dimension=0, tiled=True),
        lax.psum_scatter(dw_proj, ("dp", "row", "col"), scatter_dimension=0, tiled=True),
        lax.psum_scatter(db_proj, ("dp", "row", "col"), scatter_dimension=0, tiled=True),
        lax.psum_scatter(dw_gu, ("dp", "row", "col"), scatter_dimension=0, tiled=True),
        lax.psum_scatter(db_gu, ("dp", "row", "col"), scatter_dimension=0, tiled=True),
        lax.psum_scatter(dw_down, ("dp", "row", "col"), scatter_dimension=0, tiled=True),
        lax.psum_scatter(db_down, ("dp", "row", "col"), scatter_dimension=0, tiled=True),
    )
    (
        g_w_mod,
        g_b_mod,
        g_w_qkv,
        g_b_query_key,
        g_b_value,
        g_w_proj,
        g_b_proj,
        g_w_gu,
        g_b_gu,
        g_w_down,
        g_b_down,
    ) = summed
    return (
        block_out.reshape(item_count, tile_rows, tile_cols, model_width),
        d_tokens.reshape(item_count, tile_rows, tile_cols, model_width),
        d_cond,
        g_w_mod,
        g_b_mod,
        g_w_qkv,
        g_b_query_key,
        g_b_value,
        gain_total[0],
        gain_total[1],
        g_w_proj,
        g_b_proj,
        g_w_gu,
        g_b_gu,
        g_w_down,
        g_b_down,
    )


MESH = pl.DeviceIdType.MESH
BF = jnp.bfloat16
F32 = jnp.float32
LIMIT = 60 * 1024 * 1024
D = 1152
UNIT = 36
PAD = 48
TOK = 256
GROUP = 1024
SPLIT_Q, SPLIT_P, SPLIT_D = 384, 640, 640
ROOT = 1.0 / math.sqrt(HEAD)
ROOT2 = ROOT / math.log(2.0)


def nn(a, b):
    return lax.dot_general(a, b, (((1,), (0,)), ((), ())), preferred_element_type=F32)


def nt(a, b):
    return lax.dot_general(a, b, (((1,), (1,)), ((), ())), preferred_element_type=F32)


def tn(a, b):
    return lax.dot_general(a, b, (((0,), (0,)), ((), ())), preferred_element_type=F32)


def width_order():
    xx, zh, yy, zl, cc, jj = np.indices((2, 2, 2, 2, 2, UNIT)).reshape(6, -1)
    return ((((xx * 2 + cc) * 2 + zh) * 2 + zl) * 2 + yy) * UNIT + jj


def constants():
    perm = np.zeros((D, D), np.float32)
    perm[width_order(), np.arange(D)] = 1.0
    spread = np.zeros((864, 1536), np.float32)
    tt, hh, yy, jj = np.indices((3, 4, 2, UNIT)).reshape(4, -1)
    spread[tt * 288 + hh * 72 + yy * 36 + jj, tt * 512 + hh * 128 + yy * 64 + jj] = 1.0
    pick = np.zeros((144, 192), np.float32)
    kk, jj = np.indices((4, UNIT)).reshape(2, -1)
    pick[kk * 36 + jj, kk * 48 + jj] = 1.0
    spot = np.arange(512)
    row = spot // 128 * 4 + spot // 16 % 4
    col = spot // 64 % 2 * 16 + spot % 16
    lane = np.arange(128)
    part = lane % 64
    freq = np.exp(-math.log(10000.0) * 2.0 * (part // 2) / 36.0)
    place = np.where(lane[None, :] >= 64, col[:, None], row[:, None]).astype(np.float64)
    angle = place * freq[None, :]
    live = part < UNIT
    cos = np.where(live, np.cos(angle), 0.0)
    sin = np.where(live, np.sin(angle), 0.0)
    even = lane % 2 == 0
    tabs = np.stack([cos, np.where(even, -sin, 0.0), np.where(even, 0.0, sin)]).astype(np.float32)
    return (
        jnp.asarray(perm, BF),
        jnp.asarray(spread, BF),
        jnp.asarray(pick, BF),
        jnp.asarray(tabs, F32),
    )


class Place:
    def __init__(self):
        dp = lax.axis_index("dp")
        self.z = lax.axis_index("row")
        self.y = lax.axis_index("col")
        self.x = dp // 2
        self.c = dp % 2
        self.zh = self.z // 2
        self.zl = self.z % 2
        self.m = self.zl * 2 + self.c
        self.dp = dp

    def mate(self, r):
        c = 1 - self.c if r % 2 else self.c
        zl = 1 - self.zl if r // 2 else self.zl
        return zl * 2 + c, (self.x * 2 + c, self.zh * 2 + zl, self.y)

    def xpeer(self):
        return ((1 - self.x) * 2 + self.c, self.z, self.y)

    def ypeer(self):
        return (self.dp, self.z, 1 - self.y)

    def zpeer(self):
        return (self.dp, (1 - self.zh) * 2 + self.zl, self.y)

    def item_home(self, j):
        return (self.x * 2 + self.zh, j, self.c)

    def item_source(self, blk):
        return (self.x * 2 + self.y, self.c * 2 + blk // 2, blk % 2)

    def is_me(self, dev):
        return (dev[0] == self.dp) & (dev[1] == self.z) & (dev[2] == self.y)


class Link:
    def __init__(self, here, ssem, rsem):
        self.here, self.ssem, self.rsem, self.n, self.open = here, ssem, rsem, 0, []

    def greet(self, items):
        here = self.here
        bar = pltpu.get_barrier_semaphore()
        devs = [here.mate(r)[1] for r in (1, 2, 3)]
        devs += [here.xpeer(), here.ypeer(), here.zpeer()]
        devs += [near(here, r)[3] for r in range(1, 8)] + [along_z(here, r)[1] for r in (1, 2, 3)]
        for d in devs:
            pl.semaphore_signal(bar, inc=1, device_id=d, device_id_type=MESH)
        total = len(devs)
        if items:
            for d in [here.item_home(j) for j in range(4)] + [here.item_source(j) for j in range(4)]:


                @pl.when(jnp.logical_not(here.is_me(d)))
                def _():
                    pl.semaphore_signal(bar, inc=1, device_id=d, device_id_type=MESH)

            far = (here.zh - here.c) * (here.zh - here.c)
            off = (here.y - here.c) * (here.y - here.c)
            total += 8 - 2 * (1 - far) * (1 - off)
        pl.semaphore_wait(bar, total)

    def send(self, src, dst, dev):
        k = self.n
        self.n += 1
        copy = pltpu.make_async_remote_copy(
            src_ref=src,
            dst_ref=dst,
            send_sem=self.ssem.at[k],
            recv_sem=self.rsem.at[k],
            device_id=dev,
            device_id_type=MESH,
        )
        copy.start()
        self.open.append(copy)
        return copy

    def scatter(self, src_of, dst, dev_of, slot):
        base = self.n
        self.n += 4
        here = self.here
        copies = []
        for j in range(4):
            dev = dev_of(j)
            mine = here.is_me(dev)
            remote = pltpu.make_async_remote_copy(
                src_ref=src_of(j),
                dst_ref=dst,
                send_sem=self.ssem.at[base + j],
                recv_sem=self.rsem.at[base + slot],
                device_id=dev,
                device_id_type=MESH,
            )
            local_copy = pltpu.make_async_copy(src_of(j), dst, self.rsem.at[base + slot])

            @pl.when(mine)
            def _():
                local_copy.start()

            @pl.when(jnp.logical_not(mine))
            def _():
                remote.start()

            copies.append((mine, remote))

        def wait_send():
            for mine, remote in copies:

                @pl.when(jnp.logical_not(mine))
                def _():
                    remote.wait_send()

        def wait_recv(src, dst_of):
            for j in range(4):
                pltpu.make_async_copy(src, dst_of(j), self.rsem.at[base + j]).wait()

        return wait_send, wait_recv

    def settle(self, *copies):
        for copy in copies:
            copy.wait_send()
            self.open = [c for c in self.open if c is not copy]

    def finish(self):
        for copy in self.open:
            copy.wait_send()
        self.open = []


def norm_rows(x):
    mean = jnp.sum(x, -1, keepdims=True) * (1.0 / D)
    cent = x - mean
    var = jnp.sum(cent * cent, -1, keepdims=True) * (1.0 / D)
    recip = lax.rsqrt(var + EPSILON)
    return cent * recip, recip


def norm_rows_back(g, y, recip):
    mg = jnp.sum(g, -1, keepdims=True) * (1.0 / D)
    mgy = jnp.sum(g * y, -1, keepdims=True) * (1.0 / D)
    return recip * (g - mg - y * mgy)


def at(i, n):
    return pl.ds(pl.multiple_of(i * n, n), n)


class Gather:
    def __init__(self, link, ref, rows, lo, split, hi):
        self.link, self.ref, self.rows = link, ref, rows
        self.ca, self.cb = pl.ds(lo, split - lo), pl.ds(split, hi - split)
        self.all = slice(None) if hi - lo == ref.shape[-1] else pl.ds(lo, hi - lo)

    def cut(self, i, j, k, cols):
        return self.ref.at[i, j, k, pl.ds(0, self.rows), cols]

    def hop1(self):
        h = self.link.here
        part = self.cut(h.x, h.zh, h.y, self.all)
        self.a = self.link.send(part, part, h.zpeer())

    def hop2(self):
        h = self.link.here
        self.a.wait_recv()
        pa = self.cut(h.x, slice(None), h.y, self.ca)
        pb = self.cut(h.x, slice(None), h.y, self.cb)
        self.a = self.link.send(pa, pa, h.xpeer())
        self.b = self.link.send(pb, pb, h.ypeer())

    def hop3(self):
        h = self.link.here
        self.a.wait_recv()
        self.b.wait_recv()
        pa = self.cut(slice(None), slice(None), h.y, self.ca)
        pb = self.cut(h.x, slice(None), slice(None), self.cb)
        self.a = self.link.send(pa, pa, h.ypeer())
        self.b = self.link.send(pb, pb, h.xpeer())

    def done(self):
        self.a.wait_recv()
        self.b.wait_recv()


class Reduce:
    def __init__(self, link, ref, bufs, lo, split, hi):
        self.link, self.ref, self.lo, self.split, self.hi = link, ref, lo, split, hi
        self.r1a, self.r1b, self.r2a, self.r2b, self.r3a, self.r3b = bufs

    @staticmethod
    def buffers(rows, cols, split):
        rest = cols - split
        return [
            pltpu.VMEM((2, 2, rows, split), BF),
            pltpu.VMEM((2, 2, rows, rest), BF),
            pltpu.VMEM((2, rows, split), BF),
            pltpu.VMEM((2, rows, rest), BF),
            pltpu.VMEM((rows, split), BF),
            pltpu.VMEM((rows, rest), BF),
        ]

    def hop1(self):
        h = self.link.here
        ca, cb = pl.ds(self.lo, self.split - self.lo), pl.ds(self.split, self.hi - self.split)
        self.a = self.link.send(self.ref.at[1 - h.x, :, :, :, ca], self.r1a, h.xpeer())
        self.b = self.link.send(self.ref.at[:, :, 1 - h.y, :, cb], self.r1b, h.ypeer())

    def hop2(self):
        h = self.link.here
        ca, cb = pl.ds(self.lo, self.split - self.lo), pl.ds(self.split, self.hi - self.split)
        self.a.wait_recv()
        self.b.wait_recv()

        def add(i, carry):
            u, v = i // 2, i % 2
            own = self.ref[h.x, u, v, :, ca].astype(F32)
            self.r1a[u, v] = (self.r1a[u, v].astype(F32) + own).astype(BF)
            own = self.ref[u, v, h.y, :, cb].astype(F32)
            self.r1b[u, v] = (self.r1b[u, v].astype(F32) + own).astype(BF)
            return carry

        lax.fori_loop(0, 4, add, 0)
        self.a = self.link.send(self.r1a.at[:, 1 - h.y], self.r2a, h.ypeer())
        self.b = self.link.send(self.r1b.at[1 - h.x], self.r2b, h.xpeer())

    def hop3(self):
        h = self.link.here
        self.a.wait_recv()
        self.b.wait_recv()

        def add(u, carry):
            own = self.r1a[u, h.y].astype(F32)
            self.r2a[u] = (self.r2a[u].astype(F32) + own).astype(BF)
            own = self.r1b[h.x, u].astype(F32)
            self.r2b[u] = (self.r2b[u].astype(F32) + own).astype(BF)
            return carry

        lax.fori_loop(0, 2, add, 0)
        self.a = self.link.send(self.r2a.at[1 - h.zh], self.r3a, h.zpeer())
        self.b = self.link.send(self.r2b.at[1 - h.zh], self.r3b, h.zpeer())

    def done(self):
        h = self.link.here
        self.a.wait_recv()
        self.b.wait_recv()
        left = self.r2a[h.zh].astype(F32) + self.r3a[...].astype(F32)
        right = self.r2b[h.zh].astype(F32) + self.r3b[...].astype(F32)
        return left.astype(BF), right.astype(BF)


class RowGather:
    def __init__(self, link, ref):
        self.link, self.ref = link, ref
        here = link.here
        own = ref.at[at(here.m, TOK)]
        self.far = link.send(own, own, here.mate(2)[1])
        self.near = link.send(own, own, here.mate(1)[1])

    def near_done(self):
        self.near.wait_recv()

    def pass_on(self):
        here = self.link.here
        self.far.wait_recv()
        rows = self.ref.at[at(here.mate(2)[0], TOK)]
        self.last = self.link.send(rows, rows, here.mate(1)[1])

    def last_done(self):
        self.last.wait_recv()


class RowReduce:
    def __init__(self, link, out, into):
        self.link, self.out, self.into = link, out, into

    def give(self, r, val):
        i = 0 if r == 3 else 1
        if val is not None:
            self.out[i] = val.astype(BF)
        sent = self.link.send(self.out.at[i], self.into.at[i], self.link.here.mate(1)[1])
        if r == 3:
            self.s3 = sent
        else:
            self.s1 = sent

    def keep_far(self, val):
        self.out[2] = val.astype(BF)

    def pass_on(self):
        self.s3.wait_recv()

        def add(i, carry):
            rows = at(i, 32)
            both = self.out[2, rows, :].astype(F32) + self.into[0, rows, :].astype(F32)
            self.out[2, rows, :] = both.astype(BF)
            return carry

        lax.fori_loop(0, 8, add, 0)
        self.s2 = self.link.send(self.out.at[2], self.into.at[2], self.link.here.mate(2)[1])

    def arrive(self):
        self.s1.wait_recv()
        self.s2.wait_recv()

    def total(self, rows):
        return self.into[1, rows, :].astype(F32) + self.into[2, rows, :].astype(F32)


def turn(v, cos, sina, sinb):
    return v * cos + pltpu.roll(v, 127, 1) * sina + pltpu.roll(v, 1, 1) * sinb


def turn_back(d, cos, sina, sinb):
    return d * cos - pltpu.roll(d, 127, 1) * sina - pltpu.roll(d, 1, 1) * sinb


def near(here, r):
    x = 1 - here.x if r // 4 else here.x
    c = 1 - here.c if r // 2 % 2 else here.c
    y = 1 - here.y if r % 2 else here.y
    return x, c, y, (x * 2 + c, here.z, y)


def along_z(here, r):
    z = (here.z + r) % 4
    return z, (here.dp, z, here.y)


def shard_parts(s):
    x, c, zh, zl, y = s // 16, s // 8 % 2, s // 4 % 2, s // 2 % 2, s % 2
    member, spot = zl * 2 + c, (x * 2 + zh) * 2 + y
    return spot * 4 + member, member, spot


def three(v):
    hi = v.astype(BF)
    rest = v - hi.astype(F32)
    mid = rest.astype(BF)
    return jnp.concatenate([hi, mid, (rest - mid.astype(F32)).astype(BF)], 0)


def by_member(src, out, tmp, width, pieces):
    cols = pieces * 4 * width
    for t in range(pieces):
        for h in range(16):
            unit = shard_parts(h * 2)
            dst = t * 4 * width + unit[2] // 2 * width
            tmp[unit[1], 0:UNIT, dst : dst + width] = src[
                :, (t * 16 + h) * width : (t * 16 + h + 1) * width
            ].astype(F32)
    for m in range(4):
        out[m] = tmp[m, :, 0:cols].astype(BF)


def by_column(src, out, width, pieces):
    for t in range(pieces):
        for h in range(16):
            unit = shard_parts(h * 2)
            at_ = t * 4 * width + unit[2] // 2 * width
            out[:, (t * 16 + h) * width : (t * 16 + h + 1) * width] = src[
                unit[1], 0:UNIT, at_ : at_ + width
            ].astype(F32)


def silu_slope(v):
    sig = jax.nn.sigmoid(v)
    return sig * (1.0 + v * (1.0 - sig))


def kernel_a(
    tok_in, cot_in, wqkv, wgu, wp_in, wd_in, cond, w_mod_t, vecs, perm, spread, pick, tabs,
    wq_out, wp_out, wg_out, wd_out, ha_out, raw_out, rot_out, att_out, hm, dmlp, tokp, og, attn_out,
    condg, modv, bg, bd, gains, maskb, valid,
    wq, wp, wg, wd, ha, raw, rot, att, s0q, s0g, tokr, cotr, wqe, psend, precv, pown,
    wqs, wgs, tmp, block, msg, p1, m2, got, bq4, bg4, bp, ssem, rsem, lsem,
):
    here = Place()
    link = Link(here, ssem, rsem)
    fetch = Fetch(lsem)
    m = here.m
    block[...] = jnp.zeros_like(block)
    block[0:4, :] = cond[...].astype(F32)
    block[4:5, 0:8] = vecs[5:6, 0:8]
    condg[here.dp] = block[...]
    link.greet(True)
    slot = here.zl * 2 + here.y
    rows_in = at(slot, 64)
    cs = [link.send(block, condg.at[here.dp], near(here, r)[3]) for r in (2, 4, 6)]
    tmp[...] = jnp.zeros_like(tmp)
    by_member(wqkv, wqs, tmp, 72, 3)
    for c in cs:
        c.wait_recv()
    v = condg[...].reshape(32, D)
    part = nt((v * jax.nn.sigmoid(v)).astype(BF), w_mod_t[...]) + vecs[0:1, 0:216]
    for z in range(4):
        msg[z, 4:6, :] = vecs[1:3, :]
        for d in range(4):
            msg[z, d : d + 1, 0:216] = part[d * 8 + z : d * 8 + z + 1, :]
    zs = []
    for r in (1, 2, 3):
        z, dev = along_z(here, r)
        zs.append(link.send(msg.at[z], p1.at[here.z], dev))
    p1[here.z] = msg[here.z]

    sq, sg = {}, {}
    for r in (2, 3, 1):
        k, dev = here.mate(r)
        sq[r] = link.send(wqs.at[k], s0q.at[m], dev)
    own_q = fetch.go(wqs.at[m], s0q.at[m])
    gq = Gather(link, wq, 144, 0, SPLIT_Q, 864)
    gp = Gather(link, wp, PAD, 0, SPLIT_P, D)
    g1 = Gather(link, wg, 144, 0, 384, 768)
    g2 = Gather(link, wg, 144, 768, 1152, 1536)
    gd = Gather(link, wd, 96, 0, SPLIT_D, D)
    by_member(wgu, wgs, tmp, 192, 2)
    for c in zs:
        c.wait_recv()
    for z in range(4):
        for d in range(4):
            m2[d, z, 0:1, :] = p1[z, d : d + 1, :]
            m2[d, z, 1:3, :] = p1[z, 4:6, :]
    ns = []
    for r in range(1, 8):
        x, _, y, dev = near(here, r)
        ns.append(link.send(m2.at[x * 2 + y], got.at[here.x, here.c, here.y], dev))
    got[here.x, here.c, here.y] = m2[here.x * 2 + here.y]
    tok_sent, tok_got = link.scatter(lambda j: tok_in.at[j], tokr.at[rows_in], here.item_home, slot)

    own_q.wait()
    for r in (1, 2, 3):
        sq[r].wait_recv()
    wq[here.x, here.zh, here.y] = nn(pick[...], s0q[...].reshape(192, 864)).astype(BF)
    gq.hop1()
    for r in (2, 3, 1):
        k, dev = here.mate(r)
        sg[r] = link.send(wgs.at[k], s0g.at[m], dev)
    own_g = fetch.go(wgs.at[m], s0g.at[m])
    wp[:, :, :, PAD:64, :] = jnp.zeros((2, 2, 2, 64 - PAD, D), BF)
    tmp[0, 0:UNIT, 0:D] = nn(wp_in[...], perm[...])
    tmp[0, UNIT:PAD, :] = jnp.zeros((PAD - UNIT, 1536), F32)
    wp[here.x, here.zh, here.y, 0:PAD, :] = tmp[0, :, 0:D].astype(BF)
    gp.hop1()
    ext = condg[here.x * 2 + here.y, 4:5, :]
    lane = lax.broadcasted_iota(jnp.int32, (1, D), 1)
    spot = lax.broadcasted_iota(jnp.int32, (1, 512), 1)
    row_at = spot // 128 * 4 + spot // 16 % 4
    col_at = spot // 64 % 2 * 16 + spot % 16

    def extent(item, first):
        return jnp.sum(jnp.where(lane == item + first, ext, 0.0), -1, keepdims=True)

    for i in range(2):
        tall, wide = extent(here.zh * 2 + i, 0), extent(here.zh * 2 + i, 4)
        live = (row_at.astype(F32) < tall) & (col_at.astype(F32) < wide)
        maskb[i] = jnp.where(live, 0.0, MASKED)
    spot = lax.broadcasted_iota(jnp.int32, (TOK, 1), 0) + here.c * TOK
    row_at = (spot // 128 * 4 + spot // 16 % 4).astype(F32)
    col_at = (spot // 64 % 2 * 16 + spot % 16).astype(F32)
    live = (row_at < extent(here.z, 0)) & (col_at < extent(here.z, 4))
    valid[...] = jnp.where(live, 1.0, 0.0)
    gains[...] = jnp.zeros_like(gains)
    for t in range(2):
        for e in range(2):
            gains[t : t + 1, e * 64 : e * 64 + UNIT] = vecs[3 + t : 4 + t, e * UNIT : e * UNIT + UNIT]
    for c in ns:
        c.wait_recv()
    modv[...] = jnp.zeros_like(modv)
    bq4[...] = jnp.zeros_like(bq4)
    for s in range(32):
        line = got[s // 16, s // 8 % 2, s % 2, s // 2 % 4]
        for q in range(6):
            piece, unit = divmod(6 * s + q, 32)
            to = shard_parts(unit)[0] * UNIT
            modv[piece : piece + 1, to : to + UNIT] = line[0:1, q * UNIT : q * UNIT + UNIT]
        for q in range(3):
            piece, unit = divmod(3 * s + q, 32)
            _, member, spot = shard_parts(unit)
            to = piece * 512 + spot * 64
            bq4[member, :, to : to + UNIT] = line[1:2, q * UNIT : q * UNIT + UNIT]
        to = shard_parts(s)[0] * UNIT
        bp[:, to : to + UNIT] = line[1:2, 108:144]
        bd[:, to : to + UNIT] = line[1:2, 144:180]
        for q in range(2):
            piece, unit = divmod(2 * s + q, 32)
            _, member, spot = shard_parts(unit)
            to = piece * 768 + spot * 96
            bg4[member, :, to : to + 96] = line[2:3, q * 96 : q * 96 + 96]
    bg[...] = bg4[m]
    tok_got(tok_in.at[0], lambda j: tokr.at[pl.ds(j * 64, 64)])
    tokp[...] = nn(tokr[...], perm[...]).astype(BF)

    def first_norm(i, carry):
        n, _ = norm_rows(tokp[at(i, 32), :].astype(F32))
        h = n * (1.0 + modv[1:2, :]) + modv[0:1, :]
        ha[pl.ds(pl.multiple_of(m * TOK + i * 32, 32), 32), :] = h.astype(BF)
        return carry

    lax.fori_loop(0, 8, first_norm, 0)
    ha_all = RowGather(link, ha)
    own_g.wait()
    for r in (1, 2, 3):
        sg[r].wait_recv()
    wg[here.x, here.zh, here.y] = nn(pick[...], s0g[...].reshape(192, 1536)).astype(BF)
    g1.hop1()
    g2.hop1()
    wd[here.x, here.zh, here.y] = nn(wd_in[...], perm[...]).astype(BF)
    gd.hop1()
    gq.hop2()
    gp.hop2()
    gq.hop3()
    gq.done()
    outs = [fetch.go(wq, wq_out)]

    def widen(i, carry):
        part = wq[i // 2, i % 2].reshape(288, 864)
        wqe[at(i, 288), :] = nn(part, spread[...]).astype(BF)
        return carry

    lax.fori_loop(0, 4, widen, 0)

    g1.hop2()
    cot_sent, cot_got = link.scatter(lambda j: cot_in.at[j], cotr.at[rows_in], here.item_home, slot)
    ha_all.pass_on()
    g1.hop3()
    gp.hop3()
    ha_all.near_done()
    ha_all.last_done()
    outs.append(fetch.go(ha, ha_out))

    def project(b, carry):
        acc = nn(ha[at(b, TOK), :], wqe[...]) + bq4[m]
        item, half = b // 2, at(b % 2, TOK)
        cos, sina, sinb = tabs[0, half, :], tabs[1, half, :], tabs[2, half, :]
        for h in range(4):
            p = item * 4 + h
            for t in range(2):
                v = acc[:, t * 512 + h * 128 : t * 512 + h * 128 + 128]
                recip = lax.rsqrt(jnp.sum(v * v, -1, keepdims=True) * (1.0 / HEAD) + EPSILON)
                raw[p, t, half, :] = v
                n = v * recip * gains[t : t + 1, :]
                rot[p, t, half, :] = turn(n, cos, sina, sinb).astype(BF)
            rot[p, 2, half, :] = acc[:, 1024 + h * 128 : 1152 + h * 128].astype(BF)
        return carry

    def attend(p, carry):
        item = p // 4
        lanes = at(p % 4, 128)
        for half in range(2):
            rows = pl.ds(half * TOK, TOK)
            e = jnp.exp2(nt(rot[p, 0, rows, :], rot[p, 1]) * ROOT2 + maskb[item])
            pr = (e * (1.0 / jnp.sum(e, -1, keepdims=True))).astype(BF)
            out_rows = pl.ds(pl.multiple_of(item * 512 + half * TOK, TOK), TOK)
            att[out_rows, lanes] = nn(pr, rot[p, 2]).astype(BF)
        return carry

    other = 1 - here.zl
    lax.fori_loop(other * 2, other * 2 + 2, project, 0)
    g2.hop2()
    lax.fori_loop(other * 4, other * 4 + 4, attend, 0)
    g2.hop3()
    gd.hop2()
    gp.done()
    outs.append(fetch.go(wp, wp_out))
    wpf = wp[...].reshape(512, D)
    red = RowReduce(link, psend, precv)
    red.give(3, nn(att[at(here.mate(3)[0], TOK), :], wpf))
    red.keep_far(nn(att[at(here.mate(2)[0], TOK), :], wpf))
    red.pass_on()
    lax.fori_loop(here.zl * 2, here.zl * 2 + 2, project, 0)
    cot_got(cot_in.at[0], lambda j: cotr.at[pl.ds(j * 64, 64)])
    og[...] = (nn(cotr[...], perm[...]) * valid[...]).astype(BF)

    def scale_grad(i, carry):
        g = og[at(i, 32), :].astype(F32) * modv[5:6, :]
        dmlp[pl.ds(pl.multiple_of(m * TOK + i * 32, 32), 32), :] = g.astype(BF)
        return carry

    lax.fori_loop(0, 8, scale_grad, 0)
    dm_all = RowGather(link, dmlp)
    outs.append(fetch.go(raw, raw_out))
    outs.append(fetch.go(rot, rot_out))
    gd.hop3()
    lax.fori_loop(here.zl * 4, here.zl * 4 + 4, attend, 0)
    outs.append(fetch.go(att, att_out))
    red.give(1, nn(att[at(here.mate(1)[0], TOK), :], wpf))
    pown[...] = nn(att[at(m, TOK), :], wpf)
    red.arrive()

    def second_norm(i, carry):
        rows = at(i, 32)
        a = pown[rows, :] + bp[...] + red.total(rows)
        attn_out[rows, :] = a
        n, _ = norm_rows(tokp[rows, :].astype(F32) + modv[2:3, :] * a)
        h = n * (1.0 + modv[4:5, :]) + modv[3:4, :]
        hm[rows, :] = h.astype(BF)
        return carry

    lax.fori_loop(0, 8, second_norm, 0)
    g1.done()
    g2.done()
    outs.append(fetch.go(wg, wg_out))
    gd.done()
    outs.append(fetch.go(wd, wd_out))
    dm_all.pass_on()
    dm_all.near_done()
    dm_all.last_done()
    for c in outs:
        c.wait()
    link.finish()
    tok_sent()
    cot_sent()


def store_tiles(val, ref, base, piece, keep):
    block = ref.shape[3] if keep is None else piece
    for q in range(val.shape[0] // piece):
        row = base + q * piece
        f, off = row // block, row % block
        n = piece if keep is None else keep
        part = val[q * piece : q * piece + n, :].astype(BF)
        ref[f // 4, f // 2 % 2, f % 2, off : off + n, 0 : val.shape[1]] = part


class Fetch:
    def __init__(self, sems):
        self.sems, self.n = sems, 0

    def go(self, src, dst):
        copy = pltpu.make_async_copy(src, dst, self.sems.at[self.n])
        self.n += 1
        copy.start()
        return copy


def kernel_b(
    wg_in, wd_in, hm_in, dm_in, tok_in, og_in, attn_in, att_in, wp_in, wq_in, ha_in, raw_in, rot_in, perm_in,
    spread_in, tabs_in, modv, bg, bd, gains, maskb, valid, pick, condg, w_mod_t,
    dtok, bout, g_qkv, g_gu, fp, fd, dwm, sums, dbm, dcond,
    wg, wd, hm, dmlp, tokp, og, attn_out, att, wp, wq, perm, tabs, gu, coef, hid, rsend, rrecv, mrecv, own32,
    dwg, dwd, dwp, dattn, raw, rot, to, bo, fq, fg, small, dbg, dbq, dgain,
    pk, q1, m2, q2, dm, e0, e1, e2, e3, line, bq4, bg4, slope,
    g1a, g1b, g2a, g2b, g3a, g3b, h1a, h1b, h2a, h2b, h3a, h3b, d1a, d1b, d2a, d2b, d3a, d3b,
    q1a, q1b, q2a, q2b, q3a, q3b, p1a, p1b, p2a, p2b, p3a, p3b, ssem, rsem, lsem,
):
    here = Place()
    link = Link(here, ssem, rsem)
    fetch = Fetch(lsem)
    m = here.m
    k1, k2, k3 = here.mate(1)[0], here.mate(2)[0], here.mate(3)[0]
    at_m, at_1, at_2, at_3 = at(m, TOK), at(k1, TOK), at(k2, TOK), at(k3, TOK)
    get_hm = fetch.go(hm_in, hm.at[at_m])
    get_dm = fetch.go(dm_in, dmlp)
    get_wg = fetch.go(wg_in, wg)
    get_wd = fetch.go(wd_in, wd)
    gets = [fetch.go(a, b) for a, b in ((tok_in, tokp), (og_in, og), (attn_in, attn_out))]
    get_wp = fetch.go(wp_in, wp)
    gets2 = [fetch.go(a, b) for a, b in ((tabs_in, tabs), (att_in, att), (wq_in, wq), (perm_in, perm))]
    base = fetch.n
    fetch.n += 4
    link.greet(True)
    get_hm.wait()
    hm_all = RowGather(link, hm)
    small[...] = jnp.zeros_like(small)
    dbg[...] = jnp.zeros_like(dbg)
    dbq[...] = jnp.zeros_like(dbq)
    dgain[...] = jnp.zeros_like(dgain)
    get_wg.wait()
    get_wd.wait()
    get_dm.wait()

    def wgf():
        return wg[...].reshape(D, 1536)

    def wdf():
        return wd[...].reshape(768, D)

    def mlp(k):
        gu[...] = nn(hm[at(k, TOK), :], wgf()) + bg[...]

        def acts(i, carry):
            rows = at(i, 32)
            out = pl.ds(pl.multiple_of(k * TOK + i * 32, 32), 32)
            g, u = gu[rows, 0:768], gu[rows, 768:1536]
            sig = jax.nn.sigmoid(g)
            act = g * sig
            hid[out, :] = (act * u).astype(BF)
            gu[rows, 0:768] = u * sig * (1.0 + g * (1.0 - sig))
            gu[rows, 768:1536] = act
            return carry

        lax.fori_loop(0, 8, acts, 0)
        dh = nt(dmlp[at(k, TOK), :], wdf())
        out = at(k, TOK)
        coef[out, 0:768] = (gu[:, 0:768] * dh).astype(BF)
        coef[out, 768:1536] = (gu[:, 768:1536] * dh).astype(BF)
        dbg[0:1, :] += jnp.sum(coef[out, :].astype(F32), 0, keepdims=True)
        return nt(coef[out, :], wgf())

    hred = RowReduce(link, rsend, rrecv)
    own32[...] = mlp(m)
    hm_all.near_done()
    hred.give(1, mlp(k1))
    hm_all.pass_on()
    hred.keep_far(mlp(k2))
    hm_all.last_done()
    hred.give(3, mlp(k3))
    hred.pass_on()

    ra = Reduce(link, dwg, (g1a, g1b, g2a, g2b, g3a, g3b), 0, 384, 768)
    rb = Reduce(link, dwg, (h1a, h1b, h2a, h2b, h3a, h3b), 768, 1152, 1536)
    rd = Reduce(link, dwd, (d1a, d1b, d2a, d2b, d3a, d3b), 0, SPLIT_D, D)
    rq = Reduce(link, wg, (q1a, q1b, q2a, q2b, q3a, q3b), 0, SPLIT_Q, 896)
    rp = Reduce(link, dwp, (p1a, p1b, p2a, p2b, p3a, p3b), 0, SPLIT_P, D)
    for n, red in ((0, ra), (1, rb)):
        cols = slice(n * 768, n * 768 + 768)
        for i in range(3):
            t = tn(hm[:, i * 384 : i * 384 + 384], coef[:, cols])
            for q in range(8):
                row = i * 384 + q * 48
                f, off = row // 144, row % 144
                dwg[f // 4, f // 2 % 2, f % 2, off : off + 48, cols] = t[q * 48 : q * 48 + 48].astype(BF)
        red.hop1()
    spread_got = fetch.go(spread_in, wg)
    for i in range(2):
        store_tiles(tn(hid[:, i * 384 : i * 384 + 384], dmlp[...]), dwd, i * 384, 96, None)
    rd.hop1()
    link.settle(hred.s1, hred.s3)
    mred = RowReduce(link, rsend, mrecv)
    mred.give(3, nn(hid[at_3, :], wdf()))
    mred.give(1, nn(hid[at_1, :], wdf()))
    bo[...] = nn(hid[at_m, :], wdf()).astype(BF)
    for c in gets:
        c.wait()
    hred.arrive()

    def mid_back(i, carry):
        rows = at(i, 32)
        mine = pl.ds(pl.multiple_of(m * TOK + i * 32, 32), 32)
        d = own32[rows, :] + hred.total(rows)
        a = attn_out[rows, :]
        n, recip = norm_rows(tokp[rows, :].astype(F32) + modv[2:3, :] * a)
        small[1:2, :] += jnp.sum(d, 0, keepdims=True)
        small[2:3, :] += jnp.sum(d * n, 0, keepdims=True)
        g = og[rows, :].astype(F32) + norm_rows_back(d * (1.0 + modv[4:5, :]), n, recip)
        gu[rows, 0:D] = g
        small[3:4, :] += jnp.sum(g * a, 0, keepdims=True)
        low = (modv[2:3, :] * g).astype(BF)
        dattn[mine, :] = low
        small[5:6, :] += jnp.sum(low.astype(F32), 0, keepdims=True)
        small[4:5, :] += jnp.sum(dmlp[mine, :].astype(F32), 0, keepdims=True)
        return carry

    lax.fori_loop(0, 8, mid_back, 0)
    da_all = RowGather(link, dattn)
    link.settle(hred.s2, hm_all.far, hm_all.near, hm_all.last)
    ha_got = fetch.go(ha_in, dmlp)
    mred.keep_far(nn(hid[at_2, :], wdf()))
    da_all.near_done()

    def pair_of(n):
        item = here.zl + (1 - 2 * here.zl) * (n // 4)
        return item, item * 4 + n % 4

    def pair_copies(n):
        p = pair_of(n)[1]
        s = n % 2
        return (
            pltpu.make_async_copy(raw_in.at[p], raw.at[s], lsem.at[base + 2 * s]),
            pltpu.make_async_copy(rot_in.at[p], rot.at[s], lsem.at[base + 2 * s + 1]),
        )

    for c in pair_copies(0):
        c.start()
    get_wp.wait()
    for c in gets2:
        c.wait()

    def back_proj(rows):
        hid[rows, 0:512] = nt(dattn[rows, :], wp[...].reshape(512, D)).astype(BF)

    def attend_back(n, carry):
        item, p = pair_of(n)
        s = n % 2
        lanes = at(n % 4, 128)
        for c in pair_copies(n):
            c.wait()

        @pl.when(n < 7)
        def _():
            for c in pair_copies(n + 1):
                c.start()

        dk = jnp.zeros((512, 128), F32)
        dv = jnp.zeros((512, 128), F32)

        def head_back_store(d, t, rows, out_rows):
            cos, sina, sinb = tabs[0, rows, :], tabs[1, rows, :], tabs[2, rows, :]
            v = raw[s, t, rows, :]
            recip = lax.rsqrt(jnp.sum(v * v, -1, keepdims=True) * (1.0 / HEAD) + EPSILON)
            dn = turn_back(d, cos, sina, sinb)
            dgain[t : t + 1, :] += jnp.sum(dn * v * recip, 0, keepdims=True)
            u = dn * gains[t : t + 1, :]
            mean = jnp.sum(u * v, -1, keepdims=True) * (1.0 / HEAD)
            res = recip * u - v * (recip * recip * recip * mean)
            coef[out_rows, at(t * 4 + n % 4, 128)] = res.astype(BF)

        for half in range(2):
            rows = pl.ds(half * TOK, TOK)
            out_rows = pl.ds(pl.multiple_of(item * 512 + half * TOK, TOK), TOK)
            do = hid[out_rows, lanes]
            e = jnp.exp2(nt(rot[s, 0, rows, :], rot[s, 1]) * ROOT2 + maskb[item])
            pf = e * (1.0 / jnp.sum(e, -1, keepdims=True))
            dp = nt(do, rot[s, 2])
            delta = jnp.sum(pf * dp, -1, keepdims=True)
            ds = (pf * (dp - delta)).astype(BF)
            dq = nn(ds, rot[s, 1]) * ROOT
            dk += tn(ds, rot[s, 0, rows, :])
            dv += tn(pf.astype(BF), do)
            head_back_store(dq, 0, rows, out_rows)
        dk = dk * ROOT
        for half in range(2):
            rows = pl.ds(half * TOK, TOK)
            out_rows = pl.ds(pl.multiple_of(item * 512 + half * TOK, TOK), TOK)
            head_back_store(dk[half * TOK : half * TOK + TOK], 1, rows, out_rows)
        coef[at(item, 512), at(8 + n % 4, 128)] = dv.astype(BF)
        return carry

    back_proj(at_m)
    back_proj(at_1)
    lax.fori_loop(0, 3, attend_back, 0)
    da_all.pass_on()
    mred.pass_on()
    ra.hop2()
    lax.fori_loop(3, 4, attend_back, 0)
    da_all.last_done()
    rb.hop2()
    back_proj(at_2)
    back_proj(at_3)
    store_tiles(tn(att[...], dattn[...]), dwp, 0, 64, PAD)
    rp.hop1()
    ra.hop3()
    lax.fori_loop(4, 5, attend_back, 0)
    rd.hop2()
    rb.hop3()
    lax.fori_loop(5, 6, attend_back, 0)
    mred.arrive()

    def finish_out(i, carry):
        rows = at(i, 32)
        o = bo[rows, :].astype(F32) + bd[...] + mred.total(rows)
        small[0:1, :] += jnp.sum(og[rows, :].astype(F32) * o, 0, keepdims=True)
        mid = tokp[rows, :].astype(F32) + modv[2:3, :] * attn_out[rows, :]
        bo[rows, :] = ((mid + modv[5:6, :] * o) * valid[rows, :]).astype(BF)
        return carry

    lax.fori_loop(0, 8, finish_out, 0)
    bo[...] = nt(bo[...], perm[...]).astype(BF)
    b_sent, b_got = link.scatter(
        lambda j: bo.at[pl.ds(j * 64, 64)], bout.at[here.z], here.item_source, here.z
    )
    lax.fori_loop(6, 7, attend_back, 0)
    rp.hop2()
    lax.fori_loop(7, 8, attend_back, 0)
    spread_got.wait()

    def squeeze(rows):
        v = coef[rows, :]
        dbq[0:1, :] += jnp.sum(v.astype(F32), 0, keepdims=True)
        hm[rows, 0:864] = nt(v, wg[...].reshape(D, 1536)[0:864]).astype(BF)

    def to_input(rows):
        return nt(hm[rows, 0:864], wq[...].reshape(D, 864))

    link.settle(mred.s1, mred.s2, mred.s3)
    tred = RowReduce(link, rsend, rrecv)
    squeeze(at_3)
    tred.give(3, to_input(at_3))
    squeeze(at_2)
    tred.keep_far(to_input(at_2))
    tred.pass_on()
    rd.hop3()
    squeeze(at_1)
    tred.give(1, to_input(at_1))
    squeeze(at_m)
    own32[...] = to_input(at_m)
    pk[...] = jnp.zeros_like(pk)
    bq4[...] = jnp.zeros_like(bq4)
    bg4[...] = jnp.zeros_like(bg4)
    bq4[m] = dbq[0:1, :]
    bg4[m] = dbg[0:1, :]
    for t in range(2):
        for e in range(2):
            to_ = t * 72 + e * UNIT
            line[:, to_ : to_ + UNIT] = dgain[t : t + 1, e * 64 : e * 64 + UNIT]
    for s in range(32):
        x, c, z, y = s // 16, s // 8 % 2, s // 2 % 4, s % 2
        for q in range(3):
            piece, unit = divmod(2 * s + q, 32) if q < 2 else (2, s)
            _, member, spot = shard_parts(unit)
            from_ = piece * 512 + spot * 64
            pk[x, c, y, z, 1:2, q * UNIT : q * UNIT + UNIT] = bq4[member, :, from_ : from_ + UNIT]
        from_ = shard_parts(s)[0] * UNIT
        pk[x, c, y, z, 1:2, 108:144] = small[5:6, from_ : from_ + UNIT]
        pk[x, c, y, z, 1:2, 144:180] = small[4:5, from_ : from_ + UNIT]
        for q in range(2):
            piece, unit = divmod(2 * s + q, 32)
            _, member, spot = shard_parts(unit)
            from_ = piece * 768 + spot * 96
            pk[x, c, y, z, 2:3, q * 96 : q * 96 + 96] = bg4[member, :, from_ : from_ + 96]
        pk[x, c, y, z, 3:4, 0:144] = line[:, 0:144]
    full_slope = silu_slope(condg[here.dp])
    for b in range(8):
        slope[b] = full_slope[:, b * 144 : b * 144 + 144]
    ha_got.wait()
    for i in range(3):
        store_tiles(tn(dmlp[:, i * 384 : i * 384 + 384], hm[:, 0:864]), wg, i * 384, 48, None)
    rq.hop1()
    rp.hop3()

    def hand_out(reds, base_row, cols, out):
        rows = slice(base_row, base_row + 4 * PAD)
        for red in reds:
            left, right = red.done()
            coef[rows, red.lo : red.split] = tn(pick[...], left).astype(BF)
            coef[rows, red.split : red.hi] = tn(pick[...], right).astype(BF)

        def share(k):
            return coef.at[pl.ds(pl.multiple_of(base_row + k * PAD, 16), PAD), pl.ds(0, cols)]

        over = [link.send(share(here.mate(r)[0]), out.at[m], here.mate(r)[1]) for r in (2, 3, 1)]
        return over, fetch.go(share(m), out.at[m])

    g_over, g_own = hand_out((ra, rb), 0, 1536, fg)
    tred.arrive()

    def first_back(i, carry):
        rows = at(i, 32)
        d = own32[rows, :] + tred.total(rows)
        n, recip = norm_rows(tokp[rows, :].astype(F32))
        small[6:7, :] += jnp.sum(d, 0, keepdims=True)
        small[7:8, :] += jnp.sum(d * n, 0, keepdims=True)
        g = gu[rows, 0:D] + norm_rows_back(d * (1.0 + modv[1:2, :]), n, recip)
        to[rows, :] = g.astype(BF)
        return carry

    lax.fori_loop(0, 8, first_back, 0)
    rows_of = (6, 7, 3, 1, 2, 0)
    for s in range(32):
        x, c, z, y = s // 16, s // 8 % 2, s // 2 % 4, s % 2
        for q in range(6):
            piece, unit = divmod(6 * s + q, 32)
            from_ = shard_parts(unit)[0] * UNIT
            row = rows_of[piece]
            pk[x, c, y, z, 0:1, q * UNIT : q * UNIT + UNIT] = small[row : row + 1, from_ : from_ + UNIT]
    ns = []
    for r in range(1, 8):
        x, c, y, dev = near(here, r)
        ns.append(link.send(pk.at[x, c, y], q1.at[here.x, here.c, here.y], dev))
    q1[here.x, here.c, here.y] = pk[here.x, here.c, here.y]
    rq.hop2()
    to[...] = nt(to[...], perm[...]).astype(BF)
    for n in ns:
        n.wait_recv()
    for z in range(4):
        for x in range(2):
            for y in range(2):
                d = x * 2 + y
                m2[z, d : d + 1, :] = q1[x, 0, y, z, 0:1, :] + q1[x, 1, y, z, 0:1, :]
        total = q1[0, 0, 0, z, 1:4, :]
        for i in range(1, 8):
            total += q1[i // 4, i // 2 % 2, i % 2, z, 1:4, :]
        m2[z, 4:7, :] = total
    zs = []
    for r in (1, 2, 3):
        z, dev = along_z(here, r)
        zs.append(link.send(m2.at[z], q2.at[here.z], dev))
    sent, got = link.scatter(
        lambda j: to.at[pl.ds(j * 64, 64)], dtok.at[here.z], here.item_source, here.z
    )
    rq.hop3()
    q2[here.z] = m2[here.z]
    dm[...] = jnp.zeros_like(dm)
    v = condg[...].reshape(32, D)
    act = (v * jax.nn.sigmoid(v)).astype(BF)

    def plain(red, out):
        left, right = red.done()
        out[...] = nt(left, perm[:, 0 : red.split]) + nt(right, perm[:, red.split : D])

    for c in zs:
        c.wait_recv()
    for z in range(4):
        for d in range(4):
            dm[d * 8 + z : d * 8 + z + 1, :] = q2[z, d : d + 1, 0:216]
    sums[...] = q2[0] + q2[1] + q2[2] + q2[3]
    dbm[...] = jnp.broadcast_to(jnp.sum(dm[...], 0, keepdims=True), (8, 216))
    d3 = three(dm[...])
    da = nn(d3, w_mod_t[...])
    da = da[0:32] + da[32:64] + da[64:96]
    for b in range(8):
        for d in range(4):
            e0[d, b % 2, b // 2] = da[d * 8 : d * 8 + 8, b * 144 : b * 144 + 144]
    ns = []
    for r in range(1, 8):
        x, c, y, dev = near(here, r)
        ns.append(link.send(e0.at[x * 2 + c, y], e1.at[here.x, here.c, here.y], dev))
    e1[here.x, here.c, here.y] = e0[here.dp, here.y]
    plain(rd, fd)
    for n in ns:
        n.wait_recv()
    total = e1[0, 0, 0]
    for i in range(1, 8):
        total += e1[i // 4, i // 2 % 2, i % 2]
    e2[...] = total
    zs = []
    for r in (1, 2, 3):
        z, dev = along_z(here, r)
        zs.append(link.send(e2.at[z], e3.at[here.z], dev))
    e3[here.z] = e2[here.z]
    plain(rp, fp)
    dwm[...] = tn(d3, jnp.concatenate([act, act, act], 0))
    g_own.wait()
    for c in g_over:
        c.wait_recv()
    by_column(fg, g_gu, 192, 2)
    q_over, q_own = hand_out((rq,), 4 * PAD, 896, fq)
    for c in zs:
        c.wait_recv()
    dcond[...] = (e3[0] + e3[1] + e3[2] + e3[3]) * slope[here.z * 2 + here.y]
    q_own.wait()
    for c in q_over:
        c.wait_recv()
    by_column(fq, g_qkv, 72, 3)
    b_got(bo.at[pl.ds(0, 64)], lambda j: bout.at[j])
    got(to.at[pl.ds(0, 64)], lambda j: dtok.at[j])
    link.finish()
    b_sent()
    sent()


def call(kernel, ident, outs, scratch, args, hbm=(), hbm_out=(), sems=64, local=32):
    vm = pl.BlockSpec(memory_space=pltpu.VMEM)
    hb = pl.BlockSpec(memory_space=pltpu.HBM)
    return pl.pallas_call(
        kernel,
        out_shape=[jax.ShapeDtypeStruct(s, t) for s, t in outs],
        in_specs=[hb if i in hbm else vm for i in range(len(args))],
        out_specs=[hb if i in hbm_out else vm for i in range(len(outs))],
        scratch_shapes=scratch + [pltpu.SemaphoreType.DMA((sems,)), pltpu.SemaphoreType.DMA((sems,))]
        + ([pltpu.SemaphoreType.DMA((local,))] if hbm else []),
        compiler_params=pltpu.CompilerParams(
            collective_id=ident, has_side_effects=True, vmem_limit_bytes=LIMIT
        ),
    )(*args)


def local(
    tokens, conditioning, heights, widths, cotangent, w_mod, b_mod, w_qkv, b_qkv, query_gain, key_gain,
    w_proj, b_proj, w_gu, b_gu, w_down, b_down,
):
    args = (
        tokens, conditioning, heights, widths, cotangent, w_mod, b_mod, w_qkv, b_qkv, query_gain, key_gain,
        w_proj, b_proj, w_gu, b_gu, w_down, b_down,
    )
    sizes = tuple(lax.axis_size(a) for a in ("dp", "row", "col"))
    if sizes != (4, 4, 2) or tokens.shape != (4, 4, 16, D):
        return general(*args)
    every = ("dp", "row", "col")
    perm, spread, pick, tabs = constants()
    row = lambda *v: jnp.pad(jnp.concatenate([a.astype(F32) for a in v]), (0, 256 - sum(a.shape[0] for a in v)))
    vecs = [row(b_mod), row(b_qkv, b_proj, b_down), row(b_gu), row(query_gain), row(key_gain), row(heights, widths)]
    vecs = jnp.concatenate(vecs + [jnp.zeros((512,), F32)]).reshape(8, 256)
    w_mod_t = w_mod.T
    full = (GROUP, D)
    block = (TOK, D)
    weights = [(2, 2, 2, 144, 864), (2, 2, 2, 64, D), (2, 2, 2, 144, 1536), (2, 2, 2, 96, D)]
    pairs = [((8, 2, 512, 128), F32), ((8, 3, 512, 128), BF)]
    small_rows = pltpu.VMEM((4, 8, 256), F32)
    (
        wq_all, wp_all, wg_all, wd_all, ha, raw, rot, att, hm, dmlp, tokp, og, attn_out,
        condg, modv, bg, bd, gains, maskb, valid,
    ) = call(
        kernel_a, 0,
        [(w, BF) for w in weights] + [(full, BF)] + pairs + [((GROUP, 512), BF)]
        + [(block, BF), (full, BF), (block, BF), (block, BF)]
        + [
            (s, F32)
            for s in (block, (4, 8, D), (8, D), (1, 1536), (1, D), (8, 128), (2, 1, 512), (TOK, 1))
        ],
        [pltpu.VMEM(w, BF) for w in weights] + [pltpu.VMEM(full, BF)] + [pltpu.VMEM(w, t) for w, t in pairs]
        + [
            pltpu.VMEM((GROUP, 512), BF), pltpu.VMEM((4, PAD, 864), BF), pltpu.VMEM((4, PAD, 1536), BF),
            pltpu.VMEM(block, BF), pltpu.VMEM(block, BF), pltpu.VMEM((D, 1536), BF), pltpu.VMEM((3, TOK, D), BF),
            pltpu.VMEM((3, TOK, D), BF), pltpu.VMEM(block, F32),
            pltpu.VMEM((4, PAD, 864), BF), pltpu.VMEM((4, PAD, 1536), BF), pltpu.VMEM((4, PAD, 1536), F32),
            pltpu.VMEM((8, D), F32), small_rows, small_rows, pltpu.VMEM((4, 4, 8, 256), F32),
            pltpu.VMEM((2, 2, 2, 4, 8, 256), F32), pltpu.VMEM((4, 1, 1536), F32), pltpu.VMEM((4, 1, 1536), F32),
            pltpu.VMEM((1, D), F32),
        ],
        (
            tokens.reshape(4, 64, D), cotangent.reshape(4, 64, D), w_qkv, w_gu, w_proj, w_down, conditioning, w_mod_t,
            vecs, perm, spread, pick, tabs,
        ),
        hbm=(0, 1),
        hbm_out=range(8),
        sems=128,
    )
    spread = jnp.pad(spread, ((0, D - 864), (0, 0))).reshape(2, 2, 2, 144, 1536)
    dtok, bout, g_w_qkv, g_w_gu, fp, fd, g_w_mod, sums, g_b_mod, d_cond = call(
        kernel_b, 1,
        [
            ((4, 64, D), BF), ((4, 64, D), BF), ((UNIT, 3456), F32), ((UNIT, 6144), F32), ((PAD, D), F32),
            ((96, D), F32), ((216, D), F32), ((8, 256), F32), ((8, 216), F32), ((8, 144), F32),
        ],
        [
            pltpu.VMEM((2, 2, 2, 144, 1536), BF), pltpu.VMEM((2, 2, 2, 96, D), BF), pltpu.VMEM(full, BF),
            pltpu.VMEM(full, BF), pltpu.VMEM(block, BF), pltpu.VMEM(block, BF), pltpu.VMEM(block, F32),
            pltpu.VMEM((GROUP, 512), BF), pltpu.VMEM((2, 2, 2, 64, D), BF), pltpu.VMEM((2, 2, 2, 144, 864), BF),
            pltpu.VMEM((D, D), BF), pltpu.VMEM((3, 512, 128), F32), pltpu.VMEM((TOK, 1536), F32),
            pltpu.VMEM((GROUP, 1536), BF), pltpu.VMEM((GROUP, 768), BF), pltpu.VMEM((3, TOK, D), BF),
            pltpu.VMEM((3, TOK, D), BF), pltpu.VMEM((3, TOK, D), BF), pltpu.VMEM(block, F32),
            pltpu.VMEM((2, 2, 2, 144, 1536), BF), pltpu.VMEM((2, 2, 2, 96, D), BF), pltpu.VMEM((2, 2, 2, PAD, D), BF),
            pltpu.VMEM(full, BF), pltpu.VMEM((2, 2, 512, 128), F32), pltpu.VMEM((2, 3, 512, 128), BF),
            pltpu.VMEM(block, BF), pltpu.VMEM(block, BF), pltpu.VMEM((4, PAD, 896), BF), pltpu.VMEM((4, PAD, 1536), BF),
            pltpu.VMEM((8, D), F32), pltpu.VMEM((8, 1536), F32), pltpu.VMEM((8, 1536), F32), pltpu.VMEM((8, 128), F32),
            pltpu.VMEM((2, 2, 2, 4, 8, 256), F32), pltpu.VMEM((2, 2, 2, 4, 8, 256), F32), small_rows, small_rows,
            pltpu.VMEM((32, 216), F32), pltpu.VMEM((4, 2, 4, 8, 144), F32), pltpu.VMEM((2, 2, 2, 4, 8, 144), F32),
            pltpu.VMEM((4, 8, 144), F32), pltpu.VMEM((4, 8, 144), F32), pltpu.VMEM((1, 256), F32),
            pltpu.VMEM((4, 1, 1536), F32), pltpu.VMEM((4, 1, 1536), F32), pltpu.VMEM((8, 8, 144), F32),
        ]
        + Reduce.buffers(144, 768, 384) * 2 + Reduce.buffers(96, D, SPLIT_D)
        + Reduce.buffers(144, 896, SPLIT_Q) + Reduce.buffers(PAD, D, SPLIT_P),
        (
            wg_all, wd_all, hm, dmlp, tokp, og, attn_out, att, wp_all, wq_all, ha, raw, rot, perm, spread, tabs,
            modv, bg, bd, gains, maskb, valid, pick, condg, w_mod_t,
        ),
        hbm=range(16),
        hbm_out=range(2),
        sems=128,
    )

    one, two = sums[4], sums[5]
    gains_out = sums[6]
    return (
        bout.reshape(tokens.shape),
        dtok.reshape(tokens.shape).astype(F32),
        d_cond[:4],
        g_w_mod.T,
        g_b_mod[0],
        g_w_qkv,
        one[:72],
        one[72:108],
        gains_out[:72],
        gains_out[72:144],
        fp[:UNIT],
        one[108:144],
        g_w_gu,
        two[:192],
        fd,
        one[144:180],
    )


def solution(mesh):
    in_specs = (
        P("dp", "row", "col", None),
        P("dp", None),
        P("dp"),
        P("dp"),
        P("dp", "row", "col", None),
        P(None, ("dp", "row", "col")),
        P(("dp", "row", "col")),
        P(("dp", "row", "col"), None),
        P(("dp", "row", "col")),
        P(),
        P(),
        P(("dp", "row", "col"), None),
        P(("dp", "row", "col")),
        P(("dp", "row", "col"), None),
        P(("dp", "row", "col")),
        P(("dp", "row", "col"), None),
        P(("dp", "row", "col")),
    )
    out_specs = (
        P("dp", "row", "col", None),
        P("dp", "row", "col", None),
        P("dp", ("row", "col")),
        P(None, ("dp", "row", "col")),
        P(("dp", "row", "col")),
        P(("dp", "row", "col"), None),
        P(("dp", "row", "col")),
        P(("dp", "row", "col")),
        P(),
        P(),
        P(("dp", "row", "col"), None),
        P(("dp", "row", "col")),
        P(("dp", "row", "col"), None),
        P(("dp", "row", "col")),
        P(("dp", "row", "col"), None),
        P(("dp", "row", "col")),
    )
    return jax.shard_map(local, mesh=mesh, in_specs=in_specs, out_specs=out_specs, check_vma=False)
```

```python
import math

import jax
import jax.numpy as jnp
import numpy as np
from jax import lax
from jax.experimental import pallas as pl
from jax.experimental.pallas import tpu as pltpu
from jax.sharding import PartitionSpec as P

HEADS = 16
HEAD = 72
FF = 3072


EPSILON = 1e-06
MASKED = -1000000000.0
PRECISE = lax.Precision.HIGHEST


def rope_tables(row_pos, col_pos, head_size):
    half_size = head_size // 2
    lane_index = jnp.arange(head_size)
    pair_index = (lane_index % half_size // 2).astype(jnp.float32)
    frequency = jnp.exp(-math.log(10000.0) * 2.0 * pair_index / half_size)
    places = jnp.where(lane_index[None, :] >= half_size, col_pos[:, None], row_pos[:, None]).astype(
        jnp.float32
    )
    angles = places * frequency[None, :]
    return (jnp.cos(angles), jnp.sin(angles))


def rotate(values):
    pair_view = values.reshape(values.shape[:-1] + (values.shape[-1] // 2, 2))
    turned = jnp.stack((-pair_view[..., 1], pair_view[..., 0]), axis=-1)
    return turned.reshape(values.shape)


def norm_parts(values):
    centered = values - jnp.mean(values, -1, keepdims=True)
    recip = lax.rsqrt(jnp.mean(centered * centered, -1, keepdims=True) + EPSILON)
    return (centered * recip, recip)


def norm_back(gradient, normed, recip):
    return recip * (
        gradient
        - jnp.mean(gradient, -1, keepdims=True)
        - normed * jnp.mean(gradient * normed, -1, keepdims=True)
    )


def head_back(gradient, raw_value, recip, gain_vec):
    scaled = gradient * gain_vec
    gain_grad = jnp.sum(gradient * raw_value * recip, axis=(0, 1, 2))
    raw_grad = recip * scaled - raw_value * (recip * recip * recip) * jnp.mean(
        scaled * raw_value, -1, keepdims=True
    )
    return (raw_grad, gain_grad)


def general(
    tokens,
    conditioning,
    heights,
    widths,
    cotangent,
    w_mod,
    b_mod,
    w_qkv,
    b_qkv,
    query_gain,
    key_gain,
    w_proj,
    b_proj,
    w_gu,
    b_gu,
    w_down,
    b_down,
):
    item_count, tile_rows, tile_cols, model_width = tokens.shape
    tile_span = tile_rows * tile_cols
    n_row = lax.axis_size("row")
    n_col = lax.axis_size("col")
    groups = n_row * n_col
    key_count = tile_span * groups
    inv_root = 1.0 / math.sqrt(HEAD)
    row_at = lax.axis_index("row")
    col_at = lax.axis_index("col")
    local_index = jnp.arange(tile_span)
    query_rows = row_at * tile_rows + local_index // tile_cols
    query_cols = col_at * tile_cols + local_index % tile_cols
    valid_query = (query_rows[None, :] < heights[:, None]) & (query_cols[None, :] < widths[:, None])
    key_index = jnp.arange(key_count)
    key_owner = key_index // tile_span
    key_spot = key_index % tile_span
    key_rows = key_owner // n_col * tile_rows + key_spot // tile_cols
    key_cols = key_owner % n_col * tile_cols + key_spot % tile_cols
    valid_key = (key_rows[None, :] < heights[:, None]) & (key_cols[None, :] < widths[:, None])
    cos_tab, sin_tab = rope_tables(query_rows, query_cols, HEAD)
    cos_four = cos_tab[None, :, None, :]
    sin_four = sin_tab[None, :, None, :]
    cond_f = conditioning.astype(jnp.float32)
    cond_sig = jax.nn.sigmoid(cond_f)
    act_low = (cond_f * cond_sig).astype(jnp.bfloat16)
    gathered = (
        lax.all_gather(w_mod, ("dp", "row", "col"), axis=1, tiled=True),
        lax.all_gather(b_mod, ("dp", "row", "col"), axis=0, tiled=True),
        lax.all_gather(w_qkv, ("dp", "row", "col"), axis=0, tiled=True),
        lax.all_gather(b_qkv, ("dp", "row", "col"), axis=0, tiled=True),
        lax.all_gather(w_proj, ("dp", "row", "col"), axis=0, tiled=True),
        lax.all_gather(b_proj, ("dp", "row", "col"), axis=0, tiled=True),
        lax.all_gather(w_gu, ("dp", "row", "col"), axis=0, tiled=True),
        lax.all_gather(b_gu, ("dp", "row", "col"), axis=0, tiled=True),
        lax.all_gather(w_down, ("dp", "row", "col"), axis=0, tiled=True),
        lax.all_gather(b_down, ("dp", "row", "col"), axis=0, tiled=True),
    )
    (
        w_mod_all,
        b_mod_all,
        w_qkv_all,
        b_qkv_all,
        w_proj_all,
        b_proj_all,
        w_gu_all,
        b_gu_all,
        w_down_all,
        b_down_all,
    ) = gathered
    modul = jnp.dot(act_low, w_mod_all, preferred_element_type=jnp.float32) + b_mod_all.astype(
        jnp.float32
    )
    shift_a, scale_a, gate_a, shift_m, scale_m, gate_m = [
        modul[:, piece * model_width : (piece + 1) * model_width][:, None, :] for piece in range(6)
    ]
    resid_in = tokens.reshape(item_count, tile_span, model_width).astype(jnp.float32)
    normed_a, recip_a = norm_parts(resid_in)
    h_attn = (normed_a * (1.0 + scale_a) + shift_a).astype(jnp.bfloat16)
    qkv_all = jnp.dot(h_attn, w_qkv_all, preferred_element_type=jnp.float32) + b_qkv_all.astype(
        jnp.float32
    )
    query_raw = qkv_all[..., :model_width].reshape(item_count, tile_span, HEADS, HEAD)
    key_raw = qkv_all[..., model_width : 2 * model_width].reshape(
        item_count, tile_span, HEADS, HEAD
    )
    value_raw = qkv_all[..., 2 * model_width :]
    query_recip = lax.rsqrt(jnp.mean(query_raw * query_raw, -1, keepdims=True) + EPSILON)
    key_recip = lax.rsqrt(jnp.mean(key_raw * key_raw, -1, keepdims=True) + EPSILON)
    query_normed = query_raw * query_recip * query_gain
    key_normed = key_raw * key_recip * key_gain
    query_rot = (query_normed * cos_four + rotate(query_normed) * sin_four).astype(jnp.bfloat16)
    key_rot = (key_normed * cos_four + rotate(key_normed) * sin_four).astype(jnp.bfloat16)
    value_low = value_raw.astype(jnp.bfloat16)
    kv_local = jnp.concatenate([key_rot.reshape(item_count, tile_span, model_width), value_low], -1)
    kv_every = lax.all_gather(kv_local, ("row", "col"), axis=1, tiled=True)
    query_heads = query_rot.transpose(2, 0, 1, 3)
    key_part = (
        kv_every[..., :model_width]
        .reshape(item_count, key_count, HEADS, HEAD)
        .transpose(2, 0, 1, 3)
    )
    value_part = (
        kv_every[..., model_width:]
        .reshape(item_count, key_count, HEADS, HEAD)
        .transpose(2, 0, 1, 3)
    )
    key_mask = valid_key[:, None, :]

    def attend(head_block):
        query_h, key_h, value_h = head_block
        scores = (
            jnp.einsum("itd,ikd->itk", query_h, key_h, preferred_element_type=jnp.float32)
            * inv_root
        )
        scores = jnp.where(key_mask, scores, MASKED)
        row_max = jnp.max(scores, -1, keepdims=True)
        exponent = jnp.exp(scores - row_max)
        row_sum = jnp.sum(exponent, -1, keepdims=True)
        probs = (exponent / row_sum).astype(jnp.bfloat16)
        result = jnp.einsum("itk,ikd->itd", probs, value_h, preferred_element_type=jnp.float32)
        return (result, row_max, row_sum)

    attended_heads, max_kept, sum_kept = lax.map(attend, (query_heads, key_part, value_part))
    attended = (
        attended_heads.transpose(1, 2, 0, 3)
        .reshape(item_count, tile_span, model_width)
        .astype(jnp.bfloat16)
    )
    attn_out = jnp.dot(
        attended, w_proj_all, preferred_element_type=jnp.float32
    ) + b_proj_all.astype(jnp.float32)
    resid_mid = resid_in + gate_a * attn_out
    normed_m, recip_m = norm_parts(resid_mid)
    h_mlp = (normed_m * (1.0 + scale_m) + shift_m).astype(jnp.bfloat16)
    gate_up = jnp.dot(h_mlp, w_gu_all, preferred_element_type=jnp.float32) + b_gu_all.astype(
        jnp.float32
    )
    gate_part = gate_up[..., :FF]
    up_part = gate_up[..., FF:]
    gate_sig = jax.nn.sigmoid(gate_part)
    gate_act = gate_part * gate_sig
    hidden = (gate_act * up_part).astype(jnp.bfloat16)
    mlp_out = jnp.dot(hidden, w_down_all, preferred_element_type=jnp.float32) + b_down_all.astype(
        jnp.float32
    )
    mask_f = valid_query[..., None].astype(jnp.float32)
    block_out = ((resid_mid + gate_m * mlp_out) * mask_f).astype(jnp.bfloat16)
    out_grad = cotangent.reshape(item_count, tile_span, model_width).astype(jnp.float32) * mask_f
    d_mlp = (gate_m * out_grad).astype(jnp.bfloat16)
    d_gate_m = jnp.sum(out_grad * mlp_out, 1)
    dw_down = jnp.einsum("itf,itd->fd", hidden, d_mlp, preferred_element_type=jnp.float32)
    db_down = jnp.sum(d_mlp.astype(jnp.float32), (0, 1))
    d_hidden = jnp.einsum("itd,fd->itf", d_mlp, w_down_all, preferred_element_type=jnp.float32)
    d_gate = d_hidden * up_part * gate_sig * (1.0 + gate_part * (1.0 - gate_sig))
    d_up = d_hidden * gate_act
    d_gate_up = jnp.concatenate([d_gate, d_up], -1).astype(jnp.bfloat16)
    dw_gu = jnp.einsum("itd,ite->de", h_mlp, d_gate_up, preferred_element_type=jnp.float32)
    db_gu = jnp.sum(d_gate_up.astype(jnp.float32), (0, 1))
    d_hmlp = jnp.einsum("ite,de->itd", d_gate_up, w_gu_all, preferred_element_type=jnp.float32)
    d_shift_m = jnp.sum(d_hmlp, 1)
    d_scale_m = jnp.sum(d_hmlp * normed_m, 1)
    d_mid = out_grad + norm_back(d_hmlp * (1.0 + scale_m), normed_m, recip_m)
    d_attn = (gate_a * d_mid).astype(jnp.bfloat16)
    d_gate_a = jnp.sum(d_mid * attn_out, 1)
    dw_proj = jnp.einsum("itd,ite->de", attended, d_attn, preferred_element_type=jnp.float32)
    db_proj = jnp.sum(d_attn.astype(jnp.float32), (0, 1))
    d_attended = jnp.einsum(
        "ite,de->itd", d_attn, w_proj_all, preferred_element_type=jnp.float32
    ).astype(jnp.bfloat16)
    d_att_heads = d_attended.reshape(item_count, tile_span, HEADS, HEAD).transpose(2, 0, 1, 3)
    key_back, value_back = (key_part, value_part)

    def attend_back(head_block):
        query_h, key_h, value_h, grad_h, max_h, sum_h = head_block
        scores = (
            jnp.einsum("itd,ikd->itk", query_h, key_h, preferred_element_type=jnp.float32)
            * inv_root
        )
        scores = jnp.where(key_mask, scores, MASKED)
        probs = jnp.exp(scores - max_h) / sum_h
        d_probs = jnp.einsum("itd,ikd->itk", grad_h, value_h, preferred_element_type=jnp.float32)
        delta = jnp.sum(probs * d_probs, -1, keepdims=True)
        d_scores = (probs * (d_probs - delta)).astype(jnp.bfloat16)
        d_query = (
            jnp.einsum("itk,ikd->itd", d_scores, key_h, preferred_element_type=jnp.float32)
            * inv_root
        )
        d_key = (
            jnp.einsum("itk,itd->ikd", d_scores, query_h, preferred_element_type=jnp.float32)
            * inv_root
        )
        d_value = jnp.einsum(
            "itk,itd->ikd", probs.astype(jnp.bfloat16), grad_h, preferred_element_type=jnp.float32
        )
        return (d_query, d_key, d_value)

    dq_heads, dk_heads, dv_heads = lax.map(
        attend_back, (query_heads, key_back, value_back, d_att_heads, max_kept, sum_kept)
    )
    dkv_term = jnp.concatenate(
        [
            dk_heads.transpose(1, 2, 0, 3).reshape(item_count, key_count, model_width),
            dv_heads.transpose(1, 2, 0, 3).reshape(item_count, key_count, model_width),
        ],
        -1,
    )
    dkv_own = lax.psum_scatter(dkv_term, ("row", "col"), scatter_dimension=1, tiled=True)
    d_key_rot = dkv_own[..., :model_width].reshape(item_count, tile_span, HEADS, HEAD)
    d_value = dkv_own[..., model_width:]
    d_query_rot = dq_heads.transpose(1, 2, 0, 3)
    d_query_n = d_query_rot * cos_four - rotate(d_query_rot * sin_four)
    d_key_n = d_key_rot * cos_four - rotate(d_key_rot * sin_four)
    d_query_raw, dq_gain = head_back(d_query_n, query_raw, query_recip, query_gain)
    d_key_raw, dk_gain = head_back(d_key_n, key_raw, key_recip, key_gain)
    gain_total = lax.psum((dq_gain, dk_gain), ("dp", "row", "col"))
    d_qkv = jnp.concatenate(
        [
            d_query_raw.reshape(item_count, tile_span, model_width),
            d_key_raw.reshape(item_count, tile_span, model_width),
            d_value,
        ],
        -1,
    ).astype(jnp.bfloat16)
    dw_qkv = jnp.einsum("itd,ite->de", h_attn, d_qkv, preferred_element_type=jnp.float32)
    db_qkv = jnp.sum(d_qkv.astype(jnp.float32), (0, 1))
    db_query_key = db_qkv[: 2 * model_width]
    db_value = db_qkv[2 * model_width :]
    d_hattn = jnp.einsum("ite,de->itd", d_qkv, w_qkv_all, preferred_element_type=jnp.float32)
    d_shift_a = jnp.sum(d_hattn, 1)
    d_scale_a = jnp.sum(d_hattn * normed_a, 1)
    d_tokens = d_mid + norm_back(d_hattn * (1.0 + scale_a), normed_a, recip_a)
    d_modul = jnp.concatenate([d_shift_a, d_scale_a, d_gate_a, d_shift_m, d_scale_m, d_gate_m], -1)
    act_f = act_low.astype(jnp.float32)
    dw_mod = jnp.einsum("id,ie->de", act_f, d_modul, precision=PRECISE)
    db_mod = jnp.sum(d_modul, 0)
    d_act = jnp.einsum("ie,de->id", d_modul, w_mod_all.astype(jnp.float32), precision=PRECISE)
    d_cond_part = d_act * cond_sig * (1.0 + cond_f * (1.0 - cond_sig))
    d_cond = lax.psum_scatter(d_cond_part, ("row", "col"), scatter_dimension=1, tiled=True)
    summed = (
        lax.psum_scatter(dw_mod, ("dp", "row", "col"), scatter_dimension=1, tiled=True),
        lax.psum_scatter(db_mod, ("dp", "row", "col"), scatter_dimension=0, tiled=True),
        lax.psum_scatter(dw_qkv, ("dp", "row", "col"), scatter_dimension=0, tiled=True),
        lax.psum_scatter(db_query_key, ("dp", "row", "col"), scatter_dimension=0, tiled=True),
        lax.psum_scatter(db_value, ("dp", "row", "col"), scatter_dimension=0, tiled=True),
        lax.psum_scatter(dw_proj, ("dp", "row", "col"), scatter_dimension=0, tiled=True),
        lax.psum_scatter(db_proj, ("dp", "row", "col"), scatter_dimension=0, tiled=True),
        lax.psum_scatter(dw_gu, ("dp", "row", "col"), scatter_dimension=0, tiled=True),
        lax.psum_scatter(db_gu, ("dp", "row", "col"), scatter_dimension=0, tiled=True),
        lax.psum_scatter(dw_down, ("dp", "row", "col"), scatter_dimension=0, tiled=True),
        lax.psum_scatter(db_down, ("dp", "row", "col"), scatter_dimension=0, tiled=True),
    )
    (
        g_w_mod,
        g_b_mod,
        g_w_qkv,
        g_b_query_key,
        g_b_value,
        g_w_proj,
        g_b_proj,
        g_w_gu,
        g_b_gu,
        g_w_down,
        g_b_down,
    ) = summed
    return (
        block_out.reshape(item_count, tile_rows, tile_cols, model_width),
        d_tokens.reshape(item_count, tile_rows, tile_cols, model_width),
        d_cond,
        g_w_mod,
        g_b_mod,
        g_w_qkv,
        g_b_query_key,
        g_b_value,
        gain_total[0],
        gain_total[1],
        g_w_proj,
        g_b_proj,
        g_w_gu,
        g_b_gu,
        g_w_down,
        g_b_down,
    )


MESH = pl.DeviceIdType.MESH
BF = jnp.bfloat16
F32 = jnp.float32
LIMIT = 60 * 1024 * 1024
D = 1152
UNIT = 36
PAD = 48
TOK = 256
GROUP = 1024
SPLIT_Q, SPLIT_P, SPLIT_D = 384, 640, 640
ROOT = 1.0 / math.sqrt(HEAD)
ROOT2 = ROOT / math.log(2.0)


def nn(a, b):
    return lax.dot_general(a, b, (((1,), (0,)), ((), ())), preferred_element_type=F32)


def nt(a, b):
    return lax.dot_general(a, b, (((1,), (1,)), ((), ())), preferred_element_type=F32)


def tn(a, b):
    return lax.dot_general(a, b, (((0,), (0,)), ((), ())), preferred_element_type=F32)


def width_order():
    xx, zh, yy, zl, cc, jj = np.indices((2, 2, 2, 2, 2, UNIT)).reshape(6, -1)
    return ((((xx * 2 + cc) * 2 + zh) * 2 + zl) * 2 + yy) * UNIT + jj


def constants():
    perm = np.zeros((D, D), np.float32)
    perm[width_order(), np.arange(D)] = 1.0
    spread = np.zeros((864, 1536), np.float32)
    tt, hh, yy, jj = np.indices((3, 4, 2, UNIT)).reshape(4, -1)
    spread[tt * 288 + hh * 72 + yy * 36 + jj, tt * 512 + hh * 128 + yy * 64 + jj] = 1.0
    pick = np.zeros((144, 192), np.float32)
    kk, jj = np.indices((4, UNIT)).reshape(2, -1)
    pick[kk * 36 + jj, kk * 48 + jj] = 1.0
    spot = np.arange(512)
    row = spot // 128 * 4 + spot // 16 % 4
    col = spot // 64 % 2 * 16 + spot % 16
    lane = np.arange(128)
    part = lane % 64
    freq = np.exp(-math.log(10000.0) * 2.0 * (part // 2) / 36.0)
    place = np.where(lane[None, :] >= 64, col[:, None], row[:, None]).astype(np.float64)
    angle = place * freq[None, :]
    live = part < UNIT
    cos = np.where(live, np.cos(angle), 0.0)
    sin = np.where(live, np.sin(angle), 0.0)
    even = lane % 2 == 0
    tabs = np.stack([cos, np.where(even, -sin, 0.0), np.where(even, 0.0, sin)]).astype(np.float32)
    return (
        jnp.asarray(perm, BF),
        jnp.asarray(spread, BF),
        jnp.asarray(pick, BF),
        jnp.asarray(tabs, F32),
    )


class Place:
    def __init__(self):
        dp = lax.axis_index("dp")
        self.z = lax.axis_index("row")
        self.y = lax.axis_index("col")
        self.x = dp // 2
        self.c = dp % 2
        self.zh = self.z // 2
        self.zl = self.z % 2
        self.m = self.zl * 2 + self.c
        self.dp = dp

    def mate(self, r):
        c = 1 - self.c if r % 2 else self.c
        zl = 1 - self.zl if r // 2 else self.zl
        return zl * 2 + c, (self.x * 2 + c, self.zh * 2 + zl, self.y)

    def xpeer(self):
        return ((1 - self.x) * 2 + self.c, self.z, self.y)

    def ypeer(self):
        return (self.dp, self.z, 1 - self.y)

    def zpeer(self):
        return (self.dp, (1 - self.zh) * 2 + self.zl, self.y)

    def item_home(self, j):
        return (self.x * 2 + self.zh, j, self.c)

    def item_source(self, blk):
        return (self.x * 2 + self.y, self.c * 2 + blk // 2, blk % 2)

    def is_me(self, dev):
        return (dev[0] == self.dp) & (dev[1] == self.z) & (dev[2] == self.y)


class Link:
    def __init__(self, here, ssem, rsem):
        self.here, self.ssem, self.rsem, self.n, self.open = here, ssem, rsem, 0, []

    def greet(self, items):
        here = self.here
        bar = pltpu.get_barrier_semaphore()
        devs = [here.mate(r)[1] for r in (1, 2, 3)]
        devs += [here.xpeer(), here.ypeer(), here.zpeer()]
        devs += [near(here, r)[3] for r in range(1, 8)] + [along_z(here, r)[1] for r in (1, 2, 3)]
        for d in devs:
            pl.semaphore_signal(bar, inc=1, device_id=d, device_id_type=MESH)
        total = len(devs)
        if items:
            for d in [here.item_home(j) for j in range(4)] + [here.item_source(j) for j in range(4)]:


                @pl.when(jnp.logical_not(here.is_me(d)))
                def _():
                    pl.semaphore_signal(bar, inc=1, device_id=d, device_id_type=MESH)

            far = (here.zh - here.c) * (here.zh - here.c)
            off = (here.y - here.c) * (here.y - here.c)
            total += 8 - 2 * (1 - far) * (1 - off)
        pl.semaphore_wait(bar, total)

    def send(self, src, dst, dev):
        k = self.n
        self.n += 1
        copy = pltpu.make_async_remote_copy(
            src_ref=src,
            dst_ref=dst,
            send_sem=self.ssem.at[k],
            recv_sem=self.rsem.at[k],
            device_id=dev,
            device_id_type=MESH,
        )
        copy.start()
        self.open.append(copy)
        return copy

    def scatter(self, src_of, dst, dev_of, slot):
        base = self.n
        self.n += 4
        here = self.here
        copies = []
        for j in range(4):
            dev = dev_of(j)
            mine = here.is_me(dev)
            remote = pltpu.make_async_remote_copy(
                src_ref=src_of(j),
                dst_ref=dst,
                send_sem=self.ssem.at[base + j],
                recv_sem=self.rsem.at[base + slot],
                device_id=dev,
                device_id_type=MESH,
            )
            local_copy = pltpu.make_async_copy(src_of(j), dst, self.rsem.at[base + slot])

            @pl.when(mine)
            def _():
                local_copy.start()

            @pl.when(jnp.logical_not(mine))
            def _():
                remote.start()

            copies.append((mine, remote))

        def wait_send():
            for mine, remote in copies:

                @pl.when(jnp.logical_not(mine))
                def _():
                    remote.wait_send()

        def wait_recv(src, dst_of):
            for j in range(4):
                pltpu.make_async_copy(src, dst_of(j), self.rsem.at[base + j]).wait()

        return wait_send, wait_recv

    def settle(self, *copies):
        for copy in copies:
            copy.wait_send()
            self.open = [c for c in self.open if c is not copy]

    def finish(self):
        for copy in self.open:
            copy.wait_send()
        self.open = []


def norm_rows(x):
    mean = jnp.sum(x, -1, keepdims=True) * (1.0 / D)
    cent = x - mean
    var = jnp.sum(cent * cent, -1, keepdims=True) * (1.0 / D)
    recip = lax.rsqrt(var + EPSILON)
    return cent * recip, recip


def norm_rows_back(g, y, recip):
    mg = jnp.sum(g, -1, keepdims=True) * (1.0 / D)
    mgy = jnp.sum(g * y, -1, keepdims=True) * (1.0 / D)
    return recip * (g - mg - y * mgy)


def at(i, n):
    return pl.ds(pl.multiple_of(i * n, n), n)


class Gather:
    def __init__(self, link, ref, rows, lo, split, hi):
        self.link, self.ref, self.rows = link, ref, rows
        self.ca, self.cb = pl.ds(lo, split - lo), pl.ds(split, hi - split)
        self.all = slice(None) if hi - lo == ref.shape[-1] else pl.ds(lo, hi - lo)

    def cut(self, i, j, k, cols):
        return self.ref.at[i, j, k, pl.ds(0, self.rows), cols]

    def hop1(self):
        h = self.link.here
        part = self.cut(h.x, h.zh, h.y, self.all)
        self.a = self.link.send(part, part, h.zpeer())

    def hop2(self):
        h = self.link.here
        self.a.wait_recv()
        pa = self.cut(h.x, slice(None), h.y, self.ca)
        pb = self.cut(h.x, slice(None), h.y, self.cb)
        self.a = self.link.send(pa, pa, h.xpeer())
        self.b = self.link.send(pb, pb, h.ypeer())

    def hop3(self):
        h = self.link.here
        self.a.wait_recv()
        self.b.wait_recv()
        pa = self.cut(slice(None), slice(None), h.y, self.ca)
        pb = self.cut(h.x, slice(None), slice(None), self.cb)
        self.a = self.link.send(pa, pa, h.ypeer())
        self.b = self.link.send(pb, pb, h.xpeer())

    def done(self):
        self.a.wait_recv()
        self.b.wait_recv()


class Reduce:
    def __init__(self, link, ref, bufs, lo, split, hi):
        self.link, self.ref, self.lo, self.split, self.hi = link, ref, lo, split, hi
        self.r1a, self.r1b, self.r2a, self.r2b, self.r3a, self.r3b = bufs

    @staticmethod
    def buffers(rows, cols, split):
        rest = cols - split
        return [
            pltpu.VMEM((2, 2, rows, split), BF),
            pltpu.VMEM((2, 2, rows, rest), BF),
            pltpu.VMEM((2, rows, split), BF),
            pltpu.VMEM((2, rows, rest), BF),
            pltpu.VMEM((rows, split), BF),
            pltpu.VMEM((rows, rest), BF),
        ]

    def hop1(self):
        h = self.link.here
        ca, cb = pl.ds(self.lo, self.split - self.lo), pl.ds(self.split, self.hi - self.split)
        self.a = self.link.send(self.ref.at[1 - h.x, :, :, :, ca], self.r1a, h.xpeer())
        self.b = self.link.send(self.ref.at[:, :, 1 - h.y, :, cb], self.r1b, h.ypeer())

    def hop2(self):
        h = self.link.here
        ca, cb = pl.ds(self.lo, self.split - self.lo), pl.ds(self.split, self.hi - self.split)
        self.a.wait_recv()
        self.b.wait_recv()

        def add(i, carry):
            u, v = i // 2, i % 2
            own = self.ref[h.x, u, v, :, ca].astype(F32)
            self.r1a[u, v] = (self.r1a[u, v].astype(F32) + own).astype(BF)
            own = self.ref[u, v, h.y, :, cb].astype(F32)
            self.r1b[u, v] = (self.r1b[u, v].astype(F32) + own).astype(BF)
            return carry

        lax.fori_loop(0, 4, add, 0)
        self.a = self.link.send(self.r1a.at[:, 1 - h.y], self.r2a, h.ypeer())
        self.b = self.link.send(self.r1b.at[1 - h.x], self.r2b, h.xpeer())

    def hop3(self):
        h = self.link.here
        self.a.wait_recv()
        self.b.wait_recv()

        def add(u, carry):
            own = self.r1a[u, h.y].astype(F32)
            self.r2a[u] = (self.r2a[u].astype(F32) + own).astype(BF)
            own = self.r1b[h.x, u].astype(F32)
            self.r2b[u] = (self.r2b[u].astype(F32) + own).astype(BF)
            return carry

        lax.fori_loop(0, 2, add, 0)
        self.a = self.link.send(self.r2a.at[1 - h.zh], self.r3a, h.zpeer())
        self.b = self.link.send(self.r2b.at[1 - h.zh], self.r3b, h.zpeer())

    def done(self):
        h = self.link.here
        self.a.wait_recv()
        self.b.wait_recv()
        left = self.r2a[h.zh].astype(F32) + self.r3a[...].astype(F32)
        right = self.r2b[h.zh].astype(F32) + self.r3b[...].astype(F32)
        return left.astype(BF), right.astype(BF)


class RowGather:
    def __init__(self, link, ref):
        self.link, self.ref = link, ref
        here = link.here
        own = ref.at[at(here.m, TOK)]
        self.far = link.send(own, own, here.mate(2)[1])
        self.near = link.send(own, own, here.mate(1)[1])

    def near_done(self):
        self.near.wait_recv()

    def pass_on(self):
        here = self.link.here
        self.far.wait_recv()
        rows = self.ref.at[at(here.mate(2)[0], TOK)]
        self.last = self.link.send(rows, rows, here.mate(1)[1])

    def last_done(self):
        self.last.wait_recv()


class RowReduce:
    def __init__(self, link, out, into):
        self.link, self.out, self.into = link, out, into

    def give(self, r, val):
        i = 0 if r == 3 else 1
        if val is not None:
            self.out[i] = val.astype(BF)
        sent = self.link.send(self.out.at[i], self.into.at[i], self.link.here.mate(1)[1])
        if r == 3:
            self.s3 = sent
        else:
            self.s1 = sent

    def keep_far(self, val):
        self.out[2] = val.astype(BF)

    def pass_on(self):
        self.s3.wait_recv()

        def add(i, carry):
            rows = at(i, 32)
            both = self.out[2, rows, :].astype(F32) + self.into[0, rows, :].astype(F32)
            self.out[2, rows, :] = both.astype(BF)
            return carry

        lax.fori_loop(0, 8, add, 0)
        self.s2 = self.link.send(self.out.at[2], self.into.at[2], self.link.here.mate(2)[1])

    def arrive(self):
        self.s1.wait_recv()
        self.s2.wait_recv()

    def total(self, rows):
        return self.into[1, rows, :].astype(F32) + self.into[2, rows, :].astype(F32)


def turn(v, cos, sina, sinb):
    return v * cos + pltpu.roll(v, 127, 1) * sina + pltpu.roll(v, 1, 1) * sinb


def turn_back(d, cos, sina, sinb):
    return d * cos - pltpu.roll(d, 127, 1) * sina - pltpu.roll(d, 1, 1) * sinb


def near(here, r):
    x = 1 - here.x if r // 4 else here.x
    c = 1 - here.c if r // 2 % 2 else here.c
    y = 1 - here.y if r % 2 else here.y
    return x, c, y, (x * 2 + c, here.z, y)


def along_z(here, r):
    z = (here.z + r) % 4
    return z, (here.dp, z, here.y)


def shard_parts(s):
    x, c, zh, zl, y = s // 16, s // 8 % 2, s // 4 % 2, s // 2 % 2, s % 2
    member, spot = zl * 2 + c, (x * 2 + zh) * 2 + y
    return spot * 4 + member, member, spot


def three(v):
    hi = v.astype(BF)
    rest = v - hi.astype(F32)
    mid = rest.astype(BF)
    return jnp.concatenate([hi, mid, (rest - mid.astype(F32)).astype(BF)], 0)


def by_member(src, out, tmp, width, pieces):
    cols = pieces * 4 * width
    for t in range(pieces):
        for h in range(16):
            unit = shard_parts(h * 2)
            dst = t * 4 * width + unit[2] // 2 * width
            tmp[unit[1], 0:UNIT, dst : dst + width] = src[
                :, (t * 16 + h) * width : (t * 16 + h + 1) * width
            ].astype(F32)
    for m in range(4):
        out[m] = tmp[m, :, 0:cols].astype(BF)


def by_column(src, out, width, pieces):
    for t in range(pieces):
        for h in range(16):
            unit = shard_parts(h * 2)
            at_ = t * 4 * width + unit[2] // 2 * width
            out[:, (t * 16 + h) * width : (t * 16 + h + 1) * width] = src[
                unit[1], 0:UNIT, at_ : at_ + width
            ].astype(F32)


def silu_slope(v):
    sig = jax.nn.sigmoid(v)
    return sig * (1.0 + v * (1.0 - sig))


def kernel_a(
    tok_in, cot_in, wqkv, wgu, wp_in, wd_in, cond, w_mod_t, vecs, perm_in, spread_in, pick, tabs_in,
    wq_out, wp_out, wg_out, wd_out, ha_out, raw_out, rot_out, att_out, hm_out, dm_out, tok_out, og_out, attn_o_out,
    condg, modv, bg, bd, gains, maskb, valid,
    wq, wp, wg, wd, ha, raw, rot, att, s0q, s0g, tokr, cotr, wqe, psend, precv, pown,
    wqs, wgs, tmp, block, msg, p1, m2, got, bq4, bg4, bp, hm, dmlp, tokp, og, attn_out, perm, spread, tabs,
    ssem, rsem, lsem,
):
    here = Place()
    link = Link(here, ssem, rsem)
    fetch = Fetch(lsem)
    m = here.m
    perm_got, spread_got, tabs_got = (
        fetch.go(a, b) for a, b in ((perm_in, perm), (spread_in, spread), (tabs_in, tabs))
    )
    block[...] = jnp.zeros_like(block)
    block[0:4, :] = cond[...].astype(F32)
    block[4:5, 0:8] = vecs[5:6, 0:8]
    condg[here.dp] = block[...]
    link.greet(True)
    slot = here.zl * 2 + here.y
    rows_in = at(slot, 64)
    cs = [link.send(block, condg.at[here.dp], near(here, r)[3]) for r in (2, 4, 6)]
    tmp[...] = jnp.zeros_like(tmp)
    by_member(wqkv, wqs, tmp, 72, 3)
    sq, sg = {}, {}
    for r in (2, 3, 1):
        k, dev = here.mate(r)
        sq[r] = link.send(wqs.at[k], s0q.at[m], dev)
    own_q = fetch.go(wqs.at[m], s0q.at[m])
    for c in cs:
        c.wait_recv()
    v = condg[...].reshape(32, D)
    part = nt((v * jax.nn.sigmoid(v)).astype(BF), w_mod_t[...]) + vecs[0:1, 0:216]
    for z in range(4):
        msg[z, 4:6, :] = vecs[1:3, :]
        for d in range(4):
            msg[z, d : d + 1, 0:216] = part[d * 8 + z : d * 8 + z + 1, :]
    zs = []
    for r in (1, 2, 3):
        z, dev = along_z(here, r)
        zs.append(link.send(msg.at[z], p1.at[here.z], dev))
    p1[here.z] = msg[here.z]

    gq = Gather(link, wq, 144, 0, SPLIT_Q, 864)
    gp = Gather(link, wp, PAD, 0, SPLIT_P, D)
    g1 = Gather(link, wg, 144, 0, 384, 768)
    g2 = Gather(link, wg, 144, 768, 1152, 1536)
    gd = Gather(link, wd, 96, 0, SPLIT_D, D)
    by_member(wgu, wgs, tmp, 192, 2)
    own_q.wait()
    for r in (1, 2, 3):
        sq[r].wait_recv()
    wq[here.x, here.zh, here.y] = nn(pick[...], s0q[...].reshape(192, 864)).astype(BF)
    gq.hop1()
    for c in zs:
        c.wait_recv()
    for z in range(4):
        for d in range(4):
            m2[d, z, 0:1, :] = p1[z, d : d + 1, :]
            m2[d, z, 1:3, :] = p1[z, 4:6, :]
    ns = []
    for r in range(1, 8):
        x, _, y, dev = near(here, r)
        ns.append(link.send(m2.at[x * 2 + y], got.at[here.x, here.c, here.y], dev))
    got[here.x, here.c, here.y] = m2[here.x * 2 + here.y]
    tok_sent, tok_got = link.scatter(lambda j: tok_in.at[j], tokr.at[rows_in], here.item_home, slot)

    for r in (2, 3, 1):
        k, dev = here.mate(r)
        sg[r] = link.send(wgs.at[k], s0g.at[m], dev)
    own_g = fetch.go(wgs.at[m], s0g.at[m])
    perm_got.wait()
    wp[:, :, :, PAD:64, :] = jnp.zeros((2, 2, 2, 64 - PAD, D), BF)
    tmp[0, 0:UNIT, 0:D] = nn(wp_in[...], perm[...])
    tmp[0, UNIT:PAD, :] = jnp.zeros((PAD - UNIT, 1536), F32)
    wp[here.x, here.zh, here.y, 0:PAD, :] = tmp[0, :, 0:D].astype(BF)
    gp.hop1()
    ext = condg[here.x * 2 + here.y, 4:5, :]
    lane = lax.broadcasted_iota(jnp.int32, (1, D), 1)
    spot = lax.broadcasted_iota(jnp.int32, (1, 512), 1)
    row_at = spot // 128 * 4 + spot // 16 % 4
    col_at = spot // 64 % 2 * 16 + spot % 16

    def extent(item, first):
        return jnp.sum(jnp.where(lane == item + first, ext, 0.0), -1, keepdims=True)

    for i in range(2):
        tall, wide = extent(here.zh * 2 + i, 0), extent(here.zh * 2 + i, 4)
        live = (row_at.astype(F32) < tall) & (col_at.astype(F32) < wide)
        maskb[i] = jnp.where(live, 0.0, MASKED)
    spot = lax.broadcasted_iota(jnp.int32, (TOK, 1), 0) + here.c * TOK
    row_at = (spot // 128 * 4 + spot // 16 % 4).astype(F32)
    col_at = (spot // 64 % 2 * 16 + spot % 16).astype(F32)
    live = (row_at < extent(here.z, 0)) & (col_at < extent(here.z, 4))
    valid[...] = jnp.where(live, 1.0, 0.0)
    gains[...] = jnp.zeros_like(gains)
    for t in range(2):
        for e in range(2):
            gains[t : t + 1, e * 64 : e * 64 + UNIT] = vecs[3 + t : 4 + t, e * UNIT : e * UNIT + UNIT]
    for c in ns:
        c.wait_recv()
    modv[...] = jnp.zeros_like(modv)
    bq4[...] = jnp.zeros_like(bq4)
    for s in range(32):
        line = got[s // 16, s // 8 % 2, s % 2, s // 2 % 4]
        for q in range(6):
            piece, unit = divmod(6 * s + q, 32)
            to = shard_parts(unit)[0] * UNIT
            modv[piece : piece + 1, to : to + UNIT] = line[0:1, q * UNIT : q * UNIT + UNIT]
        for q in range(3):
            piece, unit = divmod(3 * s + q, 32)
            _, member, spot = shard_parts(unit)
            to = piece * 512 + spot * 64
            bq4[member, :, to : to + UNIT] = line[1:2, q * UNIT : q * UNIT + UNIT]
        to = shard_parts(s)[0] * UNIT
        bp[:, to : to + UNIT] = line[1:2, 108:144]
        bd[:, to : to + UNIT] = line[1:2, 144:180]
        for q in range(2):
            piece, unit = divmod(2 * s + q, 32)
            _, member, spot = shard_parts(unit)
            to = piece * 768 + spot * 96
            bg4[member, :, to : to + 96] = line[2:3, q * 96 : q * 96 + 96]
    bg[...] = bg4[m]
    gq.hop2()
    tok_got(tok_in.at[0], lambda j: tokr.at[pl.ds(j * 64, 64)])
    gq.hop3()
    tokp[...] = nn(tokr[...], perm[...]).astype(BF)

    def first_norm(i, carry):
        n, _ = norm_rows(tokp[at(i, 32), :].astype(F32))
        h = n * (1.0 + modv[1:2, :]) + modv[0:1, :]
        ha[pl.ds(pl.multiple_of(m * TOK + i * 32, 32), 32), :] = h.astype(BF)
        return carry

    lax.fori_loop(0, 8, first_norm, 0)
    ha_all = RowGather(link, ha)
    own_g.wait()
    for r in (1, 2, 3):
        sg[r].wait_recv()
    wg[here.x, here.zh, here.y] = nn(pick[...], s0g[...].reshape(192, 1536)).astype(BF)
    g1.hop1()
    g2.hop1()
    wd[here.x, here.zh, here.y] = nn(wd_in[...], perm[...]).astype(BF)
    gd.hop1()
    gp.hop2()
    gq.done()
    outs = [fetch.go(wq, wq_out), fetch.go(tokp, tok_out)]
    spread_got.wait()

    def widen(i, carry):
        part = wq[i // 2, i % 2].reshape(288, 864)
        wqe[at(i, 288), :] = nn(part, spread[...]).astype(BF)
        return carry

    lax.fori_loop(0, 4, widen, 0)
    gp.hop3()
    tabs_got.wait()

    g1.hop2()
    cot_sent, cot_got = link.scatter(lambda j: cot_in.at[j], cotr.at[rows_in], here.item_home, slot)
    ha_all.pass_on()
    g1.hop3()
    ha_all.near_done()
    ha_all.last_done()
    outs.append(fetch.go(ha, ha_out))

    def project(b, carry):
        acc = nn(ha[at(b, TOK), :], wqe[...]) + bq4[m]
        item, half = b // 2, at(b % 2, TOK)
        cos, sina, sinb = tabs[0, half, :], tabs[1, half, :], tabs[2, half, :]
        for h in range(4):
            p = item * 4 + h
            for t in range(2):
                v = acc[:, t * 512 + h * 128 : t * 512 + h * 128 + 128]
                recip = lax.rsqrt(jnp.sum(v * v, -1, keepdims=True) * (1.0 / HEAD) + EPSILON)
                raw[p, t, half, :] = v
                n = v * recip * gains[t : t + 1, :]
                rot[p, t, half, :] = turn(n, cos, sina, sinb).astype(BF)
            rot[p, 2, half, :] = acc[:, 1024 + h * 128 : 1152 + h * 128].astype(BF)
        return carry

    def attend(p, carry):
        item = p // 4
        lanes = at(p % 4, 128)
        for half in range(2):
            rows = pl.ds(half * TOK, TOK)
            e = jnp.exp2(nt(rot[p, 0, rows, :], rot[p, 1]) * ROOT2 + maskb[item])
            pr = (e * (1.0 / jnp.sum(e, -1, keepdims=True))).astype(BF)
            out_rows = pl.ds(pl.multiple_of(item * 512 + half * TOK, TOK), TOK)
            att[out_rows, lanes] = nn(pr, rot[p, 2]).astype(BF)
        return carry

    other = 1 - here.zl
    lax.fori_loop(other * 2, other * 2 + 2, project, 0)
    g2.hop2()
    lax.fori_loop(other * 4, other * 4 + 4, attend, 0)
    gp.done()
    outs.append(fetch.go(wp, wp_out))
    wpf = wp[...].reshape(512, D)
    red = RowReduce(link, psend, precv)
    red.give(3, nn(att[at(here.mate(3)[0], TOK), :], wpf))
    red.keep_far(nn(att[at(here.mate(2)[0], TOK), :], wpf))
    red.pass_on()
    gd.hop2()
    g2.hop3()
    lax.fori_loop(here.zl * 2, here.zl * 2 + 2, project, 0)
    cot_got(cot_in.at[0], lambda j: cotr.at[pl.ds(j * 64, 64)])
    og[...] = (nn(cotr[...], perm[...]) * valid[...]).astype(BF)

    def scale_grad(i, carry):
        g = og[at(i, 32), :].astype(F32) * modv[5:6, :]
        dmlp[pl.ds(pl.multiple_of(m * TOK + i * 32, 32), 32), :] = g.astype(BF)
        return carry

    lax.fori_loop(0, 8, scale_grad, 0)
    outs.append(fetch.go(og, og_out))
    dm_all = RowGather(link, dmlp)
    outs.append(fetch.go(raw, raw_out))
    outs.append(fetch.go(rot, rot_out))
    gd.hop3()
    lax.fori_loop(here.zl * 4, here.zl * 4 + 4, attend, 0)
    outs.append(fetch.go(att, att_out))
    red.give(1, nn(att[at(here.mate(1)[0], TOK), :], wpf))
    pown[...] = nn(att[at(m, TOK), :], wpf)
    red.arrive()

    def second_norm(i, carry):
        rows = at(i, 32)
        a = pown[rows, :] + bp[...] + red.total(rows)
        attn_out[rows, :] = a
        n, _ = norm_rows(tokp[rows, :].astype(F32) + modv[2:3, :] * a)
        h = n * (1.0 + modv[4:5, :]) + modv[3:4, :]
        hm[rows, :] = h.astype(BF)
        return carry

    lax.fori_loop(0, 8, second_norm, 0)
    outs.append(fetch.go(hm, hm_out))
    outs.append(fetch.go(attn_out, attn_o_out))
    g1.done()
    g2.done()
    outs.append(fetch.go(wg, wg_out))
    gd.done()
    outs.append(fetch.go(wd, wd_out))
    dm_all.pass_on()
    dm_all.near_done()
    dm_all.last_done()
    outs.append(fetch.go(dmlp, dm_out))
    for c in outs:
        c.wait()
    link.finish()
    tok_sent()
    cot_sent()


def store_tiles(val, ref, base, piece, keep):
    block = ref.shape[3] if keep is None else piece
    for q in range(val.shape[0] // piece):
        row = base + q * piece
        f, off = row // block, row % block
        n = piece if keep is None else keep
        part = val[q * piece : q * piece + n, :].astype(BF)
        ref[f // 4, f // 2 % 2, f % 2, off : off + n, 0 : val.shape[1]] = part


class Fetch:
    def __init__(self, sems):
        self.sems, self.n = sems, 0

    def go(self, src, dst):
        copy = pltpu.make_async_copy(src, dst, self.sems.at[self.n])
        self.n += 1
        copy.start()
        return copy


def kernel_b(
    wg_in, wd_in, hm_in, dm_in, tok_in, og_in, attn_in, att_in, wp_in, wq_in, ha_in, raw_in, rot_in, perm_in,
    spread_in, tabs_in, modv, bg, bd, gains, maskb, valid, pick, condg, w_mod_t,
    dtok, bout, g_qkv_out, g_gu_out, fp_out, fd_out, dwm_out, sums, dbm, dcond,
    wg, wd, hm, dmlp, tokp, og, attn_out, att, wp, wq, perm, tabs, gu, coef, hid, rsend, rrecv, mrecv, own32,
    dwg, dwd, dwp, dattn, raw, rot, to, bo, fq, fg, small, dbg, dbq, dgain,
    pk, q1, m2, q2, dm, e0, e1, e2, e3, line, bq4, bg4, slope, g_qkv, g_gu, fp, fd, dwm,
    g1a, g1b, g2a, g2b, g3a, g3b, h1a, h1b, h2a, h2b, h3a, h3b, d1a, d1b, d2a, d2b, d3a, d3b,
    q1a, q1b, q2a, q2b, q3a, q3b, p1a, p1b, p2a, p2b, p3a, p3b, ssem, rsem, lsem,
):
    here = Place()
    link = Link(here, ssem, rsem)
    fetch = Fetch(lsem)
    m = here.m
    k1, k2, k3 = here.mate(1)[0], here.mate(2)[0], here.mate(3)[0]
    at_m, at_1, at_2, at_3 = at(m, TOK), at(k1, TOK), at(k2, TOK), at(k3, TOK)
    get_hm = fetch.go(hm_in, hm.at[at_m])
    get_dm = fetch.go(dm_in, dmlp)
    get_wg = fetch.go(wg_in, wg)
    get_wd = fetch.go(wd_in, wd)
    gets = [fetch.go(a, b) for a, b in ((tok_in, tokp), (og_in, og), (attn_in, attn_out))]
    get_wp = fetch.go(wp_in, wp)
    gets2 = [fetch.go(a, b) for a, b in ((tabs_in, tabs), (att_in, att), (wq_in, wq), (perm_in, perm))]
    base = fetch.n
    fetch.n += 4
    link.greet(True)
    get_hm.wait()
    hm_all = RowGather(link, hm)
    small[...] = jnp.zeros_like(small)
    dbg[...] = jnp.zeros_like(dbg)
    dbq[...] = jnp.zeros_like(dbq)
    dgain[...] = jnp.zeros_like(dgain)
    get_wg.wait()
    get_wd.wait()
    get_dm.wait()

    def wgf():
        return wg[...].reshape(D, 1536)

    def wdf():
        return wd[...].reshape(768, D)

    def mlp(k):
        gu[...] = nn(hm[at(k, TOK), :], wgf()) + bg[...]

        def acts(i, carry):
            rows = at(i, 32)
            out = pl.ds(pl.multiple_of(k * TOK + i * 32, 32), 32)
            g, u = gu[rows, 0:768], gu[rows, 768:1536]
            sig = jax.nn.sigmoid(g)
            act = g * sig
            hid[out, :] = (act * u).astype(BF)
            gu[rows, 0:768] = u * sig * (1.0 + g * (1.0 - sig))
            gu[rows, 768:1536] = act
            return carry

        lax.fori_loop(0, 8, acts, 0)
        dh = nt(dmlp[at(k, TOK), :], wdf())
        out = at(k, TOK)
        coef[out, 0:768] = (gu[:, 0:768] * dh).astype(BF)
        coef[out, 768:1536] = (gu[:, 768:1536] * dh).astype(BF)
        dbg[0:1, :] += jnp.sum(coef[out, :].astype(F32), 0, keepdims=True)
        return nt(coef[out, :], wgf())

    hred = RowReduce(link, rsend, rrecv)
    own32[...] = mlp(m)
    hm_all.near_done()
    hred.give(1, mlp(k1))
    hm_all.pass_on()
    hred.keep_far(mlp(k2))
    hm_all.last_done()
    hred.give(3, mlp(k3))
    hred.pass_on()

    ra = Reduce(link, dwg, (g1a, g1b, g2a, g2b, g3a, g3b), 0, 384, 768)
    rb = Reduce(link, dwg, (h1a, h1b, h2a, h2b, h3a, h3b), 768, 1152, 1536)
    rd = Reduce(link, dwd, (d1a, d1b, d2a, d2b, d3a, d3b), 0, SPLIT_D, D)
    rq = Reduce(link, wg, (q1a, q1b, q2a, q2b, q3a, q3b), 0, SPLIT_Q, 896)
    rp = Reduce(link, dwp, (p1a, p1b, p2a, p2b, p3a, p3b), 0, SPLIT_P, D)
    for n, red in ((0, ra), (1, rb)):
        cols = slice(n * 768, n * 768 + 768)
        for i in range(3):
            t = tn(hm[:, i * 384 : i * 384 + 384], coef[:, cols])
            for q in range(8):
                row = i * 384 + q * 48
                f, off = row // 144, row % 144
                dwg[f // 4, f // 2 % 2, f % 2, off : off + 48, cols] = t[q * 48 : q * 48 + 48].astype(BF)
        red.hop1()
    spread_got = fetch.go(spread_in, wg)
    for i in range(2):
        store_tiles(tn(hid[:, i * 384 : i * 384 + 384], dmlp[...]), dwd, i * 384, 96, None)
    rd.hop1()
    link.settle(hred.s1, hred.s3)
    mred = RowReduce(link, rsend, mrecv)
    mred.give(3, nn(hid[at_3, :], wdf()))
    mred.give(1, nn(hid[at_1, :], wdf()))
    bo[...] = nn(hid[at_m, :], wdf()).astype(BF)
    for c in gets:
        c.wait()
    hred.arrive()

    def mid_back(i, carry):
        rows = at(i, 32)
        mine = pl.ds(pl.multiple_of(m * TOK + i * 32, 32), 32)
        d = own32[rows, :] + hred.total(rows)
        a = attn_out[rows, :]
        n, recip = norm_rows(tokp[rows, :].astype(F32) + modv[2:3, :] * a)
        small[1:2, :] += jnp.sum(d, 0, keepdims=True)
        small[2:3, :] += jnp.sum(d * n, 0, keepdims=True)
        g = og[rows, :].astype(F32) + norm_rows_back(d * (1.0 + modv[4:5, :]), n, recip)
        gu[rows, 0:D] = g
        small[3:4, :] += jnp.sum(g * a, 0, keepdims=True)
        low = (modv[2:3, :] * g).astype(BF)
        dattn[mine, :] = low
        small[5:6, :] += jnp.sum(low.astype(F32), 0, keepdims=True)
        small[4:5, :] += jnp.sum(dmlp[mine, :].astype(F32), 0, keepdims=True)
        return carry

    lax.fori_loop(0, 8, mid_back, 0)
    da_all = RowGather(link, dattn)
    link.settle(hred.s2, hm_all.far, hm_all.near, hm_all.last)
    ha_got = fetch.go(ha_in, dmlp)
    mred.keep_far(nn(hid[at_2, :], wdf()))
    da_all.near_done()

    def pair_of(n):
        item = here.zl + (1 - 2 * here.zl) * (n // 4)
        return item, item * 4 + n % 4

    def pair_copies(n):
        p = pair_of(n)[1]
        s = n % 2
        return (
            pltpu.make_async_copy(raw_in.at[p], raw.at[s], lsem.at[base + 2 * s]),
            pltpu.make_async_copy(rot_in.at[p], rot.at[s], lsem.at[base + 2 * s + 1]),
        )

    for c in pair_copies(0):
        c.start()
    get_wp.wait()
    for c in gets2:
        c.wait()

    def back_proj(rows):
        hid[rows, 0:512] = nt(dattn[rows, :], wp[...].reshape(512, D)).astype(BF)

    def attend_back(n, carry):
        item, p = pair_of(n)
        s = n % 2
        lanes = at(n % 4, 128)
        for c in pair_copies(n):
            c.wait()

        @pl.when(n < 7)
        def _():
            for c in pair_copies(n + 1):
                c.start()

        dk = jnp.zeros((512, 128), F32)
        dv = jnp.zeros((512, 128), F32)

        def head_back_store(d, t, rows, out_rows):
            cos, sina, sinb = tabs[0, rows, :], tabs[1, rows, :], tabs[2, rows, :]
            v = raw[s, t, rows, :]
            recip = lax.rsqrt(jnp.sum(v * v, -1, keepdims=True) * (1.0 / HEAD) + EPSILON)
            dn = turn_back(d, cos, sina, sinb)
            dgain[t : t + 1, :] += jnp.sum(dn * v * recip, 0, keepdims=True)
            u = dn * gains[t : t + 1, :]
            mean = jnp.sum(u * v, -1, keepdims=True) * (1.0 / HEAD)
            res = recip * u - v * (recip * recip * recip * mean)
            coef[out_rows, at(t * 4 + n % 4, 128)] = res.astype(BF)

        for half in range(2):
            rows = pl.ds(half * TOK, TOK)
            out_rows = pl.ds(pl.multiple_of(item * 512 + half * TOK, TOK), TOK)
            do = hid[out_rows, lanes]
            e = jnp.exp2(nt(rot[s, 0, rows, :], rot[s, 1]) * ROOT2 + maskb[item])
            pf = e * (1.0 / jnp.sum(e, -1, keepdims=True))
            dp = nt(do, rot[s, 2])
            delta = jnp.sum(pf * dp, -1, keepdims=True)
            ds = (pf * (dp - delta)).astype(BF)
            dq = nn(ds, rot[s, 1]) * ROOT
            dk += tn(ds, rot[s, 0, rows, :])
            dv += tn(pf.astype(BF), do)
            head_back_store(dq, 0, rows, out_rows)
        dk = dk * ROOT
        for half in range(2):
            rows = pl.ds(half * TOK, TOK)
            out_rows = pl.ds(pl.multiple_of(item * 512 + half * TOK, TOK), TOK)
            head_back_store(dk[half * TOK : half * TOK + TOK], 1, rows, out_rows)
        coef[at(item, 512), at(8 + n % 4, 128)] = dv.astype(BF)
        return carry

    back_proj(at_m)
    back_proj(at_1)
    lax.fori_loop(0, 3, attend_back, 0)
    da_all.pass_on()
    mred.pass_on()
    ra.hop2()
    lax.fori_loop(3, 4, attend_back, 0)
    da_all.last_done()
    rb.hop2()
    back_proj(at_2)
    back_proj(at_3)
    store_tiles(tn(att[...], dattn[...]), dwp, 0, 64, PAD)
    rp.hop1()
    ra.hop3()
    lax.fori_loop(4, 5, attend_back, 0)
    rd.hop2()
    rb.hop3()
    lax.fori_loop(5, 6, attend_back, 0)
    mred.arrive()

    def finish_out(i, carry):
        rows = at(i, 32)
        o = bo[rows, :].astype(F32) + bd[...] + mred.total(rows)
        small[0:1, :] += jnp.sum(og[rows, :].astype(F32) * o, 0, keepdims=True)
        mid = tokp[rows, :].astype(F32) + modv[2:3, :] * attn_out[rows, :]
        bo[rows, :] = ((mid + modv[5:6, :] * o) * valid[rows, :]).astype(BF)
        return carry

    lax.fori_loop(0, 8, finish_out, 0)
    bo[...] = nt(bo[...], perm[...]).astype(BF)
    b_sent, b_got = link.scatter(
        lambda j: bo.at[pl.ds(j * 64, 64)], bout.at[here.z], here.item_source, here.z
    )
    lax.fori_loop(6, 7, attend_back, 0)
    rp.hop2()
    lax.fori_loop(7, 8, attend_back, 0)
    spread_got.wait()

    def squeeze(rows):
        v = coef[rows, :]
        dbq[0:1, :] += jnp.sum(v.astype(F32), 0, keepdims=True)
        hm[rows, 0:864] = nt(v, wg[...].reshape(D, 1536)[0:864]).astype(BF)

    def to_input(rows):
        return nt(hm[rows, 0:864], wq[...].reshape(D, 864))

    link.settle(mred.s1, mred.s2, mred.s3)
    tred = RowReduce(link, rsend, rrecv)
    squeeze(at_3)
    tred.give(3, to_input(at_3))
    squeeze(at_2)
    tred.keep_far(to_input(at_2))
    tred.pass_on()
    rd.hop3()
    squeeze(at_1)
    tred.give(1, to_input(at_1))
    squeeze(at_m)
    own32[...] = to_input(at_m)
    pk[...] = jnp.zeros_like(pk)
    bq4[...] = jnp.zeros_like(bq4)
    bg4[...] = jnp.zeros_like(bg4)
    bq4[m] = dbq[0:1, :]
    bg4[m] = dbg[0:1, :]
    for t in range(2):
        for e in range(2):
            to_ = t * 72 + e * UNIT
            line[:, to_ : to_ + UNIT] = dgain[t : t + 1, e * 64 : e * 64 + UNIT]
    for s in range(32):
        x, c, z, y = s // 16, s // 8 % 2, s // 2 % 4, s % 2
        for q in range(3):
            piece, unit = divmod(2 * s + q, 32) if q < 2 else (2, s)
            _, member, spot = shard_parts(unit)
            from_ = piece * 512 + spot * 64
            pk[x, c, y, z, 1:2, q * UNIT : q * UNIT + UNIT] = bq4[member, :, from_ : from_ + UNIT]
        from_ = shard_parts(s)[0] * UNIT
        pk[x, c, y, z, 1:2, 108:144] = small[5:6, from_ : from_ + UNIT]
        pk[x, c, y, z, 1:2, 144:180] = small[4:5, from_ : from_ + UNIT]
        for q in range(2):
            piece, unit = divmod(2 * s + q, 32)
            _, member, spot = shard_parts(unit)
            from_ = piece * 768 + spot * 96
            pk[x, c, y, z, 2:3, q * 96 : q * 96 + 96] = bg4[member, :, from_ : from_ + 96]
        pk[x, c, y, z, 3:4, 0:144] = line[:, 0:144]
    full_slope = silu_slope(condg[here.dp])
    for b in range(8):
        slope[b] = full_slope[:, b * 144 : b * 144 + 144]
    ha_got.wait()
    for i in range(3):
        store_tiles(tn(dmlp[:, i * 384 : i * 384 + 384], hm[:, 0:864]), wg, i * 384, 48, None)
    rq.hop1()
    rp.hop3()

    def hand_out(reds, base_row, cols, out):
        rows = slice(base_row, base_row + 4 * PAD)
        for red in reds:
            left, right = red.done()
            coef[rows, red.lo : red.split] = tn(pick[...], left).astype(BF)
            coef[rows, red.split : red.hi] = tn(pick[...], right).astype(BF)

        def share(k):
            return coef.at[pl.ds(pl.multiple_of(base_row + k * PAD, 16), PAD), pl.ds(0, cols)]

        over = [link.send(share(here.mate(r)[0]), out.at[m], here.mate(r)[1]) for r in (2, 3, 1)]
        return over, fetch.go(share(m), out.at[m])

    g_over, g_own = hand_out((ra, rb), 0, 1536, fg)
    tred.arrive()

    def first_back(i, carry):
        rows = at(i, 32)
        d = own32[rows, :] + tred.total(rows)
        n, recip = norm_rows(tokp[rows, :].astype(F32))
        small[6:7, :] += jnp.sum(d, 0, keepdims=True)
        small[7:8, :] += jnp.sum(d * n, 0, keepdims=True)
        g = gu[rows, 0:D] + norm_rows_back(d * (1.0 + modv[1:2, :]), n, recip)
        to[rows, :] = g.astype(BF)
        return carry

    lax.fori_loop(0, 8, first_back, 0)
    rows_of = (6, 7, 3, 1, 2, 0)
    for s in range(32):
        x, c, z, y = s // 16, s // 8 % 2, s // 2 % 4, s % 2
        for q in range(6):
            piece, unit = divmod(6 * s + q, 32)
            from_ = shard_parts(unit)[0] * UNIT
            row = rows_of[piece]
            pk[x, c, y, z, 0:1, q * UNIT : q * UNIT + UNIT] = small[row : row + 1, from_ : from_ + UNIT]
    ns = []
    for r in range(1, 8):
        x, c, y, dev = near(here, r)
        ns.append(link.send(pk.at[x, c, y], q1.at[here.x, here.c, here.y], dev))
    q1[here.x, here.c, here.y] = pk[here.x, here.c, here.y]
    rq.hop2()
    to[...] = nt(to[...], perm[...]).astype(BF)
    for n in ns:
        n.wait_recv()
    for z in range(4):
        for x in range(2):
            for y in range(2):
                d = x * 2 + y
                m2[z, d : d + 1, :] = q1[x, 0, y, z, 0:1, :] + q1[x, 1, y, z, 0:1, :]
        total = q1[0, 0, 0, z, 1:4, :]
        for i in range(1, 8):
            total += q1[i // 4, i // 2 % 2, i % 2, z, 1:4, :]
        m2[z, 4:7, :] = total
    zs = []
    for r in (1, 2, 3):
        z, dev = along_z(here, r)
        zs.append(link.send(m2.at[z], q2.at[here.z], dev))
    sent, got = link.scatter(
        lambda j: to.at[pl.ds(j * 64, 64)], dtok.at[here.z], here.item_source, here.z
    )
    rq.hop3()
    q2[here.z] = m2[here.z]
    dm[...] = jnp.zeros_like(dm)
    v = condg[...].reshape(32, D)
    act = (v * jax.nn.sigmoid(v)).astype(BF)

    def plain(red, out):
        left, right = red.done()
        out[...] = nt(left, perm[:, 0 : red.split]) + nt(right, perm[:, red.split : D])

    for c in zs:
        c.wait_recv()
    for z in range(4):
        for d in range(4):
            dm[d * 8 + z : d * 8 + z + 1, :] = q2[z, d : d + 1, 0:216]
    sums[...] = q2[0] + q2[1] + q2[2] + q2[3]
    dbm[...] = jnp.broadcast_to(jnp.sum(dm[...], 0, keepdims=True), (8, 216))
    d3 = three(dm[...])
    da = nn(d3, w_mod_t[...])
    da = da[0:32] + da[32:64] + da[64:96]
    for b in range(8):
        for d in range(4):
            e0[d, b % 2, b // 2] = da[d * 8 : d * 8 + 8, b * 144 : b * 144 + 144]
    ns = []
    for r in range(1, 8):
        x, c, y, dev = near(here, r)
        ns.append(link.send(e0.at[x * 2 + c, y], e1.at[here.x, here.c, here.y], dev))
    e1[here.x, here.c, here.y] = e0[here.dp, here.y]
    plain(rd, fd)
    outs = [fetch.go(fd, fd_out)]
    for n in ns:
        n.wait_recv()
    total = e1[0, 0, 0]
    for i in range(1, 8):
        total += e1[i // 4, i // 2 % 2, i % 2]
    e2[...] = total
    zs = []
    for r in (1, 2, 3):
        z, dev = along_z(here, r)
        zs.append(link.send(e2.at[z], e3.at[here.z], dev))
    e3[here.z] = e2[here.z]
    plain(rp, fp)
    outs.append(fetch.go(fp, fp_out))
    dwm[...] = tn(d3, jnp.concatenate([act, act, act], 0))
    outs.append(fetch.go(dwm, dwm_out))
    g_own.wait()
    for c in g_over:
        c.wait_recv()
    by_column(fg, g_gu, 192, 2)
    outs.append(fetch.go(g_gu, g_gu_out))
    q_over, q_own = hand_out((rq,), 4 * PAD, 896, fq)
    for c in zs:
        c.wait_recv()
    dcond[...] = (e3[0] + e3[1] + e3[2] + e3[3]) * slope[here.z * 2 + here.y]
    q_own.wait()
    for c in q_over:
        c.wait_recv()
    by_column(fq, g_qkv, 72, 3)
    outs.append(fetch.go(g_qkv, g_qkv_out))
    b_got(bo.at[pl.ds(0, 64)], lambda j: bout.at[j])
    got(to.at[pl.ds(0, 64)], lambda j: dtok.at[j])
    for c in outs:
        c.wait()
    link.finish()
    b_sent()
    sent()


def call(kernel, ident, outs, scratch, args, hbm=(), hbm_out=(), sems=64, local=32):
    vm = pl.BlockSpec(memory_space=pltpu.VMEM)
    hb = pl.BlockSpec(memory_space=pltpu.HBM)
    return pl.pallas_call(
        kernel,
        out_shape=[jax.ShapeDtypeStruct(s, t) for s, t in outs],
        in_specs=[hb if i in hbm else vm for i in range(len(args))],
        out_specs=[hb if i in hbm_out else vm for i in range(len(outs))],
        scratch_shapes=scratch + [pltpu.SemaphoreType.DMA((sems,)), pltpu.SemaphoreType.DMA((sems,))]
        + ([pltpu.SemaphoreType.DMA((local,))] if hbm else []),
        compiler_params=pltpu.CompilerParams(
            collective_id=ident, has_side_effects=True, vmem_limit_bytes=LIMIT
        ),
    )(*args)


def local(
    tokens, conditioning, heights, widths, cotangent, w_mod, b_mod, w_qkv, b_qkv, query_gain, key_gain,
    w_proj, b_proj, w_gu, b_gu, w_down, b_down,
):
    args = (
        tokens, conditioning, heights, widths, cotangent, w_mod, b_mod, w_qkv, b_qkv, query_gain, key_gain,
        w_proj, b_proj, w_gu, b_gu, w_down, b_down,
    )
    sizes = tuple(lax.axis_size(a) for a in ("dp", "row", "col"))
    if sizes != (4, 4, 2) or tokens.shape != (4, 4, 16, D):
        return general(*args)
    every = ("dp", "row", "col")
    perm, spread, pick, tabs = constants()
    row = lambda *v: jnp.pad(jnp.concatenate([a.astype(F32) for a in v]), (0, 256 - sum(a.shape[0] for a in v)))
    vecs = [row(b_mod), row(b_qkv, b_proj, b_down), row(b_gu), row(query_gain), row(key_gain), row(heights, widths)]
    vecs = jnp.concatenate(vecs + [jnp.zeros((512,), F32)]).reshape(8, 256)
    w_mod_t = w_mod.T
    full = (GROUP, D)
    block = (TOK, D)
    weights = [(2, 2, 2, 144, 864), (2, 2, 2, 64, D), (2, 2, 2, 144, 1536), (2, 2, 2, 96, D)]
    pairs = [((8, 2, 512, 128), F32), ((8, 3, 512, 128), BF)]
    small_rows = pltpu.VMEM((4, 8, 256), F32)
    (
        wq_all, wp_all, wg_all, wd_all, ha, raw, rot, att, hm, dmlp, tokp, og, attn_out,
        condg, modv, bg, bd, gains, maskb, valid,
    ) = call(
        kernel_a, 0,
        [(w, BF) for w in weights] + [(full, BF)] + pairs + [((GROUP, 512), BF)]
        + [(block, BF), (full, BF), (block, BF), (block, BF)]
        + [
            (s, F32)
            for s in (block, (4, 8, D), (8, D), (1, 1536), (1, D), (8, 128), (2, 1, 512), (TOK, 1))
        ],
        [pltpu.VMEM(w, BF) for w in weights] + [pltpu.VMEM(full, BF)] + [pltpu.VMEM(w, t) for w, t in pairs]
        + [
            pltpu.VMEM((GROUP, 512), BF), pltpu.VMEM((4, PAD, 864), BF), pltpu.VMEM((4, PAD, 1536), BF),
            pltpu.VMEM(block, BF), pltpu.VMEM(block, BF), pltpu.VMEM((D, 1536), BF), pltpu.VMEM((3, TOK, D), BF),
            pltpu.VMEM((3, TOK, D), BF), pltpu.VMEM(block, F32),
            pltpu.VMEM((4, PAD, 864), BF), pltpu.VMEM((4, PAD, 1536), BF), pltpu.VMEM((4, PAD, 1536), F32),
            pltpu.VMEM((8, D), F32), small_rows, small_rows, pltpu.VMEM((4, 4, 8, 256), F32),
            pltpu.VMEM((2, 2, 2, 4, 8, 256), F32), pltpu.VMEM((4, 1, 1536), F32), pltpu.VMEM((4, 1, 1536), F32),
            pltpu.VMEM((1, D), F32), pltpu.VMEM(block, BF), pltpu.VMEM(full, BF), pltpu.VMEM(block, BF),
            pltpu.VMEM(block, BF), pltpu.VMEM(block, F32), pltpu.VMEM((D, D), BF), pltpu.VMEM((864, 1536), BF),
            pltpu.VMEM((3, 512, 128), F32),
        ],
        (
            tokens.reshape(4, 64, D), cotangent.reshape(4, 64, D), w_qkv, w_gu, w_proj, w_down, conditioning, w_mod_t,
            vecs, perm, spread, pick, tabs,
        ),
        hbm=(0, 1, 9, 10, 12),
        hbm_out=range(13),
        sems=128,
    )
    spread = jnp.pad(spread, ((0, D - 864), (0, 0))).reshape(2, 2, 2, 144, 1536)
    dtok, bout, g_w_qkv, g_w_gu, fp, fd, g_w_mod, sums, g_b_mod, d_cond = call(
        kernel_b, 1,
        [
            ((4, 64, D), BF), ((4, 64, D), BF), ((UNIT, 3456), F32), ((UNIT, 6144), F32), ((PAD, D), F32),
            ((96, D), F32), ((216, D), F32), ((8, 256), F32), ((8, 216), F32), ((8, 144), F32),
        ],
        [
            pltpu.VMEM((2, 2, 2, 144, 1536), BF), pltpu.VMEM((2, 2, 2, 96, D), BF), pltpu.VMEM(full, BF),
            pltpu.VMEM(full, BF), pltpu.VMEM(block, BF), pltpu.VMEM(block, BF), pltpu.VMEM(block, F32),
            pltpu.VMEM((GROUP, 512), BF), pltpu.VMEM((2, 2, 2, 64, D), BF), pltpu.VMEM((2, 2, 2, 144, 864), BF),
            pltpu.VMEM((D, D), BF), pltpu.VMEM((3, 512, 128), F32), pltpu.VMEM((TOK, 1536), F32),
            pltpu.VMEM((GROUP, 1536), BF), pltpu.VMEM((GROUP, 768), BF), pltpu.VMEM((3, TOK, D), BF),
            pltpu.VMEM((3, TOK, D), BF), pltpu.VMEM((3, TOK, D), BF), pltpu.VMEM(block, F32),
            pltpu.VMEM((2, 2, 2, 144, 1536), BF), pltpu.VMEM((2, 2, 2, 96, D), BF), pltpu.VMEM((2, 2, 2, PAD, D), BF),
            pltpu.VMEM(full, BF), pltpu.VMEM((2, 2, 512, 128), F32), pltpu.VMEM((2, 3, 512, 128), BF),
            pltpu.VMEM(block, BF), pltpu.VMEM(block, BF), pltpu.VMEM((4, PAD, 896), BF), pltpu.VMEM((4, PAD, 1536), BF),
            pltpu.VMEM((8, D), F32), pltpu.VMEM((8, 1536), F32), pltpu.VMEM((8, 1536), F32), pltpu.VMEM((8, 128), F32),
            pltpu.VMEM((2, 2, 2, 4, 8, 256), F32), pltpu.VMEM((2, 2, 2, 4, 8, 256), F32), small_rows, small_rows,
            pltpu.VMEM((32, 216), F32), pltpu.VMEM((4, 2, 4, 8, 144), F32), pltpu.VMEM((2, 2, 2, 4, 8, 144), F32),
            pltpu.VMEM((4, 8, 144), F32), pltpu.VMEM((4, 8, 144), F32), pltpu.VMEM((1, 256), F32),
            pltpu.VMEM((4, 1, 1536), F32), pltpu.VMEM((4, 1, 1536), F32), pltpu.VMEM((8, 8, 144), F32),
            pltpu.VMEM((UNIT, 3456), F32), pltpu.VMEM((UNIT, 6144), F32), pltpu.VMEM((PAD, D), F32),
            pltpu.VMEM((96, D), F32), pltpu.VMEM((216, D), F32),
        ]
        + Reduce.buffers(144, 768, 384) * 2 + Reduce.buffers(96, D, SPLIT_D)
        + Reduce.buffers(144, 896, SPLIT_Q) + Reduce.buffers(PAD, D, SPLIT_P),
        (
            wg_all, wd_all, hm, dmlp, tokp, og, attn_out, att, wp_all, wq_all, ha, raw, rot, perm, spread, tabs,
            modv, bg, bd, gains, maskb, valid, pick, condg, w_mod_t,
        ),
        hbm=range(16),
        hbm_out=range(7),
        sems=128,
    )

    one, two = sums[4], sums[5]
    gains_out = sums[6]
    return (
        bout.reshape(tokens.shape),
        dtok.reshape(tokens.shape).astype(F32),
        d_cond[:4],
        g_w_mod.T,
        g_b_mod[0],
        g_w_qkv,
        one[:72],
        one[72:108],
        gains_out[:72],
        gains_out[72:144],
        fp[:UNIT],
        one[108:144],
        g_w_gu,
        two[:192],
        fd,
        one[144:180],
    )


def solution(mesh):
    in_specs = (
        P("dp", "row", "col", None),
        P("dp", None),
        P("dp"),
        P("dp"),
        P("dp", "row", "col", None),
        P(None, ("dp", "row", "col")),
        P(("dp", "row", "col")),
        P(("dp", "row", "col"), None),
        P(("dp", "row", "col")),
        P(),
        P(),
        P(("dp", "row", "col"), None),
        P(("dp", "row", "col")),
        P(("dp", "row", "col"), None),
        P(("dp", "row", "col")),
        P(("dp", "row", "col"), None),
        P(("dp", "row", "col")),
    )
    out_specs = (
        P("dp", "row", "col", None),
        P("dp", "row", "col", None),
        P("dp", ("row", "col")),
        P(None, ("dp", "row", "col")),
        P(("dp", "row", "col")),
        P(("dp", "row", "col"), None),
        P(("dp", "row", "col")),
        P(("dp", "row", "col")),
        P(),
        P(),
        P(("dp", "row", "col"), None),
        P(("dp", "row", "col")),
        P(("dp", "row", "col"), None),
        P(("dp", "row", "col")),
        P(("dp", "row", "col"), None),
        P(("dp", "row", "col")),
    )
    return jax.shard_map(local, mesh=mesh, in_specs=in_specs, out_specs=out_specs, check_vma=False)
```

```python
import math

import jax
import jax.numpy as jnp
import numpy as np
from jax import lax
from jax.experimental import pallas as pl
from jax.experimental.pallas import tpu as pltpu
from jax.sharding import PartitionSpec as P

HEADS = 16
HEAD = 72
FF = 3072


EPSILON = 1e-06
MASKED = -1000000000.0
PRECISE = lax.Precision.HIGHEST


def rope_tables(row_pos, col_pos, head_size):
    half_size = head_size // 2
    lane_index = jnp.arange(head_size)
    pair_index = (lane_index % half_size // 2).astype(jnp.float32)
    frequency = jnp.exp(-math.log(10000.0) * 2.0 * pair_index / half_size)
    places = jnp.where(lane_index[None, :] >= half_size, col_pos[:, None], row_pos[:, None]).astype(
        jnp.float32
    )
    angles = places * frequency[None, :]
    return (jnp.cos(angles), jnp.sin(angles))


def rotate(values):
    pair_view = values.reshape(values.shape[:-1] + (values.shape[-1] // 2, 2))
    turned = jnp.stack((-pair_view[..., 1], pair_view[..., 0]), axis=-1)
    return turned.reshape(values.shape)


def norm_parts(values):
    centered = values - jnp.mean(values, -1, keepdims=True)
    recip = lax.rsqrt(jnp.mean(centered * centered, -1, keepdims=True) + EPSILON)
    return (centered * recip, recip)


def norm_back(gradient, normed, recip):
    return recip * (
        gradient
        - jnp.mean(gradient, -1, keepdims=True)
        - normed * jnp.mean(gradient * normed, -1, keepdims=True)
    )


def head_back(gradient, raw_value, recip, gain_vec):
    scaled = gradient * gain_vec
    gain_grad = jnp.sum(gradient * raw_value * recip, axis=(0, 1, 2))
    raw_grad = recip * scaled - raw_value * (recip * recip * recip) * jnp.mean(
        scaled * raw_value, -1, keepdims=True
    )
    return (raw_grad, gain_grad)


def general(
    tokens,
    conditioning,
    heights,
    widths,
    cotangent,
    w_mod,
    b_mod,
    w_qkv,
    b_qkv,
    query_gain,
    key_gain,
    w_proj,
    b_proj,
    w_gu,
    b_gu,
    w_down,
    b_down,
):
    item_count, tile_rows, tile_cols, model_width = tokens.shape
    tile_span = tile_rows * tile_cols
    n_row = lax.axis_size("row")
    n_col = lax.axis_size("col")
    groups = n_row * n_col
    key_count = tile_span * groups
    inv_root = 1.0 / math.sqrt(HEAD)
    row_at = lax.axis_index("row")
    col_at = lax.axis_index("col")
    local_index = jnp.arange(tile_span)
    query_rows = row_at * tile_rows + local_index // tile_cols
    query_cols = col_at * tile_cols + local_index % tile_cols
    valid_query = (query_rows[None, :] < heights[:, None]) & (query_cols[None, :] < widths[:, None])
    key_index = jnp.arange(key_count)
    key_owner = key_index // tile_span
    key_spot = key_index % tile_span
    key_rows = key_owner // n_col * tile_rows + key_spot // tile_cols
    key_cols = key_owner % n_col * tile_cols + key_spot % tile_cols
    valid_key = (key_rows[None, :] < heights[:, None]) & (key_cols[None, :] < widths[:, None])
    cos_tab, sin_tab = rope_tables(query_rows, query_cols, HEAD)
    cos_four = cos_tab[None, :, None, :]
    sin_four = sin_tab[None, :, None, :]
    cond_f = conditioning.astype(jnp.float32)
    cond_sig = jax.nn.sigmoid(cond_f)
    act_low = (cond_f * cond_sig).astype(jnp.bfloat16)
    gathered = (
        lax.all_gather(w_mod, ("dp", "row", "col"), axis=1, tiled=True),
        lax.all_gather(b_mod, ("dp", "row", "col"), axis=0, tiled=True),
        lax.all_gather(w_qkv, ("dp", "row", "col"), axis=0, tiled=True),
        lax.all_gather(b_qkv, ("dp", "row", "col"), axis=0, tiled=True),
        lax.all_gather(w_proj, ("dp", "row", "col"), axis=0, tiled=True),
        lax.all_gather(b_proj, ("dp", "row", "col"), axis=0, tiled=True),
        lax.all_gather(w_gu, ("dp", "row", "col"), axis=0, tiled=True),
        lax.all_gather(b_gu, ("dp", "row", "col"), axis=0, tiled=True),
        lax.all_gather(w_down, ("dp", "row", "col"), axis=0, tiled=True),
        lax.all_gather(b_down, ("dp", "row", "col"), axis=0, tiled=True),
    )
    (
        w_mod_all,
        b_mod_all,
        w_qkv_all,
        b_qkv_all,
        w_proj_all,
        b_proj_all,
        w_gu_all,
        b_gu_all,
        w_down_all,
        b_down_all,
    ) = gathered
    modul = jnp.dot(act_low, w_mod_all, preferred_element_type=jnp.float32) + b_mod_all.astype(
        jnp.float32
    )
    shift_a, scale_a, gate_a, shift_m, scale_m, gate_m = [
        modul[:, piece * model_width : (piece + 1) * model_width][:, None, :] for piece in range(6)
    ]
    resid_in = tokens.reshape(item_count, tile_span, model_width).astype(jnp.float32)
    normed_a, recip_a = norm_parts(resid_in)
    h_attn = (normed_a * (1.0 + scale_a) + shift_a).astype(jnp.bfloat16)
    qkv_all = jnp.dot(h_attn, w_qkv_all, preferred_element_type=jnp.float32) + b_qkv_all.astype(
        jnp.float32
    )
    query_raw = qkv_all[..., :model_width].reshape(item_count, tile_span, HEADS, HEAD)
    key_raw = qkv_all[..., model_width : 2 * model_width].reshape(
        item_count, tile_span, HEADS, HEAD
    )
    value_raw = qkv_all[..., 2 * model_width :]
    query_recip = lax.rsqrt(jnp.mean(query_raw * query_raw, -1, keepdims=True) + EPSILON)
    key_recip = lax.rsqrt(jnp.mean(key_raw * key_raw, -1, keepdims=True) + EPSILON)
    query_normed = query_raw * query_recip * query_gain
    key_normed = key_raw * key_recip * key_gain
    query_rot = (query_normed * cos_four + rotate(query_normed) * sin_four).astype(jnp.bfloat16)
    key_rot = (key_normed * cos_four + rotate(key_normed) * sin_four).astype(jnp.bfloat16)
    value_low = value_raw.astype(jnp.bfloat16)
    kv_local = jnp.concatenate([key_rot.reshape(item_count, tile_span, model_width), value_low], -1)
    kv_every = lax.all_gather(kv_local, ("row", "col"), axis=1, tiled=True)
    query_heads = query_rot.transpose(2, 0, 1, 3)
    key_part = (
        kv_every[..., :model_width]
        .reshape(item_count, key_count, HEADS, HEAD)
        .transpose(2, 0, 1, 3)
    )
    value_part = (
        kv_every[..., model_width:]
        .reshape(item_count, key_count, HEADS, HEAD)
        .transpose(2, 0, 1, 3)
    )
    key_mask = valid_key[:, None, :]

    def attend(head_block):
        query_h, key_h, value_h = head_block
        scores = (
            jnp.einsum("itd,ikd->itk", query_h, key_h, preferred_element_type=jnp.float32)
            * inv_root
        )
        scores = jnp.where(key_mask, scores, MASKED)
        row_max = jnp.max(scores, -1, keepdims=True)
        exponent = jnp.exp(scores - row_max)
        row_sum = jnp.sum(exponent, -1, keepdims=True)
        probs = (exponent / row_sum).astype(jnp.bfloat16)
        result = jnp.einsum("itk,ikd->itd", probs, value_h, preferred_element_type=jnp.float32)
        return (result, row_max, row_sum)

    attended_heads, max_kept, sum_kept = lax.map(attend, (query_heads, key_part, value_part))
    attended = (
        attended_heads.transpose(1, 2, 0, 3)
        .reshape(item_count, tile_span, model_width)
        .astype(jnp.bfloat16)
    )
    attn_out = jnp.dot(
        attended, w_proj_all, preferred_element_type=jnp.float32
    ) + b_proj_all.astype(jnp.float32)
    resid_mid = resid_in + gate_a * attn_out
    normed_m, recip_m = norm_parts(resid_mid)
    h_mlp = (normed_m * (1.0 + scale_m) + shift_m).astype(jnp.bfloat16)
    gate_up = jnp.dot(h_mlp, w_gu_all, preferred_element_type=jnp.float32) + b_gu_all.astype(
        jnp.float32
    )
    gate_part = gate_up[..., :FF]
    up_part = gate_up[..., FF:]
    gate_sig = jax.nn.sigmoid(gate_part)
    gate_act = gate_part * gate_sig
    hidden = (gate_act * up_part).astype(jnp.bfloat16)
    mlp_out = jnp.dot(hidden, w_down_all, preferred_element_type=jnp.float32) + b_down_all.astype(
        jnp.float32
    )
    mask_f = valid_query[..., None].astype(jnp.float32)
    block_out = ((resid_mid + gate_m * mlp_out) * mask_f).astype(jnp.bfloat16)
    out_grad = cotangent.reshape(item_count, tile_span, model_width).astype(jnp.float32) * mask_f
    d_mlp = (gate_m * out_grad).astype(jnp.bfloat16)
    d_gate_m = jnp.sum(out_grad * mlp_out, 1)
    dw_down = jnp.einsum("itf,itd->fd", hidden, d_mlp, preferred_element_type=jnp.float32)
    db_down = jnp.sum(d_mlp.astype(jnp.float32), (0, 1))
    d_hidden = jnp.einsum("itd,fd->itf", d_mlp, w_down_all, preferred_element_type=jnp.float32)
    d_gate = d_hidden * up_part * gate_sig * (1.0 + gate_part * (1.0 - gate_sig))
    d_up = d_hidden * gate_act
    d_gate_up = jnp.concatenate([d_gate, d_up], -1).astype(jnp.bfloat16)
    dw_gu = jnp.einsum("itd,ite->de", h_mlp, d_gate_up, preferred_element_type=jnp.float32)
    db_gu = jnp.sum(d_gate_up.astype(jnp.float32), (0, 1))
    d_hmlp = jnp.einsum("ite,de->itd", d_gate_up, w_gu_all, preferred_element_type=jnp.float32)
    d_shift_m = jnp.sum(d_hmlp, 1)
    d_scale_m = jnp.sum(d_hmlp * normed_m, 1)
    d_mid = out_grad + norm_back(d_hmlp * (1.0 + scale_m), normed_m, recip_m)
    d_attn = (gate_a * d_mid).astype(jnp.bfloat16)
    d_gate_a = jnp.sum(d_mid * attn_out, 1)
    dw_proj = jnp.einsum("itd,ite->de", attended, d_attn, preferred_element_type=jnp.float32)
    db_proj = jnp.sum(d_attn.astype(jnp.float32), (0, 1))
    d_attended = jnp.einsum(
        "ite,de->itd", d_attn, w_proj_all, preferred_element_type=jnp.float32
    ).astype(jnp.bfloat16)
    d_att_heads = d_attended.reshape(item_count, tile_span, HEADS, HEAD).transpose(2, 0, 1, 3)
    key_back, value_back = (key_part, value_part)

    def attend_back(head_block):
        query_h, key_h, value_h, grad_h, max_h, sum_h = head_block
        scores = (
            jnp.einsum("itd,ikd->itk", query_h, key_h, preferred_element_type=jnp.float32)
            * inv_root
        )
        scores = jnp.where(key_mask, scores, MASKED)
        probs = jnp.exp(scores - max_h) / sum_h
        d_probs = jnp.einsum("itd,ikd->itk", grad_h, value_h, preferred_element_type=jnp.float32)
        delta = jnp.sum(probs * d_probs, -1, keepdims=True)
        d_scores = (probs * (d_probs - delta)).astype(jnp.bfloat16)
        d_query = (
            jnp.einsum("itk,ikd->itd", d_scores, key_h, preferred_element_type=jnp.float32)
            * inv_root
        )
        d_key = (
            jnp.einsum("itk,itd->ikd", d_scores, query_h, preferred_element_type=jnp.float32)
            * inv_root
        )
        d_value = jnp.einsum(
            "itk,itd->ikd", probs.astype(jnp.bfloat16), grad_h, preferred_element_type=jnp.float32
        )
        return (d_query, d_key, d_value)

    dq_heads, dk_heads, dv_heads = lax.map(
        attend_back, (query_heads, key_back, value_back, d_att_heads, max_kept, sum_kept)
    )
    dkv_term = jnp.concatenate(
        [
            dk_heads.transpose(1, 2, 0, 3).reshape(item_count, key_count, model_width),
            dv_heads.transpose(1, 2, 0, 3).reshape(item_count, key_count, model_width),
        ],
        -1,
    )
    dkv_own = lax.psum_scatter(dkv_term, ("row", "col"), scatter_dimension=1, tiled=True)
    d_key_rot = dkv_own[..., :model_width].reshape(item_count, tile_span, HEADS, HEAD)
    d_value = dkv_own[..., model_width:]
    d_query_rot = dq_heads.transpose(1, 2, 0, 3)
    d_query_n = d_query_rot * cos_four - rotate(d_query_rot * sin_four)
    d_key_n = d_key_rot * cos_four - rotate(d_key_rot * sin_four)
    d_query_raw, dq_gain = head_back(d_query_n, query_raw, query_recip, query_gain)
    d_key_raw, dk_gain = head_back(d_key_n, key_raw, key_recip, key_gain)
    gain_total = lax.psum((dq_gain, dk_gain), ("dp", "row", "col"))
    d_qkv = jnp.concatenate(
        [
            d_query_raw.reshape(item_count, tile_span, model_width),
            d_key_raw.reshape(item_count, tile_span, model_width),
            d_value,
        ],
        -1,
    ).astype(jnp.bfloat16)
    dw_qkv = jnp.einsum("itd,ite->de", h_attn, d_qkv, preferred_element_type=jnp.float32)
    db_qkv = jnp.sum(d_qkv.astype(jnp.float32), (0, 1))
    db_query_key = db_qkv[: 2 * model_width]
    db_value = db_qkv[2 * model_width :]
    d_hattn = jnp.einsum("ite,de->itd", d_qkv, w_qkv_all, preferred_element_type=jnp.float32)
    d_shift_a = jnp.sum(d_hattn, 1)
    d_scale_a = jnp.sum(d_hattn * normed_a, 1)
    d_tokens = d_mid + norm_back(d_hattn * (1.0 + scale_a), normed_a, recip_a)
    d_modul = jnp.concatenate([d_shift_a, d_scale_a, d_gate_a, d_shift_m, d_scale_m, d_gate_m], -1)
    act_f = act_low.astype(jnp.float32)
    dw_mod = jnp.einsum("id,ie->de", act_f, d_modul, precision=PRECISE)
    db_mod = jnp.sum(d_modul, 0)
    d_act = jnp.einsum("ie,de->id", d_modul, w_mod_all.astype(jnp.float32), precision=PRECISE)
    d_cond_part = d_act * cond_sig * (1.0 + cond_f * (1.0 - cond_sig))
    d_cond = lax.psum_scatter(d_cond_part, ("row", "col"), scatter_dimension=1, tiled=True)
    summed = (
        lax.psum_scatter(dw_mod, ("dp", "row", "col"), scatter_dimension=1, tiled=True),
        lax.psum_scatter(db_mod, ("dp", "row", "col"), scatter_dimension=0, tiled=True),
        lax.psum_scatter(dw_qkv, ("dp", "row", "col"), scatter_dimension=0, tiled=True),
        lax.psum_scatter(db_query_key, ("dp", "row", "col"), scatter_dimension=0, tiled=True),
        lax.psum_scatter(db_value, ("dp", "row", "col"), scatter_dimension=0, tiled=True),
        lax.psum_scatter(dw_proj, ("dp", "row", "col"), scatter_dimension=0, tiled=True),
        lax.psum_scatter(db_proj, ("dp", "row", "col"), scatter_dimension=0, tiled=True),
        lax.psum_scatter(dw_gu, ("dp", "row", "col"), scatter_dimension=0, tiled=True),
        lax.psum_scatter(db_gu, ("dp", "row", "col"), scatter_dimension=0, tiled=True),
        lax.psum_scatter(dw_down, ("dp", "row", "col"), scatter_dimension=0, tiled=True),
        lax.psum_scatter(db_down, ("dp", "row", "col"), scatter_dimension=0, tiled=True),
    )
    (
        g_w_mod,
        g_b_mod,
        g_w_qkv,
        g_b_query_key,
        g_b_value,
        g_w_proj,
        g_b_proj,
        g_w_gu,
        g_b_gu,
        g_w_down,
        g_b_down,
    ) = summed
    return (
        block_out.reshape(item_count, tile_rows, tile_cols, model_width),
        d_tokens.reshape(item_count, tile_rows, tile_cols, model_width),
        d_cond,
        g_w_mod,
        g_b_mod,
        g_w_qkv,
        g_b_query_key,
        g_b_value,
        gain_total[0],
        gain_total[1],
        g_w_proj,
        g_b_proj,
        g_w_gu,
        g_b_gu,
        g_w_down,
        g_b_down,
    )


MESH = pl.DeviceIdType.MESH
BF = jnp.bfloat16
F32 = jnp.float32
LIMIT = 60 * 1024 * 1024
D = 1152
UNIT = 36
PAD = 48
TOK = 256
GROUP = 1024
SPLIT_Q, SPLIT_P, SPLIT_D = 384, 640, 640
ROOT = 1.0 / math.sqrt(HEAD)
ROOT2 = ROOT / math.log(2.0)


def nn(a, b):
    return lax.dot_general(a, b, (((1,), (0,)), ((), ())), preferred_element_type=F32)


def nt(a, b):
    return lax.dot_general(a, b, (((1,), (1,)), ((), ())), preferred_element_type=F32)


def tn(a, b):
    return lax.dot_general(a, b, (((0,), (0,)), ((), ())), preferred_element_type=F32)


def width_order():
    xx, zh, yy, zl, cc, jj = np.indices((2, 2, 2, 2, 2, UNIT)).reshape(6, -1)
    return ((((xx * 2 + cc) * 2 + zh) * 2 + zl) * 2 + yy) * UNIT + jj


def constants():
    perm = np.zeros((D, D), np.float32)
    perm[width_order(), np.arange(D)] = 1.0
    spread = np.zeros((864, 1536), np.float32)
    tt, hh, yy, jj = np.indices((3, 4, 2, UNIT)).reshape(4, -1)
    spread[tt * 288 + hh * 72 + yy * 36 + jj, tt * 512 + hh * 128 + yy * 64 + jj] = 1.0
    pick = np.zeros((144, 192), np.float32)
    kk, jj = np.indices((4, UNIT)).reshape(2, -1)
    pick[kk * 36 + jj, kk * 48 + jj] = 1.0
    spot = np.arange(512)
    row = spot // 128 * 4 + spot // 16 % 4
    col = spot // 64 % 2 * 16 + spot % 16
    lane = np.arange(128)
    part = lane % 64
    freq = np.exp(-math.log(10000.0) * 2.0 * (part // 2) / 36.0)
    place = np.where(lane[None, :] >= 64, col[:, None], row[:, None]).astype(np.float64)
    angle = place * freq[None, :]
    live = part < UNIT
    cos = np.where(live, np.cos(angle), 0.0)
    sin = np.where(live, np.sin(angle), 0.0)
    even = lane % 2 == 0
    tabs = np.stack([cos, np.where(even, -sin, 0.0), np.where(even, 0.0, sin)]).astype(np.float32)
    return (
        jnp.asarray(perm, BF),
        jnp.asarray(spread, BF),
        jnp.asarray(pick, BF),
        jnp.asarray(tabs, F32),
    )


class Place:
    def __init__(self):
        dp = lax.axis_index("dp")
        self.z = lax.axis_index("row")
        self.y = lax.axis_index("col")
        self.x = dp // 2
        self.c = dp % 2
        self.zh = self.z // 2
        self.zl = self.z % 2
        self.m = self.zl * 2 + self.c
        self.dp = dp

    def mate(self, r):
        c = 1 - self.c if r % 2 else self.c
        zl = 1 - self.zl if r // 2 else self.zl
        return zl * 2 + c, (self.x * 2 + c, self.zh * 2 + zl, self.y)

    def xpeer(self):
        return ((1 - self.x) * 2 + self.c, self.z, self.y)

    def ypeer(self):
        return (self.dp, self.z, 1 - self.y)

    def zpeer(self):
        return (self.dp, (1 - self.zh) * 2 + self.zl, self.y)

    def item_home(self, j):
        return (self.x * 2 + self.zh, j, self.c)

    def item_source(self, blk):
        return (self.x * 2 + self.y, self.c * 2 + blk // 2, blk % 2)

    def is_me(self, dev):
        return (dev[0] == self.dp) & (dev[1] == self.z) & (dev[2] == self.y)


class Link:
    def __init__(self, here, ssem, rsem):
        self.here, self.ssem, self.rsem, self.n, self.open = here, ssem, rsem, 0, []

    def greet(self, items):
        here = self.here
        bar = pltpu.get_barrier_semaphore()
        devs = [here.mate(r)[1] for r in (1, 2, 3)]
        devs += [here.xpeer(), here.ypeer(), here.zpeer()]
        devs += [near(here, r)[3] for r in range(1, 8)] + [along_z(here, r)[1] for r in (1, 2, 3)]
        for d in devs:
            pl.semaphore_signal(bar, inc=1, device_id=d, device_id_type=MESH)
        total = len(devs)
        if items:
            for d in [here.item_home(j) for j in range(4)] + [here.item_source(j) for j in range(4)]:


                @pl.when(jnp.logical_not(here.is_me(d)))
                def _():
                    pl.semaphore_signal(bar, inc=1, device_id=d, device_id_type=MESH)

            far = (here.zh - here.c) * (here.zh - here.c)
            off = (here.y - here.c) * (here.y - here.c)
            total += 8 - 2 * (1 - far) * (1 - off)
        pl.semaphore_wait(bar, total)

    def send(self, src, dst, dev):
        k = self.n
        self.n += 1
        copy = pltpu.make_async_remote_copy(
            src_ref=src,
            dst_ref=dst,
            send_sem=self.ssem.at[k],
            recv_sem=self.rsem.at[k],
            device_id=dev,
            device_id_type=MESH,
        )
        copy.start()
        self.open.append(copy)
        return copy

    def scatter(self, src_of, dst, dev_of, slot):
        base = self.n
        self.n += 4
        here = self.here
        copies = []
        for j in range(4):
            dev = dev_of(j)
            mine = here.is_me(dev)
            remote = pltpu.make_async_remote_copy(
                src_ref=src_of(j),
                dst_ref=dst,
                send_sem=self.ssem.at[base + j],
                recv_sem=self.rsem.at[base + slot],
                device_id=dev,
                device_id_type=MESH,
            )
            local_copy = pltpu.make_async_copy(src_of(j), dst, self.rsem.at[base + slot])

            @pl.when(mine)
            def _():
                local_copy.start()

            @pl.when(jnp.logical_not(mine))
            def _():
                remote.start()

            copies.append((mine, remote))

        def wait_send():
            for mine, remote in copies:

                @pl.when(jnp.logical_not(mine))
                def _():
                    remote.wait_send()

        def wait_recv(src, dst_of):
            for j in range(4):
                pltpu.make_async_copy(src, dst_of(j), self.rsem.at[base + j]).wait()

        return wait_send, wait_recv

    def settle(self, *copies):
        for copy in copies:
            copy.wait_send()
            self.open = [c for c in self.open if c is not copy]

    def finish(self):
        for copy in self.open:
            copy.wait_send()
        self.open = []


def norm_rows(x):
    mean = jnp.sum(x, -1, keepdims=True) * (1.0 / D)
    cent = x - mean
    var = jnp.sum(cent * cent, -1, keepdims=True) * (1.0 / D)
    recip = lax.rsqrt(var + EPSILON)
    return cent * recip, recip


def norm_rows_back(g, y, recip):
    mg = jnp.sum(g, -1, keepdims=True) * (1.0 / D)
    mgy = jnp.sum(g * y, -1, keepdims=True) * (1.0 / D)
    return recip * (g - mg - y * mgy)


def at(i, n):
    return pl.ds(pl.multiple_of(i * n, n), n)


class Gather:
    def __init__(self, link, ref, rows, lo, split, hi):
        self.link, self.ref, self.rows = link, ref, rows
        self.ca, self.cb = pl.ds(lo, split - lo), pl.ds(split, hi - split)
        self.all = slice(None) if hi - lo == ref.shape[-1] else pl.ds(lo, hi - lo)

    def cut(self, i, j, k, cols):
        return self.ref.at[i, j, k, pl.ds(0, self.rows), cols]

    def hop1(self):
        h = self.link.here
        part = self.cut(h.x, h.zh, h.y, self.all)
        self.a = self.link.send(part, part, h.zpeer())

    def hop2(self):
        h = self.link.here
        self.a.wait_recv()
        pa = self.cut(h.x, slice(None), h.y, self.ca)
        pb = self.cut(h.x, slice(None), h.y, self.cb)
        self.a = self.link.send(pa, pa, h.xpeer())
        self.b = self.link.send(pb, pb, h.ypeer())

    def parts(self, ref):
        h = self.link.here
        rows = pl.ds(0, self.rows)
        return ref.at[:, :, h.y, rows, self.ca], ref.at[h.x, :, :, rows, self.cb]

    def hop3(self):
        self.done()
        self.last_hop()

    def last_hop(self, held=None):
        h = self.link.here
        pa, pb = self.parts(self.ref)
        if held is not None:
            ha, hb = self.parts(held)
            self.a = self.link.send(ha, pa, h.ypeer())
            self.b = self.link.send(hb, pb, h.xpeer())
            return
        self.a = self.link.send(pa, pa, h.ypeer())
        self.b = self.link.send(pb, pb, h.xpeer())

    def done(self):
        self.a.wait_recv()
        self.b.wait_recv()


class Reduce:
    def __init__(self, link, ref, bufs, lo, split, hi):
        self.link, self.ref, self.lo, self.split, self.hi = link, ref, lo, split, hi
        self.r1a, self.r1b, self.r2a, self.r2b, self.r3a, self.r3b = bufs

    @staticmethod
    def buffers(rows, cols, split):
        rest = cols - split
        return [
            pltpu.VMEM((2, 2, rows, split), BF),
            pltpu.VMEM((2, 2, rows, rest), BF),
            pltpu.VMEM((2, rows, split), BF),
            pltpu.VMEM((2, rows, rest), BF),
            pltpu.VMEM((rows, split), BF),
            pltpu.VMEM((rows, rest), BF),
        ]

    def hop1(self):
        h = self.link.here
        ca, cb = pl.ds(self.lo, self.split - self.lo), pl.ds(self.split, self.hi - self.split)
        self.a = self.link.send(self.ref.at[1 - h.x, :, :, :, ca], self.r1a, h.xpeer())
        self.b = self.link.send(self.ref.at[:, :, 1 - h.y, :, cb], self.r1b, h.ypeer())

    def hop2(self):
        h = self.link.here
        ca, cb = pl.ds(self.lo, self.split - self.lo), pl.ds(self.split, self.hi - self.split)
        self.a.wait_recv()
        self.b.wait_recv()

        def add(i, carry):
            u, v = i // 2, i % 2
            own = self.ref[h.x, u, v, :, ca].astype(F32)
            self.r1a[u, v] = (self.r1a[u, v].astype(F32) + own).astype(BF)
            own = self.ref[u, v, h.y, :, cb].astype(F32)
            self.r1b[u, v] = (self.r1b[u, v].astype(F32) + own).astype(BF)
            return carry

        lax.fori_loop(0, 4, add, 0)
        self.a = self.link.send(self.r1a.at[:, 1 - h.y], self.r2a, h.ypeer())
        self.b = self.link.send(self.r1b.at[1 - h.x], self.r2b, h.xpeer())

    def hop3(self):
        h = self.link.here
        self.a.wait_recv()
        self.b.wait_recv()

        def add(u, carry):
            own = self.r1a[u, h.y].astype(F32)
            self.r2a[u] = (self.r2a[u].astype(F32) + own).astype(BF)
            own = self.r1b[h.x, u].astype(F32)
            self.r2b[u] = (self.r2b[u].astype(F32) + own).astype(BF)
            return carry

        lax.fori_loop(0, 2, add, 0)
        self.a = self.link.send(self.r2a.at[1 - h.zh], self.r3a, h.zpeer())
        self.b = self.link.send(self.r2b.at[1 - h.zh], self.r3b, h.zpeer())

    def done(self):
        h = self.link.here
        self.a.wait_recv()
        self.b.wait_recv()
        left = self.r2a[h.zh].astype(F32) + self.r3a[...].astype(F32)
        right = self.r2b[h.zh].astype(F32) + self.r3b[...].astype(F32)
        return left.astype(BF), right.astype(BF)


class RowGather:
    def __init__(self, link, ref):
        self.link, self.ref = link, ref
        here = link.here
        own = ref.at[at(here.m, TOK)]
        self.far = link.send(own, own, here.mate(2)[1])
        self.near = link.send(own, own, here.mate(1)[1])

    def near_done(self):
        self.near.wait_recv()

    def pass_on(self):
        here = self.link.here
        self.far.wait_recv()
        rows = self.ref.at[at(here.mate(2)[0], TOK)]
        self.last = self.link.send(rows, rows, here.mate(1)[1])

    def last_done(self):
        self.last.wait_recv()


class RowReduce:
    def __init__(self, link, out, into):
        self.link, self.out, self.into = link, out, into

    def give(self, r, val):
        i = 0 if r == 3 else 1
        if val is not None:
            self.out[i] = val.astype(BF)
        sent = self.link.send(self.out.at[i], self.into.at[i], self.link.here.mate(1)[1])
        if r == 3:
            self.s3 = sent
        else:
            self.s1 = sent

    def keep_far(self, val):
        self.out[2] = val.astype(BF)

    def pass_on(self):
        self.s3.wait_recv()

        def add(i, carry):
            rows = at(i, 32)
            both = self.out[2, rows, :].astype(F32) + self.into[0, rows, :].astype(F32)
            self.out[2, rows, :] = both.astype(BF)
            return carry

        lax.fori_loop(0, 8, add, 0)
        self.s2 = self.link.send(self.out.at[2], self.into.at[2], self.link.here.mate(2)[1])

    def arrive(self):
        self.s1.wait_recv()
        self.s2.wait_recv()

    def total(self, rows):
        return self.into[1, rows, :].astype(F32) + self.into[2, rows, :].astype(F32)


def turn(v, cos, sina, sinb):
    return v * cos + pltpu.roll(v, 127, 1) * sina + pltpu.roll(v, 1, 1) * sinb


def turn_back(d, cos, sina, sinb):
    return d * cos - pltpu.roll(d, 127, 1) * sina - pltpu.roll(d, 1, 1) * sinb


def near(here, r):
    x = 1 - here.x if r // 4 else here.x
    c = 1 - here.c if r // 2 % 2 else here.c
    y = 1 - here.y if r % 2 else here.y
    return x, c, y, (x * 2 + c, here.z, y)


def along_z(here, r):
    z = (here.z + r) % 4
    return z, (here.dp, z, here.y)


def shard_parts(s):
    x, c, zh, zl, y = s // 16, s // 8 % 2, s // 4 % 2, s // 2 % 2, s % 2
    member, spot = zl * 2 + c, (x * 2 + zh) * 2 + y
    return spot * 4 + member, member, spot


def three(v):
    hi = v.astype(BF)
    rest = v - hi.astype(F32)
    mid = rest.astype(BF)
    return jnp.concatenate([hi, mid, (rest - mid.astype(F32)).astype(BF)], 0)


def by_member(src, out, tmp, width, pieces):
    cols = pieces * 4 * width
    for t in range(pieces):
        for h in range(16):
            unit = shard_parts(h * 2)
            dst = t * 4 * width + unit[2] // 2 * width
            tmp[unit[1], 0:UNIT, dst : dst + width] = src[
                :, (t * 16 + h) * width : (t * 16 + h + 1) * width
            ].astype(F32)
    for m in range(4):
        out[m] = tmp[m, :, 0:cols].astype(BF)


def by_column(src, out, width, pieces):
    for t in range(pieces):
        for h in range(16):
            unit = shard_parts(h * 2)
            at_ = t * 4 * width + unit[2] // 2 * width
            out[:, (t * 16 + h) * width : (t * 16 + h + 1) * width] = src[
                unit[1], 0:UNIT, at_ : at_ + width
            ].astype(F32)


def silu_slope(v):
    sig = jax.nn.sigmoid(v)
    return sig * (1.0 + v * (1.0 - sig))


def kernel_a(
    tok_in, cot_in, wqkv, wgu, wp_in, wd_in, cond, w_mod_t, bm_in, bq_in, bp_in, bd_in, bg_in, qg_in, kg_in, tall_in,
    wide_in, perm_in, spread_in, pick, tabs_in,
    wq_out, wp_out, wg_out, wd_out, ha_out, raw_out, rot_out, att_out, hm_out, dm_out, tok_out, og_out, attn_o_out,
    condg, modv, bg, bd, gains, maskb, valid,
    wq, wp, wg, wd, ha, raw, rot, att, s0q, s0g, tokr, cotr, wqe, psend, precv, pown,
    wqs, wgs, tmp, block, msg, p1, m2, got, bq4, bg4, bp, hm, dmlp, tokp, og, attn_out, perm, spread, tabs, vecs,
    ssem, rsem, lsem,
):
    here = Place()
    link = Link(here, ssem, rsem)
    fetch = Fetch(lsem)
    m = here.m
    perm_got, spread_got, tabs_got = (
        fetch.go(a, b) for a, b in ((perm_in, perm), (spread_in, spread), (tabs_in, tabs))
    )
    vecs[...] = jnp.zeros_like(vecs)
    for line, lo, ref in (
        (0, 0, bm_in), (1, 0, bq_in), (1, 108, bp_in), (1, 144, bd_in), (2, 0, bg_in), (3, 0, qg_in), (4, 0, kg_in),
    ):
        n = ref.shape[0]
        vecs[line : line + 1, lo : lo + n] = ref[...].astype(F32).reshape(1, n)
    lane = lax.broadcasted_iota(jnp.int32, (1, 256), 1)
    sizes = jnp.zeros((1, 256), F32)
    for i in range(4):
        sizes = jnp.where(lane == i, tall_in[i].astype(F32), sizes)
        sizes = jnp.where(lane == 4 + i, wide_in[i].astype(F32), sizes)
    vecs[5:6, :] = sizes
    block[...] = jnp.zeros_like(block)
    block[0:4, :] = cond[...].astype(F32)
    block[4:5, 0:8] = vecs[5:6, 0:8]
    condg[here.dp] = block[...]
    link.greet(True)
    slot = here.zl * 2 + here.y
    rows_in = at(slot, 64)
    cs = [link.send(block, condg.at[here.dp], near(here, r)[3]) for r in (2, 4, 6)]
    tmp[...] = jnp.zeros_like(tmp)
    by_member(wqkv, wqs, tmp, 72, 3)
    sq, sg = {}, {}
    for r in (2, 3, 1):
        k, dev = here.mate(r)
        sq[r] = link.send(wqs.at[k], s0q.at[m], dev)
    own_q = fetch.go(wqs.at[m], s0q.at[m])
    for c in cs:
        c.wait_recv()
    v = condg[...].reshape(32, D)
    part = nt((v * jax.nn.sigmoid(v)).astype(BF), w_mod_t[...]) + vecs[0:1, 0:216]
    for z in range(4):
        msg[z, 4:6, :] = vecs[1:3, :]
        for d in range(4):
            msg[z, d : d + 1, 0:216] = part[d * 8 + z : d * 8 + z + 1, :]
    zs = []
    for r in (1, 2, 3):
        z, dev = along_z(here, r)
        zs.append(link.send(msg.at[z], p1.at[here.z], dev))
    p1[here.z] = msg[here.z]

    gq = Gather(link, wq, 144, 0, SPLIT_Q, 864)
    gp = Gather(link, wp, PAD, 0, SPLIT_P, D)
    g1 = Gather(link, wg, 144, 0, 384, 768)
    g2 = Gather(link, wg, 144, 768, 1152, 1536)
    gd = Gather(link, wd, 96, 0, SPLIT_D, D)
    by_member(wgu, wgs, tmp, 192, 2)
    own_q.wait()
    for r in (1, 2, 3):
        sq[r].wait_recv()
    wq[here.x, here.zh, here.y] = nn(pick[...], s0q[...].reshape(192, 864)).astype(BF)
    gq.hop1()
    for c in zs:
        c.wait_recv()
    for z in range(4):
        for d in range(4):
            m2[d, z, 0:1, :] = p1[z, d : d + 1, :]
            m2[d, z, 1:3, :] = p1[z, 4:6, :]
    ns = []
    for r in range(1, 8):
        x, _, y, dev = near(here, r)
        ns.append(link.send(m2.at[x * 2 + y], got.at[here.x, here.c, here.y], dev))
    got[here.x, here.c, here.y] = m2[here.x * 2 + here.y]
    tok_sent, tok_got = link.scatter(lambda j: tok_in.at[j], tokr.at[rows_in], here.item_home, slot)

    for r in (2, 3, 1):
        k, dev = here.mate(r)
        sg[r] = link.send(wgs.at[k], s0g.at[m], dev)
    own_g = fetch.go(wgs.at[m], s0g.at[m])
    perm_got.wait()
    wp[:, :, :, PAD:64, :] = jnp.zeros((2, 2, 2, 64 - PAD, D), BF)
    tmp[0, 0:UNIT, 0:D] = nn(wp_in[...], perm[...])
    tmp[0, UNIT:PAD, :] = jnp.zeros((PAD - UNIT, 1536), F32)
    wp[here.x, here.zh, here.y, 0:PAD, :] = tmp[0, :, 0:D].astype(BF)
    gp.hop1()
    ext = condg[here.x * 2 + here.y, 4:5, :]
    lane = lax.broadcasted_iota(jnp.int32, (1, D), 1)
    spot = lax.broadcasted_iota(jnp.int32, (1, 512), 1)
    row_at = spot // 128 * 4 + spot // 16 % 4
    col_at = spot // 64 % 2 * 16 + spot % 16

    def extent(item, first):
        return jnp.sum(jnp.where(lane == item + first, ext, 0.0), -1, keepdims=True)

    for i in range(2):
        tall, wide = extent(here.zh * 2 + i, 0), extent(here.zh * 2 + i, 4)
        live = (row_at.astype(F32) < tall) & (col_at.astype(F32) < wide)
        maskb[i] = jnp.where(live, 0.0, MASKED)
    spot = lax.broadcasted_iota(jnp.int32, (TOK, 1), 0) + here.c * TOK
    row_at = (spot // 128 * 4 + spot // 16 % 4).astype(F32)
    col_at = (spot // 64 % 2 * 16 + spot % 16).astype(F32)
    live = (row_at < extent(here.z, 0)) & (col_at < extent(here.z, 4))
    valid[...] = jnp.where(live, 1.0, 0.0)
    gains[...] = jnp.zeros_like(gains)
    for t in range(2):
        for e in range(2):
            gains[t : t + 1, e * 64 : e * 64 + UNIT] = vecs[3 + t : 4 + t, e * UNIT : e * UNIT + UNIT]
    for c in ns:
        c.wait_recv()
    modv[...] = jnp.zeros_like(modv)
    bq4[...] = jnp.zeros_like(bq4)
    for s in range(32):
        line = got[s // 16, s // 8 % 2, s % 2, s // 2 % 4]
        for q in range(6):
            piece, unit = divmod(6 * s + q, 32)
            to = shard_parts(unit)[0] * UNIT
            modv[piece : piece + 1, to : to + UNIT] = line[0:1, q * UNIT : q * UNIT + UNIT]
        for q in range(3):
            piece, unit = divmod(3 * s + q, 32)
            _, member, spot = shard_parts(unit)
            to = piece * 512 + spot * 64
            bq4[member, :, to : to + UNIT] = line[1:2, q * UNIT : q * UNIT + UNIT]
        to = shard_parts(s)[0] * UNIT
        bp[:, to : to + UNIT] = line[1:2, 108:144]
        bd[:, to : to + UNIT] = line[1:2, 144:180]
        for q in range(2):
            piece, unit = divmod(2 * s + q, 32)
            _, member, spot = shard_parts(unit)
            to = piece * 768 + spot * 96
            bg4[member, :, to : to + 96] = line[2:3, q * 96 : q * 96 + 96]
    bg[...] = bg4[m]
    gq.hop2()
    tok_got(tok_in.at[0], lambda j: tokr.at[pl.ds(j * 64, 64)])
    gq.hop3()
    tokp[...] = nn(tokr[...], perm[...]).astype(BF)

    def first_norm(i, carry):
        n, _ = norm_rows(tokp[at(i, 32), :].astype(F32))
        h = n * (1.0 + modv[1:2, :]) + modv[0:1, :]
        ha[pl.ds(pl.multiple_of(m * TOK + i * 32, 32), 32), :] = h.astype(BF)
        return carry

    lax.fori_loop(0, 8, first_norm, 0)
    ha_all = RowGather(link, ha)
    own_g.wait()
    for r in (1, 2, 3):
        sg[r].wait_recv()
    wg[here.x, here.zh, here.y] = nn(pick[...], s0g[...].reshape(192, 1536)).astype(BF)
    g1.hop1()
    g2.hop1()
    wd[here.x, here.zh, here.y] = nn(wd_in[...], perm[...]).astype(BF)
    gd.hop1()
    cot_sent, cot_got = link.scatter(lambda j: cot_in.at[j], cotr.at[rows_in], here.item_home, slot)
    gp.hop2()
    gq.done()
    outs = [fetch.go(wq, wq_out), fetch.go(tokp, tok_out)]
    spread_got.wait()

    def widen(i, carry):
        part = wq[i // 2, i % 2].reshape(288, 864)
        wqe[at(i, 288), :] = nn(part, spread[...]).astype(BF)
        return carry

    lax.fori_loop(0, 4, widen, 0)
    gp.hop3()
    tabs_got.wait()

    g1.hop2()
    ha_all.pass_on()
    g1.hop3()
    ha_all.near_done()
    ha_all.last_done()
    outs.append(fetch.go(ha, ha_out))

    def project(b, carry):
        acc = nn(ha[at(b, TOK), :], wqe[...]) + bq4[m]
        item, half = b // 2, at(b % 2, TOK)
        cos, sina, sinb = tabs[0, half, :], tabs[1, half, :], tabs[2, half, :]
        for h in range(4):
            p = item * 4 + h
            for t in range(2):
                v = acc[:, t * 512 + h * 128 : t * 512 + h * 128 + 128]
                recip = lax.rsqrt(jnp.sum(v * v, -1, keepdims=True) * (1.0 / HEAD) + EPSILON)
                raw[p, t, half, :] = v
                n = v * recip * gains[t : t + 1, :]
                rot[p, t, half, :] = turn(n, cos, sina, sinb).astype(BF)
            rot[p, 2, half, :] = acc[:, 1024 + h * 128 : 1152 + h * 128].astype(BF)
        return carry

    def attend(p, carry):
        item = p // 4
        lanes = at(p % 4, 128)
        for half in range(2):
            rows = pl.ds(half * TOK, TOK)
            e = jnp.exp2(nt(rot[p, 0, rows, :], rot[p, 1]) * ROOT2 + maskb[item])
            pr = (e * (1.0 / jnp.sum(e, -1, keepdims=True))).astype(BF)
            out_rows = pl.ds(pl.multiple_of(item * 512 + half * TOK, TOK), TOK)
            att[out_rows, lanes] = nn(pr, rot[p, 2]).astype(BF)
        return carry

    other = 1 - here.zl
    lax.fori_loop(other * 2, other * 2 + 2, project, 0)
    g2.hop2()
    lax.fori_loop(other * 4, other * 4 + 4, attend, 0)
    gp.done()
    outs.append(fetch.go(wp, wp_out))
    wpf = wp[...].reshape(512, D)
    red = RowReduce(link, psend, precv)
    red.give(3, nn(att[at(here.mate(3)[0], TOK), :], wpf))
    red.keep_far(nn(att[at(here.mate(2)[0], TOK), :], wpf))
    red.pass_on()
    gd.hop2()
    g2.hop3()
    lax.fori_loop(here.zl * 2, here.zl * 2 + 2, project, 0)
    cot_got(cot_in.at[0], lambda j: cotr.at[pl.ds(j * 64, 64)])
    og[...] = (nn(cotr[...], perm[...]) * valid[...]).astype(BF)

    def scale_grad(i, carry):
        g = og[at(i, 32), :].astype(F32) * modv[5:6, :]
        dmlp[pl.ds(pl.multiple_of(m * TOK + i * 32, 32), 32), :] = g.astype(BF)
        return carry

    lax.fori_loop(0, 8, scale_grad, 0)
    outs.append(fetch.go(og, og_out))
    dm_all = RowGather(link, dmlp)
    outs.append(fetch.go(raw, raw_out))
    outs.append(fetch.go(rot, rot_out))
    lax.fori_loop(here.zl * 4, here.zl * 4 + 4, attend, 0)
    outs.append(fetch.go(att, att_out))
    red.give(1, nn(att[at(here.mate(1)[0], TOK), :], wpf))
    pown[...] = nn(att[at(m, TOK), :], wpf)
    red.arrive()

    def second_norm(i, carry):
        rows = at(i, 32)
        a = pown[rows, :] + bp[...] + red.total(rows)
        attn_out[rows, :] = a
        n, _ = norm_rows(tokp[rows, :].astype(F32) + modv[2:3, :] * a)
        h = n * (1.0 + modv[4:5, :]) + modv[3:4, :]
        hm[rows, :] = h.astype(BF)
        return carry

    lax.fori_loop(0, 8, second_norm, 0)
    outs.append(fetch.go(hm, hm_out))
    outs.append(fetch.go(attn_out, attn_o_out))
    g1.done()
    g2.done()
    outs.append(fetch.go(wg, wg_out))
    gd.done()
    outs += [fetch.go(a, b) for a, b in zip(gd.parts(wd), gd.parts(wd_out))]
    dm_all.pass_on()
    dm_all.near_done()
    dm_all.last_done()
    outs.append(fetch.go(dmlp, dm_out))
    for c in outs:
        c.wait()
    link.finish()
    tok_sent()
    cot_sent()


def store_tiles(val, ref, base, piece, keep):
    block = ref.shape[3] if keep is None else piece
    for q in range(val.shape[0] // piece):
        row = base + q * piece
        f, off = row // block, row % block
        n = piece if keep is None else keep
        part = val[q * piece : q * piece + n, :].astype(BF)
        ref[f // 4, f // 2 % 2, f % 2, off : off + n, 0 : val.shape[1]] = part


class Fetch:
    def __init__(self, sems):
        self.sems, self.n = sems, 0

    def go(self, src, dst):
        copy = pltpu.make_async_copy(src, dst, self.sems.at[self.n])
        self.n += 1
        copy.start()
        return copy


def kernel_b(
    wg_in, wd_in, hm_in, dm_in, tok_in, og_in, attn_in, att_in, wp_in, wq_in, ha_in, raw_in, rot_in, perm_in,
    spread_in, tabs_in, modv, bg, bd, gains, maskb, valid, pick, condg, w_mod_t,
    dtok, bout, g_qkv_out, g_gu_out, fp_out, fd_out, dwm_out, sums, dbm, dcond,
    wg, wd, hm, dmlp, tokp, og, attn_out, att, wp, wq, perm, tabs, gu, coef, hid, rsend, rrecv, mrecv, own32,
    dwg, dwd, dwp, dattn, raw, rot, to, bo, fq, fg, small, dbg, dbq, dgain,
    pk, q1, m2, q2, dm, e0, e1, e2, e3, line, bq4, bg4, slope, g_qkv, g_gu, fp, fd, dwm,
    g1a, g1b, g2a, g2b, g3a, g3b, h1a, h1b, h2a, h2b, h3a, h3b, d1a, d1b, d2a, d2b, d3a, d3b,
    q1a, q1b, q2a, q2b, q3a, q3b, p1a, p1b, p2a, p2b, p3a, p3b, ssem, rsem, lsem,
):
    here = Place()
    link = Link(here, ssem, rsem)
    fetch = Fetch(lsem)
    m = here.m
    k1, k2, k3 = here.mate(1)[0], here.mate(2)[0], here.mate(3)[0]
    at_m, at_1, at_2, at_3 = at(m, TOK), at(k1, TOK), at(k2, TOK), at(k3, TOK)
    get_hm = fetch.go(hm_in, hm.at[at_m])
    get_dm = fetch.go(dm_in, dmlp)
    get_wg = fetch.go(wg_in, wg)
    gd = Gather(link, wd, 96, 0, SPLIT_D, D)
    get_wd = [fetch.go(a, b) for a, b in zip(gd.parts(wd_in), gd.parts(wd))]
    gets = [fetch.go(a, b) for a, b in ((tok_in, tokp), (og_in, og), (attn_in, attn_out))]
    get_wp = fetch.go(wp_in, wp)
    gets2 = [fetch.go(a, b) for a, b in ((tabs_in, tabs), (att_in, att), (wq_in, wq), (perm_in, perm))]
    base = fetch.n
    fetch.n += 4
    link.greet(True)
    get_hm.wait()
    hm_all = RowGather(link, hm)
    gd.last_hop(wd_in)
    small[...] = jnp.zeros_like(small)
    dbg[...] = jnp.zeros_like(dbg)
    dbq[...] = jnp.zeros_like(dbq)
    dgain[...] = jnp.zeros_like(dgain)
    get_wg.wait()
    get_dm.wait()

    def wgf():
        return wg[...].reshape(D, 1536)

    def wdf():
        return wd[...].reshape(768, D)

    def mlp(k):
        gu[...] = nn(hm[at(k, TOK), :], wgf()) + bg[...]

        def acts(i, carry):
            rows = at(i, 32)
            out = pl.ds(pl.multiple_of(k * TOK + i * 32, 32), 32)
            g, u = gu[rows, 0:768], gu[rows, 768:1536]
            sig = jax.nn.sigmoid(g)
            act = g * sig
            hid[out, :] = (act * u).astype(BF)
            coef[out, 0:768] = (u * sig * (1.0 + g * (1.0 - sig))).astype(BF)
            coef[out, 768:1536] = act.astype(BF)
            return carry

        lax.fori_loop(0, 8, acts, 0)

    def mlp_back(k):
        dh = nt(dmlp[at(k, TOK), :], wdf())
        out = at(k, TOK)
        coef[out, 0:768] = (coef[out, 0:768].astype(F32) * dh).astype(BF)
        coef[out, 768:1536] = (coef[out, 768:1536].astype(F32) * dh).astype(BF)
        dbg[0:1, :] += jnp.sum(coef[out, :].astype(F32), 0, keepdims=True)
        return nt(coef[out, :], wgf())

    hred = RowReduce(link, rsend, rrecv)
    mlp(m)
    hm_all.near_done()
    mlp(k1)
    for c in get_wd:
        c.wait()
    gd.done()
    own32[...] = mlp_back(m)
    hred.give(1, mlp_back(k1))
    hm_all.pass_on()
    mlp(k2)
    hm_all.last_done()
    hred.keep_far(mlp_back(k2))
    mlp(k3)
    hred.give(3, mlp_back(k3))
    hred.pass_on()

    ra = Reduce(link, dwg, (g1a, g1b, g2a, g2b, g3a, g3b), 0, 384, 768)
    rb = Reduce(link, dwg, (h1a, h1b, h2a, h2b, h3a, h3b), 768, 1152, 1536)
    rd = Reduce(link, dwd, (d1a, d1b, d2a, d2b, d3a, d3b), 0, SPLIT_D, D)
    rq = Reduce(link, wg, (q1a, q1b, q2a, q2b, q3a, q3b), 0, SPLIT_Q, 896)
    rp = Reduce(link, dwp, (p1a, p1b, p2a, p2b, p3a, p3b), 0, SPLIT_P, D)
    for n, red in ((0, ra), (1, rb)):
        cols = slice(n * 768, n * 768 + 768)
        for i in range(3):
            t = tn(hm[:, i * 384 : i * 384 + 384], coef[:, cols])
            for q in range(8):
                row = i * 384 + q * 48
                f, off = row // 144, row % 144
                dwg[f // 4, f // 2 % 2, f % 2, off : off + 48, cols] = t[q * 48 : q * 48 + 48].astype(BF)
        red.hop1()
    spread_got = fetch.go(spread_in, wg)
    for i in range(2):
        store_tiles(tn(hid[:, i * 384 : i * 384 + 384], dmlp[...]), dwd, i * 384, 96, None)
    rd.hop1()
    link.settle(hred.s1, hred.s3)
    mred = RowReduce(link, rsend, mrecv)
    mred.give(3, nn(hid[at_3, :], wdf()))
    mred.give(1, nn(hid[at_1, :], wdf()))
    bo[...] = nn(hid[at_m, :], wdf()).astype(BF)
    for c in gets:
        c.wait()
    hred.arrive()

    def mid_back(i, carry):
        rows = at(i, 32)
        mine = pl.ds(pl.multiple_of(m * TOK + i * 32, 32), 32)
        d = own32[rows, :] + hred.total(rows)
        a = attn_out[rows, :]
        n, recip = norm_rows(tokp[rows, :].astype(F32) + modv[2:3, :] * a)
        small[1:2, :] += jnp.sum(d, 0, keepdims=True)
        small[2:3, :] += jnp.sum(d * n, 0, keepdims=True)
        g = og[rows, :].astype(F32) + norm_rows_back(d * (1.0 + modv[4:5, :]), n, recip)
        gu[rows, 0:D] = g
        small[3:4, :] += jnp.sum(g * a, 0, keepdims=True)
        low = (modv[2:3, :] * g).astype(BF)
        dattn[mine, :] = low
        small[5:6, :] += jnp.sum(low.astype(F32), 0, keepdims=True)
        small[4:5, :] += jnp.sum(dmlp[mine, :].astype(F32), 0, keepdims=True)
        return carry

    lax.fori_loop(0, 8, mid_back, 0)
    da_all = RowGather(link, dattn)
    link.settle(hred.s2, hm_all.far, hm_all.near, hm_all.last)
    ha_got = fetch.go(ha_in, dmlp)
    mred.keep_far(nn(hid[at_2, :], wdf()))
    da_all.near_done()

    def pair_of(n):
        item = here.zl + (1 - 2 * here.zl) * (n // 4)
        return item, item * 4 + n % 4

    def pair_copies(n):
        p = pair_of(n)[1]
        s = n % 2
        return (
            pltpu.make_async_copy(raw_in.at[p], raw.at[s], lsem.at[base + 2 * s]),
            pltpu.make_async_copy(rot_in.at[p], rot.at[s], lsem.at[base + 2 * s + 1]),
        )

    for c in pair_copies(0):
        c.start()
    get_wp.wait()
    for c in gets2:
        c.wait()

    def back_proj(rows):
        hid[rows, 0:512] = nt(dattn[rows, :], wp[...].reshape(512, D)).astype(BF)

    def attend_back(n, carry):
        item, p = pair_of(n)
        s = n % 2
        lanes = at(n % 4, 128)
        for c in pair_copies(n):
            c.wait()

        @pl.when(n < 7)
        def _():
            for c in pair_copies(n + 1):
                c.start()

        dk = jnp.zeros((512, 128), F32)
        dv = jnp.zeros((512, 128), F32)

        def head_back_store(d, t, rows, out_rows):
            cos, sina, sinb = tabs[0, rows, :], tabs[1, rows, :], tabs[2, rows, :]
            v = raw[s, t, rows, :]
            recip = lax.rsqrt(jnp.sum(v * v, -1, keepdims=True) * (1.0 / HEAD) + EPSILON)
            dn = turn_back(d, cos, sina, sinb)
            dgain[t : t + 1, :] += jnp.sum(dn * v * recip, 0, keepdims=True)
            u = dn * gains[t : t + 1, :]
            mean = jnp.sum(u * v, -1, keepdims=True) * (1.0 / HEAD)
            res = recip * u - v * (recip * recip * recip * mean)
            coef[out_rows, at(t * 4 + n % 4, 128)] = res.astype(BF)

        for half in range(2):
            rows = pl.ds(half * TOK, TOK)
            out_rows = pl.ds(pl.multiple_of(item * 512 + half * TOK, TOK), TOK)
            do = hid[out_rows, lanes]
            e = jnp.exp2(nt(rot[s, 0, rows, :], rot[s, 1]) * ROOT2 + maskb[item])
            pf = e * (1.0 / jnp.sum(e, -1, keepdims=True))
            dp = nt(do, rot[s, 2])
            delta = jnp.sum(pf * dp, -1, keepdims=True)
            ds = (pf * (dp - delta)).astype(BF)
            dq = nn(ds, rot[s, 1]) * ROOT
            dk += tn(ds, rot[s, 0, rows, :])
            dv += tn(pf.astype(BF), do)
            head_back_store(dq, 0, rows, out_rows)
        dk = dk * ROOT
        for half in range(2):
            rows = pl.ds(half * TOK, TOK)
            out_rows = pl.ds(pl.multiple_of(item * 512 + half * TOK, TOK), TOK)
            head_back_store(dk[half * TOK : half * TOK + TOK], 1, rows, out_rows)
        coef[at(item, 512), at(8 + n % 4, 128)] = dv.astype(BF)
        return carry

    back_proj(at_m)
    back_proj(at_1)
    lax.fori_loop(0, 3, attend_back, 0)
    da_all.pass_on()
    mred.pass_on()
    ra.hop2()
    lax.fori_loop(3, 4, attend_back, 0)
    da_all.last_done()
    rb.hop2()
    back_proj(at_2)
    back_proj(at_3)
    store_tiles(tn(att[...], dattn[...]), dwp, 0, 64, PAD)
    rp.hop1()
    ra.hop3()
    lax.fori_loop(4, 5, attend_back, 0)
    rd.hop2()
    rb.hop3()
    lax.fori_loop(5, 6, attend_back, 0)
    mred.arrive()

    def finish_out(i, carry):
        rows = at(i, 32)
        o = bo[rows, :].astype(F32) + bd[...] + mred.total(rows)
        small[0:1, :] += jnp.sum(og[rows, :].astype(F32) * o, 0, keepdims=True)
        mid = tokp[rows, :].astype(F32) + modv[2:3, :] * attn_out[rows, :]
        bo[rows, :] = ((mid + modv[5:6, :] * o) * valid[rows, :]).astype(BF)
        return carry

    lax.fori_loop(0, 8, finish_out, 0)
    bo[...] = nt(bo[...], perm[...]).astype(BF)
    b_sent, b_got = link.scatter(
        lambda j: bo.at[pl.ds(j * 64, 64)], bout.at[here.z], here.item_source, here.z
    )
    lax.fori_loop(6, 7, attend_back, 0)
    rp.hop2()
    lax.fori_loop(7, 8, attend_back, 0)
    spread_got.wait()

    def squeeze(rows):
        v = coef[rows, :]
        dbq[0:1, :] += jnp.sum(v.astype(F32), 0, keepdims=True)
        hm[rows, 0:864] = nt(v, wg[...].reshape(D, 1536)[0:864]).astype(BF)

    def to_input(rows):
        return nt(hm[rows, 0:864], wq[...].reshape(D, 864))

    link.settle(mred.s1, mred.s2, mred.s3)
    tred = RowReduce(link, rsend, rrecv)
    squeeze(at_3)
    tred.give(3, to_input(at_3))
    squeeze(at_2)
    tred.keep_far(to_input(at_2))
    tred.pass_on()
    rd.hop3()
    squeeze(at_1)
    tred.give(1, to_input(at_1))
    squeeze(at_m)
    own32[...] = to_input(at_m)
    pk[...] = jnp.zeros_like(pk)
    bq4[...] = jnp.zeros_like(bq4)
    bg4[...] = jnp.zeros_like(bg4)
    bq4[m] = dbq[0:1, :]
    bg4[m] = dbg[0:1, :]
    for t in range(2):
        for e in range(2):
            to_ = t * 72 + e * UNIT
            line[:, to_ : to_ + UNIT] = dgain[t : t + 1, e * 64 : e * 64 + UNIT]
    for s in range(32):
        x, c, z, y = s // 16, s // 8 % 2, s // 2 % 4, s % 2
        for q in range(3):
            piece, unit = divmod(2 * s + q, 32) if q < 2 else (2, s)
            _, member, spot = shard_parts(unit)
            from_ = piece * 512 + spot * 64
            pk[x, c, y, z, 1:2, q * UNIT : q * UNIT + UNIT] = bq4[member, :, from_ : from_ + UNIT]
        from_ = shard_parts(s)[0] * UNIT
        pk[x, c, y, z, 1:2, 108:144] = small[5:6, from_ : from_ + UNIT]
        pk[x, c, y, z, 1:2, 144:180] = small[4:5, from_ : from_ + UNIT]
        for q in range(2):
            piece, unit = divmod(2 * s + q, 32)
            _, member, spot = shard_parts(unit)
            from_ = piece * 768 + spot * 96
            pk[x, c, y, z, 2:3, q * 96 : q * 96 + 96] = bg4[member, :, from_ : from_ + 96]
        pk[x, c, y, z, 3:4, 0:144] = line[:, 0:144]
    full_slope = silu_slope(condg[here.dp])
    for b in range(8):
        slope[b] = full_slope[:, b * 144 : b * 144 + 144]
    ha_got.wait()
    for i in range(3):
        store_tiles(tn(dmlp[:, i * 384 : i * 384 + 384], hm[:, 0:864]), wg, i * 384, 48, None)
    rq.hop1()
    rp.hop3()

    def hand_out(reds, base_row, cols, out):
        rows = slice(base_row, base_row + 4 * PAD)
        for red in reds:
            left, right = red.done()
            coef[rows, red.lo : red.split] = tn(pick[...], left).astype(BF)
            coef[rows, red.split : red.hi] = tn(pick[...], right).astype(BF)

        def share(k):
            return coef.at[pl.ds(pl.multiple_of(base_row + k * PAD, 16), PAD), pl.ds(0, cols)]

        over = [link.send(share(here.mate(r)[0]), out.at[m], here.mate(r)[1]) for r in (2, 3, 1)]
        return over, fetch.go(share(m), out.at[m])

    g_over, g_own = hand_out((ra, rb), 0, 1536, fg)
    tred.arrive()

    def first_back(i, carry):
        rows = at(i, 32)
        d = own32[rows, :] + tred.total(rows)
        n, recip = norm_rows(tokp[rows, :].astype(F32))
        small[6:7, :] += jnp.sum(d, 0, keepdims=True)
        small[7:8, :] += jnp.sum(d * n, 0, keepdims=True)
        g = gu[rows, 0:D] + norm_rows_back(d * (1.0 + modv[1:2, :]), n, recip)
        to[rows, :] = g.astype(BF)
        return carry

    lax.fori_loop(0, 8, first_back, 0)
    rows_of = (6, 7, 3, 1, 2, 0)
    for s in range(32):
        x, c, z, y = s // 16, s // 8 % 2, s // 2 % 4, s % 2
        for q in range(6):
            piece, unit = divmod(6 * s + q, 32)
            from_ = shard_parts(unit)[0] * UNIT
            row = rows_of[piece]
            pk[x, c, y, z, 0:1, q * UNIT : q * UNIT + UNIT] = small[row : row + 1, from_ : from_ + UNIT]
    ns = []
    for r in range(1, 8):
        x, c, y, dev = near(here, r)
        ns.append(link.send(pk.at[x, c, y], q1.at[here.x, here.c, here.y], dev))
    q1[here.x, here.c, here.y] = pk[here.x, here.c, here.y]
    rq.hop2()
    to[...] = nt(to[...], perm[...]).astype(BF)
    for n in ns:
        n.wait_recv()
    for z in range(4):
        for x in range(2):
            for y in range(2):
                d = x * 2 + y
                m2[z, d : d + 1, :] = q1[x, 0, y, z, 0:1, :] + q1[x, 1, y, z, 0:1, :]
        total = q1[0, 0, 0, z, 1:4, :]
        for i in range(1, 8):
            total += q1[i // 4, i // 2 % 2, i % 2, z, 1:4, :]
        m2[z, 4:7, :] = total
    zs = []
    for r in (1, 2, 3):
        z, dev = along_z(here, r)
        zs.append(link.send(m2.at[z], q2.at[here.z], dev))
    sent, got = link.scatter(
        lambda j: to.at[pl.ds(j * 64, 64)], dtok.at[here.z], here.item_source, here.z
    )
    rq.hop3()
    q2[here.z] = m2[here.z]
    dm[...] = jnp.zeros_like(dm)
    v = condg[...].reshape(32, D)
    act = (v * jax.nn.sigmoid(v)).astype(BF)

    def plain(red, out):
        left, right = red.done()
        out[...] = nt(left, perm[:, 0 : red.split]) + nt(right, perm[:, red.split : D])

    for c in zs:
        c.wait_recv()
    for z in range(4):
        for d in range(4):
            dm[d * 8 + z : d * 8 + z + 1, :] = q2[z, d : d + 1, 0:216]
    sums[...] = q2[0] + q2[1] + q2[2] + q2[3]
    dbm[...] = jnp.broadcast_to(jnp.sum(dm[...], 0, keepdims=True), (8, 216))
    d3 = three(dm[...])
    da = nn(d3, w_mod_t[...])
    da = da[0:32] + da[32:64] + da[64:96]
    for b in range(8):
        for d in range(4):
            e0[d, b % 2, b // 2] = da[d * 8 : d * 8 + 8, b * 144 : b * 144 + 144]
    ns = []
    for r in range(1, 8):
        x, c, y, dev = near(here, r)
        ns.append(link.send(e0.at[x * 2 + c, y], e1.at[here.x, here.c, here.y], dev))
    e1[here.x, here.c, here.y] = e0[here.dp, here.y]
    plain(rd, fd)
    outs = [fetch.go(fd, fd_out)]
    for n in ns:
        n.wait_recv()
    total = e1[0, 0, 0]
    for i in range(1, 8):
        total += e1[i // 4, i // 2 % 2, i % 2]
    e2[...] = total
    zs = []
    for r in (1, 2, 3):
        z, dev = along_z(here, r)
        zs.append(link.send(e2.at[z], e3.at[here.z], dev))
    e3[here.z] = e2[here.z]
    plain(rp, fp)
    outs.append(fetch.go(fp, fp_out))
    dwm[...] = tn(d3, jnp.concatenate([act, act, act], 0))
    outs.append(fetch.go(dwm, dwm_out))
    g_own.wait()
    for c in g_over:
        c.wait_recv()
    by_column(fg, g_gu, 192, 2)
    outs.append(fetch.go(g_gu, g_gu_out))
    q_over, q_own = hand_out((rq,), 4 * PAD, 896, fq)
    for c in zs:
        c.wait_recv()
    dcond[...] = (e3[0] + e3[1] + e3[2] + e3[3]) * slope[here.z * 2 + here.y]
    q_own.wait()
    for c in q_over:
        c.wait_recv()
    by_column(fq, g_qkv, 72, 3)
    outs.append(fetch.go(g_qkv, g_qkv_out))
    b_got(bo.at[pl.ds(0, 64)], lambda j: bout.at[j])
    got(to.at[pl.ds(0, 64)], lambda j: dtok.at[j])
    for c in outs:
        c.wait()
    link.finish()
    b_sent()
    sent()


def call(kernel, ident, outs, scratch, args, hbm=(), smem=(), hbm_out=(), sems=64, local=32):
    vm = pl.BlockSpec(memory_space=pltpu.VMEM)
    hb = pl.BlockSpec(memory_space=pltpu.HBM)
    sm = pl.BlockSpec(memory_space=pltpu.SMEM)
    return pl.pallas_call(
        kernel,
        out_shape=[jax.ShapeDtypeStruct(s, t) for s, t in outs],
        in_specs=[hb if i in hbm else sm if i in smem else vm for i in range(len(args))],
        out_specs=[hb if i in hbm_out else vm for i in range(len(outs))],
        scratch_shapes=scratch + [pltpu.SemaphoreType.DMA((sems,)), pltpu.SemaphoreType.DMA((sems,))]
        + ([pltpu.SemaphoreType.DMA((local,))] if hbm else []),
        compiler_params=pltpu.CompilerParams(
            collective_id=ident, has_side_effects=True, vmem_limit_bytes=LIMIT
        ),
    )(*args)


def local(
    tokens, conditioning, heights, widths, cotangent, w_mod, b_mod, w_qkv, b_qkv, query_gain, key_gain,
    w_proj, b_proj, w_gu, b_gu, w_down, b_down,
):
    args = (
        tokens, conditioning, heights, widths, cotangent, w_mod, b_mod, w_qkv, b_qkv, query_gain, key_gain,
        w_proj, b_proj, w_gu, b_gu, w_down, b_down,
    )
    sizes = tuple(lax.axis_size(a) for a in ("dp", "row", "col"))
    if sizes != (4, 4, 2) or tokens.shape != (4, 4, 16, D):
        return general(*args)
    every = ("dp", "row", "col")
    perm, spread, pick, tabs = constants()
    w_mod_t = w_mod.T
    full = (GROUP, D)
    block = (TOK, D)
    weights = [(2, 2, 2, 144, 864), (2, 2, 2, 64, D), (2, 2, 2, 144, 1536), (2, 2, 2, 96, D)]
    pairs = [((8, 2, 512, 128), F32), ((8, 3, 512, 128), BF)]
    small_rows = pltpu.VMEM((4, 8, 256), F32)
    (
        wq_all, wp_all, wg_all, wd_all, ha, raw, rot, att, hm, dmlp, tokp, og, attn_out,
        condg, modv, bg, bd, gains, maskb, valid,
    ) = call(
        kernel_a, 0,
        [(w, BF) for w in weights] + [(full, BF)] + pairs + [((GROUP, 512), BF)]
        + [(block, BF), (full, BF), (block, BF), (block, BF)]
        + [
            (s, F32)
            for s in (block, (4, 8, D), (8, D), (1, 1536), (1, D), (8, 128), (2, 1, 512), (TOK, 1))
        ],
        [pltpu.VMEM(w, BF) for w in weights] + [pltpu.VMEM(full, BF)] + [pltpu.VMEM(w, t) for w, t in pairs]
        + [
            pltpu.VMEM((GROUP, 512), BF), pltpu.VMEM((4, PAD, 864), BF), pltpu.VMEM((4, PAD, 1536), BF),
            pltpu.VMEM(block, BF), pltpu.VMEM(block, BF), pltpu.VMEM((D, 1536), BF), pltpu.VMEM((3, TOK, D), BF),
            pltpu.VMEM((3, TOK, D), BF), pltpu.VMEM(block, F32),
            pltpu.VMEM((4, PAD, 864), BF), pltpu.VMEM((4, PAD, 1536), BF), pltpu.VMEM((4, PAD, 1536), F32),
            pltpu.VMEM((8, D), F32), small_rows, small_rows, pltpu.VMEM((4, 4, 8, 256), F32),
            pltpu.VMEM((2, 2, 2, 4, 8, 256), F32), pltpu.VMEM((4, 1, 1536), F32), pltpu.VMEM((4, 1, 1536), F32),
            pltpu.VMEM((1, D), F32), pltpu.VMEM(block, BF), pltpu.VMEM(full, BF), pltpu.VMEM(block, BF),
            pltpu.VMEM(block, BF), pltpu.VMEM(block, F32), pltpu.VMEM((D, D), BF), pltpu.VMEM((864, 1536), BF),
            pltpu.VMEM((3, 512, 128), F32), pltpu.VMEM((8, 256), F32),
        ],
        (
            tokens.reshape(4, 64, D), cotangent.reshape(4, 64, D), w_qkv, w_gu, w_proj, w_down, conditioning, w_mod_t,
            b_mod, b_qkv, b_proj, b_down, b_gu, query_gain, key_gain, heights, widths, perm, spread, pick, tabs,
        ),
        hbm=(0, 1, 17, 18, 20),
        smem=(15, 16),
        hbm_out=range(13),
        sems=128,
    )
    spread = jnp.pad(spread, ((0, D - 864), (0, 0))).reshape(2, 2, 2, 144, 1536)
    dtok, bout, g_w_qkv, g_w_gu, fp, fd, g_w_mod, sums, g_b_mod, d_cond = call(
        kernel_b, 1,
        [
            ((4, 64, D), BF), ((4, 64, D), BF), ((UNIT, 3456), F32), ((UNIT, 6144), F32), ((PAD, D), F32),
            ((96, D), F32), ((216, D), F32), ((8, 256), F32), ((8, 216), F32), ((8, 144), F32),
        ],
        [
            pltpu.VMEM((2, 2, 2, 144, 1536), BF), pltpu.VMEM((2, 2, 2, 96, D), BF), pltpu.VMEM(full, BF),
            pltpu.VMEM(full, BF), pltpu.VMEM(block, BF), pltpu.VMEM(block, BF), pltpu.VMEM(block, F32),
            pltpu.VMEM((GROUP, 512), BF), pltpu.VMEM((2, 2, 2, 64, D), BF), pltpu.VMEM((2, 2, 2, 144, 864), BF),
            pltpu.VMEM((D, D), BF), pltpu.VMEM((3, 512, 128), F32), pltpu.VMEM((TOK, 1536), F32),
            pltpu.VMEM((GROUP, 1536), BF), pltpu.VMEM((GROUP, 768), BF), pltpu.VMEM((3, TOK, D), BF),
            pltpu.VMEM((3, TOK, D), BF), pltpu.VMEM((3, TOK, D), BF), pltpu.VMEM(block, F32),
            pltpu.VMEM((2, 2, 2, 144, 1536), BF), pltpu.VMEM((2, 2, 2, 96, D), BF), pltpu.VMEM((2, 2, 2, PAD, D), BF),
            pltpu.VMEM(full, BF), pltpu.VMEM((2, 2, 512, 128), F32), pltpu.VMEM((2, 3, 512, 128), BF),
            pltpu.VMEM(block, BF), pltpu.VMEM(block, BF), pltpu.VMEM((4, PAD, 896), BF), pltpu.VMEM((4, PAD, 1536), BF),
            pltpu.VMEM((8, D), F32), pltpu.VMEM((8, 1536), F32), pltpu.VMEM((8, 1536), F32), pltpu.VMEM((8, 128), F32),
            pltpu.VMEM((2, 2, 2, 4, 8, 256), F32), pltpu.VMEM((2, 2, 2, 4, 8, 256), F32), small_rows, small_rows,
            pltpu.VMEM((32, 216), F32), pltpu.VMEM((4, 2, 4, 8, 144), F32), pltpu.VMEM((2, 2, 2, 4, 8, 144), F32),
            pltpu.VMEM((4, 8, 144), F32), pltpu.VMEM((4, 8, 144), F32), pltpu.VMEM((1, 256), F32),
            pltpu.VMEM((4, 1, 1536), F32), pltpu.VMEM((4, 1, 1536), F32), pltpu.VMEM((8, 8, 144), F32),
            pltpu.VMEM((UNIT, 3456), F32), pltpu.VMEM((UNIT, 6144), F32), pltpu.VMEM((PAD, D), F32),
            pltpu.VMEM((96, D), F32), pltpu.VMEM((216, D), F32),
        ]
        + Reduce.buffers(144, 768, 384) * 2 + Reduce.buffers(96, D, SPLIT_D)
        + Reduce.buffers(144, 896, SPLIT_Q) + Reduce.buffers(PAD, D, SPLIT_P),
        (
            wg_all, wd_all, hm, dmlp, tokp, og, attn_out, att, wp_all, wq_all, ha, raw, rot, perm, spread, tabs,
            modv, bg, bd, gains, maskb, valid, pick, condg, w_mod_t,
        ),
        hbm=range(16),
        hbm_out=range(7),
        sems=128,
    )

    one, two = sums[4], sums[5]
    gains_out = sums[6]
    return (
        bout.reshape(tokens.shape),
        dtok.reshape(tokens.shape).astype(F32),
        d_cond[:4],
        g_w_mod.T,
        g_b_mod[0],
        g_w_qkv,
        one[:72],
        one[72:108],
        gains_out[:72],
        gains_out[72:144],
        fp[:UNIT],
        one[108:144],
        g_w_gu,
        two[:192],
        fd,
        one[144:180],
    )


def solution(mesh):
    in_specs = (
        P("dp", "row", "col", None),
        P("dp", None),
        P("dp"),
        P("dp"),
        P("dp", "row", "col", None),
        P(None, ("dp", "row", "col")),
        P(("dp", "row", "col")),
        P(("dp", "row", "col"), None),
        P(("dp", "row", "col")),
        P(),
        P(),
        P(("dp", "row", "col"), None),
        P(("dp", "row", "col")),
        P(("dp", "row", "col"), None),
        P(("dp", "row", "col")),
        P(("dp", "row", "col"), None),
        P(("dp", "row", "col")),
    )
    out_specs = (
        P("dp", "row", "col", None),
        P("dp", "row", "col", None),
        P("dp", ("row", "col")),
        P(None, ("dp", "row", "col")),
        P(("dp", "row", "col")),
        P(("dp", "row", "col"), None),
        P(("dp", "row", "col")),
        P(("dp", "row", "col")),
        P(),
        P(),
        P(("dp", "row", "col"), None),
        P(("dp", "row", "col")),
        P(("dp", "row", "col"), None),
        P(("dp", "row", "col")),
        P(("dp", "row", "col"), None),
        P(("dp", "row", "col")),
    )
    return jax.shard_map(local, mesh=mesh, in_specs=in_specs, out_specs=out_specs, check_vma=False)
```

```python
import math

import jax
import jax.numpy as jnp
import numpy as np
from jax import lax
from jax.experimental import pallas as pl
from jax.experimental.pallas import tpu as pltpu
from jax.sharding import PartitionSpec as P

HEADS = 16
HEAD = 72
FF = 3072


EPSILON = 1e-06
MASKED = -1000000000.0
PRECISE = lax.Precision.HIGHEST


def rope_tables(row_pos, col_pos, head_size):
    half_size = head_size // 2
    lane_index = jnp.arange(head_size)
    pair_index = (lane_index % half_size // 2).astype(jnp.float32)
    frequency = jnp.exp(-math.log(10000.0) * 2.0 * pair_index / half_size)
    places = jnp.where(lane_index[None, :] >= half_size, col_pos[:, None], row_pos[:, None]).astype(
        jnp.float32
    )
    angles = places * frequency[None, :]
    return (jnp.cos(angles), jnp.sin(angles))


def rotate(values):
    pair_view = values.reshape(values.shape[:-1] + (values.shape[-1] // 2, 2))
    turned = jnp.stack((-pair_view[..., 1], pair_view[..., 0]), axis=-1)
    return turned.reshape(values.shape)


def norm_parts(values):
    centered = values - jnp.mean(values, -1, keepdims=True)
    recip = lax.rsqrt(jnp.mean(centered * centered, -1, keepdims=True) + EPSILON)
    return (centered * recip, recip)


def norm_back(gradient, normed, recip):
    return recip * (
        gradient
        - jnp.mean(gradient, -1, keepdims=True)
        - normed * jnp.mean(gradient * normed, -1, keepdims=True)
    )


def head_back(gradient, raw_value, recip, gain_vec):
    scaled = gradient * gain_vec
    gain_grad = jnp.sum(gradient * raw_value * recip, axis=(0, 1, 2))
    raw_grad = recip * scaled - raw_value * (recip * recip * recip) * jnp.mean(
        scaled * raw_value, -1, keepdims=True
    )
    return (raw_grad, gain_grad)


def general(
    tokens,
    conditioning,
    heights,
    widths,
    cotangent,
    w_mod,
    b_mod,
    w_qkv,
    b_qkv,
    query_gain,
    key_gain,
    w_proj,
    b_proj,
    w_gu,
    b_gu,
    w_down,
    b_down,
):
    item_count, tile_rows, tile_cols, model_width = tokens.shape
    tile_span = tile_rows * tile_cols
    n_row = lax.axis_size("row")
    n_col = lax.axis_size("col")
    groups = n_row * n_col
    key_count = tile_span * groups
    inv_root = 1.0 / math.sqrt(HEAD)
    row_at = lax.axis_index("row")
    col_at = lax.axis_index("col")
    local_index = jnp.arange(tile_span)
    query_rows = row_at * tile_rows + local_index // tile_cols
    query_cols = col_at * tile_cols + local_index % tile_cols
    valid_query = (query_rows[None, :] < heights[:, None]) & (query_cols[None, :] < widths[:, None])
    key_index = jnp.arange(key_count)
    key_owner = key_index // tile_span
    key_spot = key_index % tile_span
    key_rows = key_owner // n_col * tile_rows + key_spot // tile_cols
    key_cols = key_owner % n_col * tile_cols + key_spot % tile_cols
    valid_key = (key_rows[None, :] < heights[:, None]) & (key_cols[None, :] < widths[:, None])
    cos_tab, sin_tab = rope_tables(query_rows, query_cols, HEAD)
    cos_four = cos_tab[None, :, None, :]
    sin_four = sin_tab[None, :, None, :]
    cond_f = conditioning.astype(jnp.float32)
    cond_sig = jax.nn.sigmoid(cond_f)
    act_low = (cond_f * cond_sig).astype(jnp.bfloat16)
    gathered = (
        lax.all_gather(w_mod, ("dp", "row", "col"), axis=1, tiled=True),
        lax.all_gather(b_mod, ("dp", "row", "col"), axis=0, tiled=True),
        lax.all_gather(w_qkv, ("dp", "row", "col"), axis=0, tiled=True),
        lax.all_gather(b_qkv, ("dp", "row", "col"), axis=0, tiled=True),
        lax.all_gather(w_proj, ("dp", "row", "col"), axis=0, tiled=True),
        lax.all_gather(b_proj, ("dp", "row", "col"), axis=0, tiled=True),
        lax.all_gather(w_gu, ("dp", "row", "col"), axis=0, tiled=True),
        lax.all_gather(b_gu, ("dp", "row", "col"), axis=0, tiled=True),
        lax.all_gather(w_down, ("dp", "row", "col"), axis=0, tiled=True),
        lax.all_gather(b_down, ("dp", "row", "col"), axis=0, tiled=True),
    )
    (
        w_mod_all,
        b_mod_all,
        w_qkv_all,
        b_qkv_all,
        w_proj_all,
        b_proj_all,
        w_gu_all,
        b_gu_all,
        w_down_all,
        b_down_all,
    ) = gathered
    modul = jnp.dot(act_low, w_mod_all, preferred_element_type=jnp.float32) + b_mod_all.astype(
        jnp.float32
    )
    shift_a, scale_a, gate_a, shift_m, scale_m, gate_m = [
        modul[:, piece * model_width : (piece + 1) * model_width][:, None, :] for piece in range(6)
    ]
    resid_in = tokens.reshape(item_count, tile_span, model_width).astype(jnp.float32)
    normed_a, recip_a = norm_parts(resid_in)
    h_attn = (normed_a * (1.0 + scale_a) + shift_a).astype(jnp.bfloat16)
    qkv_all = jnp.dot(h_attn, w_qkv_all, preferred_element_type=jnp.float32) + b_qkv_all.astype(
        jnp.float32
    )
    query_raw = qkv_all[..., :model_width].reshape(item_count, tile_span, HEADS, HEAD)
    key_raw = qkv_all[..., model_width : 2 * model_width].reshape(
        item_count, tile_span, HEADS, HEAD
    )
    value_raw = qkv_all[..., 2 * model_width :]
    query_recip = lax.rsqrt(jnp.mean(query_raw * query_raw, -1, keepdims=True) + EPSILON)
    key_recip = lax.rsqrt(jnp.mean(key_raw * key_raw, -1, keepdims=True) + EPSILON)
    query_normed = query_raw * query_recip * query_gain
    key_normed = key_raw * key_recip * key_gain
    query_rot = (query_normed * cos_four + rotate(query_normed) * sin_four).astype(jnp.bfloat16)
    key_rot = (key_normed * cos_four + rotate(key_normed) * sin_four).astype(jnp.bfloat16)
    value_low = value_raw.astype(jnp.bfloat16)
    kv_local = jnp.concatenate([key_rot.reshape(item_count, tile_span, model_width), value_low], -1)
    kv_every = lax.all_gather(kv_local, ("row", "col"), axis=1, tiled=True)
    query_heads = query_rot.transpose(2, 0, 1, 3)
    key_part = (
        kv_every[..., :model_width]
        .reshape(item_count, key_count, HEADS, HEAD)
        .transpose(2, 0, 1, 3)
    )
    value_part = (
        kv_every[..., model_width:]
        .reshape(item_count, key_count, HEADS, HEAD)
        .transpose(2, 0, 1, 3)
    )
    key_mask = valid_key[:, None, :]

    def attend(head_block):
        query_h, key_h, value_h = head_block
        scores = (
            jnp.einsum("itd,ikd->itk", query_h, key_h, preferred_element_type=jnp.float32)
            * inv_root
        )
        scores = jnp.where(key_mask, scores, MASKED)
        row_max = jnp.max(scores, -1, keepdims=True)
        exponent = jnp.exp(scores - row_max)
        row_sum = jnp.sum(exponent, -1, keepdims=True)
        probs = (exponent / row_sum).astype(jnp.bfloat16)
        result = jnp.einsum("itk,ikd->itd", probs, value_h, preferred_element_type=jnp.float32)
        return (result, row_max, row_sum)

    attended_heads, max_kept, sum_kept = lax.map(attend, (query_heads, key_part, value_part))
    attended = (
        attended_heads.transpose(1, 2, 0, 3)
        .reshape(item_count, tile_span, model_width)
        .astype(jnp.bfloat16)
    )
    attn_out = jnp.dot(
        attended, w_proj_all, preferred_element_type=jnp.float32
    ) + b_proj_all.astype(jnp.float32)
    resid_mid = resid_in + gate_a * attn_out
    normed_m, recip_m = norm_parts(resid_mid)
    h_mlp = (normed_m * (1.0 + scale_m) + shift_m).astype(jnp.bfloat16)
    gate_up = jnp.dot(h_mlp, w_gu_all, preferred_element_type=jnp.float32) + b_gu_all.astype(
        jnp.float32
    )
    gate_part = gate_up[..., :FF]
    up_part = gate_up[..., FF:]
    gate_sig = jax.nn.sigmoid(gate_part)
    gate_act = gate_part * gate_sig
    hidden = (gate_act * up_part).astype(jnp.bfloat16)
    mlp_out = jnp.dot(hidden, w_down_all, preferred_element_type=jnp.float32) + b_down_all.astype(
        jnp.float32
    )
    mask_f = valid_query[..., None].astype(jnp.float32)
    block_out = ((resid_mid + gate_m * mlp_out) * mask_f).astype(jnp.bfloat16)
    out_grad = cotangent.reshape(item_count, tile_span, model_width).astype(jnp.float32) * mask_f
    d_mlp = (gate_m * out_grad).astype(jnp.bfloat16)
    d_gate_m = jnp.sum(out_grad * mlp_out, 1)
    dw_down = jnp.einsum("itf,itd->fd", hidden, d_mlp, preferred_element_type=jnp.float32)
    db_down = jnp.sum(d_mlp.astype(jnp.float32), (0, 1))
    d_hidden = jnp.einsum("itd,fd->itf", d_mlp, w_down_all, preferred_element_type=jnp.float32)
    d_gate = d_hidden * up_part * gate_sig * (1.0 + gate_part * (1.0 - gate_sig))
    d_up = d_hidden * gate_act
    d_gate_up = jnp.concatenate([d_gate, d_up], -1).astype(jnp.bfloat16)
    dw_gu = jnp.einsum("itd,ite->de", h_mlp, d_gate_up, preferred_element_type=jnp.float32)
    db_gu = jnp.sum(d_gate_up.astype(jnp.float32), (0, 1))
    d_hmlp = jnp.einsum("ite,de->itd", d_gate_up, w_gu_all, preferred_element_type=jnp.float32)
    d_shift_m = jnp.sum(d_hmlp, 1)
    d_scale_m = jnp.sum(d_hmlp * normed_m, 1)
    d_mid = out_grad + norm_back(d_hmlp * (1.0 + scale_m), normed_m, recip_m)
    d_attn = (gate_a * d_mid).astype(jnp.bfloat16)
    d_gate_a = jnp.sum(d_mid * attn_out, 1)
    dw_proj = jnp.einsum("itd,ite->de", attended, d_attn, preferred_element_type=jnp.float32)
    db_proj = jnp.sum(d_attn.astype(jnp.float32), (0, 1))
    d_attended = jnp.einsum(
        "ite,de->itd", d_attn, w_proj_all, preferred_element_type=jnp.float32
    ).astype(jnp.bfloat16)
    d_att_heads = d_attended.reshape(item_count, tile_span, HEADS, HEAD).transpose(2, 0, 1, 3)
    key_back, value_back = (key_part, value_part)

    def attend_back(head_block):
        query_h, key_h, value_h, grad_h, max_h, sum_h = head_block
        scores = (
            jnp.einsum("itd,ikd->itk", query_h, key_h, preferred_element_type=jnp.float32)
            * inv_root
        )
        scores = jnp.where(key_mask, scores, MASKED)
        probs = jnp.exp(scores - max_h) / sum_h
        d_probs = jnp.einsum("itd,ikd->itk", grad_h, value_h, preferred_element_type=jnp.float32)
        delta = jnp.sum(probs * d_probs, -1, keepdims=True)
        d_scores = (probs * (d_probs - delta)).astype(jnp.bfloat16)
        d_query = (
            jnp.einsum("itk,ikd->itd", d_scores, key_h, preferred_element_type=jnp.float32)
            * inv_root
        )
        d_key = (
            jnp.einsum("itk,itd->ikd", d_scores, query_h, preferred_element_type=jnp.float32)
            * inv_root
        )
        d_value = jnp.einsum(
            "itk,itd->ikd", probs.astype(jnp.bfloat16), grad_h, preferred_element_type=jnp.float32
        )
        return (d_query, d_key, d_value)

    dq_heads, dk_heads, dv_heads = lax.map(
        attend_back, (query_heads, key_back, value_back, d_att_heads, max_kept, sum_kept)
    )
    dkv_term = jnp.concatenate(
        [
            dk_heads.transpose(1, 2, 0, 3).reshape(item_count, key_count, model_width),
            dv_heads.transpose(1, 2, 0, 3).reshape(item_count, key_count, model_width),
        ],
        -1,
    )
    dkv_own = lax.psum_scatter(dkv_term, ("row", "col"), scatter_dimension=1, tiled=True)
    d_key_rot = dkv_own[..., :model_width].reshape(item_count, tile_span, HEADS, HEAD)
    d_value = dkv_own[..., model_width:]
    d_query_rot = dq_heads.transpose(1, 2, 0, 3)
    d_query_n = d_query_rot * cos_four - rotate(d_query_rot * sin_four)
    d_key_n = d_key_rot * cos_four - rotate(d_key_rot * sin_four)
    d_query_raw, dq_gain = head_back(d_query_n, query_raw, query_recip, query_gain)
    d_key_raw, dk_gain = head_back(d_key_n, key_raw, key_recip, key_gain)
    gain_total = lax.psum((dq_gain, dk_gain), ("dp", "row", "col"))
    d_qkv = jnp.concatenate(
        [
            d_query_raw.reshape(item_count, tile_span, model_width),
            d_key_raw.reshape(item_count, tile_span, model_width),
            d_value,
        ],
        -1,
    ).astype(jnp.bfloat16)
    dw_qkv = jnp.einsum("itd,ite->de", h_attn, d_qkv, preferred_element_type=jnp.float32)
    db_qkv = jnp.sum(d_qkv.astype(jnp.float32), (0, 1))
    db_query_key = db_qkv[: 2 * model_width]
    db_value = db_qkv[2 * model_width :]
    d_hattn = jnp.einsum("ite,de->itd", d_qkv, w_qkv_all, preferred_element_type=jnp.float32)
    d_shift_a = jnp.sum(d_hattn, 1)
    d_scale_a = jnp.sum(d_hattn * normed_a, 1)
    d_tokens = d_mid + norm_back(d_hattn * (1.0 + scale_a), normed_a, recip_a)
    d_modul = jnp.concatenate([d_shift_a, d_scale_a, d_gate_a, d_shift_m, d_scale_m, d_gate_m], -1)
    act_f = act_low.astype(jnp.float32)
    dw_mod = jnp.einsum("id,ie->de", act_f, d_modul, precision=PRECISE)
    db_mod = jnp.sum(d_modul, 0)
    d_act = jnp.einsum("ie,de->id", d_modul, w_mod_all.astype(jnp.float32), precision=PRECISE)
    d_cond_part = d_act * cond_sig * (1.0 + cond_f * (1.0 - cond_sig))
    d_cond = lax.psum_scatter(d_cond_part, ("row", "col"), scatter_dimension=1, tiled=True)
    summed = (
        lax.psum_scatter(dw_mod, ("dp", "row", "col"), scatter_dimension=1, tiled=True),
        lax.psum_scatter(db_mod, ("dp", "row", "col"), scatter_dimension=0, tiled=True),
        lax.psum_scatter(dw_qkv, ("dp", "row", "col"), scatter_dimension=0, tiled=True),
        lax.psum_scatter(db_query_key, ("dp", "row", "col"), scatter_dimension=0, tiled=True),
        lax.psum_scatter(db_value, ("dp", "row", "col"), scatter_dimension=0, tiled=True),
        lax.psum_scatter(dw_proj, ("dp", "row", "col"), scatter_dimension=0, tiled=True),
        lax.psum_scatter(db_proj, ("dp", "row", "col"), scatter_dimension=0, tiled=True),
        lax.psum_scatter(dw_gu, ("dp", "row", "col"), scatter_dimension=0, tiled=True),
        lax.psum_scatter(db_gu, ("dp", "row", "col"), scatter_dimension=0, tiled=True),
        lax.psum_scatter(dw_down, ("dp", "row", "col"), scatter_dimension=0, tiled=True),
        lax.psum_scatter(db_down, ("dp", "row", "col"), scatter_dimension=0, tiled=True),
    )
    (
        g_w_mod,
        g_b_mod,
        g_w_qkv,
        g_b_query_key,
        g_b_value,
        g_w_proj,
        g_b_proj,
        g_w_gu,
        g_b_gu,
        g_w_down,
        g_b_down,
    ) = summed
    return (
        block_out.reshape(item_count, tile_rows, tile_cols, model_width),
        d_tokens.reshape(item_count, tile_rows, tile_cols, model_width),
        d_cond,
        g_w_mod,
        g_b_mod,
        g_w_qkv,
        g_b_query_key,
        g_b_value,
        gain_total[0],
        gain_total[1],
        g_w_proj,
        g_b_proj,
        g_w_gu,
        g_b_gu,
        g_w_down,
        g_b_down,
    )


MESH = pl.DeviceIdType.MESH
BF = jnp.bfloat16
F32 = jnp.float32
LIMIT = 60 * 1024 * 1024
D = 1152
UNIT = 36
PAD = 48
TOK = 256
GROUP = 1024
SPLIT_Q, SPLIT_P, SPLIT_D = 384, 640, 640
ROOT = 1.0 / math.sqrt(HEAD)
ROOT2 = ROOT / math.log(2.0)


def nn(a, b):
    return lax.dot_general(a, b, (((1,), (0,)), ((), ())), preferred_element_type=F32)


def nt(a, b):
    return lax.dot_general(a, b, (((1,), (1,)), ((), ())), preferred_element_type=F32)


def tn(a, b):
    return lax.dot_general(a, b, (((0,), (0,)), ((), ())), preferred_element_type=F32)


def width_order():
    xx, zh, yy, zl, cc, jj = np.indices((2, 2, 2, 2, 2, UNIT)).reshape(6, -1)
    return ((((xx * 2 + cc) * 2 + zh) * 2 + zl) * 2 + yy) * UNIT + jj


def constants():
    perm = np.zeros((D, D), np.float32)
    perm[width_order(), np.arange(D)] = 1.0
    spread = np.zeros((864, 1536), np.float32)
    tt, hh, yy, jj = np.indices((3, 4, 2, UNIT)).reshape(4, -1)
    spread[tt * 288 + hh * 72 + yy * 36 + jj, tt * 512 + hh * 128 + yy * 64 + jj] = 1.0
    pick = np.zeros((144, 192), np.float32)
    kk, jj = np.indices((4, UNIT)).reshape(2, -1)
    pick[kk * 36 + jj, kk * 48 + jj] = 1.0
    spot = np.arange(512)
    row = spot // 128 * 4 + spot // 16 % 4
    col = spot // 64 % 2 * 16 + spot % 16
    lane = np.arange(128)
    part = lane % 64
    freq = np.exp(-math.log(10000.0) * 2.0 * (part // 2) / 36.0)
    place = np.where(lane[None, :] >= 64, col[:, None], row[:, None]).astype(np.float64)
    angle = place * freq[None, :]
    live = part < UNIT
    cos = np.where(live, np.cos(angle), 0.0)
    sin = np.where(live, np.sin(angle), 0.0)
    even = lane % 2 == 0
    tabs = np.stack([cos, np.where(even, -sin, 0.0), np.where(even, 0.0, sin)]).astype(np.float32)
    return (
        jnp.asarray(perm, BF),
        jnp.asarray(spread, BF),
        jnp.asarray(pick, BF),
        jnp.asarray(tabs, F32),
    )


class Place:
    def __init__(self):
        dp = lax.axis_index("dp")
        self.z = lax.axis_index("row")
        self.y = lax.axis_index("col")
        self.x = dp // 2
        self.c = dp % 2
        self.zh = self.z // 2
        self.zl = self.z % 2
        self.m = self.zl * 2 + self.c
        self.dp = dp

    def mate(self, r):
        c = 1 - self.c if r % 2 else self.c
        zl = 1 - self.zl if r // 2 else self.zl
        return zl * 2 + c, (self.x * 2 + c, self.zh * 2 + zl, self.y)

    def xpeer(self):
        return ((1 - self.x) * 2 + self.c, self.z, self.y)

    def ypeer(self):
        return (self.dp, self.z, 1 - self.y)

    def zpeer(self):
        return (self.dp, (1 - self.zh) * 2 + self.zl, self.y)

    def item_home(self, j):
        return (self.x * 2 + self.zh, j, self.c)

    def item_source(self, blk):
        return (self.x * 2 + self.y, self.c * 2 + blk // 2, blk % 2)

    def is_me(self, dev):
        return (dev[0] == self.dp) & (dev[1] == self.z) & (dev[2] == self.y)


class Link:
    def __init__(self, here, ssem, rsem):
        self.here, self.ssem, self.rsem, self.n, self.open = here, ssem, rsem, 0, []

    def greet(self, items):
        here = self.here
        bar = pltpu.get_barrier_semaphore()
        devs = [here.mate(r)[1] for r in (1, 2, 3)]
        devs += [here.xpeer(), here.ypeer(), here.zpeer()]
        devs += [near(here, r)[3] for r in range(1, 8)] + [along_z(here, r)[1] for r in (1, 2, 3)]
        for d in devs:
            pl.semaphore_signal(bar, inc=1, device_id=d, device_id_type=MESH)
        total = len(devs)
        if items:
            for d in [here.item_home(j) for j in range(4)] + [here.item_source(j) for j in range(4)]:


                @pl.when(jnp.logical_not(here.is_me(d)))
                def _():
                    pl.semaphore_signal(bar, inc=1, device_id=d, device_id_type=MESH)

            far = (here.zh - here.c) * (here.zh - here.c)
            off = (here.y - here.c) * (here.y - here.c)
            total += 8 - 2 * (1 - far) * (1 - off)
        pl.semaphore_wait(bar, total)

    def send(self, src, dst, dev):
        k = self.n
        self.n += 1
        copy = pltpu.make_async_remote_copy(
            src_ref=src,
            dst_ref=dst,
            send_sem=self.ssem.at[k],
            recv_sem=self.rsem.at[k],
            device_id=dev,
            device_id_type=MESH,
        )
        copy.start()
        self.open.append(copy)
        return copy

    def scatter(self, src_of, dst, dev_of, slot):
        base = self.n
        self.n += 4
        here = self.here
        copies = []
        for j in range(4):
            dev = dev_of(j)
            mine = here.is_me(dev)
            remote = pltpu.make_async_remote_copy(
                src_ref=src_of(j),
                dst_ref=dst,
                send_sem=self.ssem.at[base + j],
                recv_sem=self.rsem.at[base + slot],
                device_id=dev,
                device_id_type=MESH,
            )
            local_copy = pltpu.make_async_copy(src_of(j), dst, self.rsem.at[base + slot])

            @pl.when(mine)
            def _():
                local_copy.start()

            @pl.when(jnp.logical_not(mine))
            def _():
                remote.start()

            copies.append((mine, remote))

        def wait_send():
            for mine, remote in copies:

                @pl.when(jnp.logical_not(mine))
                def _():
                    remote.wait_send()

        def wait_recv(src, dst_of):
            for j in range(4):
                pltpu.make_async_copy(src, dst_of(j), self.rsem.at[base + j]).wait()

        return wait_send, wait_recv

    def settle(self, *copies):
        for copy in copies:
            copy.wait_send()
            self.open = [c for c in self.open if c is not copy]

    def finish(self):
        for copy in self.open:
            copy.wait_send()
        self.open = []


def norm_rows(x):
    mean = jnp.sum(x, -1, keepdims=True) * (1.0 / D)
    cent = x - mean
    var = jnp.sum(cent * cent, -1, keepdims=True) * (1.0 / D)
    recip = lax.rsqrt(var + EPSILON)
    return cent * recip, recip


def norm_rows_back(g, y, recip):
    mg = jnp.sum(g, -1, keepdims=True) * (1.0 / D)
    mgy = jnp.sum(g * y, -1, keepdims=True) * (1.0 / D)
    return recip * (g - mg - y * mgy)


def at(i, n):
    return pl.ds(pl.multiple_of(i * n, n), n)


class Gather:
    def __init__(self, link, ref, rows, lo, split, hi):
        self.link, self.ref, self.rows = link, ref, rows
        self.ca, self.cb = pl.ds(lo, split - lo), pl.ds(split, hi - split)
        self.all = slice(None) if hi - lo == ref.shape[-1] else pl.ds(lo, hi - lo)

    def cut(self, i, j, k, cols):
        return self.ref.at[i, j, k, pl.ds(0, self.rows), cols]

    def hop1(self):
        h = self.link.here
        part = self.cut(h.x, h.zh, h.y, self.all)
        self.a = self.link.send(part, part, h.zpeer())

    def hop2(self):
        h = self.link.here
        self.a.wait_recv()
        pa = self.cut(h.x, slice(None), h.y, self.ca)
        pb = self.cut(h.x, slice(None), h.y, self.cb)
        self.a = self.link.send(pa, pa, h.xpeer())
        self.b = self.link.send(pb, pb, h.ypeer())

    def parts(self, ref):
        h = self.link.here
        rows = pl.ds(0, self.rows)
        return ref.at[:, :, h.y, rows, self.ca], ref.at[h.x, :, :, rows, self.cb]

    def hop3(self):
        self.done()
        self.last_hop()

    def last_hop(self, held=None):
        h = self.link.here
        pa, pb = self.parts(self.ref)
        if held is not None:
            ha, hb = self.parts(held)
            self.a = self.link.send(ha, pa, h.ypeer())
            self.b = self.link.send(hb, pb, h.xpeer())
            return
        self.a = self.link.send(pa, pa, h.ypeer())
        self.b = self.link.send(pb, pb, h.xpeer())

    def done(self):
        self.a.wait_recv()
        self.b.wait_recv()


class Reduce:
    def __init__(self, link, ref, bufs, lo, split, hi):
        self.link, self.ref, self.lo, self.split, self.hi = link, ref, lo, split, hi
        self.r1a, self.r1b, self.r2a, self.r2b, self.r3a, self.r3b = bufs

    @staticmethod
    def buffers(rows, cols, split):
        rest = cols - split
        return [
            pltpu.VMEM((2, 2, rows, split), BF),
            pltpu.VMEM((2, 2, rows, rest), BF),
            pltpu.VMEM((2, rows, split), BF),
            pltpu.VMEM((2, rows, rest), BF),
            pltpu.VMEM((rows, split), BF),
            pltpu.VMEM((rows, rest), BF),
        ]

    def hop1(self):
        h = self.link.here
        ca, cb = pl.ds(self.lo, self.split - self.lo), pl.ds(self.split, self.hi - self.split)
        self.a = self.link.send(self.ref.at[1 - h.x, :, :, :, ca], self.r1a, h.xpeer())
        self.b = self.link.send(self.ref.at[:, :, 1 - h.y, :, cb], self.r1b, h.ypeer())

    def hop2(self):
        h = self.link.here
        ca, cb = pl.ds(self.lo, self.split - self.lo), pl.ds(self.split, self.hi - self.split)
        self.a.wait_recv()
        self.b.wait_recv()

        def add(i, carry):
            u, v = i // 2, i % 2
            own = self.ref[h.x, u, v, :, ca].astype(F32)
            self.r1a[u, v] = (self.r1a[u, v].astype(F32) + own).astype(BF)
            own = self.ref[u, v, h.y, :, cb].astype(F32)
            self.r1b[u, v] = (self.r1b[u, v].astype(F32) + own).astype(BF)
            return carry

        lax.fori_loop(0, 4, add, 0)
        self.a = self.link.send(self.r1a.at[:, 1 - h.y], self.r2a, h.ypeer())
        self.b = self.link.send(self.r1b.at[1 - h.x], self.r2b, h.xpeer())

    def hop3(self):
        h = self.link.here
        self.a.wait_recv()
        self.b.wait_recv()

        def add(u, carry):
            own = self.r1a[u, h.y].astype(F32)
            self.r2a[u] = (self.r2a[u].astype(F32) + own).astype(BF)
            own = self.r1b[h.x, u].astype(F32)
            self.r2b[u] = (self.r2b[u].astype(F32) + own).astype(BF)
            return carry

        lax.fori_loop(0, 2, add, 0)
        self.a = self.link.send(self.r2a.at[1 - h.zh], self.r3a, h.zpeer())
        self.b = self.link.send(self.r2b.at[1 - h.zh], self.r3b, h.zpeer())

    def done(self):
        h = self.link.here
        self.a.wait_recv()
        self.b.wait_recv()
        left = self.r2a[h.zh].astype(F32) + self.r3a[...].astype(F32)
        right = self.r2b[h.zh].astype(F32) + self.r3b[...].astype(F32)
        return left.astype(BF), right.astype(BF)


class RowGather:
    def __init__(self, link, ref):
        self.link, self.ref = link, ref
        here = link.here
        own = ref.at[at(here.m, TOK)]
        self.far = link.send(own, own, here.mate(2)[1])
        self.near = link.send(own, own, here.mate(1)[1])

    def near_done(self):
        self.near.wait_recv()

    def pass_on(self):
        here = self.link.here
        self.far.wait_recv()
        rows = self.ref.at[at(here.mate(2)[0], TOK)]
        self.last = self.link.send(rows, rows, here.mate(1)[1])

    def last_done(self):
        self.last.wait_recv()


class RowReduce:
    def __init__(self, link, out, into):
        self.link, self.out, self.into = link, out, into

    def give(self, r, val):
        i = 0 if r == 3 else 1
        if val is not None:
            self.out[i] = val.astype(BF)
        sent = self.link.send(self.out.at[i], self.into.at[i], self.link.here.mate(1)[1])
        if r == 3:
            self.s3 = sent
        else:
            self.s1 = sent

    def keep_far(self, val):
        self.out[2] = val.astype(BF)

    def pass_on(self):
        self.s3.wait_recv()

        def add(i, carry):
            rows = at(i, 32)
            both = self.out[2, rows, :].astype(F32) + self.into[0, rows, :].astype(F32)
            self.out[2, rows, :] = both.astype(BF)
            return carry

        lax.fori_loop(0, 8, add, 0)
        self.s2 = self.link.send(self.out.at[2], self.into.at[2], self.link.here.mate(2)[1])

    def arrive(self):
        self.s1.wait_recv()
        self.s2.wait_recv()

    def total(self, rows):
        return self.into[1, rows, :].astype(F32) + self.into[2, rows, :].astype(F32)


def turn(v, cos, sina, sinb):
    return v * cos + pltpu.roll(v, 127, 1) * sina + pltpu.roll(v, 1, 1) * sinb


def turn_back(d, cos, sina, sinb):
    return d * cos - pltpu.roll(d, 127, 1) * sina - pltpu.roll(d, 1, 1) * sinb


def near(here, r):
    x = 1 - here.x if r // 4 else here.x
    c = 1 - here.c if r // 2 % 2 else here.c
    y = 1 - here.y if r % 2 else here.y
    return x, c, y, (x * 2 + c, here.z, y)


def along_z(here, r):
    z = (here.z + r) % 4
    return z, (here.dp, z, here.y)


def shard_parts(s):
    x, c, zh, zl, y = s // 16, s // 8 % 2, s // 4 % 2, s // 2 % 2, s % 2
    member, spot = zl * 2 + c, (x * 2 + zh) * 2 + y
    return spot * 4 + member, member, spot


def three(v):
    hi = v.astype(BF)
    rest = v - hi.astype(F32)
    mid = rest.astype(BF)
    return jnp.concatenate([hi, mid, (rest - mid.astype(F32)).astype(BF)], 0)


def by_member(src, out, tmp, width, pieces):
    cols = pieces * 4 * width
    for t in range(pieces):
        for h in range(16):
            unit = shard_parts(h * 2)
            dst = t * 4 * width + unit[2] // 2 * width
            tmp[unit[1], 0:UNIT, dst : dst + width] = src[
                :, (t * 16 + h) * width : (t * 16 + h + 1) * width
            ].astype(F32)
    for m in range(4):
        out[m] = tmp[m, :, 0:cols].astype(BF)


def by_column(src, out, width, pieces):
    for t in range(pieces):
        for h in range(16):
            unit = shard_parts(h * 2)
            at_ = t * 4 * width + unit[2] // 2 * width
            out[:, (t * 16 + h) * width : (t * 16 + h + 1) * width] = src[
                unit[1], 0:UNIT, at_ : at_ + width
            ].astype(F32)


def silu_slope(v):
    sig = jax.nn.sigmoid(v)
    return sig * (1.0 + v * (1.0 - sig))


def kernel_a(
    tok_in, cot_in, wqkv, wgu, wp_in, wd_in, cond, w_mod_t, bm_in, bq_in, bp_in, bd_in, bg_in, qg_in, kg_in, tall_in,
    wide_in, perm_in, spread_in, pick, tabs_in,
    wq_out, wp_out, wg_out, wd_out, ha_out, raw_out, rot_out, att_out, hm_out, dm_out, tok_out, og_out, attn_o_out,
    condg, modv, bg, bd, gains, maskb, valid,
    wq, wp, wg, wd, ha, raw, rot, att, s0q, s0g, tokr, cotr, wqe, psend, precv, pown,
    wqs, wgs, tmp, block, msg, p1, m2, got, bq4, bg4, bp, hm, dmlp, tokp, og, attn_out, perm, spread, tabs, vecs,
    ssem, rsem, lsem,
):
    here = Place()
    link = Link(here, ssem, rsem)
    fetch = Fetch(lsem)
    m = here.m
    perm_got, spread_got, tabs_got = (
        fetch.go(a, b) for a, b in ((perm_in, perm), (spread_in, spread), (tabs_in, tabs))
    )
    vecs[...] = jnp.zeros_like(vecs)
    for line, lo, ref in (
        (0, 0, bm_in), (1, 0, bq_in), (1, 108, bp_in), (1, 144, bd_in), (2, 0, bg_in), (3, 0, qg_in), (4, 0, kg_in),
    ):
        n = ref.shape[0]
        vecs[line : line + 1, lo : lo + n] = ref[...].astype(F32).reshape(1, n)
    lane = lax.broadcasted_iota(jnp.int32, (1, 256), 1)
    sizes = jnp.zeros((1, 256), F32)
    for i in range(4):
        sizes = jnp.where(lane == i, tall_in[i].astype(F32), sizes)
        sizes = jnp.where(lane == 4 + i, wide_in[i].astype(F32), sizes)
    vecs[5:6, :] = sizes
    block[...] = jnp.zeros_like(block)
    block[0:4, :] = cond[...].astype(F32)
    block[4:5, 0:8] = vecs[5:6, 0:8]
    condg[here.dp] = block[...]
    link.greet(True)
    slot = here.zl * 2 + here.y
    rows_in = at(slot, 64)
    cs = [link.send(block, condg.at[here.dp], near(here, r)[3]) for r in (2, 4, 6)]
    tmp[...] = jnp.zeros_like(tmp)
    by_member(wqkv, wqs, tmp, 72, 3)
    sq, sg = {}, {}
    for r in (2, 3, 1):
        k, dev = here.mate(r)
        sq[r] = link.send(wqs.at[k], s0q.at[m], dev)
    own_q = fetch.go(wqs.at[m], s0q.at[m])
    for c in cs:
        c.wait_recv()
    v = condg[...].reshape(32, D)
    part = nt((v * jax.nn.sigmoid(v)).astype(BF), w_mod_t[...]) + vecs[0:1, 0:216]
    for z in range(4):
        msg[z, 4:6, :] = vecs[1:3, :]
        for d in range(4):
            msg[z, d : d + 1, 0:216] = part[d * 8 + z : d * 8 + z + 1, :]
    zs = []
    for r in (1, 2, 3):
        z, dev = along_z(here, r)
        zs.append(link.send(msg.at[z], p1.at[here.z], dev))
    p1[here.z] = msg[here.z]

    gq = Gather(link, wq, 144, 0, SPLIT_Q, 864)
    gp = Gather(link, wp, PAD, 0, SPLIT_P, D)
    g1 = Gather(link, wg, 144, 0, 384, 768)
    g2 = Gather(link, wg, 144, 768, 1152, 1536)
    gd = Gather(link, wd, 96, 0, SPLIT_D, D)
    by_member(wgu, wgs, tmp, 192, 2)
    own_q.wait()
    for r in (1, 2, 3):
        sq[r].wait_recv()
    wq[here.x, here.zh, here.y] = nn(pick[...], s0q[...].reshape(192, 864)).astype(BF)
    gq.hop1()
    for c in zs:
        c.wait_recv()
    for z in range(4):
        for d in range(4):
            m2[d, z, 0:1, :] = p1[z, d : d + 1, :]
            m2[d, z, 1:3, :] = p1[z, 4:6, :]
    ns = []
    for r in range(1, 8):
        x, _, y, dev = near(here, r)
        ns.append(link.send(m2.at[x * 2 + y], got.at[here.x, here.c, here.y], dev))
    got[here.x, here.c, here.y] = m2[here.x * 2 + here.y]
    tok_sent, tok_got = link.scatter(lambda j: tok_in.at[j], tokr.at[rows_in], here.item_home, slot)

    for r in (2, 3, 1):
        k, dev = here.mate(r)
        sg[r] = link.send(wgs.at[k], s0g.at[m], dev)
    own_g = fetch.go(wgs.at[m], s0g.at[m])
    perm_got.wait()
    wp[:, :, :, PAD:64, :] = jnp.zeros((2, 2, 2, 64 - PAD, D), BF)
    tmp[0, 0:UNIT, 0:D] = nn(wp_in[...], perm[...])
    tmp[0, UNIT:PAD, :] = jnp.zeros((PAD - UNIT, 1536), F32)
    wp[here.x, here.zh, here.y, 0:PAD, :] = tmp[0, :, 0:D].astype(BF)
    gp.hop1()
    ext = condg[here.x * 2 + here.y, 4:5, :]
    lane = lax.broadcasted_iota(jnp.int32, (1, D), 1)
    spot = lax.broadcasted_iota(jnp.int32, (1, 512), 1)
    row_at = spot // 128 * 4 + spot // 16 % 4
    col_at = spot // 64 % 2 * 16 + spot % 16

    def extent(item, first):
        return jnp.sum(jnp.where(lane == item + first, ext, 0.0), -1, keepdims=True)

    for i in range(2):
        tall, wide = extent(here.zh * 2 + i, 0), extent(here.zh * 2 + i, 4)
        live = (row_at.astype(F32) < tall) & (col_at.astype(F32) < wide)
        maskb[i] = jnp.where(live, 0.0, MASKED)
    spot = lax.broadcasted_iota(jnp.int32, (TOK, 1), 0) + here.c * TOK
    row_at = (spot // 128 * 4 + spot // 16 % 4).astype(F32)
    col_at = (spot // 64 % 2 * 16 + spot % 16).astype(F32)
    live = (row_at < extent(here.z, 0)) & (col_at < extent(here.z, 4))
    valid[...] = jnp.where(live, 1.0, 0.0)
    gains[...] = jnp.zeros_like(gains)
    for t in range(2):
        for e in range(2):
            gains[t : t + 1, e * 64 : e * 64 + UNIT] = vecs[3 + t : 4 + t, e * UNIT : e * UNIT + UNIT]
    for c in ns:
        c.wait_recv()
    modv[...] = jnp.zeros_like(modv)
    bq4[...] = jnp.zeros_like(bq4)
    for s in range(32):
        line = got[s // 16, s // 8 % 2, s % 2, s // 2 % 4]
        for q in range(6):
            piece, unit = divmod(6 * s + q, 32)
            to = shard_parts(unit)[0] * UNIT
            modv[piece : piece + 1, to : to + UNIT] = line[0:1, q * UNIT : q * UNIT + UNIT]
        for q in range(3):
            piece, unit = divmod(3 * s + q, 32)
            _, member, spot = shard_parts(unit)
            to = piece * 512 + spot * 64
            bq4[member, :, to : to + UNIT] = line[1:2, q * UNIT : q * UNIT + UNIT]
        to = shard_parts(s)[0] * UNIT
        bp[:, to : to + UNIT] = line[1:2, 108:144]
        bd[:, to : to + UNIT] = line[1:2, 144:180]
        for q in range(2):
            piece, unit = divmod(2 * s + q, 32)
            _, member, spot = shard_parts(unit)
            to = piece * 768 + spot * 96
            bg4[member, :, to : to + 96] = line[2:3, q * 96 : q * 96 + 96]
    bg[...] = bg4[m]
    gq.hop2()
    tok_got(tok_in.at[0], lambda j: tokr.at[pl.ds(j * 64, 64)])
    gq.hop3()
    tokp[...] = nn(tokr[...], perm[...]).astype(BF)

    def first_norm(i, carry):
        n, _ = norm_rows(tokp[at(i, 32), :].astype(F32))
        h = n * (1.0 + modv[1:2, :]) + modv[0:1, :]
        ha[pl.ds(pl.multiple_of(m * TOK + i * 32, 32), 32), :] = h.astype(BF)
        return carry

    lax.fori_loop(0, 8, first_norm, 0)
    ha_all = RowGather(link, ha)
    own_g.wait()
    for r in (1, 2, 3):
        sg[r].wait_recv()
    wg[here.x, here.zh, here.y] = nn(pick[...], s0g[...].reshape(192, 1536)).astype(BF)
    g1.hop1()
    g2.hop1()
    wd[here.x, here.zh, here.y] = nn(wd_in[...], perm[...]).astype(BF)
    gd.hop1()
    cot_sent, cot_got = link.scatter(lambda j: cot_in.at[j], cotr.at[rows_in], here.item_home, slot)
    gp.hop2()
    gq.done()
    outs = [fetch.go(wq, wq_out), fetch.go(tokp, tok_out)]
    spread_got.wait()

    def widen(i, carry):
        part = wq[i // 2, i % 2].reshape(288, 864)
        wqe[at(i, 288), :] = nn(part, spread[...]).astype(BF)
        return carry

    lax.fori_loop(0, 4, widen, 0)
    gp.hop3()
    tabs_got.wait()

    g1.hop2()
    ha_all.pass_on()
    g1.hop3()
    ha_all.near_done()
    ha_all.last_done()
    outs.append(fetch.go(ha, ha_out))

    def project(b, carry):
        acc = nn(ha[at(b, TOK), :], wqe[...]) + bq4[m]
        item, half = b // 2, at(b % 2, TOK)
        cos, sina, sinb = tabs[0, half, :], tabs[1, half, :], tabs[2, half, :]
        for h in range(4):
            p = item * 4 + h
            for t in range(2):
                v = acc[:, t * 512 + h * 128 : t * 512 + h * 128 + 128]
                recip = lax.rsqrt(jnp.sum(v * v, -1, keepdims=True) * (1.0 / HEAD) + EPSILON)
                raw[p, t, half, :] = v
                n = v * recip * gains[t : t + 1, :]
                rot[p, t, half, :] = turn(n, cos, sina, sinb).astype(BF)
            rot[p, 2, half, :] = acc[:, 1024 + h * 128 : 1152 + h * 128].astype(BF)
        return carry

    def attend(p, carry):
        item = p // 4
        lanes = at(p % 4, 128)
        for half in range(2):
            rows = pl.ds(half * TOK, TOK)
            e = jnp.exp2(nt(rot[p, 0, rows, :], rot[p, 1]) * ROOT2 + maskb[item])
            pr = (e * (1.0 / jnp.sum(e, -1, keepdims=True))).astype(BF)
            out_rows = pl.ds(pl.multiple_of(item * 512 + half * TOK, TOK), TOK)
            att[out_rows, lanes] = nn(pr, rot[p, 2]).astype(BF)
        return carry

    other = 1 - here.zl
    lax.fori_loop(other * 2, other * 2 + 2, project, 0)
    g2.hop2()
    lax.fori_loop(other * 4, other * 4 + 4, attend, 0)
    gp.done()
    outs.append(fetch.go(wp, wp_out))
    wpf = wp[...].reshape(512, D)
    red = RowReduce(link, psend, precv)
    red.give(3, nn(att[at(here.mate(3)[0], TOK), :], wpf))
    red.keep_far(nn(att[at(here.mate(2)[0], TOK), :], wpf))
    red.pass_on()
    gd.hop2()
    g2.hop3()
    lax.fori_loop(here.zl * 2, here.zl * 2 + 2, project, 0)
    cot_got(cot_in.at[0], lambda j: cotr.at[pl.ds(j * 64, 64)])
    og[...] = (nn(cotr[...], perm[...]) * valid[...]).astype(BF)

    def scale_grad(i, carry):
        g = og[at(i, 32), :].astype(F32) * modv[5:6, :]
        dmlp[pl.ds(pl.multiple_of(m * TOK + i * 32, 32), 32), :] = g.astype(BF)
        return carry

    lax.fori_loop(0, 8, scale_grad, 0)
    outs.append(fetch.go(og, og_out))
    dm_all = RowGather(link, dmlp)
    outs.append(fetch.go(raw, raw_out))
    outs.append(fetch.go(rot, rot_out))
    lax.fori_loop(here.zl * 4, here.zl * 4 + 4, attend, 0)
    outs.append(fetch.go(att, att_out))
    red.give(1, nn(att[at(here.mate(1)[0], TOK), :], wpf))
    pown[...] = nn(att[at(m, TOK), :], wpf)
    red.arrive()

    def second_norm(i, carry):
        rows = at(i, 32)
        a = pown[rows, :] + bp[...] + red.total(rows)
        attn_out[rows, :] = a
        n, _ = norm_rows(tokp[rows, :].astype(F32) + modv[2:3, :] * a)
        h = n * (1.0 + modv[4:5, :]) + modv[3:4, :]
        hm[rows, :] = h.astype(BF)
        return carry

    lax.fori_loop(0, 8, second_norm, 0)
    outs.append(fetch.go(hm, hm_out))
    outs.append(fetch.go(attn_out, attn_o_out))
    g1.done()
    g2.done()
    outs.append(fetch.go(wg, wg_out))
    gd.done()
    outs += [fetch.go(a, b) for a, b in zip(gd.parts(wd), gd.parts(wd_out))]
    dm_all.pass_on()
    dm_all.near_done()
    dm_all.last_done()
    outs.append(fetch.go(dmlp, dm_out))
    for c in outs:
        c.wait()
    link.finish()
    tok_sent()
    cot_sent()


def store_tiles(val, ref, base, piece, keep):
    block = ref.shape[3] if keep is None else piece
    for q in range(val.shape[0] // piece):
        row = base + q * piece
        f, off = row // block, row % block
        n = piece if keep is None else keep
        part = val[q * piece : q * piece + n, :].astype(BF)
        ref[f // 4, f // 2 % 2, f % 2, off : off + n, 0 : val.shape[1]] = part


class Fetch:
    def __init__(self, sems):
        self.sems, self.n = sems, 0

    def go(self, src, dst):
        copy = pltpu.make_async_copy(src, dst, self.sems.at[self.n])
        self.n += 1
        copy.start()
        return copy


def kernel_b(
    wg_in, wd_in, hm_in, dm_in, tok_in, og_in, attn_in, att_in, wp_in, wq_in, ha_in, raw_in, rot_in, perm_in,
    spread_in, tabs_in, modv, bg, bd, gains, maskb, valid, pick, condg, w_mod_t,
    dtok, bout, g_qkv_out, g_gu_out, fp_out, fd_out, dwm_out, dbm, dcond, o_qk, o_v, o_p, o_d, o_gu, o_qg, o_kg,
    wg, wd, hm, dmlp, tokp, og, attn_out, att, wp, wq, perm, tabs, gu, coef, hid, rsend, rrecv, mrecv, own32,
    dwg, dwd, dwp, dattn, raw, rot, to, bo, fq, fg, small, dbg, dbq, dgain,
    pk, q1, m2, q2, dm, e0, e1, e2, e3, line, bq4, bg4, slope, g_qkv, g_gu, fp, fd, dwm, sums,
    g1a, g1b, g2a, g2b, g3a, g3b, h1a, h1b, h2a, h2b, h3a, h3b, d1a, d1b, d2a, d2b, d3a, d3b,
    q1a, q1b, q2a, q2b, q3a, q3b, p1a, p1b, p2a, p2b, p3a, p3b, ssem, rsem, lsem,
):
    here = Place()
    link = Link(here, ssem, rsem)
    fetch = Fetch(lsem)
    m = here.m
    k1, k2, k3 = here.mate(1)[0], here.mate(2)[0], here.mate(3)[0]
    at_m, at_1, at_2, at_3 = at(m, TOK), at(k1, TOK), at(k2, TOK), at(k3, TOK)
    get_hm = fetch.go(hm_in, hm.at[at_m])
    get_dm = fetch.go(dm_in, dmlp)
    get_wg = fetch.go(wg_in, wg)
    gd = Gather(link, wd, 96, 0, SPLIT_D, D)
    get_wd = [fetch.go(a, b) for a, b in zip(gd.parts(wd_in), gd.parts(wd))]
    gets = [fetch.go(a, b) for a, b in ((tok_in, tokp), (og_in, og), (attn_in, attn_out))]
    get_wp = fetch.go(wp_in, wp)
    gets2 = [fetch.go(a, b) for a, b in ((tabs_in, tabs), (att_in, att), (wq_in, wq), (perm_in, perm))]
    base = fetch.n
    fetch.n += 4
    link.greet(True)
    get_hm.wait()
    hm_all = RowGather(link, hm)
    gd.last_hop(wd_in)
    small[...] = jnp.zeros_like(small)
    dbg[...] = jnp.zeros_like(dbg)
    dbq[...] = jnp.zeros_like(dbq)
    dgain[...] = jnp.zeros_like(dgain)
    get_wg.wait()
    get_dm.wait()

    def wgf():
        return wg[...].reshape(D, 1536)

    def wdf():
        return wd[...].reshape(768, D)

    def mlp(k):
        gu[...] = nn(hm[at(k, TOK), :], wgf()) + bg[...]

        def acts(i, carry):
            rows = at(i, 32)
            out = pl.ds(pl.multiple_of(k * TOK + i * 32, 32), 32)
            g, u = gu[rows, 0:768], gu[rows, 768:1536]
            sig = jax.nn.sigmoid(g)
            act = g * sig
            hid[out, :] = (act * u).astype(BF)
            coef[out, 0:768] = (u * sig * (1.0 + g * (1.0 - sig))).astype(BF)
            coef[out, 768:1536] = act.astype(BF)
            return carry

        lax.fori_loop(0, 8, acts, 0)

    def mlp_back(k):
        dh = nt(dmlp[at(k, TOK), :], wdf())
        out = at(k, TOK)
        coef[out, 0:768] = (coef[out, 0:768].astype(F32) * dh).astype(BF)
        coef[out, 768:1536] = (coef[out, 768:1536].astype(F32) * dh).astype(BF)
        dbg[0:1, :] += jnp.sum(coef[out, :].astype(F32), 0, keepdims=True)
        return nt(coef[out, :], wgf())

    hred = RowReduce(link, rsend, rrecv)
    mlp(m)
    hm_all.near_done()
    mlp(k1)
    for c in get_wd:
        c.wait()
    gd.done()
    own32[...] = mlp_back(m)
    hred.give(1, mlp_back(k1))
    hm_all.pass_on()
    mlp(k2)
    hm_all.last_done()
    hred.keep_far(mlp_back(k2))
    mlp(k3)
    hred.give(3, mlp_back(k3))
    hred.pass_on()

    ra = Reduce(link, dwg, (g1a, g1b, g2a, g2b, g3a, g3b), 0, 384, 768)
    rb = Reduce(link, dwg, (h1a, h1b, h2a, h2b, h3a, h3b), 768, 1152, 1536)
    rd = Reduce(link, dwd, (d1a, d1b, d2a, d2b, d3a, d3b), 0, SPLIT_D, D)
    rq = Reduce(link, wg, (q1a, q1b, q2a, q2b, q3a, q3b), 0, SPLIT_Q, 896)
    rp = Reduce(link, dwp, (p1a, p1b, p2a, p2b, p3a, p3b), 0, SPLIT_P, D)
    for n, red in ((0, ra), (1, rb)):
        cols = slice(n * 768, n * 768 + 768)
        for i in range(3):
            t = tn(hm[:, i * 384 : i * 384 + 384], coef[:, cols])
            for q in range(8):
                row = i * 384 + q * 48
                f, off = row // 144, row % 144
                dwg[f // 4, f // 2 % 2, f % 2, off : off + 48, cols] = t[q * 48 : q * 48 + 48].astype(BF)
        red.hop1()
    spread_got = fetch.go(spread_in, wg)
    for i in range(2):
        store_tiles(tn(hid[:, i * 384 : i * 384 + 384], dmlp[...]), dwd, i * 384, 96, None)
    rd.hop1()
    link.settle(hred.s1, hred.s3)
    mred = RowReduce(link, rsend, mrecv)
    mred.give(3, nn(hid[at_3, :], wdf()))
    mred.give(1, nn(hid[at_1, :], wdf()))
    bo[...] = nn(hid[at_m, :], wdf()).astype(BF)
    for c in gets:
        c.wait()
    hred.arrive()

    def mid_back(i, carry):
        rows = at(i, 32)
        mine = pl.ds(pl.multiple_of(m * TOK + i * 32, 32), 32)
        d = own32[rows, :] + hred.total(rows)
        a = attn_out[rows, :]
        n, recip = norm_rows(tokp[rows, :].astype(F32) + modv[2:3, :] * a)
        small[1:2, :] += jnp.sum(d, 0, keepdims=True)
        small[2:3, :] += jnp.sum(d * n, 0, keepdims=True)
        g = og[rows, :].astype(F32) + norm_rows_back(d * (1.0 + modv[4:5, :]), n, recip)
        gu[rows, 0:D] = g
        small[3:4, :] += jnp.sum(g * a, 0, keepdims=True)
        low = (modv[2:3, :] * g).astype(BF)
        dattn[mine, :] = low
        small[5:6, :] += jnp.sum(low.astype(F32), 0, keepdims=True)
        small[4:5, :] += jnp.sum(dmlp[mine, :].astype(F32), 0, keepdims=True)
        return carry

    lax.fori_loop(0, 8, mid_back, 0)
    da_all = RowGather(link, dattn)
    link.settle(hred.s2, hm_all.far, hm_all.near, hm_all.last)
    ha_got = fetch.go(ha_in, dmlp)
    mred.keep_far(nn(hid[at_2, :], wdf()))
    da_all.near_done()

    def pair_of(n):
        item = here.zl + (1 - 2 * here.zl) * (n // 4)
        return item, item * 4 + n % 4

    def pair_copies(n):
        p = pair_of(n)[1]
        s = n % 2
        return (
            pltpu.make_async_copy(raw_in.at[p], raw.at[s], lsem.at[base + 2 * s]),
            pltpu.make_async_copy(rot_in.at[p], rot.at[s], lsem.at[base + 2 * s + 1]),
        )

    for c in pair_copies(0):
        c.start()
    get_wp.wait()
    for c in gets2:
        c.wait()

    def back_proj(rows):
        hid[rows, 0:512] = nt(dattn[rows, :], wp[...].reshape(512, D)).astype(BF)

    def attend_back(n, carry):
        item, p = pair_of(n)
        s = n % 2
        lanes = at(n % 4, 128)
        for c in pair_copies(n):
            c.wait()

        @pl.when(n < 7)
        def _():
            for c in pair_copies(n + 1):
                c.start()

        dk = jnp.zeros((512, 128), F32)
        dv = jnp.zeros((512, 128), F32)

        def head_back_store(d, t, rows, out_rows):
            cos, sina, sinb = tabs[0, rows, :], tabs[1, rows, :], tabs[2, rows, :]
            v = raw[s, t, rows, :]
            recip = lax.rsqrt(jnp.sum(v * v, -1, keepdims=True) * (1.0 / HEAD) + EPSILON)
            dn = turn_back(d, cos, sina, sinb)
            dgain[t : t + 1, :] += jnp.sum(dn * v * recip, 0, keepdims=True)
            u = dn * gains[t : t + 1, :]
            mean = jnp.sum(u * v, -1, keepdims=True) * (1.0 / HEAD)
            res = recip * u - v * (recip * recip * recip * mean)
            coef[out_rows, at(t * 4 + n % 4, 128)] = res.astype(BF)

        for half in range(2):
            rows = pl.ds(half * TOK, TOK)
            out_rows = pl.ds(pl.multiple_of(item * 512 + half * TOK, TOK), TOK)
            do = hid[out_rows, lanes]
            e = jnp.exp2(nt(rot[s, 0, rows, :], rot[s, 1]) * ROOT2 + maskb[item])
            pf = e * (1.0 / jnp.sum(e, -1, keepdims=True))
            dp = nt(do, rot[s, 2])
            delta = jnp.sum(pf * dp, -1, keepdims=True)
            ds = (pf * (dp - delta)).astype(BF)
            dq = nn(ds, rot[s, 1]) * ROOT
            dk += tn(ds, rot[s, 0, rows, :])
            dv += tn(pf.astype(BF), do)
            head_back_store(dq, 0, rows, out_rows)
        dk = dk * ROOT
        for half in range(2):
            rows = pl.ds(half * TOK, TOK)
            out_rows = pl.ds(pl.multiple_of(item * 512 + half * TOK, TOK), TOK)
            head_back_store(dk[half * TOK : half * TOK + TOK], 1, rows, out_rows)
        coef[at(item, 512), at(8 + n % 4, 128)] = dv.astype(BF)
        return carry

    back_proj(at_m)
    back_proj(at_1)
    lax.fori_loop(0, 3, attend_back, 0)
    da_all.pass_on()
    mred.pass_on()
    ra.hop2()
    lax.fori_loop(3, 4, attend_back, 0)
    da_all.last_done()
    rb.hop2()
    back_proj(at_2)
    back_proj(at_3)
    store_tiles(tn(att[...], dattn[...]), dwp, 0, 64, PAD)
    rp.hop1()
    ra.hop3()
    lax.fori_loop(4, 5, attend_back, 0)
    rd.hop2()
    rb.hop3()
    lax.fori_loop(5, 6, attend_back, 0)
    mred.arrive()

    def finish_out(i, carry):
        rows = at(i, 32)
        o = bo[rows, :].astype(F32) + bd[...] + mred.total(rows)
        small[0:1, :] += jnp.sum(og[rows, :].astype(F32) * o, 0, keepdims=True)
        mid = tokp[rows, :].astype(F32) + modv[2:3, :] * attn_out[rows, :]
        bo[rows, :] = ((mid + modv[5:6, :] * o) * valid[rows, :]).astype(BF)
        return carry

    lax.fori_loop(0, 8, finish_out, 0)
    bo[...] = nt(bo[...], perm[...]).astype(BF)
    b_sent, b_got = link.scatter(
        lambda j: bo.at[pl.ds(j * 64, 64)], bout.at[here.z], here.item_source, here.z
    )
    lax.fori_loop(6, 7, attend_back, 0)
    rp.hop2()
    lax.fori_loop(7, 8, attend_back, 0)
    spread_got.wait()

    def squeeze(rows):
        v = coef[rows, :]
        dbq[0:1, :] += jnp.sum(v.astype(F32), 0, keepdims=True)
        hm[rows, 0:864] = nt(v, wg[...].reshape(D, 1536)[0:864]).astype(BF)

    def to_input(rows):
        return nt(hm[rows, 0:864], wq[...].reshape(D, 864))

    link.settle(mred.s1, mred.s2, mred.s3)
    tred = RowReduce(link, rsend, rrecv)
    squeeze(at_3)
    tred.give(3, to_input(at_3))
    squeeze(at_2)
    tred.keep_far(to_input(at_2))
    tred.pass_on()
    rd.hop3()
    squeeze(at_1)
    tred.give(1, to_input(at_1))
    squeeze(at_m)
    own32[...] = to_input(at_m)
    pk[...] = jnp.zeros_like(pk)
    bq4[...] = jnp.zeros_like(bq4)
    bg4[...] = jnp.zeros_like(bg4)
    bq4[m] = dbq[0:1, :]
    bg4[m] = dbg[0:1, :]
    for t in range(2):
        for e in range(2):
            to_ = t * 72 + e * UNIT
            line[:, to_ : to_ + UNIT] = dgain[t : t + 1, e * 64 : e * 64 + UNIT]
    for s in range(32):
        x, c, z, y = s // 16, s // 8 % 2, s // 2 % 4, s % 2
        for q in range(3):
            piece, unit = divmod(2 * s + q, 32) if q < 2 else (2, s)
            _, member, spot = shard_parts(unit)
            from_ = piece * 512 + spot * 64
            pk[x, c, y, z, 1:2, q * UNIT : q * UNIT + UNIT] = bq4[member, :, from_ : from_ + UNIT]
        from_ = shard_parts(s)[0] * UNIT
        pk[x, c, y, z, 1:2, 108:144] = small[5:6, from_ : from_ + UNIT]
        pk[x, c, y, z, 1:2, 144:180] = small[4:5, from_ : from_ + UNIT]
        for q in range(2):
            piece, unit = divmod(2 * s + q, 32)
            _, member, spot = shard_parts(unit)
            from_ = piece * 768 + spot * 96
            pk[x, c, y, z, 2:3, q * 96 : q * 96 + 96] = bg4[member, :, from_ : from_ + 96]
        pk[x, c, y, z, 3:4, 0:144] = line[:, 0:144]
    full_slope = silu_slope(condg[here.dp])
    for b in range(8):
        slope[b] = full_slope[:, b * 144 : b * 144 + 144]
    ha_got.wait()
    for i in range(3):
        store_tiles(tn(dmlp[:, i * 384 : i * 384 + 384], hm[:, 0:864]), wg, i * 384, 48, None)
    rq.hop1()
    rp.hop3()

    def hand_out(reds, base_row, cols, out):
        rows = slice(base_row, base_row + 4 * PAD)
        for red in reds:
            left, right = red.done()
            coef[rows, red.lo : red.split] = tn(pick[...], left).astype(BF)
            coef[rows, red.split : red.hi] = tn(pick[...], right).astype(BF)

        def share(k):
            return coef.at[pl.ds(pl.multiple_of(base_row + k * PAD, 16), PAD), pl.ds(0, cols)]

        over = [link.send(share(here.mate(r)[0]), out.at[m], here.mate(r)[1]) for r in (2, 3, 1)]
        return over, fetch.go(share(m), out.at[m])

    g_over, g_own = hand_out((ra, rb), 0, 1536, fg)
    tred.arrive()

    def first_back(i, carry):
        rows = at(i, 32)
        d = own32[rows, :] + tred.total(rows)
        n, recip = norm_rows(tokp[rows, :].astype(F32))
        small[6:7, :] += jnp.sum(d, 0, keepdims=True)
        small[7:8, :] += jnp.sum(d * n, 0, keepdims=True)
        g = gu[rows, 0:D] + norm_rows_back(d * (1.0 + modv[1:2, :]), n, recip)
        to[rows, :] = g.astype(BF)
        return carry

    lax.fori_loop(0, 8, first_back, 0)
    rows_of = (6, 7, 3, 1, 2, 0)
    for s in range(32):
        x, c, z, y = s // 16, s // 8 % 2, s // 2 % 4, s % 2
        for q in range(6):
            piece, unit = divmod(6 * s + q, 32)
            from_ = shard_parts(unit)[0] * UNIT
            row = rows_of[piece]
            pk[x, c, y, z, 0:1, q * UNIT : q * UNIT + UNIT] = small[row : row + 1, from_ : from_ + UNIT]
    ns = []
    for r in range(1, 8):
        x, c, y, dev = near(here, r)
        ns.append(link.send(pk.at[x, c, y], q1.at[here.x, here.c, here.y], dev))
    q1[here.x, here.c, here.y] = pk[here.x, here.c, here.y]
    rq.hop2()
    to[...] = nt(to[...], perm[...]).astype(BF)
    for n in ns:
        n.wait_recv()
    for z in range(4):
        for x in range(2):
            for y in range(2):
                d = x * 2 + y
                m2[z, d : d + 1, :] = q1[x, 0, y, z, 0:1, :] + q1[x, 1, y, z, 0:1, :]
        total = q1[0, 0, 0, z, 1:4, :]
        for i in range(1, 8):
            total += q1[i // 4, i // 2 % 2, i % 2, z, 1:4, :]
        m2[z, 4:7, :] = total
    zs = []
    for r in (1, 2, 3):
        z, dev = along_z(here, r)
        zs.append(link.send(m2.at[z], q2.at[here.z], dev))
    sent, got = link.scatter(
        lambda j: to.at[pl.ds(j * 64, 64)], dtok.at[here.z], here.item_source, here.z
    )
    rq.hop3()
    q2[here.z] = m2[here.z]
    dm[...] = jnp.zeros_like(dm)
    v = condg[...].reshape(32, D)
    act = (v * jax.nn.sigmoid(v)).astype(BF)

    def plain(red, out):
        left, right = red.done()
        both = nt(left, perm[:, 0 : red.split]) + nt(right, perm[:, red.split : D])
        out[...] = both[0 : out.shape[0]]

    for c in zs:
        c.wait_recv()
    for z in range(4):
        for d in range(4):
            dm[d * 8 + z : d * 8 + z + 1, :] = q2[z, d : d + 1, 0:216]
    sums[...] = q2[0] + q2[1] + q2[2] + q2[3]
    for out, line_at, lo in (
        (o_qk, 4, 0), (o_v, 4, 72), (o_p, 4, 108), (o_d, 4, 144), (o_gu, 5, 0), (o_qg, 6, 0), (o_kg, 6, 72),
    ):
        out[...] = sums[line_at : line_at + 1, lo : lo + out.shape[1]]
    dbm[...] = jnp.sum(dm[...], 0, keepdims=True)
    d3 = three(dm[...])
    da = nn(d3, w_mod_t[...])
    da = da[0:32] + da[32:64] + da[64:96]
    for b in range(8):
        for d in range(4):
            e0[d, b % 2, b // 2] = da[d * 8 : d * 8 + 8, b * 144 : b * 144 + 144]
    ns = []
    for r in range(1, 8):
        x, c, y, dev = near(here, r)
        ns.append(link.send(e0.at[x * 2 + c, y], e1.at[here.x, here.c, here.y], dev))
    e1[here.x, here.c, here.y] = e0[here.dp, here.y]
    plain(rd, fd)
    outs = [fetch.go(fd, fd_out)]
    for n in ns:
        n.wait_recv()
    total = e1[0, 0, 0]
    for i in range(1, 8):
        total += e1[i // 4, i // 2 % 2, i % 2]
    e2[...] = total
    zs = []
    for r in (1, 2, 3):
        z, dev = along_z(here, r)
        zs.append(link.send(e2.at[z], e3.at[here.z], dev))
    e3[here.z] = e2[here.z]
    plain(rp, fp)
    outs.append(fetch.go(fp, fp_out))
    dwm[...] = tn(d3, jnp.concatenate([act, act, act], 0))
    outs.append(fetch.go(dwm, dwm_out))
    g_own.wait()
    for c in g_over:
        c.wait_recv()
    by_column(fg, g_gu, 192, 2)
    outs.append(fetch.go(g_gu, g_gu_out))
    q_over, q_own = hand_out((rq,), 4 * PAD, 896, fq)
    for c in zs:
        c.wait_recv()
    both = (e3[0] + e3[1] + e3[2] + e3[3]) * slope[here.z * 2 + here.y]
    dcond[...] = both[0:4]
    q_own.wait()
    for c in q_over:
        c.wait_recv()
    by_column(fq, g_qkv, 72, 3)
    outs.append(fetch.go(g_qkv, g_qkv_out))
    b_got(bo.at[pl.ds(0, 64)], lambda j: bout.at[j])
    got(to.at[pl.ds(0, 64)], lambda j: dtok.at[j])
    for c in outs:
        c.wait()
    link.finish()
    b_sent()
    sent()


def call(kernel, ident, outs, scratch, args, hbm=(), smem=(), hbm_out=(), sems=64, local=32):
    vm = pl.BlockSpec(memory_space=pltpu.VMEM)
    hb = pl.BlockSpec(memory_space=pltpu.HBM)
    sm = pl.BlockSpec(memory_space=pltpu.SMEM)
    return pl.pallas_call(
        kernel,
        out_shape=[jax.ShapeDtypeStruct(s, t) for s, t in outs],
        in_specs=[hb if i in hbm else sm if i in smem else vm for i in range(len(args))],
        out_specs=[hb if i in hbm_out else vm for i in range(len(outs))],
        scratch_shapes=scratch + [pltpu.SemaphoreType.DMA((sems,)), pltpu.SemaphoreType.DMA((sems,))]
        + ([pltpu.SemaphoreType.DMA((local,))] if hbm else []),
        compiler_params=pltpu.CompilerParams(
            collective_id=ident, has_side_effects=True, vmem_limit_bytes=LIMIT
        ),
    )(*args)


def local(
    tokens, conditioning, heights, widths, cotangent, w_mod, b_mod, w_qkv, b_qkv, query_gain, key_gain,
    w_proj, b_proj, w_gu, b_gu, w_down, b_down,
):
    args = (
        tokens, conditioning, heights, widths, cotangent, w_mod, b_mod, w_qkv, b_qkv, query_gain, key_gain,
        w_proj, b_proj, w_gu, b_gu, w_down, b_down,
    )
    sizes = tuple(lax.axis_size(a) for a in ("dp", "row", "col"))
    if sizes != (4, 4, 2) or tokens.shape != (4, 4, 16, D):
        return general(*args)
    every = ("dp", "row", "col")
    perm, spread, pick, tabs = constants()
    w_mod_t = w_mod.T
    full = (GROUP, D)
    block = (TOK, D)
    weights = [(2, 2, 2, 144, 864), (2, 2, 2, 64, D), (2, 2, 2, 144, 1536), (2, 2, 2, 96, D)]
    pairs = [((8, 2, 512, 128), F32), ((8, 3, 512, 128), BF)]
    small_rows = pltpu.VMEM((4, 8, 256), F32)
    (
        wq_all, wp_all, wg_all, wd_all, ha, raw, rot, att, hm, dmlp, tokp, og, attn_out,
        condg, modv, bg, bd, gains, maskb, valid,
    ) = call(
        kernel_a, 0,
        [(w, BF) for w in weights] + [(full, BF)] + pairs + [((GROUP, 512), BF)]
        + [(block, BF), (full, BF), (block, BF), (block, BF)]
        + [
            (s, F32)
            for s in (block, (4, 8, D), (8, D), (1, 1536), (1, D), (8, 128), (2, 1, 512), (TOK, 1))
        ],
        [pltpu.VMEM(w, BF) for w in weights] + [pltpu.VMEM(full, BF)] + [pltpu.VMEM(w, t) for w, t in pairs]
        + [
            pltpu.VMEM((GROUP, 512), BF), pltpu.VMEM((4, PAD, 864), BF), pltpu.VMEM((4, PAD, 1536), BF),
            pltpu.VMEM(block, BF), pltpu.VMEM(block, BF), pltpu.VMEM((D, 1536), BF), pltpu.VMEM((3, TOK, D), BF),
            pltpu.VMEM((3, TOK, D), BF), pltpu.VMEM(block, F32),
            pltpu.VMEM((4, PAD, 864), BF), pltpu.VMEM((4, PAD, 1536), BF), pltpu.VMEM((4, PAD, 1536), F32),
            pltpu.VMEM((8, D), F32), small_rows, small_rows, pltpu.VMEM((4, 4, 8, 256), F32),
            pltpu.VMEM((2, 2, 2, 4, 8, 256), F32), pltpu.VMEM((4, 1, 1536), F32), pltpu.VMEM((4, 1, 1536), F32),
            pltpu.VMEM((1, D), F32), pltpu.VMEM(block, BF), pltpu.VMEM(full, BF), pltpu.VMEM(block, BF),
            pltpu.VMEM(block, BF), pltpu.VMEM(block, F32), pltpu.VMEM((D, D), BF), pltpu.VMEM((864, 1536), BF),
            pltpu.VMEM((3, 512, 128), F32), pltpu.VMEM((8, 256), F32),
        ],
        (
            tokens.reshape(4, 64, D), cotangent.reshape(4, 64, D), w_qkv, w_gu, w_proj, w_down, conditioning, w_mod_t,
            b_mod, b_qkv, b_proj, b_down, b_gu, query_gain, key_gain, heights, widths, perm, spread, pick, tabs,
        ),
        hbm=(0, 1, 17, 18, 20),
        smem=(15, 16),
        hbm_out=range(13),
        sems=128,
    )
    spread = jnp.pad(spread, ((0, D - 864), (0, 0))).reshape(2, 2, 2, 144, 1536)
    dtok, bout, g_w_qkv, g_w_gu, fp, fd, g_w_mod, g_b_mod, d_cond, o_qk, o_v, o_p, o_d, o_gu, o_qg, o_kg = call(
        kernel_b, 1,
        [
            ((4, 64, D), BF), ((4, 64, D), BF), ((UNIT, 3456), F32), ((UNIT, 6144), F32), ((UNIT, D), F32),
            ((96, D), F32), ((216, D), F32), ((1, 216), F32), ((4, 144), F32),
        ]
        + [((1, n), F32) for n in (72, 36, 36, 36, 192, 72, 72)],
        [
            pltpu.VMEM((2, 2, 2, 144, 1536), BF), pltpu.VMEM((2, 2, 2, 96, D), BF), pltpu.VMEM(full, BF),
            pltpu.VMEM(full, BF), pltpu.VMEM(block, BF), pltpu.VMEM(block, BF), pltpu.VMEM(block, F32),
            pltpu.VMEM((GROUP, 512), BF), pltpu.VMEM((2, 2, 2, 64, D), BF), pltpu.VMEM((2, 2, 2, 144, 864), BF),
            pltpu.VMEM((D, D), BF), pltpu.VMEM((3, 512, 128), F32), pltpu.VMEM((TOK, 1536), F32),
            pltpu.VMEM((GROUP, 1536), BF), pltpu.VMEM((GROUP, 768), BF), pltpu.VMEM((3, TOK, D), BF),
            pltpu.VMEM((3, TOK, D), BF), pltpu.VMEM((3, TOK, D), BF), pltpu.VMEM(block, F32),
            pltpu.VMEM((2, 2, 2, 144, 1536), BF), pltpu.VMEM((2, 2, 2, 96, D), BF), pltpu.VMEM((2, 2, 2, PAD, D), BF),
            pltpu.VMEM(full, BF), pltpu.VMEM((2, 2, 512, 128), F32), pltpu.VMEM((2, 3, 512, 128), BF),
            pltpu.VMEM(block, BF), pltpu.VMEM(block, BF), pltpu.VMEM((4, PAD, 896), BF), pltpu.VMEM((4, PAD, 1536), BF),
            pltpu.VMEM((8, D), F32), pltpu.VMEM((8, 1536), F32), pltpu.VMEM((8, 1536), F32), pltpu.VMEM((8, 128), F32),
            pltpu.VMEM((2, 2, 2, 4, 8, 256), F32), pltpu.VMEM((2, 2, 2, 4, 8, 256), F32), small_rows, small_rows,
            pltpu.VMEM((32, 216), F32), pltpu.VMEM((4, 2, 4, 8, 144), F32), pltpu.VMEM((2, 2, 2, 4, 8, 144), F32),
            pltpu.VMEM((4, 8, 144), F32), pltpu.VMEM((4, 8, 144), F32), pltpu.VMEM((1, 256), F32),
            pltpu.VMEM((4, 1, 1536), F32), pltpu.VMEM((4, 1, 1536), F32), pltpu.VMEM((8, 8, 144), F32),
            pltpu.VMEM((UNIT, 3456), F32), pltpu.VMEM((UNIT, 6144), F32), pltpu.VMEM((UNIT, D), F32),
            pltpu.VMEM((96, D), F32), pltpu.VMEM((216, D), F32), pltpu.VMEM((8, 256), F32),
        ]
        + Reduce.buffers(144, 768, 384) * 2 + Reduce.buffers(96, D, SPLIT_D)
        + Reduce.buffers(144, 896, SPLIT_Q) + Reduce.buffers(PAD, D, SPLIT_P),
        (
            wg_all, wd_all, hm, dmlp, tokp, og, attn_out, att, wp_all, wq_all, ha, raw, rot, perm, spread, tabs,
            modv, bg, bd, gains, maskb, valid, pick, condg, w_mod_t,
        ),
        hbm=range(16),
        hbm_out=range(7),
        sems=128,
    )

    return (
        bout.reshape(tokens.shape),
        dtok.reshape(tokens.shape).astype(F32),
        d_cond,
        g_w_mod.T,
        g_b_mod[0],
        g_w_qkv,
        o_qk[0],
        o_v[0],
        o_qg[0],
        o_kg[0],
        fp,
        o_p[0],
        g_w_gu,
        o_gu[0],
        fd,
        o_d[0],
    )


def solution(mesh):
    in_specs = (
        P("dp", "row", "col", None),
        P("dp", None),
        P("dp"),
        P("dp"),
        P("dp", "row", "col", None),
        P(None, ("dp", "row", "col")),
        P(("dp", "row", "col")),
        P(("dp", "row", "col"), None),
        P(("dp", "row", "col")),
        P(),
        P(),
        P(("dp", "row", "col"), None),
        P(("dp", "row", "col")),
        P(("dp", "row", "col"), None),
        P(("dp", "row", "col")),
        P(("dp", "row", "col"), None),
        P(("dp", "row", "col")),
    )
    out_specs = (
        P("dp", "row", "col", None),
        P("dp", "row", "col", None),
        P("dp", ("row", "col")),
        P(None, ("dp", "row", "col")),
        P(("dp", "row", "col")),
        P(("dp", "row", "col"), None),
        P(("dp", "row", "col")),
        P(("dp", "row", "col")),
        P(),
        P(),
        P(("dp", "row", "col"), None),
        P(("dp", "row", "col")),
        P(("dp", "row", "col"), None),
        P(("dp", "row", "col")),
        P(("dp", "row", "col"), None),
        P(("dp", "row", "col")),
    )
    return jax.shard_map(local, mesh=mesh, in_specs=in_specs, out_specs=out_specs, check_vma=False)
```
